32 devices in a mesh: gx: 4 (over y, x), gy: 8 (over z, core).
Axes of the slice: x: 2, y: 2, z: 4, core: 2. Of those that a mesh axis runs over, the one named last changes fastest.
Arguments:
- params: bfloat16 [128, 8, 32, 128], P(None, 'gx', 'gy'), may hold values from -6 to 6
- predicted: float32 [4, 8, 128, 128], P('gx', 'gy'), may hold values from -6 to 6
- measured_value: float32 [4, 8, 128], P('gx', 'gy'), may hold values from -6 to 6
- measurement_variance: float32 [4, 8, 128], P('gx', 'gy'), may hold values from 0.25 to 1
- observation_jitter: float32 [4, 8, 128, 128], P('gx', 'gy'), may hold values from -6 to 6
- obs_block: int32 [4, 8, 128], replicated, may hold values from 0 to 7
- taper_radius: int32 [8, 32], P('gx', 'gy'), may hold values from 1 to 2
- taper_pattern: int32 [8, 32, 25], P('gx', 'gy'), may hold values 0 or 1
Outputs:
- updated: bfloat16 [128, 8, 32, 128], P('gy', 'gx')
The draws below stay inside these ranges and needn't reach their ends.
All inputs are finite; a program needn't handle non-finite values. No bound on the sum of `taper_pattern` on one device may be relied on, other than what follows from the above.
Results may differ from the reference program's by a relative error of at most 0.0039.
Values may be sent and summed in bfloat16 or wider, within the bound.
No kernel may reach another device: no remote copies, remote signals or barrier semaphores. Data moves between devices by JAX's collectives and lax.ppermute only.
A program may use at most 64 MiB of HBM per device.

```python
import math
import jax
import jax.numpy as jnp
from jax import lax

CELLS = 128
BLK_X = 2
BLK_Y = 4
OBS_TILE = 128
PATTERN = 25
MEMBERS = 128
NGX = 4
NGY = 8
NBX = 8
NBY = 32


def set_ends(drawn, key, least, top_value):
    longest = drawn.shape.index(max(drawn.shape))
    spots = []
    for shift in (0, 1):
        where = [jax.random.randint(jax.random.fold_in(key, axis), (), 0, length) for axis, length in enumerate(drawn.shape)]
        where[longest] = (where[longest] + shift) % drawn.shape[longest]
        spots.append(tuple(where))
    return drawn.at[spots[0]].set(least).at[spots[1]].set(top_value)


def levels(rng, shape, shards, low, top_value):
    level, own = 1.0, jax.random.fold_in(rng, 6)
    for dim, parts in shards:
        draws = jnp.exp(jax.random.uniform(jax.random.fold_in(own, dim), (parts,), jnp.float32, low / len(shards), top_value / len(shards)))
        level = level * jnp.repeat(draws, shape[dim] // parts).reshape([-1 if axis == dim else 1 for axis in range(len(shape))])
    return level


def normal_values(own_key, shape, scale, limit, pieces=(), held_as=jnp.bfloat16):
    entries = jax.random.normal(own_key, shape, jnp.float32) * scale
    if len(pieces) > 0:
        entries = levels(own_key, shape, pieces, -0.22, 0.18) * entries
    return jnp.clip(entries, min=-limit, max=limit).astype(held_as)


def setup_inputs(seed: int = 0) -> dict:
    splits = jax.random.split(jax.random.key(seed), 9)
    params = normal_values(splits[0], (MEMBERS, NBX, NBY, CELLS), 1.0, 6.0, ((1, 4), (2, 8)))
    predicted = normal_values(splits[1], (NGX, NGY, MEMBERS, OBS_TILE), 1.0, 6.0, ((0, 4), (1, 8)), jnp.float32)
    measured_value = normal_values(splits[2], (NGX, NGY, OBS_TILE), 1.0, 6.0, ((0, 4), (1, 8)), jnp.float32)
    measurement_variance = jnp.clip(jnp.exp(math.log(1.0) - 1.3862944 * jax.random.uniform(splits[3], (NGX, NGY, OBS_TILE), jnp.float32) ** levels(splits[3], (NGX, NGY, OBS_TILE), ((0, 4), (1, 8)), -0.2, 0.2)), 0.25, 1.0)
    observation_jitter = normal_values(splits[4], (NGX, NGY, MEMBERS, OBS_TILE), 1.0, 6.0, ((0, 4), (1, 8)), jnp.float32)
    obs_block = set_ends(jax.random.randint(splits[5], (NGX, NGY, OBS_TILE), 0, BLK_X * BLK_Y), jax.random.fold_in(splits[5], 1), 0, (BLK_X * BLK_Y) - 1).astype(jnp.int32)
    taper_radius = set_ends(jax.random.randint(splits[6], (NBX, NBY), 1, 3), jax.random.fold_in(splits[6], 1), 1, 2).astype(jnp.int32)
    taper_pattern = set_ends((jax.random.randint(splits[7], (NBX, NBY, PATTERN), 0, 4) < 3).astype(jnp.int32), jax.random.fold_in(splits[7], 1), 0, 1)
    return dict(params=params, predicted=predicted, measured_value=measured_value, measurement_variance=measurement_variance, observation_jitter=observation_jitter, obs_block=obs_block, taper_radius=taper_radius, taper_pattern=taper_pattern)


def tapers(radius, pattern, own_x, own_y, obs_x, obs_y):
    step_x = obs_x[None, :] - own_x[:, None]
    step_y = obs_y[None, :] - own_y[:, None]
    inside = (jnp.abs(step_x) <= 2) & (jnp.abs(step_y) <= 2)
    offset = (step_x + 2) * 5 + (step_y + 2)
    slots = jnp.arange(PATTERN, dtype=jnp.int32)
    picked = lax.optimization_barrier(jnp.sum(jnp.where(offset[:, :, None] == slots, pattern[:, None, :], 0), axis=2))
    reach = (radius + 1).astype(jnp.float32)
    spread = (step_x * step_x + step_y * step_y).astype(jnp.float32)
    shaped = jnp.maximum(1.0 - spread / (reach * reach)[:, None], 0.0)
    return jnp.where(inside, picked.astype(jnp.float32), 0.0) * shaped

def obs_places(obs_map, tiles_x, tiles_y):
    place_x = tiles_x[:, None, None] * BLK_X + obs_map // BLK_Y
    place_y = tiles_y[None, :, None] * BLK_Y + obs_map % BLK_Y
    return (place_x.reshape(-1), place_y.reshape(-1))

def contribution(anomaly, d_set, z_set, obs_map, tiles_x, tiles_y, own_x, own_y, radius, pattern):
    members = anomaly.shape[0]
    blocks = own_x.shape[0]
    place_x, place_y = obs_places(obs_map, tiles_x, tiles_y)
    weights = tapers(radius, pattern, own_x, own_y, place_x, place_y) / (members - 1)
    cross = lax.dot_general(anomaly.astype(jnp.float32), d_set.astype(jnp.float32), (((0,), (2,)), ((), ())), preferred_element_type=jnp.float32)
    complete_extent = cross.shape
    gain = (cross.reshape(blocks, -1, weights.shape[1]) * weights[:, None, :]).reshape(complete_extent).astype(jnp.bfloat16)
    return lax.dot_general(z_set.astype(jnp.float32), gain.astype(jnp.float32), (((0, 1, 3), (1, 2, 3)), ((), ())), preferred_element_type=jnp.float32)

def weigh(d_tile, observation_residual, variance, obs_map):
    members = d_tile.shape[0]
    gram = jnp.dot(d_tile.T.astype(jnp.float32), d_tile.astype(jnp.float32), preferred_element_type=jnp.float32) / (members - 1)
    same = obs_map[:, None] == obs_map[None, :]
    system = jnp.where(same, gram, 0.0) + jnp.diag(variance)
    factor = jnp.linalg.cholesky(system)
    solved = jax.scipy.linalg.cho_solve((factor, True), observation_residual.T)
    return solved.T.astype(jnp.bfloat16)

def weigh_packed(packed):
    return weigh(packed[0], packed[1], packed[2], packed[3])

def reference(params, predicted, measured_value, measurement_variance, observation_jitter, obs_block, taper_radius, taper_pattern):
    members = params.shape[0]
    blocks = BLK_X * BLK_Y
    tiles = NGX * NGY
    predicted_deviation = (predicted - lax.optimization_barrier(jnp.mean(predicted, axis=2, keepdims=True))).astype(jnp.bfloat16)
    observation_residual = measured_value[:, :, None, :] + jnp.sqrt(measurement_variance)[:, :, None, :] * observation_jitter - predicted
    weighted = lax.map(weigh_packed, (predicted_deviation.reshape(tiles, members, OBS_TILE), observation_residual.reshape(tiles, members, OBS_TILE), measurement_variance.reshape(tiles, OBS_TILE), obs_block.reshape(tiles, OBS_TILE)))
    weighted = weighted.reshape(NGX, NGY, members, OBS_TILE)
    stacked = jnp.stack([predicted_deviation, weighted], axis=2)
    padded = jnp.pad(stacked, ((1, 1), (1, 1), (0, 0), (0, 0), (0, 0)))
    map_pad = jnp.pad(obs_block, ((1, 1), (1, 1), (0, 0)))
    adjacent_everything = jnp.arange(3, dtype=jnp.int32) - 1
    local_ids = jnp.arange(blocks, dtype=jnp.int32)

    def per_tile(index):
        tile_x = (index // NGY).astype(jnp.int32)
        tile_y = (index % NGY).astype(jnp.int32)
        zero = jnp.int32(0)
        near = lax.dynamic_slice(padded, (tile_x, tile_y, zero, zero, zero), (3, 3, 2, members, OBS_TILE))
        near_map = lax.dynamic_slice(map_pad, (tile_x, tile_y, zero), (3, 3, OBS_TILE))
        start_x = (tile_x * BLK_X).astype(jnp.int32)
        start_y = (tile_y * BLK_Y).astype(jnp.int32)
        own_params = lax.dynamic_slice(params, (zero, start_x, start_y, zero), (members, BLK_X, BLK_Y, CELLS))
        wide = own_params.astype(jnp.float32)
        anomaly = (wide - lax.optimization_barrier(jnp.mean(wide, axis=0, keepdims=True))).astype(jnp.bfloat16).reshape(members, blocks * CELLS)
        radius = lax.dynamic_slice(taper_radius, (start_x, start_y), (BLK_X, BLK_Y)).reshape(blocks)
        pattern = lax.dynamic_slice(taper_pattern, (start_x, start_y, zero), (BLK_X, BLK_Y, PATTERN)).reshape(blocks, PATTERN)
        own_x = start_x + local_ids // BLK_Y
        own_y = start_y + local_ids % BLK_Y
        delta = contribution(anomaly, near[:, :, 0], near[:, :, 1], near_map, tile_x + adjacent_everything, tile_y + adjacent_everything, own_x, own_y, radius, pattern)
        return (wide + delta.reshape(members, BLK_X, BLK_Y, CELLS)).astype(jnp.bfloat16)
    updated = lax.map(per_tile, jnp.arange(tiles, dtype=jnp.int32))
    updated = updated.reshape(NGX, NGY, members, BLK_X, BLK_Y, CELLS).transpose(2, 0, 3, 1, 4, 5)
    return updated.reshape(members, NGX * BLK_X, NGY * BLK_Y, CELLS)
```

```python
import functools

import jax
import jax.numpy as jnp
from jax import lax
from jax.experimental import pallas as pl
from jax.experimental.pallas import tpu as pltpu
from jax.sharding import PartitionSpec as P

CELLS = 128
BLK_X = 2
BLK_Y = 4
BLOCKS = BLK_X * BLK_Y
OBS_TILE = 128
PATTERN = 25
SMALL = 32

F32 = jnp.float32
BF16 = jnp.bfloat16


def iota(shape, dim):
    return lax.broadcasted_iota(jnp.int32, shape, dim)


def split3(x):
    high = x.astype(BF16)
    rest = x - high.astype(F32)
    mid = rest.astype(BF16)
    low = (rest - mid.astype(F32)).astype(BF16)
    return high, mid, low


def dot(a, b, dims, precision=None):
    return lax.dot_general(a, b, ((dims[0], dims[1]), ((), ())), precision=precision, preferred_element_type=F32)


def sweep(rows, count, x_ref, idx_ref, rank, size):
    row = iota((rows, OBS_TILE), 0)
    exists = row < size

    def step(t):
        x = x_ref[0:rows, :]
        pivot_row = x_ref[pl.ds(t, 1), :]
        spread = jnp.broadcast_to(pivot_row, (rows, OBS_TILE))
        column = jnp.take_along_axis(spread, idx_ref[0:rows, :], axis=1, mode="promise_in_bounds")
        column = jnp.where(exists, column, 0.0)
        at = jnp.broadcast_to(idx_ref[pl.ds(t, 1), :], (8, OBS_TILE))
        pivot = jnp.take_along_axis(spread[0:8], at, axis=1, mode="promise_in_bounds")[0:1]
        pivot = jnp.where(t < size, pivot, 1.0)
        own = rank == t
        scaled = jnp.where(own, -1.0, pivot_row) / pivot
        at_row = row == t
        column = jnp.where(at_row, -1.0, column)
        x_ref[0:rows, :] = jnp.where(at_row | own, 0.0, x) - column * scaled

    def pair(k, carry):
        step(2 * k)
        step(2 * k + 1)
        return carry

    lax.fori_loop(0, (count + 1) // 2, pair, 0)


def weigh_kernel(pred_ref, mv_ref, var_ref, jit_ref, obs_ref, out_ref, x_ref, idx_ref, full_ref):
    members = pred_ref.shape[2]
    tile_x = lax.axis_index("gx")
    tile_y = lax.axis_index("gy")
    square = (OBS_TILE, OBS_TILE)
    pred = pred_ref[0, 0]
    var = var_ref[0]
    mean = jnp.sum(pred, axis=0, keepdims=True) / members
    deviation = (pred - mean).astype(BF16)
    out_ref[0] = deviation
    obs = obs_ref[tile_x, pl.ds(tile_y, 1), :]
    groups = (iota((BLOCKS, OBS_TILE), 0) == obs).astype(BF16)
    same = dot(groups, groups, ((0,), (0,)))
    gram = dot(deviation, deviation, ((0,), (0,))) / (members - 1)
    row, col = iota(square, 0), iota(square, 1)
    system = jnp.where(same > 0.5, gram, 0.0) + jnp.where(row == col, var, 0.0)
    size = jnp.sum(same, axis=0, keepdims=True)
    count = jnp.max(size).astype(jnp.int32)
    size = size.astype(jnp.int32)
    rank = jnp.sum(jnp.where(row < col, same, 0.0), axis=0, keepdims=True).astype(jnp.int32)
    place = row == rank
    hot = place.astype(BF16)
    high, mid, low = split3(system)
    x_ref[...] = (
        dot(hot, low, ((1,), (0,))) + dot(hot, mid, ((1,), (0,))) + dot(hot, high, ((1,), (0,)))
    )
    numbered = jnp.where(place, col, 0).astype(F32).astype(BF16)
    idx_ref[...] = dot(numbered, same.astype(BF16), ((1,), (0,))).astype(jnp.int32)

    def solve(rows):
        sweep(rows, count, x_ref, idx_ref, rank, size)
        high, mid, low = split3(x_ref[0:rows, :])
        taken = hot[0:rows]
        full = dot(taken, low, ((0,), (0,))) + dot(taken, mid, ((0,), (0,))) + dot(taken, high, ((0,), (0,)))
        full_ref[...] = jnp.where(same > 0.5, -full, 0.0)

    @pl.when(count <= SMALL)
    def _():
        solve(SMALL)

    @pl.when(count > SMALL)
    def _():
        solve(OBS_TILE)

    innovation = mv_ref[0] + jnp.sqrt(var) * jit_ref[0, 0] - pred
    weighted = dot(innovation, full_ref[...], ((1,), (0,)), lax.Precision.HIGHEST)
    out_ref[1] = weighted.astype(BF16)


def weigh(predicted, measured_value, measurement_variance, observation_jitter, obs_block):
    members = predicted.shape[2]
    return pl.pallas_call(
        weigh_kernel,
        out_shape=jax.ShapeDtypeStruct((2, members, OBS_TILE), BF16),
        in_specs=[pl.BlockSpec(memory_space=pltpu.VMEM)] * 5,
        out_specs=pl.BlockSpec(memory_space=pltpu.VMEM),
        scratch_shapes=[
            pltpu.VMEM((OBS_TILE, OBS_TILE), F32),
            pltpu.VMEM((OBS_TILE, OBS_TILE), jnp.int32),
            pltpu.VMEM((OBS_TILE, OBS_TILE), F32),
        ],
        compiler_params=pltpu.CompilerParams(vmem_limit_bytes=16 * 2**20),
        name="weigh",
    )(predicted, measured_value, measurement_variance, observation_jitter, obs_block)


def prepare_kernel(params_ref, radius_ref, pattern_ref, obs_ref, turned_ref, taper_ref):
    members = params_ref.shape[1]
    tile_x = lax.axis_index("gx")
    tile_y = lax.axis_index("gy")
    count_x, count_y = obs_ref.shape[0], obs_ref.shape[1]
    for b in range(BLOCKS):
        block = params_ref[b].astype(F32)
        mean = jnp.sum(block, axis=0, keepdims=True) / members
        anomaly = block - mean
        turned_ref[b] = anomaly.T.astype(BF16)

    shape = (BLOCKS, OBS_TILE)
    block = iota(shape, 0)
    radius = jnp.zeros(shape, jnp.int32)
    for b in range(BLOCKS):
        radius = jnp.where(block == b, radius_ref[b // BLK_Y, b % BLK_Y], radius)
    reach = (radius + 1).astype(F32)
    reach = reach * reach
    pattern = pattern_ref[...].astype(F32)
    slots = [jnp.broadcast_to(pattern[:, p : p + 1], shape) for p in range(PATTERN)]
    for dx in range(3):
        for dy in range(3):
            at_x, at_y = tile_x + (dx - 1), tile_y + (dy - 1)
            valid = (at_x >= 0) & (at_x < count_x) & (at_y >= 0) & (at_y < count_y)
            at_x = jnp.clip(at_x, 0, count_x - 1)
            at_y = jnp.clip(at_y, 0, count_y - 1)
            obs = obs_ref[at_x, pl.ds(at_y, 1), :]
            step_x = (dx - 1) * BLK_X + (obs >> 2) - (block >> 2)
            step_y = (dy - 1) * BLK_Y + (obs & 3) - (block & 3)
            inside = (jnp.abs(step_x) <= 2) & (jnp.abs(step_y) <= 2) & valid
            offset = (step_x + 2) * 5 + (step_y + 2)
            picked = jnp.zeros(shape, F32)
            for p in range(PATTERN):
                picked = jnp.where(offset == p, slots[p], picked)
            spread = (step_x * step_x + step_y * step_y).astype(F32)
            shaped = jnp.maximum(1.0 - spread / reach, 0.0)
            taper_ref[dx * 3 + dy] = jnp.where(inside, picked, 0.0) * shaped / (members - 1)


def prepare(by_block, taper_radius, taper_pattern, obs_block):
    members = by_block.shape[1]
    return pl.pallas_call(
        prepare_kernel,
        out_shape=(
            jax.ShapeDtypeStruct((BLOCKS, CELLS, members), BF16),
            jax.ShapeDtypeStruct((9, BLOCKS, OBS_TILE), F32),
        ),
        in_specs=[
            pl.BlockSpec(memory_space=pltpu.VMEM),
            pl.BlockSpec(memory_space=pltpu.SMEM),
            pl.BlockSpec(memory_space=pltpu.VMEM),
            pl.BlockSpec(memory_space=pltpu.VMEM),
        ],
        out_specs=(pl.BlockSpec(memory_space=pltpu.VMEM), pl.BlockSpec(memory_space=pltpu.VMEM)),
        compiler_params=pltpu.CompilerParams(vmem_limit_bytes=16 * 2**20),
        cost_estimate=pl.CostEstimate(flops=4_000_000, bytes_accessed=1_000_000, transcendentals=0),
        name="prepare",
    )(by_block, taper_radius, taper_pattern.reshape(BLOCKS, PATTERN), obs_block)


def update_kernel(params_ref, turned_ref, taper_ref, own_ref, low_ref, high_ref, out_ref):
    share = out_ref.shape[2]
    near = [ref.at[dx] for dx in range(3) for ref in (low_ref, own_ref, high_ref)]
    deviations = jnp.concatenate([tile[0] for tile in near], axis=1)
    weighted = jnp.concatenate([tile[1] for tile in near], axis=1)

    def one(b, carry):
        cross = dot(turned_ref[b], deviations, ((1,), (0,)))
        taper = jnp.concatenate([taper_ref[t, pl.ds(b, 1), :] for t in range(9)], axis=1)
        gain = (cross * taper).astype(BF16)
        delta = dot(weighted, gain, ((1,), (1,)))
        updated = (params_ref[b].astype(F32) + delta).astype(BF16)
        for d in range(out_ref.shape[0]):
            out_ref[d, b] = updated[d * share : (d + 1) * share]
        return carry

    lax.fori_loop(0, BLOCKS, one, 0, unroll=True)


def update(by_block, turned, taper, own, low, high, parts):
    members = by_block.shape[1]
    return pl.pallas_call(
        update_kernel,
        out_shape=jax.ShapeDtypeStruct((parts, BLOCKS, members // parts, CELLS), BF16),
        in_specs=[pl.BlockSpec(memory_space=pltpu.VMEM)] * 6,
        out_specs=pl.BlockSpec(memory_space=pltpu.VMEM),
        compiler_params=pltpu.CompilerParams(vmem_limit_bytes=40 * 2**20),
        name="update",
    )(by_block, turned, taper, own, low, high)


def neighbours(block, axis):
    count = lax.axis_size(axis)
    low = lax.ppermute(block, axis, [(i, i + 1) for i in range(count - 1)])
    high = lax.ppermute(block, axis, [(i + 1, i) for i in range(count - 1)])
    return low, high


def per_device(
    params,
    predicted,
    measured_value,
    measurement_variance,
    observation_jitter,
    obs_block,
    taper_radius,
    taper_pattern,
):
    members = params.shape[0]
    parts = lax.axis_size("gy")
    by_block = params.reshape(members, BLOCKS, CELLS).transpose(1, 0, 2)
    own = weigh(predicted, measured_value, measurement_variance, observation_jitter, obs_block)
    low_x, high_x = neighbours(own, "gx")
    turned, taper = prepare(by_block, taper_radius, taper_pattern, obs_block)
    column = jnp.stack([low_x, own, high_x])
    low, high = neighbours(column, "gy")
    updated = update(by_block, turned, taper, column, low, high, parts)
    arrived = lax.all_to_all(updated, "gy", split_axis=0, concat_axis=0, tiled=True)
    share = members // parts
    arrived = arrived.reshape(parts, BLK_X, BLK_Y, share, CELLS).transpose(3, 1, 0, 2, 4)
    return arrived.reshape(share, BLK_X, parts * BLK_Y, CELLS)


def solution(mesh):
    placed = (
        P(None, "gx", "gy", None),
        P("gx", "gy", None, None),
        P("gx", "gy", None),
        P("gx", "gy", None),
        P("gx", "gy", None, None),
        P(),
        P("gx", "gy"),
        P("gx", "gy", None),
    )
    return jax.shard_map(
        per_device, mesh=mesh, in_specs=placed, out_specs=P("gy", "gx", None, None), check_vma=False
    )
```

```python
import functools

import jax
import jax.numpy as jnp
from jax import lax
from jax.experimental import pallas as pl
from jax.experimental.pallas import tpu as pltpu
from jax.sharding import PartitionSpec as P

CELLS = 128
BLK_X = 2
BLK_Y = 4
BLOCKS = BLK_X * BLK_Y
OBS_TILE = 128
PATTERN = 25
SMALL = 32
EXTRA = 16

F32 = jnp.float32
BF16 = jnp.bfloat16


def iota(shape, dim):
    return lax.broadcasted_iota(jnp.int32, shape, dim)


def split3(x):
    high = x.astype(BF16)
    rest = x - high.astype(F32)
    mid = rest.astype(BF16)
    low = (rest - mid.astype(F32)).astype(BF16)
    return high, mid, low


def dot(a, b, dims, precision=None):
    return lax.dot_general(a, b, ((dims[0], dims[1]), ((), ())), precision=precision, preferred_element_type=F32)


def sweep(rows, count, x_ref, idx_ref, rank, size):
    row = iota((rows, OBS_TILE), 0)
    exists = row < size

    def step(t):
        x = x_ref[0:rows, :]
        pivot_row = x_ref[pl.ds(t, 1), :]
        spread = jnp.broadcast_to(pivot_row, (rows, OBS_TILE))
        column = jnp.take_along_axis(spread, idx_ref[0:rows, :], axis=1, mode="promise_in_bounds")
        column = jnp.where(exists, column, 0.0)
        at = jnp.broadcast_to(idx_ref[pl.ds(t, 1), :], (8, OBS_TILE))
        pivot = jnp.take_along_axis(spread[0:8], at, axis=1, mode="promise_in_bounds")[0:1]
        pivot = jnp.where(t < size, pivot, 1.0)
        own = rank == t
        scaled = jnp.where(own, -1.0, pivot_row) / pivot
        at_row = row == t
        column = jnp.where(at_row, -1.0, column)
        x_ref[0:rows, :] = jnp.where(at_row | own, 0.0, x) - column * scaled

    def pair(k, carry):
        step(2 * k)
        step(2 * k + 1)
        return carry

    lax.fori_loop(0, (count + 1) // 2, pair, 0)


def weigh_kernel(pred_ref, mv_ref, var_ref, jit_ref, obs_ref, out_ref, x_ref, idx_ref, full_ref):
    members = pred_ref.shape[2]
    tile_x = lax.axis_index("gx")
    tile_y = lax.axis_index("gy")
    square = (OBS_TILE, OBS_TILE)
    pred = pred_ref[0, 0]
    var = var_ref[0]
    mean = jnp.sum(pred, axis=0, keepdims=True) / members
    deviation = (pred - mean).astype(BF16)
    out_ref[0] = deviation
    obs = obs_ref[tile_x, pl.ds(tile_y, 1), :]
    groups = (iota((BLOCKS, OBS_TILE), 0) == obs).astype(BF16)
    same = dot(groups, groups, ((0,), (0,)))
    gram = dot(deviation, deviation, ((0,), (0,))) / (members - 1)
    row, col = iota(square, 0), iota(square, 1)
    system = jnp.where(same > 0.5, gram, 0.0) + jnp.where(row == col, var, 0.0)
    size = jnp.sum(same, axis=0, keepdims=True)
    count = jnp.max(size).astype(jnp.int32)
    size = size.astype(jnp.int32)
    rank = jnp.sum(jnp.where(row < col, same, 0.0), axis=0, keepdims=True).astype(jnp.int32)
    place = row == rank
    hot = place.astype(BF16)
    high, mid, low = split3(system)
    x_ref[...] = (
        dot(hot, low, ((1,), (0,))) + dot(hot, mid, ((1,), (0,))) + dot(hot, high, ((1,), (0,)))
    )
    numbered = jnp.where(place, col, 0).astype(F32).astype(BF16)
    idx_ref[...] = dot(numbered, same.astype(BF16), ((1,), (0,))).astype(jnp.int32)

    def solve(rows):
        sweep(rows, count, x_ref, idx_ref, rank, size)
        high, mid, low = split3(x_ref[0:rows, :])
        taken = hot[0:rows]
        full = dot(taken, low, ((0,), (0,))) + dot(taken, mid, ((0,), (0,))) + dot(taken, high, ((0,), (0,)))
        full_ref[...] = jnp.where(same > 0.5, -full, 0.0)

    @pl.when(count <= SMALL)
    def _():
        solve(SMALL)

    @pl.when(count > SMALL)
    def _():
        solve(OBS_TILE)

    innovation = mv_ref[0] + jnp.sqrt(var) * jit_ref[0, 0] - pred
    weighted = dot(innovation, full_ref[...], ((1,), (0,)), lax.Precision.HIGHEST)
    out_ref[1] = weighted.astype(BF16)


def weigh(predicted, measured_value, measurement_variance, observation_jitter, obs_block):
    members = predicted.shape[2]
    return pl.pallas_call(
        weigh_kernel,
        out_shape=jax.ShapeDtypeStruct((2, members, OBS_TILE), BF16),
        in_specs=[pl.BlockSpec(memory_space=pltpu.VMEM)] * 5,
        out_specs=pl.BlockSpec(memory_space=pltpu.VMEM),
        scratch_shapes=[
            pltpu.VMEM((OBS_TILE, OBS_TILE), F32),
            pltpu.VMEM((OBS_TILE, OBS_TILE), jnp.int32),
            pltpu.VMEM((OBS_TILE, OBS_TILE), F32),
        ],
        compiler_params=pltpu.CompilerParams(vmem_limit_bytes=16 * 2**20),
        name="weigh",
    )(predicted, measured_value, measurement_variance, observation_jitter, obs_block)


def prepare_kernel(params_ref, radius_ref, pattern_ref, obs_ref, turned_ref, taper_ref):
    members = params_ref.shape[1]
    tile_x = lax.axis_index("gx")
    tile_y = lax.axis_index("gy")
    count_x, count_y = obs_ref.shape[0], obs_ref.shape[1]
    for b in range(BLOCKS):
        block = params_ref[b].astype(F32)
        mean = jnp.sum(block, axis=0, keepdims=True) / members
        anomaly = block - mean
        turned_ref[b] = anomaly.T.astype(BF16)

    shape = (BLOCKS, OBS_TILE)
    block = iota(shape, 0)
    radius = jnp.zeros(shape, jnp.int32)
    for b in range(BLOCKS):
        radius = jnp.where(block == b, radius_ref[b // BLK_Y, b % BLK_Y], radius)
    reach = (radius + 1).astype(F32)
    reach = reach * reach
    pattern = pattern_ref[...].astype(F32)
    slots = [jnp.broadcast_to(pattern[:, p : p + 1], shape) for p in range(PATTERN)]
    for dx in range(3):
        for dy in range(3):
            at_x, at_y = tile_x + (dx - 1), tile_y + (dy - 1)
            valid = (at_x >= 0) & (at_x < count_x) & (at_y >= 0) & (at_y < count_y)
            at_x = jnp.clip(at_x, 0, count_x - 1)
            at_y = jnp.clip(at_y, 0, count_y - 1)
            obs = obs_ref[at_x, pl.ds(at_y, 1), :]
            step_x = (dx - 1) * BLK_X + (obs >> 2) - (block >> 2)
            step_y = (dy - 1) * BLK_Y + (obs & 3) - (block & 3)
            inside = (jnp.abs(step_x) <= 2) & (jnp.abs(step_y) <= 2) & valid
            offset = (step_x + 2) * 5 + (step_y + 2)
            picked = jnp.zeros(shape, F32)
            for p in range(PATTERN):
                picked = jnp.where(offset == p, slots[p], picked)
            spread = (step_x * step_x + step_y * step_y).astype(F32)
            shaped = jnp.maximum(1.0 - spread / reach, 0.0)
            taper_ref[dx * 3 + dy] = jnp.where(inside, picked, 0.0) * shaped / (members - 1)


def prepare(by_block, taper_radius, taper_pattern, obs_block):
    members = by_block.shape[1]
    return pl.pallas_call(
        prepare_kernel,
        out_shape=(
            jax.ShapeDtypeStruct((BLOCKS, CELLS, members), BF16),
            jax.ShapeDtypeStruct((9, BLOCKS, OBS_TILE), F32),
        ),
        in_specs=[
            pl.BlockSpec(memory_space=pltpu.VMEM),
            pl.BlockSpec(memory_space=pltpu.SMEM),
            pl.BlockSpec(memory_space=pltpu.VMEM),
            pl.BlockSpec(memory_space=pltpu.VMEM),
        ],
        out_specs=(pl.BlockSpec(memory_space=pltpu.VMEM), pl.BlockSpec(memory_space=pltpu.VMEM)),
        compiler_params=pltpu.CompilerParams(vmem_limit_bytes=16 * 2**20),
        cost_estimate=pl.CostEstimate(flops=4_000_000, bytes_accessed=1_000_000, transcendentals=0),
        name="prepare",
    )(by_block, taper_radius, taper_pattern.reshape(BLOCKS, PATTERN), obs_block)


def update_kernel(params_ref, turned_ref, taper_ref, own_ref, low_ref, high_ref, out_ref):
    share = out_ref.shape[2]
    near = [ref.at[dx] for dx in range(3) for ref in (low_ref, own_ref, high_ref)]
    deviations = jnp.concatenate([tile[0] for tile in near], axis=1)
    weighted = jnp.concatenate([tile[1] for tile in near], axis=1)

    def one(b, carry):
        cross = dot(turned_ref[b], deviations, ((1,), (0,)))
        taper = jnp.concatenate([taper_ref[t, pl.ds(b, 1), :] for t in range(9)], axis=1)
        gain = (cross * taper).astype(BF16)
        delta = dot(weighted, gain, ((1,), (1,)))
        updated = (params_ref[b].astype(F32) + delta).astype(BF16)
        for d in range(out_ref.shape[0]):
            out_ref[d, b] = updated[d * share : (d + 1) * share]
        return carry

    lax.fori_loop(0, BLOCKS, one, 0, unroll=True)


def update(by_block, turned, taper, own, low, high, parts):
    members = by_block.shape[1]
    return pl.pallas_call(
        update_kernel,
        out_shape=jax.ShapeDtypeStruct((parts, BLOCKS, members // parts, CELLS), BF16),
        in_specs=[pl.BlockSpec(memory_space=pltpu.VMEM)] * 6,
        out_specs=pl.BlockSpec(memory_space=pltpu.VMEM),
        compiler_params=pltpu.CompilerParams(vmem_limit_bytes=40 * 2**20),
        name="update",
    )(by_block, turned, taper, own, low, high)


def neighbours(block, axis):
    count = lax.axis_size(axis)
    low = lax.ppermute(block, axis, [(i, i + 1) for i in range(count - 1)])
    high = lax.ppermute(block, axis, [(i + 1, i) for i in range(count - 1)])
    return low, high


def deviate_kernel(pred_ref, radius_ref, pattern_ref, out_ref):
    members = pred_ref.shape[2]
    pred = pred_ref[0, 0]
    mean = jnp.sum(pred, axis=0, keepdims=True) / members
    out_ref[0:members] = (pred - mean).astype(BF16)
    row, col = iota((EXTRA, OBS_TILE), 0), iota((EXTRA, OBS_TILE), 1)
    extra = jnp.zeros((EXTRA, OBS_TILE), F32)
    for b in range(BLOCKS):
        extra = jnp.where((row == b) & (col == PATTERN), radius_ref[b // BLK_Y, b % BLK_Y].astype(F32), extra)
    pattern = pattern_ref[...].astype(F32)
    pattern = jnp.concatenate([pattern, jnp.zeros((BLOCKS, OBS_TILE - PATTERN), F32)], axis=1)
    pattern = jnp.concatenate([pattern, jnp.zeros((EXTRA - BLOCKS, OBS_TILE), F32)], axis=0)
    out_ref[members : members + EXTRA] = (extra + pattern).astype(BF16)


def deviate(predicted, taper_radius, taper_pattern):
    members = predicted.shape[2]
    return pl.pallas_call(
        deviate_kernel,
        out_shape=jax.ShapeDtypeStruct((members + EXTRA, OBS_TILE), BF16),
        in_specs=[
            pl.BlockSpec(memory_space=pltpu.VMEM),
            pl.BlockSpec(memory_space=pltpu.SMEM),
            pl.BlockSpec(memory_space=pltpu.VMEM),
        ],
        out_specs=pl.BlockSpec(memory_space=pltpu.VMEM),
        name="deviate",
    )(predicted, taper_radius, taper_pattern.reshape(BLOCKS, PATTERN))


def tapers_of(radius, pattern, tile_x, tile_y, obs_ref, members):
    count_x, count_y = obs_ref.shape[0], obs_ref.shape[1]
    shape = (BLOCKS, OBS_TILE)
    block = iota(shape, 0)
    reach = radius + 1.0
    reach = reach * reach
    slots = [jnp.broadcast_to(pattern[:, p : p + 1], shape) for p in range(PATTERN)]
    found = []
    for dx in range(3):
        for dy in range(3):
            at_x, at_y = tile_x + (dx - 1), tile_y + (dy - 1)
            valid = (at_x >= 0) & (at_x < count_x) & (at_y >= 0) & (at_y < count_y)
            at_x = jnp.clip(at_x, 0, count_x - 1)
            at_y = jnp.clip(at_y, 0, count_y - 1)
            obs = obs_ref[at_x, pl.ds(at_y, 1), :]
            step_x = (dx - 1) * BLK_X + (obs >> 2) - (block >> 2)
            step_y = (dy - 1) * BLK_Y + (obs & 3) - (block & 3)
            inside = (jnp.abs(step_x) <= 2) & (jnp.abs(step_y) <= 2) & valid
            offset = (step_x + 2) * 5 + (step_y + 2)
            picked = jnp.zeros(shape, F32)
            for p in range(PATTERN):
                picked = jnp.where(offset == p, slots[p], picked)
            spread = (step_x * step_x + step_y * step_y).astype(F32)
            shaped = jnp.maximum(1.0 - spread / reach, 0.0)
            found.append(jnp.where(inside, picked, 0.0) * shaped / (members - 1))
    return found


def regroup_kernel(params_ref, around_ref, weighted_ref, obs_ref, out_ref):
    count_x, parts = obs_ref.shape[0], obs_ref.shape[1]
    share = out_ref.shape[0]
    rows = share * BLOCKS
    members = share * parts
    cells = members * BLOCKS
    tile_x = lax.axis_index("gx")
    mine = lax.axis_index("gy")
    spread = (iota((members, cells), 1) // BLOCKS == iota((members, cells), 0)).astype(BF16)
    diagonal = (iota((rows, cells), 0) % BLOCKS) == (iota((rows, cells), 1) % BLOCKS)
    top = iota((share, BLOCKS, CELLS), 1) < BLK_Y
    before = None
    for s in range(parts):
        wide = params_ref[s].astype(F32).reshape(members, BLOCKS, CELLS)
        mean = jnp.sum(wide, axis=0, keepdims=True) / members
        anomaly = (wide - mean).reshape(cells, CELLS).astype(BF16)
        extra = around_ref[tile_x * parts + s, members : members + EXTRA].astype(F32)[0:BLOCKS]
        tapers = tapers_of(extra[:, PATTERN : PATTERN + 1], extra, tile_x, s, obs_ref, members)
        turned = jnp.zeros((rows, members), F32)
        for t, (dx, dy) in enumerate([(dx, dy) for dx in (-1, 0, 1) for dy in (-1, 0, 1)]):
            if not 0 <= s + dy < parts:
                continue
            tile = jnp.clip(tile_x + dx, 0, count_x - 1) * parts + s + dy
            weighted = weighted_ref[tile].astype(F32)
            scaled = weighted[:, None, :] * tapers[t][None]
            scaled = scaled.reshape(rows, OBS_TILE).astype(BF16)
            turned = turned + dot(scaled, around_ref[tile, 0:members], ((1,), (1,)))
        wide_k = dot(turned.astype(BF16), spread, ((1,), (0,)))
        wide_k = jnp.where(diagonal, wide_k, 0.0).astype(BF16)
        delta = dot(wide_k, anomaly, ((1,), (0,)))
        own = params_ref[s, pl.ds(pl.multiple_of(mine * rows, rows), rows), :].astype(F32)
        now = (own + delta).reshape(share, BLOCKS, CELLS)
        if s % 2 == 0:
            before = now
        else:
            place = slice((s - 1) * BLK_Y, (s + 1) * BLK_Y)
            out_ref[:, 0, place, :] = jnp.where(top, before, jnp.roll(now, BLK_Y, axis=1)).astype(BF16)
            out_ref[:, 1, place, :] = jnp.where(top, jnp.roll(before, BLK_Y, axis=1), now).astype(BF16)


def regroup(gathered, around, weighted, obs_block):
    parts, cells, _ = gathered.shape
    share = weighted.shape[1]
    return pl.pallas_call(
        regroup_kernel,
        out_shape=jax.ShapeDtypeStruct((share, BLK_X, parts * BLK_Y, CELLS), BF16),
        in_specs=[pl.BlockSpec(memory_space=pltpu.VMEM)] * 4,
        out_specs=pl.BlockSpec(memory_space=pltpu.VMEM),
        compiler_params=pltpu.CompilerParams(vmem_limit_bytes=40 * 2**20),
        name="regroup",
    )(gathered, around, weighted, obs_block)


def gather_form(
    params,
    predicted,
    measured_value,
    measurement_variance,
    observation_jitter,
    obs_block,
    taper_radius,
    taper_pattern,
):
    members = params.shape[0]
    tiles, parts = lax.axis_size("gx"), lax.axis_size("gy")
    share = members // parts
    gathered = lax.all_gather(params.reshape(members * BLOCKS, CELLS), "gy")
    around = lax.all_gather(deviate(predicted, taper_radius, taper_pattern), ("gx", "gy"))
    own = weigh(predicted, measured_value, measurement_variance, observation_jitter, obs_block)
    sent = jnp.broadcast_to(own[1].reshape(1, parts, share, OBS_TILE), (tiles, parts, share, OBS_TILE))
    weighted = lax.all_to_all(
        sent.reshape(tiles * parts, share, OBS_TILE), ("gx", "gy"), split_axis=0, concat_axis=0, tiled=True
    )
    return regroup(gathered, around, weighted, obs_block)


def halo_form(
    params,
    predicted,
    measured_value,
    measurement_variance,
    observation_jitter,
    obs_block,
    taper_radius,
    taper_pattern,
):
    members = params.shape[0]
    parts = lax.axis_size("gy")
    by_block = params.reshape(members, BLOCKS, CELLS).transpose(1, 0, 2)
    own = weigh(predicted, measured_value, measurement_variance, observation_jitter, obs_block)
    low_x, high_x = neighbours(own, "gx")
    turned, taper = prepare(by_block, taper_radius, taper_pattern, obs_block)
    column = jnp.stack([low_x, own, high_x])
    low, high = neighbours(column, "gy")
    updated = update(by_block, turned, taper, column, low, high, parts)
    arrived = lax.all_to_all(updated, "gy", split_axis=0, concat_axis=0, tiled=True)
    share = members // parts
    arrived = arrived.reshape(parts, BLK_X, BLK_Y, share, CELLS).transpose(3, 1, 0, 2, 4)
    return arrived.reshape(share, BLK_X, parts * BLK_Y, CELLS)


def solution(mesh):
    placed = (
        P(None, "gx", "gy", None),
        P("gx", "gy", None, None),
        P("gx", "gy", None),
        P("gx", "gy", None),
        P("gx", "gy", None, None),
        P(),
        P("gx", "gy"),
        P("gx", "gy", None),
    )
    per_device = gather_form if mesh.shape["gy"] <= 8 else halo_form
    return jax.shard_map(
        per_device, mesh=mesh, in_specs=placed, out_specs=P("gy", "gx", None, None), check_vma=False
    )
```

```python
import functools

import jax
import jax.numpy as jnp
from jax import lax
from jax.experimental import pallas as pl
from jax.experimental.pallas import tpu as pltpu
from jax.sharding import PartitionSpec as P

CELLS = 128
BLK_X = 2
BLK_Y = 4
BLOCKS = BLK_X * BLK_Y
OBS_TILE = 128
PATTERN = 25
SMALL = 32

F32 = jnp.float32
BF16 = jnp.bfloat16


def iota(shape, dim):
    return lax.broadcasted_iota(jnp.int32, shape, dim)


def split3(x):
    high = x.astype(BF16)
    rest = x - high.astype(F32)
    mid = rest.astype(BF16)
    low = (rest - mid.astype(F32)).astype(BF16)
    return high, mid, low


def dot(a, b, dims, precision=None):
    return lax.dot_general(a, b, ((dims[0], dims[1]), ((), ())), precision=precision, preferred_element_type=F32)


def sweep(rows, count, x_ref, idx_ref, rank, size):
    row = iota((rows, OBS_TILE), 0)
    exists = row < size

    def step(t):
        x = x_ref[0:rows, :]
        pivot_row = x_ref[pl.ds(t, 1), :]
        spread = jnp.broadcast_to(pivot_row, (rows, OBS_TILE))
        column = jnp.take_along_axis(spread, idx_ref[0:rows, :], axis=1, mode="promise_in_bounds")
        column = jnp.where(exists, column, 0.0)
        at = jnp.broadcast_to(idx_ref[pl.ds(t, 1), :], (8, OBS_TILE))
        pivot = jnp.take_along_axis(spread[0:8], at, axis=1, mode="promise_in_bounds")[0:1]
        pivot = jnp.where(t < size, pivot, 1.0)
        own = rank == t
        scaled = jnp.where(own, -1.0, pivot_row) / pivot
        at_row = row == t
        column = jnp.where(at_row, -1.0, column)
        x_ref[0:rows, :] = jnp.where(at_row | own, 0.0, x) - column * scaled

    def pair(k, carry):
        step(2 * k)
        step(2 * k + 1)
        return carry

    lax.fori_loop(0, (count + 1) // 2, pair, 0)


def in_hbm(*arrays):
    return [pltpu.with_memory_space_constraint(array, pltpu.HBM) for array in arrays]


def fetch(pairs, sems):
    copies = [pltpu.make_async_copy(src, dst, sems.at[k]) for k, (src, dst) in enumerate(pairs)]
    for copy in copies:
        copy.start()
    return copies


def weigh_kernel(
    pred_hbm, mv_hbm, var_hbm, jit_hbm, obs_hbm, out_ref,
    pred_ref, mv_ref, var_ref, jit_ref, obs_ref, x_ref, idx_ref, full_ref, sems,
):
    members = pred_ref.shape[0]
    tile_x = lax.axis_index("gx")
    tile_y = lax.axis_index("gy")
    square = (OBS_TILE, OBS_TILE)
    pairs = [
        (pred_hbm.at[0, 0], pred_ref),
        (obs_hbm.at[tile_x], obs_ref),
        (var_hbm.at[0], var_ref),
        (mv_hbm.at[0], mv_ref),
        (jit_hbm.at[0, 0], jit_ref),
    ]
    copies = fetch(pairs, sems)
    for copy in copies[:3]:
        copy.wait()
    pred = pred_ref[...]
    var = var_ref[...]
    mean = jnp.sum(pred, axis=0, keepdims=True) / members
    deviation = (pred - mean).astype(BF16)
    out_ref[0] = deviation
    obs = obs_ref[pl.ds(tile_y, 1), :]
    groups = (iota((BLOCKS, OBS_TILE), 0) == obs).astype(BF16)
    same = dot(groups, groups, ((0,), (0,)))
    gram = dot(deviation, deviation, ((0,), (0,))) / (members - 1)
    row, col = iota(square, 0), iota(square, 1)
    system = jnp.where(same > 0.5, gram, 0.0) + jnp.where(row == col, var, 0.0)
    size = jnp.sum(same, axis=0, keepdims=True)
    count = jnp.max(size).astype(jnp.int32)
    size = size.astype(jnp.int32)
    rank = jnp.sum(jnp.where(row < col, same, 0.0), axis=0, keepdims=True).astype(jnp.int32)
    place = row == rank
    hot = place.astype(BF16)
    high, mid, low = split3(system)
    x_ref[...] = (
        dot(hot, low, ((1,), (0,))) + dot(hot, mid, ((1,), (0,))) + dot(hot, high, ((1,), (0,)))
    )
    numbered = jnp.where(place, col, 0).astype(F32).astype(BF16)
    idx_ref[...] = dot(numbered, same.astype(BF16), ((1,), (0,))).astype(jnp.int32)

    def solve(rows):
        sweep(rows, count, x_ref, idx_ref, rank, size)
        high, mid, low = split3(x_ref[0:rows, :])
        taken = hot[0:rows]
        full = dot(taken, low, ((0,), (0,))) + dot(taken, mid, ((0,), (0,))) + dot(taken, high, ((0,), (0,)))
        full_ref[...] = jnp.where(same > 0.5, -full, 0.0)

    @pl.when(count <= SMALL)
    def _():
        solve(SMALL)

    @pl.when(count > SMALL)
    def _():
        solve(OBS_TILE)

    for copy in copies[3:]:
        copy.wait()
    innovation = mv_ref[...] + jnp.sqrt(var) * jit_ref[...] - pred
    weighted = dot(innovation, full_ref[...], ((1,), (0,)), lax.Precision.HIGHEST)
    out_ref[1] = weighted.astype(BF16)


def weigh(predicted, measured_value, measurement_variance, observation_jitter, obs_block):
    members = predicted.shape[2]
    return pl.pallas_call(
        weigh_kernel,
        out_shape=jax.ShapeDtypeStruct((2, members, OBS_TILE), BF16),
        in_specs=[pl.BlockSpec(memory_space=pltpu.HBM)] * 5,
        out_specs=pl.BlockSpec(memory_space=pltpu.VMEM),
        scratch_shapes=[
            pltpu.VMEM((members, OBS_TILE), F32),
            pltpu.VMEM((1, OBS_TILE), F32),
            pltpu.VMEM((1, OBS_TILE), F32),
            pltpu.VMEM((members, OBS_TILE), F32),
            pltpu.VMEM((obs_block.shape[1], OBS_TILE), jnp.int32),
            pltpu.VMEM((OBS_TILE, OBS_TILE), F32),
            pltpu.VMEM((OBS_TILE, OBS_TILE), jnp.int32),
            pltpu.VMEM((OBS_TILE, OBS_TILE), F32),
            pltpu.SemaphoreType.DMA((5,)),
        ],
        compiler_params=pltpu.CompilerParams(vmem_limit_bytes=16 * 2**20),
        name="weigh",
    )(*in_hbm(predicted, measured_value, measurement_variance, observation_jitter, obs_block))


def offsets(place):
    even = 1 - 2 * (place & 1)
    return 0, even, -even


def prepare_kernel(
    params_ref, radius_hbm, pattern_hbm, obs_hbm, turned_ref, taper_ref, radius_ref, pattern_ref, obs_ref, sems
):
    members = params_ref.shape[1]
    tile_x = lax.axis_index("gx")
    tile_y = lax.axis_index("gy")
    count_x, count_y = obs_ref.shape[0], obs_ref.shape[1]
    copies = fetch([(radius_hbm, radius_ref), (pattern_hbm, pattern_ref), (obs_hbm, obs_ref)], sems)
    for b in range(BLOCKS):
        block = params_ref[b].astype(F32)
        mean = jnp.sum(block, axis=0, keepdims=True) / members
        anomaly = block - mean
        turned_ref[b] = anomaly.T.astype(BF16)

    for copy in copies:
        copy.wait()
    shape = (BLOCKS, OBS_TILE)
    block = iota(shape, 0)
    radius = jnp.zeros(shape, jnp.int32)
    for b in range(BLOCKS):
        radius = jnp.where(block == b, radius_ref[b // BLK_Y, b % BLK_Y], radius)
    reach = (radius + 1).astype(F32)
    reach = reach * reach
    pattern = jnp.concatenate([pattern_ref[i] for i in range(BLK_X)], axis=0).astype(F32)
    slots = [jnp.broadcast_to(pattern[:, p : p + 1], shape) for p in range(PATTERN)]
    for ix, dx in enumerate(offsets(tile_x)):
        for iy, dy in enumerate(offsets(tile_y)):
            at_x, at_y = tile_x + dx, tile_y + dy
            valid = (at_x >= 0) & (at_x < count_x) & (at_y >= 0) & (at_y < count_y)
            at_x = jnp.clip(at_x, 0, count_x - 1)
            at_y = jnp.clip(at_y, 0, count_y - 1)
            obs = obs_ref[at_x, pl.ds(at_y, 1), :]
            step_x = dx * BLK_X + (obs >> 2) - (block >> 2)
            step_y = dy * BLK_Y + (obs & 3) - (block & 3)
            inside = (jnp.abs(step_x) <= 2) & (jnp.abs(step_y) <= 2) & valid
            offset = (step_x + 2) * 5 + (step_y + 2)
            picked = jnp.zeros(shape, F32)
            for p in range(PATTERN):
                picked = jnp.where(offset == p, slots[p], picked)
            spread = (step_x * step_x + step_y * step_y).astype(F32)
            shaped = jnp.maximum(1.0 - spread / reach, 0.0)
            taper_ref[ix * 3 + iy] = jnp.where(inside, picked, 0.0) * shaped / (members - 1)


def prepare(by_block, taper_radius, taper_pattern, obs_block):
    members = by_block.shape[1]
    return pl.pallas_call(
        prepare_kernel,
        out_shape=(
            jax.ShapeDtypeStruct((BLOCKS, CELLS, members), BF16),
            jax.ShapeDtypeStruct((9, BLOCKS, OBS_TILE), F32),
        ),
        in_specs=[pl.BlockSpec(memory_space=pltpu.VMEM)] + [pl.BlockSpec(memory_space=pltpu.HBM)] * 3,
        out_specs=(pl.BlockSpec(memory_space=pltpu.VMEM), pl.BlockSpec(memory_space=pltpu.VMEM)),
        scratch_shapes=[
            pltpu.SMEM(taper_radius.shape, jnp.int32),
            pltpu.VMEM(taper_pattern.shape, jnp.int32),
            pltpu.VMEM(obs_block.shape, jnp.int32),
            pltpu.SemaphoreType.DMA((3,)),
        ],
        compiler_params=pltpu.CompilerParams(vmem_limit_bytes=16 * 2**20),
        cost_estimate=pl.CostEstimate(flops=4_000_000, bytes_accessed=1_000_000, transcendentals=0),
        name="prepare",
    )(by_block, *in_hbm(taper_radius, taper_pattern, obs_block))


def update_kernel(params_ref, turned_ref, taper_ref, own_ref, even_ref, odd_ref, out_ref):
    share = out_ref.shape[2]
    near = [ref.at[ix] for ix in range(3) for ref in (own_ref, even_ref, odd_ref)]
    deviations = jnp.concatenate([tile[0] for tile in near], axis=1)
    weighted = jnp.concatenate([tile[1] for tile in near], axis=1)

    def one(b, carry):
        cross = dot(turned_ref[b], deviations, ((1,), (0,)))
        taper = jnp.concatenate([taper_ref[t, pl.ds(b, 1), :] for t in range(9)], axis=1)
        gain = (cross * taper).astype(BF16)
        delta = dot(weighted, gain, ((1,), (1,)))
        updated = (params_ref[b].astype(F32) + delta).astype(BF16)
        for d in range(out_ref.shape[0]):
            out_ref[d, b] = updated[d * share : (d + 1) * share]
        return carry

    lax.fori_loop(0, BLOCKS, one, 0, unroll=True)


def update(by_block, turned, taper, own, even, odd, parts):
    members = by_block.shape[1]
    return pl.pallas_call(
        update_kernel,
        out_shape=jax.ShapeDtypeStruct((parts, BLOCKS, members // parts, CELLS), BF16),
        in_specs=[pl.BlockSpec(memory_space=pltpu.VMEM)] * 6,
        out_specs=pl.BlockSpec(memory_space=pltpu.VMEM),
        compiler_params=pltpu.CompilerParams(vmem_limit_bytes=40 * 2**20),
        name="update",
    )(by_block, turned, taper, own, even, odd)


def swaps(block, axis):
    count = lax.axis_size(axis)
    found = []
    for first in (0, 1):
        pairs = [(i, i + 1) for i in range(first, count - 1, 2)]
        found.append(lax.ppermute(block, axis, pairs + [(b, a) for a, b in pairs]))
    return found


def per_device(
    params,
    predicted,
    measured_value,
    measurement_variance,
    observation_jitter,
    obs_block,
    taper_radius,
    taper_pattern,
):
    members = params.shape[0]
    parts = lax.axis_size("gy")
    by_block = params.reshape(members, BLOCKS, CELLS).transpose(1, 0, 2)
    own = weigh(predicted, measured_value, measurement_variance, observation_jitter, obs_block)
    even, odd = swaps(own, "gx")
    turned, taper = prepare(by_block, taper_radius, taper_pattern, obs_block)
    column = jnp.stack([own, even, odd])
    column, turned, taper = lax.optimization_barrier((column, turned, taper))
    even, odd = swaps(column, "gy")
    updated = update(by_block, turned, taper, column, even, odd, parts)
    arrived = lax.all_to_all(updated, "gy", split_axis=0, concat_axis=0, tiled=True)
    share = members // parts
    arrived = arrived.reshape(parts, BLK_X, BLK_Y, share, CELLS).transpose(3, 1, 0, 2, 4)
    return arrived.reshape(share, BLK_X, parts * BLK_Y, CELLS)


def solution(mesh):
    placed = (
        P(None, "gx", "gy", None),
        P("gx", "gy", None, None),
        P("gx", "gy", None),
        P("gx", "gy", None),
        P("gx", "gy", None, None),
        P(),
        P("gx", "gy"),
        P("gx", "gy", None),
    )
    return jax.shard_map(
        per_device, mesh=mesh, in_specs=placed, out_specs=P("gy", "gx", None, None), check_vma=False
    )
```

```python
import functools

import jax
import jax.numpy as jnp
from jax import lax
from jax.experimental import pallas as pl
from jax.experimental.pallas import tpu as pltpu
from jax.sharding import PartitionSpec as P

CELLS = 128
BLK_X = 2
BLK_Y = 4
BLOCKS = BLK_X * BLK_Y
OBS_TILE = 128
PATTERN = 25
SMALL = 32

F32 = jnp.float32
BF16 = jnp.bfloat16


def iota(shape, dim):
    return lax.broadcasted_iota(jnp.int32, shape, dim)


def split3(x):
    high = x.astype(BF16)
    rest = x - high.astype(F32)
    mid = rest.astype(BF16)
    low = (rest - mid.astype(F32)).astype(BF16)
    return high, mid, low


def dot(a, b, dims, precision=None):
    return lax.dot_general(a, b, ((dims[0], dims[1]), ((), ())), precision=precision, preferred_element_type=F32)


def sweep(rows, count, x_ref, idx_ref, rank, size):
    row = iota((rows, OBS_TILE), 0)
    exists = row < size

    def taken(spread, indices):
        return jnp.take_along_axis(spread, indices, axis=1, mode="promise_in_bounds")

    def step(k, carry):
        t = 2 * k
        u = t + 1
        row_t, row_u = x_ref[pl.ds(t, 1), :], x_ref[pl.ds(u, 1), :]
        spread_t = jnp.broadcast_to(row_t, (rows, OBS_TILE))
        spread_u = jnp.broadcast_to(row_u, (rows, OBS_TILE))
        at_t = jnp.broadcast_to(idx_ref[pl.ds(t, 1), :], (8, OBS_TILE))
        at_u = jnp.broadcast_to(idx_ref[pl.ds(u, 1), :], (8, OBS_TILE))
        has_t, has_u = t < size, u < size
        a = jnp.where(has_t, taken(spread_t[0:8], at_t)[0:1], 1.0)
        b = jnp.where(has_u, taken(spread_t[0:8], at_u)[0:1], 0.0)
        d = jnp.where(has_u, taken(spread_u[0:8], at_u)[0:1], 1.0)
        scale = 1.0 / (a * d - b * b)
        own_t, own_u = rank == t, rank == u
        own = own_t | own_u
        head_t = jnp.where(own, jnp.where(own_t, -1.0, 0.0), row_t)
        head_u = jnp.where(own, jnp.where(own_u, -1.0, 0.0), row_u)
        scaled_t = (d * head_t - b * head_u) * scale
        scaled_u = (a * head_u - b * head_t) * scale
        column_t = jnp.where(exists, taken(spread_t, idx_ref[0:rows, :]), 0.0)
        column_u = jnp.where(exists, taken(spread_u, idx_ref[0:rows, :]), 0.0)
        on_t, on_u = row == t, row == u
        on = on_t | on_u
        column_t = jnp.where(on, jnp.where(on_t, -1.0, 0.0), column_t)
        column_u = jnp.where(on, jnp.where(on_u, -1.0, 0.0), column_u)
        x = jnp.where(on | own, 0.0, x_ref[0:rows, :])
        x_ref[0:rows, :] = x - column_t * scaled_t - column_u * scaled_u
        return carry

    lax.fori_loop(0, (count + 1) // 2, step, 0)


def in_hbm(*arrays):
    return [pltpu.with_memory_space_constraint(array, pltpu.HBM) for array in arrays]


def fetch(pairs, sems):
    copies = [pltpu.make_async_copy(src, dst, sems.at[k]) for k, (src, dst) in enumerate(pairs)]
    for copy in copies:
        copy.start()
    return copies


def weigh_kernel(
    pred_hbm, mv_hbm, var_hbm, jit_hbm, obs_hbm, out_ref,
    pred_ref, mv_ref, var_ref, jit_ref, obs_ref, x_ref, idx_ref, full_ref, sems,
):
    members = pred_ref.shape[0]
    tile_x = lax.axis_index("gx")
    tile_y = lax.axis_index("gy")
    square = (OBS_TILE, OBS_TILE)
    pairs = [
        (pred_hbm.at[0, 0], pred_ref),
        (obs_hbm.at[tile_x], obs_ref),
        (var_hbm.at[0], var_ref),
        (mv_hbm.at[0], mv_ref),
        (jit_hbm.at[0, 0], jit_ref),
    ]
    copies = fetch(pairs, sems)
    for copy in copies[:3]:
        copy.wait()
    pred = pred_ref[...]
    var = var_ref[...]
    mean = jnp.sum(pred, axis=0, keepdims=True) / members
    deviation = (pred - mean).astype(BF16)
    out_ref[0] = deviation
    obs = obs_ref[pl.ds(tile_y, 1), :]
    groups = (iota((BLOCKS, OBS_TILE), 0) == obs).astype(BF16)
    same = dot(groups, groups, ((0,), (0,)))
    gram = dot(deviation, deviation, ((0,), (0,))) / (members - 1)
    row, col = iota(square, 0), iota(square, 1)
    system = jnp.where(same > 0.5, gram, 0.0) + jnp.where(row == col, var, 0.0)
    size = jnp.sum(same, axis=0, keepdims=True)
    count = jnp.max(size).astype(jnp.int32)
    size = size.astype(jnp.int32)
    rank = jnp.sum(jnp.where(row < col, same, 0.0), axis=0, keepdims=True).astype(jnp.int32)
    place = row == rank
    hot = place.astype(BF16)
    high, mid, low = split3(system)
    x_ref[...] = (
        dot(hot, low, ((1,), (0,))) + dot(hot, mid, ((1,), (0,))) + dot(hot, high, ((1,), (0,)))
    )
    numbered = jnp.where(place, col, 0).astype(F32).astype(BF16)
    idx_ref[...] = dot(numbered, same.astype(BF16), ((1,), (0,))).astype(jnp.int32)

    def solve(rows):
        sweep(rows, count, x_ref, idx_ref, rank, size)
        high, mid, low = split3(x_ref[0:rows, :])
        taken = hot[0:rows]
        full = dot(taken, low, ((0,), (0,))) + dot(taken, mid, ((0,), (0,))) + dot(taken, high, ((0,), (0,)))
        full_ref[...] = jnp.where(same > 0.5, -full, 0.0)

    @pl.when(count <= SMALL)
    def _():
        solve(SMALL)

    @pl.when(count > SMALL)
    def _():
        solve(OBS_TILE)

    for copy in copies[3:]:
        copy.wait()
    innovation = mv_ref[...] + jnp.sqrt(var) * jit_ref[...] - pred
    weighted = dot(innovation, full_ref[...], ((1,), (0,)), lax.Precision.HIGHEST)
    out_ref[1] = weighted.astype(BF16)


def weigh(predicted, measured_value, measurement_variance, observation_jitter, obs_block):
    members = predicted.shape[2]
    return pl.pallas_call(
        weigh_kernel,
        out_shape=jax.ShapeDtypeStruct((2, members, OBS_TILE), BF16),
        in_specs=[pl.BlockSpec(memory_space=pltpu.HBM)] * 5,
        out_specs=pl.BlockSpec(memory_space=pltpu.VMEM),
        scratch_shapes=[
            pltpu.VMEM((members, OBS_TILE), F32),
            pltpu.VMEM((1, OBS_TILE), F32),
            pltpu.VMEM((1, OBS_TILE), F32),
            pltpu.VMEM((members, OBS_TILE), F32),
            pltpu.VMEM((obs_block.shape[1], OBS_TILE), jnp.int32),
            pltpu.VMEM((OBS_TILE, OBS_TILE), F32),
            pltpu.VMEM((OBS_TILE, OBS_TILE), jnp.int32),
            pltpu.VMEM((OBS_TILE, OBS_TILE), F32),
            pltpu.SemaphoreType.DMA((5,)),
        ],
        compiler_params=pltpu.CompilerParams(vmem_limit_bytes=16 * 2**20),
        name="weigh",
    )(*in_hbm(predicted, measured_value, measurement_variance, observation_jitter, obs_block))


def offset(which, place):
    even = 1 - 2 * (place & 1)
    return jnp.where(which == 0, 0, jnp.where(which == 1, even, -even))


def prepare_kernel(
    params_ref, radius_hbm, pattern_hbm, obs_hbm, turned_ref, taper_ref, radius_ref, pattern_ref, obs_ref, sems
):
    members = params_ref.shape[1]
    tile_x = lax.axis_index("gx")
    tile_y = lax.axis_index("gy")
    count_x, count_y = obs_ref.shape[0], obs_ref.shape[1]
    copies = fetch([(radius_hbm, radius_ref), (pattern_hbm, pattern_ref), (obs_hbm, obs_ref)], sems)

    def turn(b, carry):
        block = params_ref[b].astype(F32)
        mean = jnp.sum(block, axis=0, keepdims=True) / members
        turned_ref[b] = (block - mean).T.astype(BF16)
        return carry

    lax.fori_loop(0, BLOCKS, turn, 0)
    for copy in copies:
        copy.wait()
    shape = (BLOCKS, OBS_TILE)
    block = iota(shape, 0)
    radius = jnp.zeros(shape, jnp.int32)
    for b in range(BLOCKS):
        radius = jnp.where(block == b, radius_ref[b // BLK_Y, b % BLK_Y], radius)
    reach = (radius + 1).astype(F32)
    reach = reach * reach
    pattern = jnp.concatenate([pattern_ref[i] for i in range(BLK_X)], axis=0).astype(F32)
    slots = [jnp.broadcast_to(pattern[:, p : p + 1], shape) for p in range(PATTERN)]

    def tile(t, carry):
        iy, ix = t // 3, t % 3
        dx, dy = offset(ix, tile_x), offset(iy, tile_y)
        at_x, at_y = tile_x + dx, tile_y + dy
        valid = (at_x >= 0) & (at_x < count_x) & (at_y >= 0) & (at_y < count_y)
        at_x = jnp.clip(at_x, 0, count_x - 1)
        at_y = jnp.clip(at_y, 0, count_y - 1)
        obs = obs_ref[at_x, pl.ds(at_y, 1), :]
        step_x = dx * BLK_X + (obs >> 2) - (block >> 2)
        step_y = dy * BLK_Y + (obs & 3) - (block & 3)
        inside = (jnp.abs(step_x) <= 2) & (jnp.abs(step_y) <= 2) & valid
        slot = (step_x + 2) * 5 + (step_y + 2)
        picked = jnp.zeros(shape, F32)
        for p in range(PATTERN):
            picked = jnp.where(slot == p, slots[p], picked)
        spread = (step_x * step_x + step_y * step_y).astype(F32)
        shaped = jnp.maximum(1.0 - spread / reach, 0.0)
        taper_ref[iy, ix] = jnp.where(inside, picked, 0.0) * shaped / (members - 1)
        return carry

    lax.fori_loop(0, 9, tile, 0)


def prepare(by_block, taper_radius, taper_pattern, obs_block):
    members = by_block.shape[1]
    return pl.pallas_call(
        prepare_kernel,
        out_shape=(
            jax.ShapeDtypeStruct((BLOCKS, CELLS, members), BF16),
            jax.ShapeDtypeStruct((3, 3, BLOCKS, OBS_TILE), F32),
        ),
        in_specs=[pl.BlockSpec(memory_space=pltpu.VMEM)] + [pl.BlockSpec(memory_space=pltpu.HBM)] * 3,
        out_specs=(pl.BlockSpec(memory_space=pltpu.VMEM), pl.BlockSpec(memory_space=pltpu.VMEM)),
        scratch_shapes=[
            pltpu.SMEM(taper_radius.shape, jnp.int32),
            pltpu.VMEM(taper_pattern.shape, jnp.int32),
            pltpu.VMEM(obs_block.shape, jnp.int32),
            pltpu.SemaphoreType.DMA((3,)),
        ],
        compiler_params=pltpu.CompilerParams(vmem_limit_bytes=16 * 2**20),
        cost_estimate=pl.CostEstimate(flops=4_000_000, bytes_accessed=1_000_000, transcendentals=0),
        name="prepare",
    )(by_block, *in_hbm(taper_radius, taper_pattern, obs_block))


def moved(b, which, turned_ref, taper_ref, column_ref):
    cross = dot(turned_ref[b], column_ref[0], ((1,), (0,)))
    taper = jnp.concatenate([taper_ref[which, ix, pl.ds(b, 1), :] for ix in range(3)], axis=1)
    gain = (cross * taper).astype(BF16)
    return dot(column_ref[1], gain, ((1,), (1,)))


def block_of(k, side, tile_y):
    first = 2 * ((tile_y & 1) ^ 1 ^ side)
    return (k >> 1) * BLK_Y + first + (k & 1)


def put(out_ref, b, updated):
    share = out_ref.shape[2]
    for d in range(out_ref.shape[0]):
        out_ref[d, b] = updated[d * share : (d + 1) * share]


def near_kernel(params_ref, turned_ref, taper_ref, own_ref, even_ref, out_ref, part_ref):
    tile_y = lax.axis_index("gy")

    def finish(k, carry):
        b = block_of(k, 0, tile_y)
        delta = moved(b, 0, turned_ref, taper_ref, own_ref) + moved(b, 1, turned_ref, taper_ref, even_ref)
        put(out_ref, b, (params_ref[b].astype(F32) + delta).astype(BF16))
        return carry

    def begin(k, carry):
        b = block_of(k, 1, tile_y)
        part_ref[k] = params_ref[b].astype(F32) + moved(b, 0, turned_ref, taper_ref, own_ref)
        return carry

    lax.fori_loop(0, BLOCKS // 2, finish, 0)
    lax.fori_loop(0, BLOCKS // 2, begin, 0)


def far_kernel(turned_ref, taper_ref, odd_ref, part_ref, done_ref, out_ref):
    del done_ref
    tile_y = lax.axis_index("gy")

    def finish(k, carry):
        b = block_of(k, 1, tile_y)
        put(out_ref, b, (part_ref[k] + moved(b, 2, turned_ref, taper_ref, odd_ref)).astype(BF16))
        return carry

    lax.fori_loop(0, BLOCKS // 2, finish, 0)


VMEM = pl.BlockSpec(memory_space=pltpu.VMEM)


def update_near(by_block, turned, taper, own, even, parts):
    members = by_block.shape[1]
    return pl.pallas_call(
        near_kernel,
        out_shape=(
            jax.ShapeDtypeStruct((parts, BLOCKS, members // parts, CELLS), BF16),
            jax.ShapeDtypeStruct((BLOCKS // 2, members, CELLS), F32),
        ),
        in_specs=[VMEM] * 5,
        out_specs=(VMEM, VMEM),
        compiler_params=pltpu.CompilerParams(vmem_limit_bytes=24 * 2**20),
        cost_estimate=pl.CostEstimate(flops=400_000_000, bytes_accessed=2_000_000, transcendentals=0),
        name="near",
    )(by_block, turned, taper, own, even)


def update_far(turned, taper, odd, part, done):
    return pl.pallas_call(
        far_kernel,
        out_shape=jax.ShapeDtypeStruct(done.shape, BF16),
        in_specs=[VMEM] * 4 + [pl.BlockSpec(memory_space=pl.ANY)],
        out_specs=VMEM,
        input_output_aliases={4: 0},
        compiler_params=pltpu.CompilerParams(vmem_limit_bytes=24 * 2**20),
        cost_estimate=pl.CostEstimate(flops=100_000_000, bytes_accessed=1_000_000, transcendentals=0),
        name="far",
    )(turned, taper, odd, part, done)


def swap(block, axis, first):
    pairs = [(i, i + 1) for i in range(first, lax.axis_size(axis) - 1, 2)]
    return lax.ppermute(block, axis, pairs + [(b, a) for a, b in pairs])


def per_device(
    params,
    predicted,
    measured_value,
    measurement_variance,
    observation_jitter,
    obs_block,
    taper_radius,
    taper_pattern,
):
    members = params.shape[0]
    parts = lax.axis_size("gy")
    by_block = params.reshape(members, BLOCKS, CELLS).transpose(1, 0, 2)
    own = weigh(predicted, measured_value, measurement_variance, observation_jitter, obs_block)
    even = swap(own, "gx", 0)
    odd = swap(own, "gx", 1)
    turned, taper = prepare(by_block, taper_radius, taper_pattern, obs_block)
    column = jnp.concatenate([own, even, odd], axis=2)
    column, turned, taper = lax.optimization_barrier((column, turned, taper))
    odd = swap(column, "gy", 1)
    even = swap(column, "gy", 0)
    done, part = update_near(by_block, turned, taper, column, even, parts)
    updated = update_far(turned, taper, odd, part, done)
    arrived = lax.all_to_all(updated, "gy", split_axis=0, concat_axis=0, tiled=True)
    share = members // parts
    arrived = arrived.reshape(parts, BLK_X, BLK_Y, share, CELLS).transpose(3, 1, 0, 2, 4)
    return arrived.reshape(share, BLK_X, parts * BLK_Y, CELLS)


def solution(mesh):
    placed = (
        P(None, "gx", "gy", None),
        P("gx", "gy", None, None),
        P("gx", "gy", None),
        P("gx", "gy", None),
        P("gx", "gy", None, None),
        P(),
        P("gx", "gy"),
        P("gx", "gy", None),
    )
    return jax.shard_map(
        per_device, mesh=mesh, in_specs=placed, out_specs=P("gy", "gx", None, None), check_vma=False
    )
```

```python
import functools

import jax
import jax.numpy as jnp
from jax import lax
from jax.experimental import pallas as pl
from jax.experimental.pallas import tpu as pltpu
from jax.sharding import PartitionSpec as P

CELLS = 128
BLK_X = 2
BLK_Y = 4
BLOCKS = BLK_X * BLK_Y
OBS_TILE = 128
PATTERN = 25
SMALL = 32

F32 = jnp.float32
BF16 = jnp.bfloat16


def iota(shape, dim):
    return lax.broadcasted_iota(jnp.int32, shape, dim)


def split3(x):
    high = x.astype(BF16)
    rest = x - high.astype(F32)
    mid = rest.astype(BF16)
    low = (rest - mid.astype(F32)).astype(BF16)
    return high, mid, low


def dot(a, b, dims, precision=None):
    return lax.dot_general(a, b, ((dims[0], dims[1]), ((), ())), precision=precision, preferred_element_type=F32)


def sweep(rows, count, x_ref, idx_ref, rank, size):
    row = iota((rows, OBS_TILE), 0)
    exists = row < size

    def taken(spread, indices):
        return jnp.take_along_axis(spread, indices, axis=1, mode="promise_in_bounds")

    def step(k, carry):
        t = 2 * k
        u = t + 1
        row_t, row_u = x_ref[pl.ds(t, 1), :], x_ref[pl.ds(u, 1), :]
        spread_t = jnp.broadcast_to(row_t, (rows, OBS_TILE))
        spread_u = jnp.broadcast_to(row_u, (rows, OBS_TILE))
        at_t = jnp.broadcast_to(idx_ref[pl.ds(t, 1), :], (8, OBS_TILE))
        at_u = jnp.broadcast_to(idx_ref[pl.ds(u, 1), :], (8, OBS_TILE))
        has_t, has_u = t < size, u < size
        a = jnp.where(has_t, taken(spread_t[0:8], at_t)[0:1], 1.0)
        b = jnp.where(has_u, taken(spread_t[0:8], at_u)[0:1], 0.0)
        d = jnp.where(has_u, taken(spread_u[0:8], at_u)[0:1], 1.0)
        own_t, own_u = rank == t, rank == u
        own = own_t | own_u
        head_t = jnp.where(own, jnp.where(own_t, -1.0, 0.0), row_t)
        head_u = jnp.where(own, jnp.where(own_u, -1.0, 0.0), row_u)
        inverse = 1.0 / a
        factor = b * inverse
        scaled_u = (head_u - factor * head_t) / (d - b * factor)
        scaled_t = head_t * inverse - factor * scaled_u
        column_t = jnp.where(exists, taken(spread_t, idx_ref[0:rows, :]), 0.0)
        column_u = jnp.where(exists, taken(spread_u, idx_ref[0:rows, :]), 0.0)
        on_t, on_u = row == t, row == u
        on = on_t | on_u
        column_t = jnp.where(on, jnp.where(on_t, -1.0, 0.0), column_t)
        column_u = jnp.where(on, jnp.where(on_u, -1.0, 0.0), column_u)
        x = jnp.where(on | own, 0.0, x_ref[0:rows, :])
        x_ref[0:rows, :] = x - column_t * scaled_t - column_u * scaled_u
        return carry

    lax.fori_loop(0, (count + 1) // 2, step, 0)


def in_hbm(*arrays):
    return [pltpu.with_memory_space_constraint(array, pltpu.HBM) for array in arrays]


def fetch(pairs, sems):
    copies = [pltpu.make_async_copy(src, dst, sems.at[k]) for k, (src, dst) in enumerate(pairs)]
    for copy in copies:
        copy.start()
    return copies


def weigh_kernel(
    pred_hbm, mv_hbm, var_hbm, jit_hbm, obs_hbm, out_ref,
    pred_ref, mv_ref, var_ref, jit_ref, obs_ref, x_ref, idx_ref, full_ref, sems,
):
    members = pred_ref.shape[0]
    tile_x = lax.axis_index("gx")
    tile_y = lax.axis_index("gy")
    square = (OBS_TILE, OBS_TILE)
    pairs = [
        (pred_hbm.at[0, 0], pred_ref),
        (obs_hbm.at[tile_x], obs_ref),
        (var_hbm.at[0], var_ref),
        (mv_hbm.at[0], mv_ref),
        (jit_hbm.at[0, 0], jit_ref),
    ]
    copies = fetch(pairs, sems)
    for copy in copies[:3]:
        copy.wait()
    pred = pred_ref[...]
    var = var_ref[...]
    mean = jnp.sum(pred, axis=0, keepdims=True) / members
    deviation = (pred - mean).astype(BF16)
    out_ref[0] = deviation
    obs = obs_ref[pl.ds(tile_y, 1), :]
    groups = (iota((BLOCKS, OBS_TILE), 0) == obs).astype(BF16)
    same = dot(groups, groups, ((0,), (0,)))
    gram = dot(deviation, deviation, ((0,), (0,))) / (members - 1)
    row, col = iota(square, 0), iota(square, 1)
    system = jnp.where(same > 0.5, gram, 0.0) + jnp.where(row == col, var, 0.0)
    size = jnp.sum(same, axis=0, keepdims=True)
    count = jnp.max(size).astype(jnp.int32)
    size = size.astype(jnp.int32)
    rank = jnp.sum(jnp.where(row < col, same, 0.0), axis=0, keepdims=True).astype(jnp.int32)
    place = row == rank
    hot = place.astype(BF16)
    high, mid, low = split3(system)
    x_ref[...] = (
        dot(hot, low, ((1,), (0,))) + dot(hot, mid, ((1,), (0,))) + dot(hot, high, ((1,), (0,)))
    )
    numbered = jnp.where(place, col, 0).astype(F32).astype(BF16)
    idx_ref[...] = dot(numbered, same.astype(BF16), ((1,), (0,))).astype(jnp.int32)

    def solve(rows):
        sweep(rows, count, x_ref, idx_ref, rank, size)
        high, mid, low = split3(x_ref[0:rows, :])
        taken = hot[0:rows]
        full = dot(taken, low, ((0,), (0,))) + dot(taken, mid, ((0,), (0,))) + dot(taken, high, ((0,), (0,)))
        full_ref[...] = jnp.where(same > 0.5, -full, 0.0)

    @pl.when(count <= SMALL)
    def _():
        solve(SMALL)

    @pl.when(count > SMALL)
    def _():
        solve(OBS_TILE)

    for copy in copies[3:]:
        copy.wait()
    innovation = mv_ref[...] + jnp.sqrt(var) * jit_ref[...] - pred
    weighted = dot(innovation, full_ref[...], ((1,), (0,)), lax.Precision.HIGHEST)
    out_ref[1] = weighted.astype(BF16)


def weigh(predicted, measured_value, measurement_variance, observation_jitter, obs_block):
    members = predicted.shape[2]
    return pl.pallas_call(
        weigh_kernel,
        out_shape=jax.ShapeDtypeStruct((2, members, OBS_TILE), BF16),
        in_specs=[pl.BlockSpec(memory_space=pltpu.HBM)] * 5,
        out_specs=pl.BlockSpec(memory_space=pltpu.VMEM),
        scratch_shapes=[
            pltpu.VMEM((members, OBS_TILE), F32),
            pltpu.VMEM((1, OBS_TILE), F32),
            pltpu.VMEM((1, OBS_TILE), F32),
            pltpu.VMEM((members, OBS_TILE), F32),
            pltpu.VMEM((obs_block.shape[1], OBS_TILE), jnp.int32),
            pltpu.VMEM((OBS_TILE, OBS_TILE), F32),
            pltpu.VMEM((OBS_TILE, OBS_TILE), jnp.int32),
            pltpu.VMEM((OBS_TILE, OBS_TILE), F32),
            pltpu.SemaphoreType.DMA((5,)),
        ],
        compiler_params=pltpu.CompilerParams(vmem_limit_bytes=16 * 2**20),
        name="weigh",
    )(*in_hbm(predicted, measured_value, measurement_variance, observation_jitter, obs_block))


def offset(which, place):
    even = 1 - 2 * (place & 1)
    return (0, even, -even)[which]


def prepare_kernel(
    params_ref, radius_hbm, pattern_hbm, obs_hbm, turned_ref, taper_ref, radius_ref, pattern_ref, obs_ref, sems
):
    members = params_ref.shape[1]
    tile_x = lax.axis_index("gx")
    tile_y = lax.axis_index("gy")
    count_x, count_y = obs_ref.shape[0], obs_ref.shape[1]
    copies = fetch([(radius_hbm, radius_ref), (pattern_hbm, pattern_ref), (obs_hbm, obs_ref)], sems)

    for b in range(BLOCKS):
        block = params_ref[b].astype(F32)
        mean = jnp.sum(block, axis=0, keepdims=True) / members
        turned_ref[b] = (block - mean).T.astype(BF16)
    for copy in copies:
        copy.wait()
    shape = (BLOCKS, OBS_TILE)
    block = iota(shape, 0)
    radius = jnp.zeros(shape, jnp.int32)
    for b in range(BLOCKS):
        radius = jnp.where(block == b, radius_ref[b // BLK_Y, b % BLK_Y], radius)
    reach = (radius + 1).astype(F32)
    reach = reach * reach
    pattern = jnp.concatenate([pattern_ref[i] for i in range(BLK_X)], axis=0).astype(F32)
    slots = [jnp.broadcast_to(pattern[:, p : p + 1], shape) for p in range(PATTERN)]

    for t in range(9):
        iy, ix = t // 3, t % 3
        dx, dy = offset(ix, tile_x), offset(iy, tile_y)
        at_x, at_y = tile_x + dx, tile_y + dy
        valid = (at_x >= 0) & (at_x < count_x) & (at_y >= 0) & (at_y < count_y)
        at_x = jnp.clip(at_x, 0, count_x - 1)
        at_y = jnp.clip(at_y, 0, count_y - 1)
        obs = obs_ref[at_x, pl.ds(at_y, 1), :]
        step_x = dx * BLK_X + (obs >> 2) - (block >> 2)
        step_y = dy * BLK_Y + (obs & 3) - (block & 3)
        inside = (jnp.abs(step_x) <= 2) & (jnp.abs(step_y) <= 2) & valid
        slot = (step_x + 2) * 5 + (step_y + 2)
        picked = jnp.zeros(shape, F32)
        for p in range(PATTERN):
            picked = jnp.where(slot == p, slots[p], picked)
        spread = (step_x * step_x + step_y * step_y).astype(F32)
        shaped = jnp.maximum(1.0 - spread / reach, 0.0)
        taper_ref[iy, ix] = jnp.where(inside, picked, 0.0) * shaped / (members - 1)


def prepare(by_block, taper_radius, taper_pattern, obs_block):
    members = by_block.shape[1]
    return pl.pallas_call(
        prepare_kernel,
        out_shape=(
            jax.ShapeDtypeStruct((BLOCKS, CELLS, members), BF16),
            jax.ShapeDtypeStruct((3, 3, BLOCKS, OBS_TILE), F32),
        ),
        in_specs=[pl.BlockSpec(memory_space=pltpu.VMEM)] + [pl.BlockSpec(memory_space=pltpu.HBM)] * 3,
        out_specs=(pl.BlockSpec(memory_space=pltpu.VMEM), pl.BlockSpec(memory_space=pltpu.VMEM)),
        scratch_shapes=[
            pltpu.SMEM(taper_radius.shape, jnp.int32),
            pltpu.VMEM(taper_pattern.shape, jnp.int32),
            pltpu.VMEM(obs_block.shape, jnp.int32),
            pltpu.SemaphoreType.DMA((3,)),
        ],
        compiler_params=pltpu.CompilerParams(vmem_limit_bytes=16 * 2**20),
        cost_estimate=pl.CostEstimate(flops=4_000_000, bytes_accessed=1_000_000, transcendentals=0),
        name="prepare",
    )(by_block, *in_hbm(taper_radius, taper_pattern, obs_block))


def moved(b, which, turned_ref, taper_ref, tiles_ref):
    cross = dot(turned_ref[b], tiles_ref[0], ((1,), (0,)))
    count = tiles_ref.shape[2] // OBS_TILE
    taper = jnp.concatenate([taper_ref[which, k, pl.ds(b, 1), :] for k in range(count)], axis=1)
    gain = (cross * taper).astype(BF16)
    return dot(tiles_ref[1], gain, ((1,), (1,)))


def block_of(k, side, tile_y):
    first = 2 * ((tile_y & 1) ^ 1 ^ side)
    return (k >> 1) * BLK_Y + first + (k & 1)


def put(out_ref, b, updated):
    share = out_ref.shape[2]
    for d in range(out_ref.shape[0]):
        out_ref[d, b] = updated[d * share : (d + 1) * share]


def near_kernel(params_ref, turned_ref, taper_ref, own_ref, even_ref, out_ref, part_ref):
    tile_y = lax.axis_index("gy")

    for k in range(BLOCKS // 2):
        b = block_of(k, 0, tile_y)
        delta = moved(b, 0, turned_ref, taper_ref, own_ref) + moved(b, 1, turned_ref, taper_ref, even_ref)
        put(out_ref, b, (params_ref[b].astype(F32) + delta).astype(BF16))
    for k in range(BLOCKS // 2):
        b = block_of(k, 1, tile_y)
        part_ref[k] = params_ref[b].astype(F32) + moved(b, 0, turned_ref, taper_ref, own_ref)


def far_kernel(turned_ref, taper_ref, odd_ref, part_ref, done_ref, out_ref):
    del done_ref
    tile_y = lax.axis_index("gy")
    for k in range(BLOCKS // 2):
        b = block_of(k, 1, tile_y)
        put(out_ref, b, (part_ref[k] + moved(b, 2, turned_ref, taper_ref, odd_ref)).astype(BF16))


VMEM = pl.BlockSpec(memory_space=pltpu.VMEM)


def update_near(by_block, turned, taper, own, even, parts):
    members = by_block.shape[1]
    return pl.pallas_call(
        near_kernel,
        out_shape=(
            jax.ShapeDtypeStruct((parts, BLOCKS, members // parts, CELLS), BF16),
            jax.ShapeDtypeStruct((BLOCKS // 2, members, CELLS), F32),
        ),
        in_specs=[VMEM] * 5,
        out_specs=(VMEM, VMEM),
        compiler_params=pltpu.CompilerParams(vmem_limit_bytes=24 * 2**20),
        cost_estimate=pl.CostEstimate(flops=400_000_000, bytes_accessed=2_000_000, transcendentals=0),
        name="near",
    )(by_block, turned, taper, own, even)


def update_far(turned, taper, odd, part, done):
    return pl.pallas_call(
        far_kernel,
        out_shape=jax.ShapeDtypeStruct(done.shape, BF16),
        in_specs=[VMEM] * 4 + [pl.BlockSpec(memory_space=pl.ANY)],
        out_specs=VMEM,
        input_output_aliases={4: 0},
        compiler_params=pltpu.CompilerParams(vmem_limit_bytes=24 * 2**20),
        cost_estimate=pl.CostEstimate(flops=100_000_000, bytes_accessed=1_000_000, transcendentals=0),
        name="far",
    )(turned, taper, odd, part, done)


def swap(block, axis, first):
    pairs = [(i, i + 1) for i in range(first, lax.axis_size(axis) - 1, 2)]
    return lax.ppermute(block, axis, pairs + [(b, a) for a, b in pairs])


def per_device(
    params,
    predicted,
    measured_value,
    measurement_variance,
    observation_jitter,
    obs_block,
    taper_radius,
    taper_pattern,
):
    members = params.shape[0]
    parts = lax.axis_size("gy")
    by_block = params.reshape(members, BLOCKS, CELLS).transpose(1, 0, 2)
    own = weigh(predicted, measured_value, measurement_variance, observation_jitter, obs_block)
    even = swap(own, "gx", 0)
    odd = swap(own, "gx", 1)
    turned, taper = prepare(by_block, taper_radius, taper_pattern, obs_block)
    column = jnp.concatenate([own, even, odd], axis=2)
    column, turned, taper = lax.optimization_barrier((column, turned, taper))
    odd = swap(column, "gy", 1)
    even = swap(column, "gy", 0)
    done, part = update_near(by_block, turned, taper, column, even, parts)
    updated = update_far(turned, taper, odd, part, done)
    arrived = lax.all_to_all(updated, "gy", split_axis=0, concat_axis=0, tiled=True)
    share = members // parts
    arrived = arrived.reshape(parts, BLK_X, BLK_Y, share, CELLS).transpose(3, 1, 0, 2, 4)
    return arrived.reshape(share, BLK_X, parts * BLK_Y, CELLS)


def solution(mesh):
    placed = (
        P(None, "gx", "gy", None),
        P("gx", "gy", None, None),
        P("gx", "gy", None),
        P("gx", "gy", None),
        P("gx", "gy", None, None),
        P(),
        P("gx", "gy"),
        P("gx", "gy", None),
    )
    return jax.shard_map(
        per_device, mesh=mesh, in_specs=placed, out_specs=P("gy", "gx", None, None), check_vma=False
    )
```

```python
import functools

import jax
import jax.numpy as jnp
from jax import lax
from jax.experimental import pallas as pl
from jax.experimental.pallas import tpu as pltpu
from jax.sharding import PartitionSpec as P

CELLS = 128
BLK_X = 2
BLK_Y = 4
BLOCKS = BLK_X * BLK_Y
OBS_TILE = 128
PATTERN = 25
SMALL = 32

F32 = jnp.float32
BF16 = jnp.bfloat16


def iota(shape, dim):
    return lax.broadcasted_iota(jnp.int32, shape, dim)


def split3(x):
    high = x.astype(BF16)
    rest = x - high.astype(F32)
    mid = rest.astype(BF16)
    low = (rest - mid.astype(F32)).astype(BF16)
    return high, mid, low


def dot(a, b, dims, precision=None):
    return lax.dot_general(a, b, ((dims[0], dims[1]), ((), ())), precision=precision, preferred_element_type=F32)


def sweep(rows, count, x_ref, idx_ref, rank, size):
    row = iota((rows, OBS_TILE), 0)
    exists = row < size

    def taken(spread, indices):
        return jnp.take_along_axis(spread, indices, axis=1, mode="promise_in_bounds")

    def step(k, carry):
        t = 2 * k
        u = t + 1
        row_t, row_u = x_ref[pl.ds(t, 1), :], x_ref[pl.ds(u, 1), :]
        spread_t = jnp.broadcast_to(row_t, (rows, OBS_TILE))
        spread_u = jnp.broadcast_to(row_u, (rows, OBS_TILE))
        at_t = jnp.broadcast_to(idx_ref[pl.ds(t, 1), :], (8, OBS_TILE))
        at_u = jnp.broadcast_to(idx_ref[pl.ds(u, 1), :], (8, OBS_TILE))
        has_t, has_u = t < size, u < size
        a = jnp.where(has_t, taken(spread_t[0:8], at_t)[0:1], 1.0)
        b = jnp.where(has_u, taken(spread_t[0:8], at_u)[0:1], 0.0)
        d = jnp.where(has_u, taken(spread_u[0:8], at_u)[0:1], 1.0)
        own_t, own_u = rank == t, rank == u
        own = own_t | own_u
        head_t = jnp.where(own, jnp.where(own_t, -1.0, 0.0), row_t)
        head_u = jnp.where(own, jnp.where(own_u, -1.0, 0.0), row_u)
        inverse = 1.0 / a
        factor = b * inverse
        scaled_u = (head_u - factor * head_t) / (d - b * factor)
        scaled_t = head_t * inverse - factor * scaled_u
        column_t = jnp.where(exists, taken(spread_t, idx_ref[0:rows, :]), 0.0)
        column_u = jnp.where(exists, taken(spread_u, idx_ref[0:rows, :]), 0.0)
        on_t, on_u = row == t, row == u
        on = on_t | on_u
        column_t = jnp.where(on, jnp.where(on_t, -1.0, 0.0), column_t)
        column_u = jnp.where(on, jnp.where(on_u, -1.0, 0.0), column_u)
        x = jnp.where(on | own, 0.0, x_ref[0:rows, :])
        x_ref[0:rows, :] = x - column_t * scaled_t - column_u * scaled_u
        return carry

    lax.fori_loop(0, (count + 1) // 2, step, 0)


def in_hbm(*arrays):
    return [pltpu.with_memory_space_constraint(array, pltpu.HBM) for array in arrays]


def fetch(pairs, sems):
    copies = [pltpu.make_async_copy(src, dst, sems.at[k]) for k, (src, dst) in enumerate(pairs)]
    for copy in copies:
        copy.start()
    return copies


def weigh_kernel(
    pred_hbm, mv_hbm, var_hbm, jit_hbm, obs_hbm, out_ref,
    pred_ref, mv_ref, var_ref, jit_ref, obs_ref, x_ref, idx_ref, full_ref, sems,
):
    members = pred_ref.shape[0]
    tile_x = lax.axis_index("gx")
    tile_y = lax.axis_index("gy")
    square = (OBS_TILE, OBS_TILE)
    pairs = [
        (pred_hbm.at[0, 0], pred_ref),
        (obs_hbm.at[tile_x], obs_ref),
        (var_hbm.at[0], var_ref),
        (mv_hbm.at[0], mv_ref),
        (jit_hbm.at[0, 0], jit_ref),
    ]
    copies = fetch(pairs, sems)
    for copy in copies[:3]:
        copy.wait()
    pred = pred_ref[...]
    var = var_ref[...]
    mean = jnp.sum(pred, axis=0, keepdims=True) / members
    deviation = (pred - mean).astype(BF16)
    out_ref[0] = deviation
    obs = obs_ref[pl.ds(tile_y, 1), :]
    groups = (iota((BLOCKS, OBS_TILE), 0) == obs).astype(BF16)
    same = dot(groups, groups, ((0,), (0,)))
    gram = dot(deviation, deviation, ((0,), (0,))) / (members - 1)
    row, col = iota(square, 0), iota(square, 1)
    system = jnp.where(same > 0.5, gram, 0.0) + jnp.where(row == col, var, 0.0)
    size = jnp.sum(same, axis=0, keepdims=True)
    count = jnp.max(size).astype(jnp.int32)
    size = size.astype(jnp.int32)
    rank = jnp.sum(jnp.where(row < col, same, 0.0), axis=0, keepdims=True).astype(jnp.int32)
    place = row == rank
    hot = place.astype(BF16)
    high, mid, low = split3(system)
    x_ref[...] = (
        dot(hot, low, ((1,), (0,))) + dot(hot, mid, ((1,), (0,))) + dot(hot, high, ((1,), (0,)))
    )
    numbered = jnp.where(place, col, 0).astype(F32).astype(BF16)
    idx_ref[...] = dot(numbered, same.astype(BF16), ((1,), (0,))).astype(jnp.int32)

    def solve(rows):
        sweep(rows, count, x_ref, idx_ref, rank, size)
        high, mid, low = split3(x_ref[0:rows, :])
        taken = hot[0:rows]
        full = dot(taken, low, ((0,), (0,))) + dot(taken, mid, ((0,), (0,))) + dot(taken, high, ((0,), (0,)))
        full_ref[...] = jnp.where(same > 0.5, -full, 0.0)

    @pl.when(count <= SMALL)
    def _():
        solve(SMALL)

    @pl.when(count > SMALL)
    def _():
        solve(OBS_TILE)

    for copy in copies[3:]:
        copy.wait()
    innovation = mv_ref[...] + jnp.sqrt(var) * jit_ref[...] - pred
    weighted = dot(innovation, full_ref[...], ((1,), (0,)), lax.Precision.HIGHEST)
    out_ref[1] = weighted.astype(BF16)


def weigh(predicted, measured_value, measurement_variance, observation_jitter, obs_block):
    members = predicted.shape[2]
    return pl.pallas_call(
        weigh_kernel,
        out_shape=jax.ShapeDtypeStruct((2, members, OBS_TILE), BF16),
        in_specs=[pl.BlockSpec(memory_space=pltpu.HBM)] * 5,
        out_specs=pl.BlockSpec(memory_space=pltpu.VMEM),
        scratch_shapes=[
            pltpu.VMEM((members, OBS_TILE), F32),
            pltpu.VMEM((1, OBS_TILE), F32),
            pltpu.VMEM((1, OBS_TILE), F32),
            pltpu.VMEM((members, OBS_TILE), F32),
            pltpu.VMEM((obs_block.shape[1], OBS_TILE), jnp.int32),
            pltpu.VMEM((OBS_TILE, OBS_TILE), F32),
            pltpu.VMEM((OBS_TILE, OBS_TILE), jnp.int32),
            pltpu.VMEM((OBS_TILE, OBS_TILE), F32),
            pltpu.SemaphoreType.DMA((5,)),
        ],
        compiler_params=pltpu.CompilerParams(vmem_limit_bytes=16 * 2**20),
        name="weigh",
    )(*in_hbm(predicted, measured_value, measurement_variance, observation_jitter, obs_block))


def offset(which, place):
    even = 1 - 2 * (place & 1)
    return (0, even, -even)[which]


def prepare_kernel(
    params_ref, radius_hbm, pattern_hbm, obs_hbm, turned_ref, taper_ref, radius_ref, pattern_ref, obs_ref, sems
):
    members = params_ref.shape[1]
    tile_x = lax.axis_index("gx")
    tile_y = lax.axis_index("gy")
    count_x, count_y = obs_ref.shape[0], obs_ref.shape[1]
    copies = fetch([(radius_hbm, radius_ref), (pattern_hbm, pattern_ref), (obs_hbm, obs_ref)], sems)

    for b in range(BLOCKS):
        block = params_ref[b].astype(F32)
        mean = jnp.sum(block, axis=0, keepdims=True) / members
        turned_ref[b] = (block - mean).T.astype(BF16)
    for copy in copies:
        copy.wait()
    shape = (BLOCKS, OBS_TILE)
    block = iota(shape, 0)
    radius = jnp.zeros(shape, jnp.int32)
    for b in range(BLOCKS):
        radius = jnp.where(block == b, radius_ref[b // BLK_Y, b % BLK_Y], radius)
    reach = (radius + 1).astype(F32)
    reach = reach * reach
    pattern = jnp.concatenate([pattern_ref[i] for i in range(BLK_X)], axis=0).astype(F32)
    slots = [jnp.broadcast_to(pattern[:, p : p + 1], shape) for p in range(PATTERN)]

    for t in range(9):
        iy, ix = t // 3, t % 3
        dx, dy = offset(ix, tile_x), offset(iy, tile_y)
        at_x, at_y = tile_x + dx, tile_y + dy
        valid = (at_x >= 0) & (at_x < count_x) & (at_y >= 0) & (at_y < count_y)
        at_x = jnp.clip(at_x, 0, count_x - 1)
        at_y = jnp.clip(at_y, 0, count_y - 1)
        obs = obs_ref[at_x, pl.ds(at_y, 1), :]
        step_x = dx * BLK_X + (obs >> 2) - (block >> 2)
        step_y = dy * BLK_Y + (obs & 3) - (block & 3)
        inside = (jnp.abs(step_x) <= 2) & (jnp.abs(step_y) <= 2) & valid
        slot = (step_x + 2) * 5 + (step_y + 2)
        picked = jnp.zeros(shape, F32)
        for p in range(PATTERN):
            picked = jnp.where(slot == p, slots[p], picked)
        spread = (step_x * step_x + step_y * step_y).astype(F32)
        shaped = jnp.maximum(1.0 - spread / reach, 0.0)
        taper_ref[iy, ix] = jnp.where(inside, picked, 0.0) * shaped / (members - 1)


def prepare(by_block, taper_radius, taper_pattern, obs_block):
    members = by_block.shape[1]
    return pl.pallas_call(
        prepare_kernel,
        out_shape=(
            jax.ShapeDtypeStruct((BLOCKS, CELLS, members), BF16),
            jax.ShapeDtypeStruct((3, 3, BLOCKS, OBS_TILE), F32),
        ),
        in_specs=[pl.BlockSpec(memory_space=pltpu.VMEM)] + [pl.BlockSpec(memory_space=pltpu.HBM)] * 3,
        out_specs=(pl.BlockSpec(memory_space=pltpu.VMEM), pl.BlockSpec(memory_space=pltpu.VMEM)),
        scratch_shapes=[
            pltpu.SMEM(taper_radius.shape, jnp.int32),
            pltpu.VMEM(taper_pattern.shape, jnp.int32),
            pltpu.VMEM(obs_block.shape, jnp.int32),
            pltpu.SemaphoreType.DMA((3,)),
        ],
        compiler_params=pltpu.CompilerParams(vmem_limit_bytes=16 * 2**20),
        cost_estimate=pl.CostEstimate(flops=4_000_000, bytes_accessed=1_000_000, transcendentals=0),
        name="prepare",
    )(by_block, *in_hbm(taper_radius, taper_pattern, obs_block))


def moved(b, which, turned_ref, taper_ref, tiles_ref):
    cross = dot(turned_ref[b], tiles_ref[0], ((1,), (0,)))
    count = tiles_ref.shape[2] // OBS_TILE
    taper = jnp.concatenate([taper_ref[which, k, pl.ds(b, 1), :] for k in range(count)], axis=1)
    gain = (cross * taper).astype(BF16)
    return dot(tiles_ref[1], gain, ((1,), (1,)))


def block_of(k, side, tile_y):
    first = 2 * ((tile_y & 1) ^ 1 ^ side)
    return (k >> 1) * BLK_Y + first + (k & 1)


def put(out_ref, b, updated):
    share = out_ref.shape[2]
    for d in range(out_ref.shape[0]):
        out_ref[d, b] = updated[d * share : (d + 1) * share]


def near_kernel(params_ref, turned_ref, taper_ref, own_ref, even_ref, out_ref, part_ref):
    tile_y = lax.axis_index("gy")

    for k in range(BLOCKS // 2):
        b = block_of(k, 0, tile_y)
        delta = moved(b, 0, turned_ref, taper_ref, own_ref) + moved(b, 1, turned_ref, taper_ref, even_ref)
        put(out_ref, b, (params_ref[b].astype(F32) + delta).astype(BF16))
    for k in range(BLOCKS // 2):
        b = block_of(k, 1, tile_y)
        part_ref[k] = params_ref[b].astype(F32) + moved(b, 0, turned_ref, taper_ref, own_ref)


def far_kernel(turned_ref, taper_ref, odd_ref, part_ref, done_ref, out_ref):
    del done_ref
    tile_y = lax.axis_index("gy")
    for k in range(BLOCKS // 2):
        b = block_of(k, 1, tile_y)
        put(out_ref, b, (part_ref[k] + moved(b, 2, turned_ref, taper_ref, odd_ref)).astype(BF16))


VMEM = pl.BlockSpec(memory_space=pltpu.VMEM)


def update_near(by_block, turned, taper, own, even, parts):
    members = by_block.shape[1]
    return pl.pallas_call(
        near_kernel,
        out_shape=(
            jax.ShapeDtypeStruct((parts, BLOCKS, members // parts, CELLS), BF16),
            jax.ShapeDtypeStruct((BLOCKS // 2, members, CELLS), F32),
        ),
        in_specs=[VMEM] * 5,
        out_specs=(VMEM, VMEM),
        compiler_params=pltpu.CompilerParams(vmem_limit_bytes=24 * 2**20),
        cost_estimate=pl.CostEstimate(flops=400_000_000, bytes_accessed=2_000_000, transcendentals=0),
        name="near",
    )(by_block, turned, taper, own, even)


def update_far(turned, taper, odd, part, done):
    return pl.pallas_call(
        far_kernel,
        out_shape=jax.ShapeDtypeStruct(done.shape, BF16),
        in_specs=[VMEM] * 4 + [pl.BlockSpec(memory_space=pl.ANY)],
        out_specs=VMEM,
        input_output_aliases={4: 0},
        compiler_params=pltpu.CompilerParams(vmem_limit_bytes=24 * 2**20),
        cost_estimate=pl.CostEstimate(flops=100_000_000, bytes_accessed=1_000_000, transcendentals=0),
        name="far",
    )(turned, taper, odd, part, done)


def swap(block, axis, first):
    count = lax.axis_size(axis)
    pairs = [(i, i + 1) for i in range(first, count - 1, 2)]
    paired = {i for pair in pairs for i in pair}
    alone = [(i, i) for i in range(count) if i not in paired]
    return lax.ppermute(block, axis, pairs + [(b, a) for a, b in pairs] + alone)


def per_device(
    params,
    predicted,
    measured_value,
    measurement_variance,
    observation_jitter,
    obs_block,
    taper_radius,
    taper_pattern,
):
    members = params.shape[0]
    parts = lax.axis_size("gy")
    by_block = params.reshape(members, BLOCKS, CELLS).transpose(1, 0, 2)
    own = weigh(predicted, measured_value, measurement_variance, observation_jitter, obs_block)
    even = swap(own, "gx", 0)
    odd = swap(own, "gx", 1)
    turned, taper = prepare(by_block, taper_radius, taper_pattern, obs_block)
    column = jnp.concatenate([own, even, odd], axis=2)
    column, turned, taper = lax.optimization_barrier((column, turned, taper))
    even = swap(column, "gy", 0)
    odd = swap(column, "gy", 1)
    done, part = update_near(by_block, turned, taper, column, even, parts)
    updated = update_far(turned, taper, odd, part, done)
    arrived = lax.all_to_all(updated, "gy", split_axis=0, concat_axis=0, tiled=True)
    share = members // parts
    arrived = arrived.reshape(parts, BLK_X, BLK_Y, share, CELLS).transpose(3, 1, 0, 2, 4)
    return arrived.reshape(share, BLK_X, parts * BLK_Y, CELLS)


def solution(mesh):
    placed = (
        P(None, "gx", "gy", None),
        P("gx", "gy", None, None),
        P("gx", "gy", None),
        P("gx", "gy", None),
        P("gx", "gy", None, None),
        P(),
        P("gx", "gy"),
        P("gx", "gy", None),
    )
    return jax.shard_map(
        per_device, mesh=mesh, in_specs=placed, out_specs=P("gy", "gx", None, None), check_vma=False
    )
```

```python
import functools

import jax
import jax.numpy as jnp
from jax import lax
from jax.experimental import pallas as pl
from jax.experimental.pallas import tpu as pltpu
from jax.sharding import PartitionSpec as P

CELLS = 128
BLK_X = 2
BLK_Y = 4
BLOCKS = BLK_X * BLK_Y
OBS_TILE = 128
PATTERN = 25
SMALL = 32

F32 = jnp.float32
BF16 = jnp.bfloat16


def iota(shape, dim):
    return lax.broadcasted_iota(jnp.int32, shape, dim)


def split3(x):
    high = x.astype(BF16)
    rest = x - high.astype(F32)
    mid = rest.astype(BF16)
    low = (rest - mid.astype(F32)).astype(BF16)
    return high, mid, low


def dot(a, b, dims, precision=None):
    return lax.dot_general(a, b, ((dims[0], dims[1]), ((), ())), precision=precision, preferred_element_type=F32)


def sweep(rows, count, x_ref, idx_ref, rank, size):
    row = iota((rows, OBS_TILE), 0)
    exists = row < size

    def taken(spread, indices):
        return jnp.take_along_axis(spread, indices, axis=1, mode="promise_in_bounds")

    def step(k, carry):
        t = 2 * k
        u = t + 1
        row_t, row_u = x_ref[pl.ds(t, 1), :], x_ref[pl.ds(u, 1), :]
        spread_t = jnp.broadcast_to(row_t, (rows, OBS_TILE))
        spread_u = jnp.broadcast_to(row_u, (rows, OBS_TILE))
        at_t = jnp.broadcast_to(idx_ref[pl.ds(t, 1), :], (8, OBS_TILE))
        at_u = jnp.broadcast_to(idx_ref[pl.ds(u, 1), :], (8, OBS_TILE))
        has_t, has_u = t < size, u < size
        a = jnp.where(has_t, taken(spread_t[0:8], at_t)[0:1], 1.0)
        b = jnp.where(has_u, taken(spread_t[0:8], at_u)[0:1], 0.0)
        d = jnp.where(has_u, taken(spread_u[0:8], at_u)[0:1], 1.0)
        own_t, own_u = rank == t, rank == u
        own = own_t | own_u
        head_t = jnp.where(own, jnp.where(own_t, -1.0, 0.0), row_t)
        head_u = jnp.where(own, jnp.where(own_u, -1.0, 0.0), row_u)
        inverse = 1.0 / a
        factor = b * inverse
        scaled_u = (head_u - factor * head_t) / (d - b * factor)
        scaled_t = head_t * inverse - factor * scaled_u
        column_t = jnp.where(exists, taken(spread_t, idx_ref[0:rows, :]), 0.0)
        column_u = jnp.where(exists, taken(spread_u, idx_ref[0:rows, :]), 0.0)
        on_t, on_u = row == t, row == u
        on = on_t | on_u
        column_t = jnp.where(on, jnp.where(on_t, -1.0, 0.0), column_t)
        column_u = jnp.where(on, jnp.where(on_u, -1.0, 0.0), column_u)
        x = jnp.where(on | own, 0.0, x_ref[0:rows, :])
        x_ref[0:rows, :] = x - column_t * scaled_t - column_u * scaled_u
        return carry

    lax.fori_loop(0, (count + 1) // 2, step, 0)


def in_hbm(*arrays):
    return [pltpu.with_memory_space_constraint(array, pltpu.HBM) for array in arrays]


def fetch(pairs, sems):
    copies = [pltpu.make_async_copy(src, dst, sems.at[k]) for k, (src, dst) in enumerate(pairs)]
    for copy in copies:
        copy.start()
    return copies


def weigh_kernel(
    pred_hbm, mv_hbm, var_hbm, jit_hbm, obs_hbm, out_ref,
    pred_ref, mv_ref, var_ref, jit_ref, obs_ref, x_ref, idx_ref, full_ref, sems,
):
    members = pred_ref.shape[0]
    tile_x = lax.axis_index("gx")
    tile_y = lax.axis_index("gy")
    square = (OBS_TILE, OBS_TILE)
    pairs = [
        (pred_hbm.at[0, 0], pred_ref),
        (obs_hbm.at[tile_x], obs_ref),
        (var_hbm.at[0], var_ref),
        (mv_hbm.at[0], mv_ref),
        (jit_hbm.at[0, 0], jit_ref),
    ]
    copies = fetch(pairs, sems)
    for copy in copies[:3]:
        copy.wait()
    pred = pred_ref[...]
    var = var_ref[...]
    mean = jnp.sum(pred, axis=0, keepdims=True) / members
    deviation = (pred - mean).astype(BF16)
    out_ref[0] = deviation
    obs = obs_ref[pl.ds(tile_y, 1), :]
    groups = (iota((BLOCKS, OBS_TILE), 0) == obs).astype(BF16)
    same = dot(groups, groups, ((0,), (0,)))
    gram = dot(deviation, deviation, ((0,), (0,))) / (members - 1)
    row, col = iota(square, 0), iota(square, 1)
    system = jnp.where(same > 0.5, gram, 0.0) + jnp.where(row == col, var, 0.0)
    size = jnp.sum(same, axis=0, keepdims=True)
    count = jnp.max(size).astype(jnp.int32)
    size = size.astype(jnp.int32)
    rank = jnp.sum(jnp.where(row < col, same, 0.0), axis=0, keepdims=True).astype(jnp.int32)
    place = row == rank
    hot = place.astype(BF16)
    high, mid, low = split3(system)
    x_ref[...] = (
        dot(hot, low, ((1,), (0,))) + dot(hot, mid, ((1,), (0,))) + dot(hot, high, ((1,), (0,)))
    )
    numbered = jnp.where(place, col, 0).astype(F32).astype(BF16)
    idx_ref[...] = dot(numbered, same.astype(BF16), ((1,), (0,))).astype(jnp.int32)

    def solve(rows):
        sweep(rows, count, x_ref, idx_ref, rank, size)
        high, mid, low = split3(x_ref[0:rows, :])
        taken = hot[0:rows]
        full = dot(taken, low, ((0,), (0,))) + dot(taken, mid, ((0,), (0,))) + dot(taken, high, ((0,), (0,)))
        full_ref[...] = jnp.where(same > 0.5, -full, 0.0)

    @pl.when(count <= SMALL)
    def _():
        solve(SMALL)

    @pl.when(count > SMALL)
    def _():
        solve(OBS_TILE)

    for copy in copies[3:]:
        copy.wait()
    innovation = mv_ref[...] + jnp.sqrt(var) * jit_ref[...] - pred
    weighted = dot(innovation, full_ref[...], ((1,), (0,)), lax.Precision.HIGHEST)
    out_ref[1] = weighted.astype(BF16)


def weigh(predicted, measured_value, measurement_variance, observation_jitter, obs_block):
    members = predicted.shape[2]
    return pl.pallas_call(
        weigh_kernel,
        out_shape=jax.ShapeDtypeStruct((2, members, OBS_TILE), BF16),
        in_specs=[pl.BlockSpec(memory_space=pltpu.HBM)] * 5,
        out_specs=pl.BlockSpec(memory_space=pltpu.VMEM),
        scratch_shapes=[
            pltpu.VMEM((members, OBS_TILE), F32),
            pltpu.VMEM((1, OBS_TILE), F32),
            pltpu.VMEM((1, OBS_TILE), F32),
            pltpu.VMEM((members, OBS_TILE), F32),
            pltpu.VMEM((obs_block.shape[1], OBS_TILE), jnp.int32),
            pltpu.VMEM((OBS_TILE, OBS_TILE), F32),
            pltpu.VMEM((OBS_TILE, OBS_TILE), jnp.int32),
            pltpu.VMEM((OBS_TILE, OBS_TILE), F32),
            pltpu.SemaphoreType.DMA((5,)),
        ],
        compiler_params=pltpu.CompilerParams(vmem_limit_bytes=16 * 2**20),
        name="weigh",
    )(*in_hbm(predicted, measured_value, measurement_variance, observation_jitter, obs_block))


def offset(which, place):
    even = 1 - 2 * (place & 1)
    return (0, even, -even)[which]


def prepare_kernel(
    params_ref, radius_hbm, pattern_hbm, obs_hbm, turned_ref, taper_ref, radius_ref, pattern_ref, obs_ref, sems
):
    members = params_ref.shape[1]
    tile_x = lax.axis_index("gx")
    tile_y = lax.axis_index("gy")
    count_x, count_y = obs_ref.shape[0], obs_ref.shape[1]
    copies = fetch([(radius_hbm, radius_ref), (pattern_hbm, pattern_ref), (obs_hbm, obs_ref)], sems)

    for b in range(BLOCKS):
        block = params_ref[b].astype(F32)
        mean = jnp.sum(block, axis=0, keepdims=True) / members
        turned_ref[b] = (block - mean).T.astype(BF16)
    for copy in copies:
        copy.wait()
    shape = (BLOCKS, OBS_TILE)
    block = iota(shape, 0)
    radius = jnp.zeros(shape, jnp.int32)
    for b in range(BLOCKS):
        radius = jnp.where(block == b, radius_ref[b // BLK_Y, b % BLK_Y], radius)
    reach = (radius + 1).astype(F32)
    reach = reach * reach
    pattern = jnp.concatenate([pattern_ref[i] for i in range(BLK_X)], axis=0).astype(F32)
    slots = [jnp.broadcast_to(pattern[:, p : p + 1], shape) for p in range(PATTERN)]

    for t in range(9):
        iy, ix = t // 3, t % 3
        dx, dy = offset(ix, tile_x), offset(iy, tile_y)
        at_x, at_y = tile_x + dx, tile_y + dy
        valid = (at_x >= 0) & (at_x < count_x) & (at_y >= 0) & (at_y < count_y)
        at_x = jnp.clip(at_x, 0, count_x - 1)
        at_y = jnp.clip(at_y, 0, count_y - 1)
        obs = obs_ref[at_x, pl.ds(at_y, 1), :]
        step_x = dx * BLK_X + (obs >> 2) - (block >> 2)
        step_y = dy * BLK_Y + (obs & 3) - (block & 3)
        inside = (jnp.abs(step_x) <= 2) & (jnp.abs(step_y) <= 2) & valid
        slot = (step_x + 2) * 5 + (step_y + 2)
        picked = jnp.zeros(shape, F32)
        for p in range(PATTERN):
            picked = jnp.where(slot == p, slots[p], picked)
        spread = (step_x * step_x + step_y * step_y).astype(F32)
        shaped = jnp.maximum(1.0 - spread / reach, 0.0)
        taper_ref[iy, ix] = jnp.where(inside, picked, 0.0) * shaped / (members - 1)


def prepare(by_block, taper_radius, taper_pattern, obs_block):
    members = by_block.shape[1]
    return pl.pallas_call(
        prepare_kernel,
        out_shape=(
            jax.ShapeDtypeStruct((BLOCKS, CELLS, members), BF16),
            jax.ShapeDtypeStruct((3, 3, BLOCKS, OBS_TILE), F32),
        ),
        in_specs=[pl.BlockSpec(memory_space=pltpu.VMEM)] + [pl.BlockSpec(memory_space=pltpu.HBM)] * 3,
        out_specs=(pl.BlockSpec(memory_space=pltpu.VMEM), pl.BlockSpec(memory_space=pltpu.VMEM)),
        scratch_shapes=[
            pltpu.SMEM(taper_radius.shape, jnp.int32),
            pltpu.VMEM(taper_pattern.shape, jnp.int32),
            pltpu.VMEM(obs_block.shape, jnp.int32),
            pltpu.SemaphoreType.DMA((3,)),
        ],
        compiler_params=pltpu.CompilerParams(vmem_limit_bytes=16 * 2**20),
        cost_estimate=pl.CostEstimate(flops=4_000_000, bytes_accessed=1_000_000, transcendentals=0),
        name="prepare",
    )(by_block, *in_hbm(taper_radius, taper_pattern, obs_block))


def moved(b, which, turned_ref, taper_ref, tiles_ref):
    cross = dot(turned_ref[b], tiles_ref[0], ((1,), (0,)))
    count = tiles_ref.shape[2] // OBS_TILE
    taper = jnp.concatenate([taper_ref[which, k, pl.ds(b, 1), :] for k in range(count)], axis=1)
    gain = (cross * taper).astype(BF16)
    return dot(tiles_ref[1], gain, ((1,), (1,)))


def block_of(k, side, tile_y):
    first = 2 * ((tile_y & 1) ^ 1 ^ side)
    return (k >> 1) * BLK_Y + first + (k & 1)


def put(out_ref, b, updated):
    share = out_ref.shape[2]
    for d in range(out_ref.shape[0]):
        out_ref[d, b] = updated[d * share : (d + 1) * share]


def near_kernel(params_ref, turned_ref, taper_ref, own_ref, even_ref, out_ref, part_ref):
    tile_y = lax.axis_index("gy")

    for k in range(BLOCKS // 2):
        b = block_of(k, 0, tile_y)
        delta = moved(b, 0, turned_ref, taper_ref, own_ref) + moved(b, 1, turned_ref, taper_ref, even_ref)
        put(out_ref, b, (params_ref[b].astype(F32) + delta).astype(BF16))
    for k in range(BLOCKS // 2):
        b = block_of(k, 1, tile_y)
        part_ref[k] = params_ref[b].astype(F32) + moved(b, 0, turned_ref, taper_ref, own_ref)


def far_kernel(turned_ref, taper_ref, odd_ref, part_ref, done_ref, out_ref):
    del done_ref
    tile_y = lax.axis_index("gy")
    for k in range(BLOCKS // 2):
        b = block_of(k, 1, tile_y)
        put(out_ref, b, (part_ref[k] + moved(b, 2, turned_ref, taper_ref, odd_ref)).astype(BF16))


VMEM = pl.BlockSpec(memory_space=pltpu.VMEM)


def update_near(by_block, turned, taper, own, even, parts):
    members = by_block.shape[1]
    return pl.pallas_call(
        near_kernel,
        out_shape=(
            jax.ShapeDtypeStruct((parts, BLOCKS, members // parts, CELLS), BF16),
            jax.ShapeDtypeStruct((BLOCKS // 2, members, CELLS), F32),
        ),
        in_specs=[VMEM] * 5,
        out_specs=(VMEM, VMEM),
        compiler_params=pltpu.CompilerParams(vmem_limit_bytes=24 * 2**20),
        cost_estimate=pl.CostEstimate(flops=400_000_000, bytes_accessed=2_000_000, transcendentals=0),
        name="near",
    )(by_block, turned, taper, own, even)


def update_far(turned, taper, odd, part, done):
    return pl.pallas_call(
        far_kernel,
        out_shape=jax.ShapeDtypeStruct(done.shape, BF16),
        in_specs=[VMEM] * 4 + [pl.BlockSpec(memory_space=pl.ANY)],
        out_specs=VMEM,
        input_output_aliases={4: 0},
        compiler_params=pltpu.CompilerParams(vmem_limit_bytes=24 * 2**20),
        cost_estimate=pl.CostEstimate(flops=100_000_000, bytes_accessed=1_000_000, transcendentals=0),
        name="far",
    )(turned, taper, odd, part, done)


def swap(block, axis, first, close=False):
    count = lax.axis_size(axis)
    pairs = [(i, i + 1) for i in range(first, count - 1, 2)]
    if close:
        pairs.append((count - 1, 0))
    return lax.ppermute(block, axis, pairs + [(b, a) for a, b in pairs])


def per_device(
    params,
    predicted,
    measured_value,
    measurement_variance,
    observation_jitter,
    obs_block,
    taper_radius,
    taper_pattern,
):
    members = params.shape[0]
    parts = lax.axis_size("gy")
    by_block = params.reshape(members, BLOCKS, CELLS).transpose(1, 0, 2)
    own = weigh(predicted, measured_value, measurement_variance, observation_jitter, obs_block)
    even = swap(own, "gx", 0)
    odd = swap(own, "gx", 1, close=True)
    turned, taper = prepare(by_block, taper_radius, taper_pattern, obs_block)
    column = jnp.concatenate([own, even, odd], axis=2)
    column, turned, taper = lax.optimization_barrier((column, turned, taper))
    odd = swap(column, "gy", 1)
    even = swap(column, "gy", 0)
    done, part = update_near(by_block, turned, taper, column, even, parts)
    updated = update_far(turned, taper, odd, part, done)
    arrived = lax.all_to_all(updated, "gy", split_axis=0, concat_axis=0, tiled=True)
    share = members // parts
    arrived = arrived.reshape(parts, BLK_X, BLK_Y, share, CELLS).transpose(3, 1, 0, 2, 4)
    return arrived.reshape(share, BLK_X, parts * BLK_Y, CELLS)


def solution(mesh):
    placed = (
        P(None, "gx", "gy", None),
        P("gx", "gy", None, None),
        P("gx", "gy", None),
        P("gx", "gy", None),
        P("gx", "gy", None, None),
        P(),
        P("gx", "gy"),
        P("gx", "gy", None),
    )
    return jax.shard_map(
        per_device, mesh=mesh, in_specs=placed, out_specs=P("gy", "gx", None, None), check_vma=False
    )
```

```python
import functools

import jax
import jax.numpy as jnp
from jax import lax
from jax.experimental import pallas as pl
from jax.experimental.pallas import tpu as pltpu
from jax.sharding import PartitionSpec as P

CELLS = 128
BLK_X = 2
BLK_Y = 4
BLOCKS = BLK_X * BLK_Y
OBS_TILE = 128
PATTERN = 25
SMALL = 32

F32 = jnp.float32
BF16 = jnp.bfloat16


def iota(shape, dim):
    return lax.broadcasted_iota(jnp.int32, shape, dim)


def split3(x):
    high = x.astype(BF16)
    rest = x - high.astype(F32)
    mid = rest.astype(BF16)
    low = (rest - mid.astype(F32)).astype(BF16)
    return high, mid, low


def dot(a, b, dims, precision=None):
    return lax.dot_general(a, b, ((dims[0], dims[1]), ((), ())), precision=precision, preferred_element_type=F32)


def sweep(rows, count, x_ref, idx_ref, rank, size):
    row = iota((rows, OBS_TILE), 0)
    exists = row < size

    def taken(spread, indices):
        return jnp.take_along_axis(spread, indices, axis=1, mode="promise_in_bounds")

    def step(k, carry):
        t = 2 * k
        u = t + 1
        row_t, row_u = x_ref[pl.ds(t, 1), :], x_ref[pl.ds(u, 1), :]
        spread_t = jnp.broadcast_to(row_t, (rows, OBS_TILE))
        spread_u = jnp.broadcast_to(row_u, (rows, OBS_TILE))
        at_t = jnp.broadcast_to(idx_ref[pl.ds(t, 1), :], (8, OBS_TILE))
        at_u = jnp.broadcast_to(idx_ref[pl.ds(u, 1), :], (8, OBS_TILE))
        has_t, has_u = t < size, u < size
        a = jnp.where(has_t, taken(spread_t[0:8], at_t)[0:1], 1.0)
        b = jnp.where(has_u, taken(spread_t[0:8], at_u)[0:1], 0.0)
        d = jnp.where(has_u, taken(spread_u[0:8], at_u)[0:1], 1.0)
        own_t, own_u = rank == t, rank == u
        own = own_t | own_u
        head_t = jnp.where(own, jnp.where(own_t, -1.0, 0.0), row_t)
        head_u = jnp.where(own, jnp.where(own_u, -1.0, 0.0), row_u)
        inverse = 1.0 / a
        factor = b * inverse
        scaled_u = (head_u - factor * head_t) / (d - b * factor)
        scaled_t = head_t * inverse - factor * scaled_u
        column_t = jnp.where(exists, taken(spread_t, idx_ref[0:rows, :]), 0.0)
        column_u = jnp.where(exists, taken(spread_u, idx_ref[0:rows, :]), 0.0)
        on_t, on_u = row == t, row == u
        on = on_t | on_u
        column_t = jnp.where(on, jnp.where(on_t, -1.0, 0.0), column_t)
        column_u = jnp.where(on, jnp.where(on_u, -1.0, 0.0), column_u)
        x = jnp.where(on | own, 0.0, x_ref[0:rows, :])
        x_ref[0:rows, :] = x - column_t * scaled_t - column_u * scaled_u
        return carry

    lax.fori_loop(0, (count + 1) // 2, step, 0)


def in_hbm(*arrays):
    return [pltpu.with_memory_space_constraint(array, pltpu.HBM) for array in arrays]


def fetch(pairs, sems):
    copies = [pltpu.make_async_copy(src, dst, sems.at[k]) for k, (src, dst) in enumerate(pairs)]
    for copy in copies:
        copy.start()
    return copies


def weigh_kernel(
    pred_hbm, mv_hbm, var_hbm, jit_hbm, obs_hbm, out_ref,
    pred_ref, mv_ref, var_ref, jit_ref, obs_ref, x_ref, idx_ref, full_ref, sems,
):
    members = pred_ref.shape[0]
    tile_x = lax.axis_index("gx")
    tile_y = lax.axis_index("gy")
    square = (OBS_TILE, OBS_TILE)
    pairs = [
        (pred_hbm.at[0, 0], pred_ref),
        (obs_hbm.at[tile_x], obs_ref),
        (var_hbm.at[0], var_ref),
        (mv_hbm.at[0], mv_ref),
        (jit_hbm.at[0, 0], jit_ref),
    ]
    copies = fetch(pairs, sems)
    for copy in copies[:3]:
        copy.wait()
    pred = pred_ref[...]
    var = var_ref[...]
    mean = jnp.sum(pred, axis=0, keepdims=True) / members
    deviation = (pred - mean).astype(BF16)
    out_ref[0] = deviation
    obs = obs_ref[pl.ds(tile_y, 1), :]
    groups = (iota((BLOCKS, OBS_TILE), 0) == obs).astype(BF16)
    same = dot(groups, groups, ((0,), (0,)))
    gram = dot(deviation, deviation, ((0,), (0,))) / (members - 1)
    row, col = iota(square, 0), iota(square, 1)
    system = jnp.where(same > 0.5, gram, 0.0) + jnp.where(row == col, var, 0.0)
    size = jnp.sum(same, axis=0, keepdims=True)
    count = jnp.max(size).astype(jnp.int32)
    size = size.astype(jnp.int32)
    rank = jnp.sum(jnp.where(row < col, same, 0.0), axis=0, keepdims=True).astype(jnp.int32)
    place = row == rank
    hot = place.astype(BF16)
    high, mid, low = split3(system)
    x_ref[...] = (
        dot(hot, low, ((1,), (0,))) + dot(hot, mid, ((1,), (0,))) + dot(hot, high, ((1,), (0,)))
    )
    numbered = jnp.where(place, col, 0).astype(F32).astype(BF16)
    idx_ref[...] = dot(numbered, same.astype(BF16), ((1,), (0,))).astype(jnp.int32)

    def solve(rows):
        sweep(rows, count, x_ref, idx_ref, rank, size)
        high, mid, low = split3(x_ref[0:rows, :])
        taken = hot[0:rows]
        full = dot(taken, low, ((0,), (0,))) + dot(taken, mid, ((0,), (0,))) + dot(taken, high, ((0,), (0,)))
        full_ref[...] = jnp.where(same > 0.5, -full, 0.0)

    @pl.when(count <= SMALL)
    def _():
        solve(SMALL)

    @pl.when(count > SMALL)
    def _():
        solve(OBS_TILE)

    for copy in copies[3:]:
        copy.wait()
    innovation = mv_ref[...] + jnp.sqrt(var) * jit_ref[...] - pred
    weighted = dot(innovation, full_ref[...], ((1,), (0,)), lax.Precision.HIGHEST)
    out_ref[1] = weighted.astype(BF16)


def weigh(predicted, measured_value, measurement_variance, observation_jitter, obs_block):
    members = predicted.shape[2]
    return pl.pallas_call(
        weigh_kernel,
        out_shape=jax.ShapeDtypeStruct((2, members, OBS_TILE), BF16),
        in_specs=[pl.BlockSpec(memory_space=pltpu.HBM)] * 5,
        out_specs=pl.BlockSpec(memory_space=pltpu.VMEM),
        scratch_shapes=[
            pltpu.VMEM((members, OBS_TILE), F32),
            pltpu.VMEM((1, OBS_TILE), F32),
            pltpu.VMEM((1, OBS_TILE), F32),
            pltpu.VMEM((members, OBS_TILE), F32),
            pltpu.VMEM((obs_block.shape[1], OBS_TILE), jnp.int32),
            pltpu.VMEM((OBS_TILE, OBS_TILE), F32),
            pltpu.VMEM((OBS_TILE, OBS_TILE), jnp.int32),
            pltpu.VMEM((OBS_TILE, OBS_TILE), F32),
            pltpu.SemaphoreType.DMA((5,)),
        ],
        compiler_params=pltpu.CompilerParams(vmem_limit_bytes=16 * 2**20),
        name="weigh",
    )(*in_hbm(predicted, measured_value, measurement_variance, observation_jitter, obs_block))


def offset(which, place):
    even = 1 - 2 * (place & 1)
    return (0, even, -even)[which]


def prepare_kernel(
    params_ref, radius_hbm, pattern_hbm, obs_hbm, turned_ref, taper_ref, radius_ref, pattern_ref, obs_ref, sems
):
    members = params_ref.shape[1]
    tile_x = lax.axis_index("gx")
    tile_y = lax.axis_index("gy")
    count_x, count_y = obs_ref.shape[0], obs_ref.shape[1]
    copies = fetch([(radius_hbm, radius_ref), (pattern_hbm, pattern_ref), (obs_hbm, obs_ref)], sems)

    for b in range(BLOCKS):
        block = params_ref[b].astype(F32)
        mean = jnp.sum(block, axis=0, keepdims=True) / members
        turned_ref[b] = (block - mean).T.astype(BF16)
    for copy in copies:
        copy.wait()
    shape = (BLOCKS, OBS_TILE)
    block = iota(shape, 0)
    radius = jnp.zeros(shape, jnp.int32)
    for b in range(BLOCKS):
        radius = jnp.where(block == b, radius_ref[b // BLK_Y, b % BLK_Y], radius)
    reach = (radius + 1).astype(F32)
    reach = reach * reach
    pattern = jnp.concatenate([pattern_ref[i] for i in range(BLK_X)], axis=0).astype(F32)
    slots = [jnp.broadcast_to(pattern[:, p : p + 1], shape) for p in range(PATTERN)]

    for t in range(9):
        iy, ix = t // 3, t % 3
        dx, dy = offset(ix, tile_x), offset(iy, tile_y)
        at_x, at_y = tile_x + dx, tile_y + dy
        valid = (at_x >= 0) & (at_x < count_x) & (at_y >= 0) & (at_y < count_y)
        at_x = jnp.clip(at_x, 0, count_x - 1)
        at_y = jnp.clip(at_y, 0, count_y - 1)
        obs = obs_ref[at_x, pl.ds(at_y, 1), :]
        step_x = dx * BLK_X + (obs >> 2) - (block >> 2)
        step_y = dy * BLK_Y + (obs & 3) - (block & 3)
        inside = (jnp.abs(step_x) <= 2) & (jnp.abs(step_y) <= 2) & valid
        slot = (step_x + 2) * 5 + (step_y + 2)
        picked = jnp.zeros(shape, F32)
        for p in range(PATTERN):
            picked = jnp.where(slot == p, slots[p], picked)
        spread = (step_x * step_x + step_y * step_y).astype(F32)
        shaped = jnp.maximum(1.0 - spread / reach, 0.0)
        taper_ref[iy, ix] = jnp.where(inside, picked, 0.0) * shaped / (members - 1)


def prepare(by_block, taper_radius, taper_pattern, obs_block):
    members = by_block.shape[1]
    return pl.pallas_call(
        prepare_kernel,
        out_shape=(
            jax.ShapeDtypeStruct((BLOCKS, CELLS, members), BF16),
            jax.ShapeDtypeStruct((3, 3, BLOCKS, OBS_TILE), F32),
        ),
        in_specs=[pl.BlockSpec(memory_space=pltpu.VMEM)] + [pl.BlockSpec(memory_space=pltpu.HBM)] * 3,
        out_specs=(pl.BlockSpec(memory_space=pltpu.VMEM), pl.BlockSpec(memory_space=pltpu.VMEM)),
        scratch_shapes=[
            pltpu.SMEM(taper_radius.shape, jnp.int32),
            pltpu.VMEM(taper_pattern.shape, jnp.int32),
            pltpu.VMEM(obs_block.shape, jnp.int32),
            pltpu.SemaphoreType.DMA((3,)),
        ],
        compiler_params=pltpu.CompilerParams(vmem_limit_bytes=16 * 2**20),
        cost_estimate=pl.CostEstimate(flops=4_000_000, bytes_accessed=1_000_000, transcendentals=0),
        name="prepare",
    )(by_block, *in_hbm(taper_radius, taper_pattern, obs_block))


def moved(b, which, first, turned_ref, taper_ref, tiles_ref):
    cross = dot(turned_ref[b], tiles_ref[0], ((1,), (0,)))
    count = tiles_ref.shape[2] // OBS_TILE
    taper = jnp.concatenate([taper_ref[which, first + k, pl.ds(b, 1), :] for k in range(count)], axis=1)
    gain = (cross * taper).astype(BF16)
    return dot(tiles_ref[1], gain, ((1,), (1,)))


def block_of(k, side, tile_y):
    first = 2 * ((tile_y & 1) ^ 1 ^ side)
    return (k >> 1) * BLK_Y + first + (k & 1)


def put(out_ref, b, updated):
    share = out_ref.shape[2]
    for d in range(out_ref.shape[0]):
        out_ref[d, b] = updated[d * share : (d + 1) * share]


def near_kernel(params_ref, turned_ref, taper_ref, own_ref, even_ref, out_ref, part_ref):
    tile_y = lax.axis_index("gy")

    for k in range(BLOCKS // 2):
        b = block_of(k, 0, tile_y)
        delta = moved(b, 0, 0, turned_ref, taper_ref, own_ref) + moved(b, 1, 0, turned_ref, taper_ref, even_ref)
        put(out_ref, b, (params_ref[b].astype(F32) + delta).astype(BF16))
    for k in range(BLOCKS // 2):
        b = block_of(k, 1, tile_y)
        part_ref[k] = params_ref[b].astype(F32) + moved(b, 0, 0, turned_ref, taper_ref, own_ref)


def far_kernel(turned_ref, taper_ref, odd_ref, beside_ref, part_ref, done_ref, out_ref):
    del done_ref
    tile_y = lax.axis_index("gy")
    for k in range(BLOCKS // 2):
        b = block_of(k, 1, tile_y)
        delta = moved(b, 2, 0, turned_ref, taper_ref, odd_ref) + moved(b, 2, 1, turned_ref, taper_ref, beside_ref)
        put(out_ref, b, (part_ref[k] + delta).astype(BF16))


VMEM = pl.BlockSpec(memory_space=pltpu.VMEM)


def update_near(by_block, turned, taper, own, even, parts):
    members = by_block.shape[1]
    return pl.pallas_call(
        near_kernel,
        out_shape=(
            jax.ShapeDtypeStruct((parts, BLOCKS, members // parts, CELLS), BF16),
            jax.ShapeDtypeStruct((BLOCKS // 2, members, CELLS), F32),
        ),
        in_specs=[VMEM] * 5,
        out_specs=(VMEM, VMEM),
        compiler_params=pltpu.CompilerParams(vmem_limit_bytes=24 * 2**20),
        cost_estimate=pl.CostEstimate(flops=400_000_000, bytes_accessed=2_000_000, transcendentals=0),
        name="near",
    )(by_block, turned, taper, own, even)


def update_far(turned, taper, odd, beside, part, done):
    return pl.pallas_call(
        far_kernel,
        out_shape=jax.ShapeDtypeStruct(done.shape, BF16),
        in_specs=[VMEM] * 5 + [pl.BlockSpec(memory_space=pl.ANY)],
        out_specs=VMEM,
        input_output_aliases={5: 0},
        compiler_params=pltpu.CompilerParams(vmem_limit_bytes=24 * 2**20),
        cost_estimate=pl.CostEstimate(flops=100_000_000, bytes_accessed=1_000_000, transcendentals=0),
        name="far",
    )(turned, taper, odd, beside, part, done)


def swap(block, axis, first, close=False):
    count = lax.axis_size(axis)
    pairs = [(i, i + 1) for i in range(first, count - 1, 2)]
    if close:
        pairs.append((count - 1, 0))
    return lax.ppermute(block, axis, pairs + [(b, a) for a, b in pairs])


def per_device(
    params,
    predicted,
    measured_value,
    measurement_variance,
    observation_jitter,
    obs_block,
    taper_radius,
    taper_pattern,
):
    members = params.shape[0]
    parts = lax.axis_size("gy")
    by_block = params.reshape(members, BLOCKS, CELLS).transpose(1, 0, 2)
    own = weigh(predicted, measured_value, measurement_variance, observation_jitter, obs_block)
    sent, by_block = lax.optimization_barrier((own, by_block))
    across = swap(sent, "gy", 1)
    even = swap(own, "gx", 0)
    odd = swap(own, "gx", 1, close=True)
    turned, taper = prepare(by_block, taper_radius, taper_pattern, obs_block)
    even, odd, across, turned, taper = lax.optimization_barrier((even, odd, across, turned, taper))
    beside = jnp.concatenate([even, odd], axis=2)
    column = jnp.concatenate([own, even, odd], axis=2)
    across_beside = swap(beside, "gy", 1)
    even = swap(column, "gy", 0)
    done, part = update_near(by_block, turned, taper, column, even, parts)
    updated = update_far(turned, taper, across, across_beside, part, done)
    arrived = lax.all_to_all(updated, "gy", split_axis=0, concat_axis=0, tiled=True)
    share = members // parts
    arrived = arrived.reshape(parts, BLK_X, BLK_Y, share, CELLS).transpose(3, 1, 0, 2, 4)
    return arrived.reshape(share, BLK_X, parts * BLK_Y, CELLS)


def solution(mesh):
    placed = (
        P(None, "gx", "gy", None),
        P("gx", "gy", None, None),
        P("gx", "gy", None),
        P("gx", "gy", None),
        P("gx", "gy", None, None),
        P(),
        P("gx", "gy"),
        P("gx", "gy", None),
    )
    return jax.shard_map(
        per_device, mesh=mesh, in_specs=placed, out_specs=P("gy", "gx", None, None), check_vma=False
    )
```

```python
import functools

import jax
import jax.numpy as jnp
from jax import lax
from jax.experimental import pallas as pl
from jax.experimental.pallas import tpu as pltpu
from jax.sharding import PartitionSpec as P

CELLS = 128
BLK_X = 2
BLK_Y = 4
BLOCKS = BLK_X * BLK_Y
SIDE = BLOCKS // 2
OBS_TILE = 128
PATTERN = 25
SMALL = 32

F32 = jnp.float32
BF16 = jnp.bfloat16


def iota(shape, dim):
    return lax.broadcasted_iota(jnp.int32, shape, dim)


def split3(x):
    high = x.astype(BF16)
    rest = x - high.astype(F32)
    mid = rest.astype(BF16)
    low = (rest - mid.astype(F32)).astype(BF16)
    return high, mid, low


def dot(a, b, dims, precision=None):
    return lax.dot_general(a, b, ((dims[0], dims[1]), ((), ())), precision=precision, preferred_element_type=F32)


def sweep(rows, count, x_ref, idx_ref, rank, size):
    row = iota((rows, OBS_TILE), 0)
    exists = row < size

    def taken(spread, indices):
        return jnp.take_along_axis(spread, indices, axis=1, mode="promise_in_bounds")

    def step(k, carry):
        t = 2 * k
        u = t + 1
        row_t, row_u = x_ref[pl.ds(t, 1), :], x_ref[pl.ds(u, 1), :]
        spread_t = jnp.broadcast_to(row_t, (rows, OBS_TILE))
        spread_u = jnp.broadcast_to(row_u, (rows, OBS_TILE))
        at_t = jnp.broadcast_to(idx_ref[pl.ds(t, 1), :], (8, OBS_TILE))
        at_u = jnp.broadcast_to(idx_ref[pl.ds(u, 1), :], (8, OBS_TILE))
        has_t, has_u = t < size, u < size
        a = jnp.where(has_t, taken(spread_t[0:8], at_t)[0:1], 1.0)
        b = jnp.where(has_u, taken(spread_t[0:8], at_u)[0:1], 0.0)
        d = jnp.where(has_u, taken(spread_u[0:8], at_u)[0:1], 1.0)
        own_t, own_u = rank == t, rank == u
        own = own_t | own_u
        head_t = jnp.where(own, jnp.where(own_t, -1.0, 0.0), row_t)
        head_u = jnp.where(own, jnp.where(own_u, -1.0, 0.0), row_u)
        inverse = 1.0 / a
        factor = b * inverse
        scaled_u = (head_u - factor * head_t) / (d - b * factor)
        scaled_t = head_t * inverse - factor * scaled_u
        column_t = jnp.where(exists, taken(spread_t, idx_ref[0:rows, :]), 0.0)
        column_u = jnp.where(exists, taken(spread_u, idx_ref[0:rows, :]), 0.0)
        on_t, on_u = row == t, row == u
        on = on_t | on_u
        column_t = jnp.where(on, jnp.where(on_t, -1.0, 0.0), column_t)
        column_u = jnp.where(on, jnp.where(on_u, -1.0, 0.0), column_u)
        x = jnp.where(on | own, 0.0, x_ref[0:rows, :])
        x_ref[0:rows, :] = x - column_t * scaled_t - column_u * scaled_u
        return carry

    lax.fori_loop(0, (count + 1) // 2, step, 0)


def in_hbm(*arrays):
    return [pltpu.with_memory_space_constraint(array, pltpu.HBM) for array in arrays]


def fetch(pairs, sems):
    copies = [pltpu.make_async_copy(src, dst, sems.at[k]) for k, (src, dst) in enumerate(pairs)]
    for copy in copies:
        copy.start()
    return copies


def weigh_kernel(
    pred_hbm, mv_hbm, var_hbm, jit_hbm, obs_hbm, params_hbm, out_ref, params_ref,
    pred_ref, mv_ref, var_ref, jit_ref, obs_ref, x_ref, idx_ref, full_ref, sems,
):
    members = pred_ref.shape[0]
    tile_x = lax.axis_index("gx")
    tile_y = lax.axis_index("gy")
    square = (OBS_TILE, OBS_TILE)
    pairs = [
        (pred_hbm.at[0, 0], pred_ref),
        (obs_hbm.at[tile_x], obs_ref),
        (var_hbm.at[0], var_ref),
        (mv_hbm.at[0], mv_ref),
        (jit_hbm.at[0, 0], jit_ref),
        (params_hbm, params_ref),
    ]
    copies = fetch(pairs, sems)
    for copy in copies[:3]:
        copy.wait()
    pred = pred_ref[...]
    var = var_ref[...]
    mean = jnp.sum(pred, axis=0, keepdims=True) / members
    deviation = (pred - mean).astype(BF16)
    out_ref[0] = deviation
    obs = obs_ref[pl.ds(tile_y, 1), :]
    groups = (iota((BLOCKS, OBS_TILE), 0) == obs).astype(BF16)
    same = dot(groups, groups, ((0,), (0,)))
    gram = dot(deviation, deviation, ((0,), (0,))) / (members - 1)
    row, col = iota(square, 0), iota(square, 1)
    system = jnp.where(same > 0.5, gram, 0.0) + jnp.where(row == col, var, 0.0)
    size = jnp.sum(same, axis=0, keepdims=True)
    count = jnp.max(size).astype(jnp.int32)
    size = size.astype(jnp.int32)
    rank = jnp.sum(jnp.where(row < col, same, 0.0), axis=0, keepdims=True).astype(jnp.int32)
    place = row == rank
    hot = place.astype(BF16)
    high, mid, low = split3(system)
    x_ref[...] = (
        dot(hot, low, ((1,), (0,))) + dot(hot, mid, ((1,), (0,))) + dot(hot, high, ((1,), (0,)))
    )
    numbered = jnp.where(place, col, 0).astype(F32).astype(BF16)
    idx_ref[...] = dot(numbered, same.astype(BF16), ((1,), (0,))).astype(jnp.int32)

    def solve(rows):
        sweep(rows, count, x_ref, idx_ref, rank, size)
        high, mid, low = split3(x_ref[0:rows, :])
        taken = hot[0:rows]
        full = dot(taken, low, ((0,), (0,))) + dot(taken, mid, ((0,), (0,))) + dot(taken, high, ((0,), (0,)))
        full_ref[...] = jnp.where(same > 0.5, -full, 0.0)

    @pl.when(count <= SMALL)
    def _():
        solve(SMALL)

    @pl.when(count > SMALL)
    def _():
        solve(OBS_TILE)

    for copy in copies[3:]:
        copy.wait()
    innovation = mv_ref[...] + jnp.sqrt(var) * jit_ref[...] - pred
    weighted = dot(innovation, full_ref[...], ((1,), (0,)), lax.Precision.HIGHEST)
    out_ref[1] = weighted.astype(BF16)


def weigh(predicted, measured_value, measurement_variance, observation_jitter, obs_block, params):
    members = predicted.shape[2]
    return pl.pallas_call(
        weigh_kernel,
        out_shape=(jax.ShapeDtypeStruct((2, members, OBS_TILE), BF16), jax.ShapeDtypeStruct(params.shape, BF16)),
        in_specs=[pl.BlockSpec(memory_space=pltpu.HBM)] * 6,
        out_specs=(pl.BlockSpec(memory_space=pltpu.VMEM), pl.BlockSpec(memory_space=pltpu.VMEM)),
        scratch_shapes=[
            pltpu.VMEM((members, OBS_TILE), F32),
            pltpu.VMEM((1, OBS_TILE), F32),
            pltpu.VMEM((1, OBS_TILE), F32),
            pltpu.VMEM((members, OBS_TILE), F32),
            pltpu.VMEM((obs_block.shape[1], OBS_TILE), jnp.int32),
            pltpu.VMEM((OBS_TILE, OBS_TILE), F32),
            pltpu.VMEM((OBS_TILE, OBS_TILE), jnp.int32),
            pltpu.VMEM((OBS_TILE, OBS_TILE), F32),
            pltpu.SemaphoreType.DMA((6,)),
        ],
        compiler_params=pltpu.CompilerParams(vmem_limit_bytes=16 * 2**20),
        name="weigh",
    )(*in_hbm(predicted, measured_value, measurement_variance, observation_jitter, obs_block, params))


def offset(which, place):
    even = 1 - 2 * (place & 1)
    return (0, even, -even)[which]


def prepare_kernel(
    params_ref, radius_hbm, pattern_hbm, obs_hbm, turned_ref, taper_ref, message_ref,
    radius_ref, pattern_ref, obs_ref, sems,
):
    members = params_ref.shape[1]
    tile_x = lax.axis_index("gx")
    tile_y = lax.axis_index("gy")
    count_x, count_y = obs_ref.shape[0], obs_ref.shape[1]
    copies = fetch([(radius_hbm, radius_ref), (pattern_hbm, pattern_ref), (obs_hbm, obs_ref)], sems)

    for b in range(BLOCKS):
        block = params_ref[b].astype(F32)
        mean = jnp.sum(block, axis=0, keepdims=True) / members
        turned_ref[b] = (block - mean).T.astype(BF16)
    for copy in copies:
        copy.wait()
    shape = (BLOCKS, OBS_TILE)
    block = iota(shape, 0)
    radius = jnp.zeros(shape, jnp.int32)
    for b in range(BLOCKS):
        radius = jnp.where(block == b, radius_ref[b // BLK_Y, b % BLK_Y], radius)
    reach = (radius + 1).astype(F32)
    reach = reach * reach
    pattern = jnp.concatenate([pattern_ref[i] for i in range(BLK_X)], axis=0).astype(F32)
    slots = [jnp.broadcast_to(pattern[:, p : p + 1], shape) for p in range(PATTERN)]

    reached = []
    for t in range(9):
        iy, ix = t // 3, t % 3
        dx, dy = offset(ix, tile_x), offset(iy, tile_y)
        at_x, at_y = tile_x + dx, tile_y + dy
        valid = (at_x >= 0) & (at_x < count_x) & (at_y >= 0) & (at_y < count_y)
        at_x = jnp.clip(at_x, 0, count_x - 1)
        at_y = jnp.clip(at_y, 0, count_y - 1)
        obs = obs_ref[at_x, pl.ds(at_y, 1), :]
        step_x = dx * BLK_X + (obs >> 2) - (block >> 2)
        step_y = dy * BLK_Y + (obs & 3) - (block & 3)
        inside = (jnp.abs(step_x) <= 2) & (jnp.abs(step_y) <= 2) & valid
        slot = (step_x + 2) * 5 + (step_y + 2)
        picked = jnp.zeros(shape, F32)
        for p in range(PATTERN):
            picked = jnp.where(slot == p, slots[p], picked)
        spread = (step_x * step_x + step_y * step_y).astype(F32)
        shaped = jnp.maximum(1.0 - spread / reach, 0.0)
        taper = jnp.where(inside, picked, 0.0) * shaped / (members - 1)
        taper_ref[iy, ix] = taper
        if iy == 2:
            lower = jnp.concatenate([taper[0:2], taper[4:6]], axis=0)
            upper = jnp.concatenate([taper[2:4], taper[6:8]], axis=0)
            reached.append(jnp.where(first_of(1, tile_y) == 0, lower, upper))
    for k in range(SIDE):
        message_ref[k * CELLS : (k + 1) * CELLS] = turned_ref[block_of(k, 1, tile_y)]
    tapers = jnp.concatenate(reached + [jnp.zeros((SIDE, OBS_TILE), F32)], axis=0)
    high = tapers.astype(BF16)
    low = (tapers - high.astype(F32)).astype(BF16)
    message_ref[SIDE * CELLS : SIDE * CELLS + 16, 0:OBS_TILE] = high
    message_ref[SIDE * CELLS + 16 : SIDE * CELLS + 32, 0:OBS_TILE] = low
    if members > OBS_TILE:
        message_ref[SIDE * CELLS : SIDE * CELLS + 32, OBS_TILE:members] = jnp.zeros((32, members - OBS_TILE), BF16)


def prepare(by_block, taper_radius, taper_pattern, obs_block):
    members = by_block.shape[1]
    return pl.pallas_call(
        prepare_kernel,
        out_shape=(
            jax.ShapeDtypeStruct((BLOCKS, CELLS, members), BF16),
            jax.ShapeDtypeStruct((3, 3, BLOCKS, OBS_TILE), F32),
            jax.ShapeDtypeStruct((SIDE * CELLS + 32, members), BF16),
        ),
        in_specs=[pl.BlockSpec(memory_space=pltpu.VMEM)] + [pl.BlockSpec(memory_space=pltpu.HBM)] * 3,
        out_specs=(pl.BlockSpec(memory_space=pltpu.VMEM),) * 3,
        scratch_shapes=[
            pltpu.SMEM(taper_radius.shape, jnp.int32),
            pltpu.VMEM(taper_pattern.shape, jnp.int32),
            pltpu.VMEM(obs_block.shape, jnp.int32),
            pltpu.SemaphoreType.DMA((3,)),
        ],
        compiler_params=pltpu.CompilerParams(vmem_limit_bytes=16 * 2**20),
        cost_estimate=pl.CostEstimate(flops=4_000_000, bytes_accessed=1_000_000, transcendentals=0),
        name="prepare",
    )(by_block, *in_hbm(taper_radius, taper_pattern, obs_block))


def gained(turned, taper, column_ref):
    cross = dot(turned, column_ref[0], ((1,), (0,)))
    gain = (cross * taper).astype(BF16)
    return dot(column_ref[1], gain, ((1,), (1,)))


def moved(b, which, turned_ref, taper_ref, column_ref):
    taper = jnp.concatenate([taper_ref[which, ix, pl.ds(b, 1), :] for ix in range(3)], axis=1)
    return gained(turned_ref[b], taper, column_ref)


def first_of(side, tile_y):
    return 2 * ((tile_y & 1) ^ 1 ^ side)


def block_of(k, side, tile_y):
    return (k >> 1) * BLK_Y + first_of(side, tile_y) + (k & 1)


def put(out_ref, b, updated):
    share = out_ref.shape[2]
    for d in range(out_ref.shape[0]):
        out_ref[d, b] = updated[d * share : (d + 1) * share]


def own_kernel(params_ref, turned_ref, taper_ref, own_ref, out_ref, part_ref):
    tile_y = lax.axis_index("gy")
    for k in range(SIDE):
        b = block_of(k, 0, tile_y)
        part_ref[k] = params_ref[b].astype(F32) + moved(b, 0, turned_ref, taper_ref, own_ref)
    for k in range(SIDE):
        b = block_of(k, 1, tile_y)
        put(out_ref, b, (params_ref[b].astype(F32) + moved(b, 0, turned_ref, taper_ref, own_ref)).astype(BF16))


def even_kernel(turned_ref, taper_ref, even_ref, part_ref, done_ref, out_ref):
    del done_ref
    tile_y = lax.axis_index("gy")
    for k in range(SIDE):
        b = block_of(k, 0, tile_y)
        put(out_ref, b, (part_ref[k] + moved(b, 1, turned_ref, taper_ref, even_ref)).astype(BF16))


def odd_kernel(message_ref, own_ref, done_ref, out_ref):
    del done_ref
    end = SIDE * CELLS
    tapers = message_ref[end : end + 16, 0:OBS_TILE].astype(F32) + message_ref[end + 16 : end + 32, 0:OBS_TILE].astype(F32)
    for k in range(SIDE):
        taper = jnp.concatenate([tapers[ix * SIDE + k : ix * SIDE + k + 1] for ix in range(3)], axis=1)
        put(out_ref, BLOCKS + k, gained(message_ref[k * CELLS : (k + 1) * CELLS], taper, own_ref).astype(BF16))


def gather_kernel(arrived_ref, out_hbm, rows_ref, out_ref, sems):
    parts, _, share, _ = arrived_ref.shape
    line = parts * BLK_Y
    for s in range(parts):
        pair = s - 1 if s % 2 == 0 else s + 1
        first = 2 * (s % 2)
        for b in range(BLOCKS):
            x, y = b // BLK_Y, b % BLK_Y
            value = arrived_ref[s, b].astype(F32)
            if first <= y < first + 2 and 0 <= pair < parts:
                value = value + arrived_ref[pair, BLOCKS + x * 2 + y - first].astype(F32)
            rows_ref[pl.ds(x * line + s * BLK_Y + y, share, stride=BLK_X * line), :] = value
    pieces = sems.shape[0]
    step = rows_ref.shape[0] // pieces
    copies = []
    for p in range(pieces):
        place = slice(p * step, (p + 1) * step)
        out_ref[place] = rows_ref[place].astype(BF16)
        copies.append(pltpu.make_async_copy(out_ref.at[pl.ds(p * step, step)], out_hbm.at[pl.ds(p * step, step)], sems.at[p]))
        copies[-1].start()
    for copy in copies:
        copy.wait()


VMEM = pl.BlockSpec(memory_space=pltpu.VMEM)
LONG = pl.CostEstimate(flops=4_000_000_000, bytes_accessed=10_000_000, transcendentals=0)
LIMIT = pltpu.CompilerParams(vmem_limit_bytes=24 * 2**20)


def update_own(by_block, turned, taper, own, parts):
    members = by_block.shape[1]
    return pl.pallas_call(
        own_kernel,
        out_shape=(
            jax.ShapeDtypeStruct((parts, BLOCKS + SIDE, members // parts, CELLS), BF16),
            jax.ShapeDtypeStruct((SIDE, members, CELLS), F32),
        ),
        in_specs=[VMEM] * 4,
        out_specs=(VMEM, VMEM),
        compiler_params=LIMIT,
        cost_estimate=LONG,
        name="own",
    )(by_block, turned, taper, own)


def update_even(turned, taper, even, part, done):
    return pl.pallas_call(
        even_kernel,
        out_shape=jax.ShapeDtypeStruct(done.shape, BF16),
        in_specs=[VMEM] * 4 + [pl.BlockSpec(memory_space=pl.ANY)],
        out_specs=VMEM,
        input_output_aliases={4: 0},
        compiler_params=LIMIT,
        cost_estimate=LONG,
        name="even",
    )(turned, taper, even, part, done)


def update_odd(message, own, done):
    return pl.pallas_call(
        odd_kernel,
        out_shape=jax.ShapeDtypeStruct(done.shape, BF16),
        in_specs=[VMEM] * 2 + [pl.BlockSpec(memory_space=pl.ANY)],
        out_specs=VMEM,
        input_output_aliases={2: 0},
        compiler_params=LIMIT,
        cost_estimate=LONG,
        name="odd",
    )(message, own, done)


def gather(arrived):
    parts, _, share, _ = arrived.shape
    rows = share * BLOCKS * parts
    out = pl.pallas_call(
        gather_kernel,
        out_shape=jax.ShapeDtypeStruct((rows, CELLS), BF16),
        in_specs=[VMEM],
        out_specs=pl.BlockSpec(memory_space=pl.ANY),
        scratch_shapes=[
            pltpu.VMEM((rows, CELLS), F32),
            pltpu.VMEM((rows, CELLS), BF16),
            pltpu.SemaphoreType.DMA((4,)),
        ],
        compiler_params=LIMIT,
        name="gather",
    )(arrived)
    return out.reshape(share, BLK_X, parts * BLK_Y, CELLS)


def swap(block, axis, first, close=False):
    count = lax.axis_size(axis)
    pairs = [(i, i + 1) for i in range(first, count - 1, 2)]
    if close:
        pairs.append((count - 1, 0))
    return lax.ppermute(block, axis, pairs + [(b, a) for a, b in pairs])


def per_device(
    params,
    predicted,
    measured_value,
    measurement_variance,
    observation_jitter,
    obs_block,
    taper_radius,
    taper_pattern,
):
    members = params.shape[0]
    parts = lax.axis_size("gy")
    own, params = weigh(
        predicted, measured_value, measurement_variance, observation_jitter, obs_block, params
    )
    by_block = params.reshape(members, BLOCKS, CELLS).transpose(1, 0, 2)
    even = swap(own, "gx", 0)
    odd = swap(own, "gx", 1, close=True)
    turned, taper, message = prepare(by_block, taper_radius, taper_pattern, obs_block)
    message = swap(message, "gy", 1)
    column = jnp.concatenate([own, even, odd], axis=2)
    column, turned, taper = lax.optimization_barrier((column, turned, taper))
    even = swap(column, "gy", 0)
    done, part = update_own(by_block, turned, taper, column, parts)
    done = update_even(turned, taper, even, part, done)
    done = update_odd(message, column, done)
    return gather(lax.all_to_all(done, "gy", split_axis=0, concat_axis=0, tiled=True))


def solution(mesh):
    placed = (
        P(None, "gx", "gy", None),
        P("gx", "gy", None, None),
        P("gx", "gy", None),
        P("gx", "gy", None),
        P("gx", "gy", None, None),
        P(),
        P("gx", "gy"),
        P("gx", "gy", None),
    )
    return jax.shard_map(
        per_device, mesh=mesh, in_specs=placed, out_specs=P("gy", "gx", None, None), check_vma=False
    )
```

```python
import functools

import jax
import jax.numpy as jnp
from jax import lax
from jax.experimental import pallas as pl
from jax.experimental.pallas import tpu as pltpu
from jax.sharding import PartitionSpec as P

CELLS = 128
BLK_X = 2
BLK_Y = 4
BLOCKS = BLK_X * BLK_Y
SIDE = BLOCKS // 2
OBS_TILE = 128
PATTERN = 25
SMALL = 32

F32 = jnp.float32
BF16 = jnp.bfloat16


def iota(shape, dim):
    return lax.broadcasted_iota(jnp.int32, shape, dim)


def split3(x):
    high = x.astype(BF16)
    rest = x - high.astype(F32)
    mid = rest.astype(BF16)
    low = (rest - mid.astype(F32)).astype(BF16)
    return high, mid, low


def dot(a, b, dims, precision=None):
    return lax.dot_general(a, b, ((dims[0], dims[1]), ((), ())), precision=precision, preferred_element_type=F32)


def sweep(rows, count, x_ref, idx_ref, rank, size):
    row = iota((rows, OBS_TILE), 0)
    exists = row < size

    def taken(spread, indices):
        return jnp.take_along_axis(spread, indices, axis=1, mode="promise_in_bounds")

    def step(k, carry):
        t = 2 * k
        u = t + 1
        row_t, row_u = x_ref[pl.ds(t, 1), :], x_ref[pl.ds(u, 1), :]
        spread_t = jnp.broadcast_to(row_t, (rows, OBS_TILE))
        spread_u = jnp.broadcast_to(row_u, (rows, OBS_TILE))
        at_t = jnp.broadcast_to(idx_ref[pl.ds(t, 1), :], (8, OBS_TILE))
        at_u = jnp.broadcast_to(idx_ref[pl.ds(u, 1), :], (8, OBS_TILE))
        has_t, has_u = t < size, u < size
        a = jnp.where(has_t, taken(spread_t[0:8], at_t)[0:1], 1.0)
        b = jnp.where(has_u, taken(spread_t[0:8], at_u)[0:1], 0.0)
        d = jnp.where(has_u, taken(spread_u[0:8], at_u)[0:1], 1.0)
        own_t, own_u = rank == t, rank == u
        own = own_t | own_u
        head_t = jnp.where(own, jnp.where(own_t, -1.0, 0.0), row_t)
        head_u = jnp.where(own, jnp.where(own_u, -1.0, 0.0), row_u)
        inverse = 1.0 / a
        factor = b * inverse
        scaled_u = (head_u - factor * head_t) / (d - b * factor)
        scaled_t = head_t * inverse - factor * scaled_u
        column_t = jnp.where(exists, taken(spread_t, idx_ref[0:rows, :]), 0.0)
        column_u = jnp.where(exists, taken(spread_u, idx_ref[0:rows, :]), 0.0)
        on_t, on_u = row == t, row == u
        on = on_t | on_u
        column_t = jnp.where(on, jnp.where(on_t, -1.0, 0.0), column_t)
        column_u = jnp.where(on, jnp.where(on_u, -1.0, 0.0), column_u)
        x = jnp.where(on | own, 0.0, x_ref[0:rows, :])
        x_ref[0:rows, :] = x - column_t * scaled_t - column_u * scaled_u
        return carry

    lax.fori_loop(0, (count + 1) // 2, step, 0)


def in_hbm(*arrays):
    return [pltpu.with_memory_space_constraint(array, pltpu.HBM) for array in arrays]


def fetch(pairs, sems):
    copies = [pltpu.make_async_copy(src, dst, sems.at[k]) for k, (src, dst) in enumerate(pairs)]
    for copy in copies:
        copy.start()
    return copies


def weigh_kernel(
    pred_hbm, mv_hbm, var_hbm, jit_hbm, obs_hbm, params_hbm, out_ref, params_ref,
    pred_ref, mv_ref, var_ref, jit_ref, obs_ref, x_ref, idx_ref, full_ref, sems,
):
    members = pred_ref.shape[0]
    tile_x = lax.axis_index("gx")
    tile_y = lax.axis_index("gy")
    square = (OBS_TILE, OBS_TILE)
    pairs = [
        (pred_hbm.at[0, 0], pred_ref),
        (obs_hbm.at[tile_x], obs_ref),
        (var_hbm.at[0], var_ref),
        (mv_hbm.at[0], mv_ref),
        (jit_hbm.at[0, 0], jit_ref),
        (params_hbm, params_ref),
    ]
    copies = fetch(pairs, sems)
    for copy in copies[:3]:
        copy.wait()
    pred = pred_ref[...]
    var = var_ref[...]
    mean = jnp.sum(pred, axis=0, keepdims=True) / members
    deviation = (pred - mean).astype(BF16)
    out_ref[0] = deviation
    obs = obs_ref[pl.ds(tile_y, 1), :]
    groups = (iota((BLOCKS, OBS_TILE), 0) == obs).astype(BF16)
    same = dot(groups, groups, ((0,), (0,)))
    gram = dot(deviation, deviation, ((0,), (0,))) / (members - 1)
    row, col = iota(square, 0), iota(square, 1)
    system = jnp.where(same > 0.5, gram, 0.0) + jnp.where(row == col, var, 0.0)
    size = jnp.sum(same, axis=0, keepdims=True)
    count = jnp.max(size).astype(jnp.int32)
    size = size.astype(jnp.int32)
    rank = jnp.sum(jnp.where(row < col, same, 0.0), axis=0, keepdims=True).astype(jnp.int32)
    place = row == rank
    hot = place.astype(BF16)
    high, mid, low = split3(system)
    x_ref[...] = (
        dot(hot, low, ((1,), (0,))) + dot(hot, mid, ((1,), (0,))) + dot(hot, high, ((1,), (0,)))
    )
    numbered = jnp.where(place, col, 0).astype(F32).astype(BF16)
    idx_ref[...] = dot(numbered, same.astype(BF16), ((1,), (0,))).astype(jnp.int32)

    def solve(rows):
        sweep(rows, count, x_ref, idx_ref, rank, size)
        high, mid, low = split3(x_ref[0:rows, :])
        taken = hot[0:rows]
        full = dot(taken, low, ((0,), (0,))) + dot(taken, mid, ((0,), (0,))) + dot(taken, high, ((0,), (0,)))
        full_ref[...] = jnp.where(same > 0.5, -full, 0.0)

    @pl.when(count <= SMALL)
    def _():
        solve(SMALL)

    @pl.when(count > SMALL)
    def _():
        solve(OBS_TILE)

    for copy in copies[3:]:
        copy.wait()
    innovation = mv_ref[...] + jnp.sqrt(var) * jit_ref[...] - pred
    weighted = dot(innovation, full_ref[...], ((1,), (0,)), lax.Precision.HIGHEST)
    out_ref[1] = weighted.astype(BF16)


def weigh(predicted, measured_value, measurement_variance, observation_jitter, obs_block, params):
    members = predicted.shape[2]
    return pl.pallas_call(
        weigh_kernel,
        out_shape=(jax.ShapeDtypeStruct((2, members, OBS_TILE), BF16), jax.ShapeDtypeStruct(params.shape, BF16)),
        in_specs=[pl.BlockSpec(memory_space=pltpu.HBM)] * 6,
        out_specs=(pl.BlockSpec(memory_space=pltpu.VMEM), pl.BlockSpec(memory_space=pltpu.VMEM)),
        scratch_shapes=[
            pltpu.VMEM((members, OBS_TILE), F32),
            pltpu.VMEM((1, OBS_TILE), F32),
            pltpu.VMEM((1, OBS_TILE), F32),
            pltpu.VMEM((members, OBS_TILE), F32),
            pltpu.VMEM((obs_block.shape[1], OBS_TILE), jnp.int32),
            pltpu.VMEM((OBS_TILE, OBS_TILE), F32),
            pltpu.VMEM((OBS_TILE, OBS_TILE), jnp.int32),
            pltpu.VMEM((OBS_TILE, OBS_TILE), F32),
            pltpu.SemaphoreType.DMA((6,)),
        ],
        compiler_params=pltpu.CompilerParams(vmem_limit_bytes=16 * 2**20),
        name="weigh",
    )(*in_hbm(predicted, measured_value, measurement_variance, observation_jitter, obs_block, params))


def offset(which, place):
    even = 1 - 2 * (place & 1)
    return (0, even, -even)[which]


def prepare_kernel(
    params_ref, radius_hbm, pattern_hbm, obs_hbm, turned_ref, taper_ref, radius_ref, pattern_ref, obs_ref, sems
):
    members = params_ref.shape[1]
    tile_x = lax.axis_index("gx")
    tile_y = lax.axis_index("gy")
    count_x, count_y = obs_ref.shape[0], obs_ref.shape[1]
    copies = fetch([(radius_hbm, radius_ref), (pattern_hbm, pattern_ref), (obs_hbm, obs_ref)], sems)

    for b in range(BLOCKS):
        block = params_ref[b].astype(F32)
        mean = jnp.sum(block, axis=0, keepdims=True) / members
        turned_ref[b] = (block - mean).T.astype(BF16)
    for copy in copies:
        copy.wait()
    shape = (BLOCKS, OBS_TILE)
    block = iota(shape, 0)
    radius = jnp.zeros(shape, jnp.int32)
    for b in range(BLOCKS):
        radius = jnp.where(block == b, radius_ref[b // BLK_Y, b % BLK_Y], radius)
    reach = (radius + 1).astype(F32)
    reach = reach * reach
    pattern = jnp.concatenate([pattern_ref[i] for i in range(BLK_X)], axis=0).astype(F32)
    slots = [jnp.broadcast_to(pattern[:, p : p + 1], shape) for p in range(PATTERN)]

    for t in range(9):
        iy, ix = t // 3, t % 3
        dx, dy = offset(ix, tile_x), offset(iy, tile_y)
        at_x, at_y = tile_x + dx, tile_y + dy
        valid = (at_x >= 0) & (at_x < count_x) & (at_y >= 0) & (at_y < count_y)
        at_x = jnp.clip(at_x, 0, count_x - 1)
        at_y = jnp.clip(at_y, 0, count_y - 1)
        obs = obs_ref[at_x, pl.ds(at_y, 1), :]
        step_x = dx * BLK_X + (obs >> 2) - (block >> 2)
        step_y = dy * BLK_Y + (obs & 3) - (block & 3)
        inside = (jnp.abs(step_x) <= 2) & (jnp.abs(step_y) <= 2) & valid
        slot = (step_x + 2) * 5 + (step_y + 2)
        picked = jnp.zeros(shape, F32)
        for p in range(PATTERN):
            picked = jnp.where(slot == p, slots[p], picked)
        spread = (step_x * step_x + step_y * step_y).astype(F32)
        shaped = jnp.maximum(1.0 - spread / reach, 0.0)
        taper_ref[iy, ix] = jnp.where(inside, picked, 0.0) * shaped / (members - 1)


def prepare(by_block, taper_radius, taper_pattern, obs_block):
    members = by_block.shape[1]
    return pl.pallas_call(
        prepare_kernel,
        out_shape=(
            jax.ShapeDtypeStruct((BLOCKS, CELLS, members), BF16),
            jax.ShapeDtypeStruct((3, 3, BLOCKS, OBS_TILE), F32),
        ),
        in_specs=[pl.BlockSpec(memory_space=pltpu.VMEM)] + [pl.BlockSpec(memory_space=pltpu.HBM)] * 3,
        out_specs=(pl.BlockSpec(memory_space=pltpu.VMEM), pl.BlockSpec(memory_space=pltpu.VMEM)),
        scratch_shapes=[
            pltpu.SMEM(taper_radius.shape, jnp.int32),
            pltpu.VMEM(taper_pattern.shape, jnp.int32),
            pltpu.VMEM(obs_block.shape, jnp.int32),
            pltpu.SemaphoreType.DMA((3,)),
        ],
        compiler_params=pltpu.CompilerParams(vmem_limit_bytes=16 * 2**20),
        cost_estimate=pl.CostEstimate(flops=4_000_000, bytes_accessed=1_000_000, transcendentals=0),
        name="prepare",
    )(by_block, *in_hbm(taper_radius, taper_pattern, obs_block))


def moved(b, which, turned_ref, taper_ref, tiles_ref):
    cross = dot(turned_ref[b], tiles_ref[0], ((1,), (0,)))
    count = tiles_ref.shape[2] // OBS_TILE
    taper = jnp.concatenate([taper_ref[which, k, pl.ds(b, 1), :] for k in range(count)], axis=1)
    gain = (cross * taper).astype(BF16)
    return dot(tiles_ref[1], gain, ((1,), (1,)))


def first_of(side, tile_y):
    return 2 * ((tile_y & 1) ^ 1 ^ side)


def block_of(k, side, tile_y):
    return (k >> 1) * BLK_Y + first_of(side, tile_y) + (k & 1)


def target(chip, r, chips):
    return chip ^ r if chips & (chips - 1) == 0 else (chip + r) % chips


def source(chip, r, chips):
    return chip ^ r if chips & (chips - 1) == 0 else (chip + chips - r) % chips


def put(piece_refs, rows_ref, k, updated):
    chips, share = len(piece_refs), piece_refs[0].shape[2]
    mine = lax.axis_index("gy")
    rows_ref[k] = updated
    for r, ref in enumerate(piece_refs):
        for flip in (0, 1):
            owner = 2 * target(mine >> 1, r, chips) + ((mine & 1) ^ flip)
            ref[flip, k] = rows_ref[k, pl.ds(pl.multiple_of(owner * share, share), share), :]


def near_kernel(params_ref, turned_ref, taper_ref, own_ref, even_ref, part_ref, *refs):
    piece_refs, rows_ref = refs[:-1], refs[-1]
    tile_y = lax.axis_index("gy")
    for k in range(SIDE):
        b = block_of(k, 0, tile_y)
        delta = moved(b, 0, turned_ref, taper_ref, own_ref) + moved(b, 1, turned_ref, taper_ref, even_ref)
        put(piece_refs, rows_ref, k, (params_ref[b].astype(F32) + delta).astype(BF16))
    for k in range(SIDE):
        b = block_of(k, 1, tile_y)
        part_ref[k] = params_ref[b].astype(F32) + moved(b, 0, turned_ref, taper_ref, own_ref)


def far_kernel(turned_ref, taper_ref, odd_ref, part_ref, near_ref, *refs):
    both_ref, rows_ref = refs[1], refs[-1]
    piece_refs = (refs[0], both_ref.at[1], *refs[2:-1])
    both_ref[0] = near_ref[...]
    tile_y = lax.axis_index("gy")
    for k in range(SIDE):
        b = block_of(k, 1, tile_y)
        put(piece_refs, rows_ref, k, (part_ref[k] + moved(b, 2, turned_ref, taper_ref, odd_ref)).astype(BF16))


def sorted_pieces(refs):
    both_ref, rest = refs[0], refs[1:]
    near, far = rest[: len(rest) // 2], rest[len(rest) // 2 :]
    return [(near[0], both_ref.at[0], *near[1:]), (far[0], both_ref.at[1], *far[1:])]


def pack_kernel(*refs):
    out_ref = refs[-1]
    for side, pieces in enumerate(sorted_pieces(refs[:-1])):
        for r, piece in enumerate(pieces):
            out_ref[side, r] = piece[1]


def gather_kernel(even_ref, *refs):
    out_hbm, rows_ref, out_ref, sems = refs[-4:]
    pieces = sorted_pieces(refs[:-4])
    chips, share = even_ref.shape[1], even_ref.shape[3]
    mine = lax.axis_index("gy")
    chip, core = mine >> 1, mine & 1
    line = 2 * chips * BLK_Y
    for r in range(chips):
        for flip in (0, 1):
            other = core ^ flip
            tile = 2 * source(chip, r, chips) + other
            for side in (0, 1):
                for k in range(SIDE):
                    piece = even_ref[side, r, k] if flip else pieces[side][r][0, k]
                    start = (k >> 1) * line + tile * BLK_Y + first_of(side, other) + (k & 1)
                    rows_ref[pl.ds(start, share, stride=BLK_X * line), :] = piece.astype(F32)
    pieces = sems.shape[0]
    step = rows_ref.shape[0] // pieces
    copies = []
    for p in range(pieces):
        place = slice(p * step, (p + 1) * step)
        out_ref[place] = rows_ref[place].astype(BF16)
        copies.append(pltpu.make_async_copy(out_ref.at[pl.ds(p * step, step)], out_hbm.at[pl.ds(p * step, step)], sems.at[p]))
        copies[-1].start()
    for copy in copies:
        copy.wait()


VMEM = pl.BlockSpec(memory_space=pltpu.VMEM)
LONG = pl.CostEstimate(flops=4_000_000_000, bytes_accessed=10_000_000, transcendentals=0)
LIMIT = pltpu.CompilerParams(vmem_limit_bytes=24 * 2**20)


def update_near(by_block, turned, taper, own, even, parts):
    members = by_block.shape[1]
    pieces = [jax.ShapeDtypeStruct((2, SIDE, members // parts, CELLS), BF16)] * (parts // 2)
    return pl.pallas_call(
        near_kernel,
        out_shape=(jax.ShapeDtypeStruct((SIDE, members, CELLS), F32), *pieces),
        in_specs=[VMEM] * 5,
        out_specs=(VMEM,) * (1 + len(pieces)),
        scratch_shapes=[pltpu.VMEM((SIDE, members, CELLS), BF16)],
        compiler_params=LIMIT,
        cost_estimate=LONG,
        name="near",
    )(by_block, turned, taper, own, even)


def update_far(turned, taper, odd, part, near):
    members = part.shape[1]
    parts = members // near[0].shape[2]
    piece = jax.ShapeDtypeStruct(near[0].shape, BF16)
    shapes = (piece, jax.ShapeDtypeStruct((2, *piece.shape), BF16)) + (piece,) * (parts // 2 - 2)
    return pl.pallas_call(
        far_kernel,
        out_shape=shapes,
        in_specs=[VMEM] * 5,
        out_specs=(VMEM,) * len(shapes),
        scratch_shapes=[pltpu.VMEM((SIDE, members, CELLS), BF16)],
        compiler_params=LIMIT,
        cost_estimate=LONG,
        name="far",
    )(turned, taper, odd, part, near[1])


def pack(pieces):
    chips = len(pieces) // 2 + 1
    return pl.pallas_call(
        pack_kernel,
        out_shape=jax.ShapeDtypeStruct((2, chips, *pieces[1].shape[1:]), BF16),
        in_specs=[VMEM] * len(pieces),
        out_specs=VMEM,
        compiler_params=LIMIT,
        name="pack",
    )(*pieces)


def gather(even, pieces):
    _, chips, _, share, _ = even.shape
    rows = share * BLOCKS * 2 * chips
    out = pl.pallas_call(
        gather_kernel,
        out_shape=jax.ShapeDtypeStruct((rows, CELLS), BF16),
        in_specs=[VMEM] * (1 + len(pieces)),
        out_specs=pl.BlockSpec(memory_space=pl.ANY),
        scratch_shapes=[
            pltpu.VMEM((rows, CELLS), F32),
            pltpu.VMEM((rows, CELLS), BF16),
            pltpu.SemaphoreType.DMA((4,)),
        ],
        compiler_params=LIMIT,
        name="gather",
    )(even, *pieces)
    return out.reshape(share, BLK_X, 2 * chips * BLK_Y, CELLS)


def swap(block, axis, first, close=False):
    count = lax.axis_size(axis)
    pairs = [(i, i + 1) for i in range(first, count - 1, 2)]
    if close:
        pairs.append((count - 1, 0))
    return lax.ppermute(block, axis, pairs + [(b, a) for a, b in pairs])


def hop(piece, r):
    count = lax.axis_size("gy")
    pairs = [(i, 2 * target(i // 2, r, count // 2) + i % 2) for i in range(count)]
    return lax.ppermute(piece, "gy", pairs)


def per_device(
    params,
    predicted,
    measured_value,
    measurement_variance,
    observation_jitter,
    obs_block,
    taper_radius,
    taper_pattern,
):
    members = params.shape[0]
    parts = lax.axis_size("gy")
    own, params = weigh(
        predicted, measured_value, measurement_variance, observation_jitter, obs_block, params
    )
    by_block = params.reshape(members, BLOCKS, CELLS).transpose(1, 0, 2)
    even = swap(own, "gx", 0)
    odd = swap(own, "gx", 1, close=True)
    turned, taper = prepare(by_block, taper_radius, taper_pattern, obs_block)
    column = jnp.concatenate([own, even, odd], axis=2)
    column, turned, taper = lax.optimization_barrier((column, turned, taper))
    even = swap(column, "gy", 0)
    odd = swap(column, "gy", 1)
    part, *near = update_near(by_block, turned, taper, column, even, parts)
    rounds = range(parts // 2 - 1, 1, -1)
    near_hops = [hop(near[r], r) for r in rounds]
    far_own, both, *far = update_far(turned, taper, odd, part, near)
    far_hops = []
    for k, r in enumerate(rounds):
        far_hops.append(hop(far[r - 2], r))
        if k + 1 < len(rounds):
            far[r - 3], near_hops[k] = lax.optimization_barrier((far[r - 3], near_hops[k]))
        else:
            both, near_hops[k] = lax.optimization_barrier((both, near_hops[k]))
    pieces = [hop(both, 1), near[0], *near_hops[::-1], far_own, *far_hops[::-1]]
    return gather(swap(pack(pieces), "gy", 0), pieces)


def solution(mesh):
    placed = (
        P(None, "gx", "gy", None),
        P("gx", "gy", None, None),
        P("gx", "gy", None),
        P("gx", "gy", None),
        P("gx", "gy", None, None),
        P(),
        P("gx", "gy"),
        P("gx", "gy", None),
    )
    return jax.shard_map(
        per_device, mesh=mesh, in_specs=placed, out_specs=P("gy", "gx", None, None), check_vma=False
    )
```

```python
import functools

import jax
import jax.numpy as jnp
from jax import lax
from jax.experimental import pallas as pl
from jax.experimental.pallas import tpu as pltpu
from jax.sharding import PartitionSpec as P

CELLS = 128
BLK_X = 2
BLK_Y = 4
BLOCKS = BLK_X * BLK_Y
SIDE = BLOCKS // 2
OBS_TILE = 128
PATTERN = 25
SMALL = 32

F32 = jnp.float32
BF16 = jnp.bfloat16


def iota(shape, dim):
    return lax.broadcasted_iota(jnp.int32, shape, dim)


def split3(x):
    high = x.astype(BF16)
    rest = x - high.astype(F32)
    mid = rest.astype(BF16)
    low = (rest - mid.astype(F32)).astype(BF16)
    return high, mid, low


def dot(a, b, dims, precision=None):
    return lax.dot_general(a, b, ((dims[0], dims[1]), ((), ())), precision=precision, preferred_element_type=F32)


def sweep(rows, count, x_ref, idx_ref, rank, size):
    row = iota((rows, OBS_TILE), 0)
    exists = row < size

    def taken(spread, indices):
        return jnp.take_along_axis(spread, indices, axis=1, mode="promise_in_bounds")

    def step(k, carry):
        t = 2 * k
        u = t + 1
        row_t, row_u = x_ref[pl.ds(t, 1), :], x_ref[pl.ds(u, 1), :]
        spread_t = jnp.broadcast_to(row_t, (rows, OBS_TILE))
        spread_u = jnp.broadcast_to(row_u, (rows, OBS_TILE))
        at_t = jnp.broadcast_to(idx_ref[pl.ds(t, 1), :], (8, OBS_TILE))
        at_u = jnp.broadcast_to(idx_ref[pl.ds(u, 1), :], (8, OBS_TILE))
        has_t, has_u = t < size, u < size
        a = jnp.where(has_t, taken(spread_t[0:8], at_t)[0:1], 1.0)
        b = jnp.where(has_u, taken(spread_t[0:8], at_u)[0:1], 0.0)
        d = jnp.where(has_u, taken(spread_u[0:8], at_u)[0:1], 1.0)
        own_t, own_u = rank == t, rank == u
        own = own_t | own_u
        head_t = jnp.where(own, jnp.where(own_t, -1.0, 0.0), row_t)
        head_u = jnp.where(own, jnp.where(own_u, -1.0, 0.0), row_u)
        inverse = 1.0 / a
        factor = b * inverse
        scaled_u = (head_u - factor * head_t) / (d - b * factor)
        scaled_t = head_t * inverse - factor * scaled_u
        column_t = jnp.where(exists, taken(spread_t, idx_ref[0:rows, :]), 0.0)
        column_u = jnp.where(exists, taken(spread_u, idx_ref[0:rows, :]), 0.0)
        on_t, on_u = row == t, row == u
        on = on_t | on_u
        column_t = jnp.where(on, jnp.where(on_t, -1.0, 0.0), column_t)
        column_u = jnp.where(on, jnp.where(on_u, -1.0, 0.0), column_u)
        x = jnp.where(on | own, 0.0, x_ref[0:rows, :])
        x_ref[0:rows, :] = x - column_t * scaled_t - column_u * scaled_u
        return carry

    lax.fori_loop(0, (count + 1) // 2, step, 0)


def in_hbm(*arrays):
    return [pltpu.with_memory_space_constraint(array, pltpu.HBM) for array in arrays]


def fetch(pairs, sems):
    copies = [pltpu.make_async_copy(src, dst, sems.at[k]) for k, (src, dst) in enumerate(pairs)]
    for copy in copies:
        copy.start()
    return copies


def weigh_kernel(
    pred_hbm, mv_hbm, var_hbm, jit_hbm, obs_hbm, params_hbm, out_ref, params_ref,
    pred_ref, mv_ref, var_ref, jit_ref, obs_ref, x_ref, idx_ref, full_ref, sems,
):
    members = pred_ref.shape[0]
    tile_x = lax.axis_index("gx")
    tile_y = lax.axis_index("gy")
    square = (OBS_TILE, OBS_TILE)
    pairs = [
        (obs_hbm.at[tile_x], obs_ref),
        (var_hbm.at[0], var_ref),
        (pred_hbm.at[0, 0], pred_ref),
        (mv_hbm.at[0], mv_ref),
        (jit_hbm.at[0, 0], jit_ref),
        (params_hbm, params_ref),
    ]
    copies = fetch(pairs, sems)
    copies[0].wait()
    obs = obs_ref[pl.ds(tile_y, 1), :]
    groups = (iota((BLOCKS, OBS_TILE), 0) == obs).astype(BF16)
    same = dot(groups, groups, ((0,), (0,)))
    row, col = iota(square, 0), iota(square, 1)
    size = jnp.sum(same, axis=0, keepdims=True)
    count = jnp.max(size).astype(jnp.int32)
    size = size.astype(jnp.int32)
    rank = jnp.sum(jnp.where(row < col, same, 0.0), axis=0, keepdims=True).astype(jnp.int32)
    place = row == rank
    hot = place.astype(BF16)
    numbered = jnp.where(place, col, 0).astype(F32).astype(BF16)
    idx_ref[...] = dot(numbered, same.astype(BF16), ((1,), (0,))).astype(jnp.int32)
    for copy in copies[1:3]:
        copy.wait()
    var = var_ref[...]
    pred = pred_ref[...]
    mean = jnp.sum(pred, axis=0, keepdims=True) / members
    deviation = (pred - mean).astype(BF16)
    out_ref[0] = deviation
    gram = dot(deviation, deviation, ((0,), (0,))) / (members - 1)
    system = jnp.where(same > 0.5, gram, 0.0) + jnp.where(row == col, var, 0.0)
    high, mid, low = split3(system)
    x_ref[...] = (
        dot(hot, low, ((1,), (0,))) + dot(hot, mid, ((1,), (0,))) + dot(hot, high, ((1,), (0,)))
    )
    for copy in copies[3:]:
        copy.wait()
    pred_ref[...] = mv_ref[...] + jnp.sqrt(var) * jit_ref[...] - pred

    def solve(rows):
        sweep(rows, count, x_ref, idx_ref, rank, size)
        high, mid, low = split3(x_ref[0:rows, :])
        taken = hot[0:rows]
        full = dot(taken, low, ((0,), (0,))) + dot(taken, mid, ((0,), (0,))) + dot(taken, high, ((0,), (0,)))
        full_ref[...] = jnp.where(same > 0.5, -full, 0.0)

    @pl.when(count <= SMALL)
    def _():
        solve(SMALL)

    @pl.when(count > SMALL)
    def _():
        solve(OBS_TILE)

    weighted = dot(pred_ref[...], full_ref[...], ((1,), (0,)), lax.Precision.HIGHEST)
    out_ref[1] = weighted.astype(BF16)


def weigh(predicted, measured_value, measurement_variance, observation_jitter, obs_block, params):
    members = predicted.shape[2]
    return pl.pallas_call(
        weigh_kernel,
        out_shape=(jax.ShapeDtypeStruct((2, members, OBS_TILE), BF16), jax.ShapeDtypeStruct(params.shape, BF16)),
        in_specs=[pl.BlockSpec(memory_space=pltpu.HBM)] * 6,
        out_specs=(pl.BlockSpec(memory_space=pltpu.VMEM), pl.BlockSpec(memory_space=pltpu.VMEM)),
        scratch_shapes=[
            pltpu.VMEM((members, OBS_TILE), F32),
            pltpu.VMEM((1, OBS_TILE), F32),
            pltpu.VMEM((1, OBS_TILE), F32),
            pltpu.VMEM((members, OBS_TILE), F32),
            pltpu.VMEM((obs_block.shape[1], OBS_TILE), jnp.int32),
            pltpu.VMEM((OBS_TILE, OBS_TILE), F32),
            pltpu.VMEM((OBS_TILE, OBS_TILE), jnp.int32),
            pltpu.VMEM((OBS_TILE, OBS_TILE), F32),
            pltpu.SemaphoreType.DMA((6,)),
        ],
        compiler_params=pltpu.CompilerParams(vmem_limit_bytes=16 * 2**20),
        name="weigh",
    )(*in_hbm(predicted, measured_value, measurement_variance, observation_jitter, obs_block, params))


def offset(which, place):
    even = 1 - 2 * (place & 1)
    return (0, even, -even)[which]


def prepare_kernel(
    params_ref, radius_hbm, pattern_hbm, obs_hbm, turned_ref, taper_ref, radius_ref, pattern_ref, obs_ref, sems
):
    members = params_ref.shape[1]
    tile_x = lax.axis_index("gx")
    tile_y = lax.axis_index("gy")
    count_x, count_y = obs_ref.shape[0], obs_ref.shape[1]
    copies = fetch([(radius_hbm, radius_ref), (pattern_hbm, pattern_ref), (obs_hbm, obs_ref)], sems)

    for b in range(BLOCKS):
        block = params_ref[b].astype(F32)
        mean = jnp.sum(block, axis=0, keepdims=True) / members
        turned_ref[b] = (block - mean).T.astype(BF16)
    for copy in copies:
        copy.wait()
    shape = (BLOCKS, OBS_TILE)
    block = iota(shape, 0)
    radius = jnp.zeros(shape, jnp.int32)
    for b in range(BLOCKS):
        radius = jnp.where(block == b, radius_ref[b // BLK_Y, b % BLK_Y], radius)
    reach = (radius + 1).astype(F32)
    reach = reach * reach
    pattern = jnp.concatenate([pattern_ref[i] for i in range(BLK_X)], axis=0).astype(F32)
    slots = [jnp.broadcast_to(pattern[:, p : p + 1], shape) for p in range(PATTERN)]

    for t in range(9):
        iy, ix = t // 3, t % 3
        dx, dy = offset(ix, tile_x), offset(iy, tile_y)
        at_x, at_y = tile_x + dx, tile_y + dy
        valid = (at_x >= 0) & (at_x < count_x) & (at_y >= 0) & (at_y < count_y)
        at_x = jnp.clip(at_x, 0, count_x - 1)
        at_y = jnp.clip(at_y, 0, count_y - 1)
        obs = obs_ref[at_x, pl.ds(at_y, 1), :]
        step_x = dx * BLK_X + (obs >> 2) - (block >> 2)
        step_y = dy * BLK_Y + (obs & 3) - (block & 3)
        inside = (jnp.abs(step_x) <= 2) & (jnp.abs(step_y) <= 2) & valid
        slot = (step_x + 2) * 5 + (step_y + 2)
        picked = jnp.zeros(shape, F32)
        for p in range(PATTERN):
            picked = jnp.where(slot == p, slots[p], picked)
        spread = (step_x * step_x + step_y * step_y).astype(F32)
        shaped = jnp.maximum(1.0 - spread / reach, 0.0)
        taper_ref[iy, ix] = jnp.where(inside, picked, 0.0) * shaped / (members - 1)


def prepare(by_block, taper_radius, taper_pattern, obs_block):
    members = by_block.shape[1]
    return pl.pallas_call(
        prepare_kernel,
        out_shape=(
            jax.ShapeDtypeStruct((BLOCKS, CELLS, members), BF16),
            jax.ShapeDtypeStruct((3, 3, BLOCKS, OBS_TILE), F32),
        ),
        in_specs=[pl.BlockSpec(memory_space=pltpu.VMEM)] + [pl.BlockSpec(memory_space=pltpu.HBM)] * 3,
        out_specs=(pl.BlockSpec(memory_space=pltpu.VMEM), pl.BlockSpec(memory_space=pltpu.VMEM)),
        scratch_shapes=[
            pltpu.SMEM(taper_radius.shape, jnp.int32),
            pltpu.VMEM(taper_pattern.shape, jnp.int32),
            pltpu.VMEM(obs_block.shape, jnp.int32),
            pltpu.SemaphoreType.DMA((3,)),
        ],
        compiler_params=pltpu.CompilerParams(vmem_limit_bytes=16 * 2**20),
        cost_estimate=pl.CostEstimate(flops=4_000_000, bytes_accessed=1_000_000, transcendentals=0),
        name="prepare",
    )(by_block, *in_hbm(taper_radius, taper_pattern, obs_block))


def moved(b, which, turned_ref, taper_ref, tiles_ref):
    cross = dot(turned_ref[b], tiles_ref[0], ((1,), (0,)))
    count = tiles_ref.shape[2] // OBS_TILE
    taper = jnp.concatenate([taper_ref[which, k, pl.ds(b, 1), :] for k in range(count)], axis=1)
    gain = (cross * taper).astype(BF16)
    return dot(tiles_ref[1], gain, ((1,), (1,)))


def first_of(side, tile_y):
    return 2 * ((tile_y & 1) ^ 1 ^ side)


def block_of(k, side, tile_y):
    return (k >> 1) * BLK_Y + first_of(side, tile_y) + (k & 1)


def target(chip, r, chips):
    return chip ^ r if chips & (chips - 1) == 0 else (chip + r) % chips


def source(chip, r, chips):
    return chip ^ r if chips & (chips - 1) == 0 else (chip + chips - r) % chips


def put(piece_refs, rows_ref, k, updated):
    chips, share = len(piece_refs), piece_refs[0].shape[2]
    mine = lax.axis_index("gy")
    rows_ref[k] = updated
    for r, ref in enumerate(piece_refs):
        for flip in (0, 1):
            owner = 2 * target(mine >> 1, r, chips) + ((mine & 1) ^ flip)
            ref[flip, k] = rows_ref[k, pl.ds(pl.multiple_of(owner * share, share), share), :]


def near_kernel(params_ref, turned_ref, taper_ref, own_ref, even_ref, part_ref, *refs):
    piece_refs, rows_ref = refs[:-1], refs[-1]
    tile_y = lax.axis_index("gy")
    for k in range(SIDE):
        b = block_of(k, 0, tile_y)
        delta = moved(b, 0, turned_ref, taper_ref, own_ref) + moved(b, 1, turned_ref, taper_ref, even_ref)
        put(piece_refs, rows_ref, k, (params_ref[b].astype(F32) + delta).astype(BF16))
    for k in range(SIDE):
        b = block_of(k, 1, tile_y)
        part_ref[k] = params_ref[b].astype(F32) + moved(b, 0, turned_ref, taper_ref, own_ref)


def far_kernel(turned_ref, taper_ref, odd_ref, part_ref, near_ref, *refs):
    both_ref, rows_ref = refs[-2], refs[-1]
    piece_refs = (*refs[:-2], both_ref.at[1])
    both_ref[0] = near_ref[...]
    tile_y = lax.axis_index("gy")
    for k in range(SIDE):
        b = block_of(k, 1, tile_y)
        put(piece_refs, rows_ref, k, (part_ref[k] + moved(b, 2, turned_ref, taper_ref, odd_ref)).astype(BF16))


def pack_kernel(*refs):
    at = 0
    for ref in refs[:-1]:
        for piece in halves(ref):
            refs[-1][at] = piece[1]
            at += 1


def halves(ref):
    return [ref] if len(ref.shape) == 4 else [ref.at[side] for side in range(ref.shape[0])]


def gather_kernel(chips, *refs):
    early, late = refs[: chips + 1], refs[chips + 1 : 2 * chips + 1]
    out_hbm, rows_ref, out_ref, sems = refs[2 * chips + 1 :]
    last = chips - 1
    places = [(0, 0), (1, 0)] + [(0, r) for r in range(1, last)] + [(0, last), (1, last)] + [(1, r) for r in range(1, last)]
    mine_pieces = [piece for ref in early[1:] + late[1:] for piece in halves(ref)]
    even_pieces = [ref.at[k] for ref in (early[0], late[0]) for k in range(ref.shape[0])]
    share = early[0].shape[2]
    mine = lax.axis_index("gy")
    chip, core = mine >> 1, mine & 1
    line = 2 * chips * BLK_Y
    for (side, r), own, even in zip(places, mine_pieces, even_pieces):
        for flip in (0, 1):
            other = core ^ flip
            tile = 2 * source(chip, r, chips) + other
            for k in range(SIDE):
                piece = even[k] if flip else own[0, k]
                start = (k >> 1) * line + tile * BLK_Y + first_of(side, other) + (k & 1)
                rows_ref[pl.ds(start, share, stride=BLK_X * line), :] = piece.astype(F32)
    pieces = sems.shape[0]
    step = rows_ref.shape[0] // pieces
    copies = []
    for p in range(pieces):
        place = slice(p * step, (p + 1) * step)
        out_ref[place] = rows_ref[place].astype(BF16)
        copies.append(pltpu.make_async_copy(out_ref.at[pl.ds(p * step, step)], out_hbm.at[pl.ds(p * step, step)], sems.at[p]))
        copies[-1].start()
    for copy in copies:
        copy.wait()


VMEM = pl.BlockSpec(memory_space=pltpu.VMEM)
LONG = pl.CostEstimate(flops=4_000_000_000, bytes_accessed=10_000_000, transcendentals=0)
LIMIT = pltpu.CompilerParams(vmem_limit_bytes=24 * 2**20)


def update_near(by_block, turned, taper, own, even, parts):
    members = by_block.shape[1]
    pieces = [jax.ShapeDtypeStruct((2, SIDE, members // parts, CELLS), BF16)] * (parts // 2)
    return pl.pallas_call(
        near_kernel,
        out_shape=(jax.ShapeDtypeStruct((SIDE, members, CELLS), F32), *pieces),
        in_specs=[VMEM] * 5,
        out_specs=(VMEM,) * (1 + len(pieces)),
        scratch_shapes=[pltpu.VMEM((SIDE, members, CELLS), BF16)],
        compiler_params=LIMIT,
        cost_estimate=LONG,
        name="near",
    )(by_block, turned, taper, own, even)


def update_far(turned, taper, odd, part, near):
    members = part.shape[1]
    parts = members // near[0].shape[2]
    piece = jax.ShapeDtypeStruct(near[0].shape, BF16)
    shapes = (piece,) * (parts // 2 - 1) + (jax.ShapeDtypeStruct((2, *piece.shape), BF16),)
    return pl.pallas_call(
        far_kernel,
        out_shape=shapes,
        in_specs=[VMEM] * 5,
        out_specs=(VMEM,) * len(shapes),
        scratch_shapes=[pltpu.VMEM((SIDE, members, CELLS), BF16)],
        compiler_params=LIMIT,
        cost_estimate=LONG,
        name="far",
    )(turned, taper, odd, part, near[-1])


def pack(pieces):
    count = sum(1 if piece.ndim == 4 else piece.shape[0] for piece in pieces)
    return pl.pallas_call(
        pack_kernel,
        out_shape=jax.ShapeDtypeStruct((count, *pieces[-1].shape[-3:]), BF16),
        in_specs=[VMEM] * len(pieces),
        out_specs=VMEM,
        compiler_params=LIMIT,
        name="pack",
    )(*pieces)


def gather(chips, early_even, early, late_even, late):
    share = early[0].shape[2]
    rows = share * BLOCKS * 2 * chips
    out = pl.pallas_call(
        functools.partial(gather_kernel, chips),
        out_shape=jax.ShapeDtypeStruct((rows, CELLS), BF16),
        in_specs=[VMEM] * (2 + len(early) + len(late)),
        out_specs=pl.BlockSpec(memory_space=pl.ANY),
        scratch_shapes=[
            pltpu.VMEM((rows, CELLS), F32),
            pltpu.VMEM((rows, CELLS), BF16),
            pltpu.SemaphoreType.DMA((4,)),
        ],
        compiler_params=LIMIT,
        name="gather",
    )(early_even, *early, late_even, *late)
    return out.reshape(share, BLK_X, 2 * chips * BLK_Y, CELLS)


def swap(block, axis, first, close=False):
    count = lax.axis_size(axis)
    pairs = [(i, i + 1) for i in range(first, count - 1, 2)]
    if close:
        pairs.append((count - 1, 0))
    return lax.ppermute(block, axis, pairs + [(b, a) for a, b in pairs])


def hop(piece, r):
    count = lax.axis_size("gy")
    pairs = [(i, 2 * target(i // 2, r, count // 2) + i % 2) for i in range(count)]
    return lax.ppermute(piece, "gy", pairs)


def per_device(
    params,
    predicted,
    measured_value,
    measurement_variance,
    observation_jitter,
    obs_block,
    taper_radius,
    taper_pattern,
):
    members = params.shape[0]
    parts = lax.axis_size("gy")
    own, params = weigh(
        predicted, measured_value, measurement_variance, observation_jitter, obs_block, params
    )
    by_block = params.reshape(members, BLOCKS, CELLS).transpose(1, 0, 2)
    even = swap(own, "gx", 0)
    odd = swap(own, "gx", 1, close=True)
    turned, taper = prepare(by_block, taper_radius, taper_pattern, obs_block)
    column = jnp.concatenate([own, even, odd], axis=2)
    column, turned, taper = lax.optimization_barrier((column, turned, taper))
    even = swap(column, "gy", 0)
    odd = swap(column, "gy", 1)
    part, *near = update_near(by_block, turned, taper, column, even, parts)
    last = parts // 2 - 1
    near_hops = {r: hop(near[r], r) for r in range(1, last)}
    *far, both = update_far(turned, taper, odd, part, near)
    for r in range(1, last):
        far[r], near_hops[r] = lax.optimization_barrier((far[r], near_hops[r]))
    far_hops = {r: hop(far[r], r) for r in range(1, last)}
    early = [near[0], far[0], *(near_hops[r] for r in range(1, last))]
    late = [hop(both, last), *(far_hops[r] for r in range(1, last))]
    late_even = swap(pack(late), "gy", 0)
    early_even = swap(pack(early), "gy", 0)
    return gather(parts // 2, early_even, early, late_even, late)


def solution(mesh):
    placed = (
        P(None, "gx", "gy", None),
        P("gx", "gy", None, None),
        P("gx", "gy", None),
        P("gx", "gy", None),
        P("gx", "gy", None, None),
        P(),
        P("gx", "gy"),
        P("gx", "gy", None),
    )
    return jax.shard_map(
        per_device, mesh=mesh, in_specs=placed, out_specs=P("gy", "gx", None, None), check_vma=False
    )
```

```python
import functools

import jax
import jax.numpy as jnp
from jax import lax
from jax.experimental import pallas as pl
from jax.experimental.pallas import tpu as pltpu
from jax.sharding import PartitionSpec as P

CELLS = 128
BLK_X = 2
BLK_Y = 4
BLOCKS = BLK_X * BLK_Y
SIDE = BLOCKS // 2
OBS_TILE = 128
PATTERN = 25
SMALL = 32

F32 = jnp.float32
BF16 = jnp.bfloat16


def iota(shape, dim):
    return lax.broadcasted_iota(jnp.int32, shape, dim)


def split3(x):
    high = x.astype(BF16)
    rest = x - high.astype(F32)
    mid = rest.astype(BF16)
    low = (rest - mid.astype(F32)).astype(BF16)
    return high, mid, low


def dot(a, b, dims, precision=None):
    return lax.dot_general(a, b, ((dims[0], dims[1]), ((), ())), precision=precision, preferred_element_type=F32)


def sweep(rows, count, x_ref, idx_ref, rank, size):
    row = iota((rows, OBS_TILE), 0)
    exists = row < size

    def taken(spread, indices):
        return jnp.take_along_axis(spread, indices, axis=1, mode="promise_in_bounds")

    def step(k, carry):
        t = 2 * k
        u = t + 1
        row_t, row_u = x_ref[pl.ds(t, 1), :], x_ref[pl.ds(u, 1), :]
        spread_t = jnp.broadcast_to(row_t, (rows, OBS_TILE))
        spread_u = jnp.broadcast_to(row_u, (rows, OBS_TILE))
        at_t = jnp.broadcast_to(idx_ref[pl.ds(t, 1), :], (8, OBS_TILE))
        at_u = jnp.broadcast_to(idx_ref[pl.ds(u, 1), :], (8, OBS_TILE))
        has_t, has_u = t < size, u < size
        a = jnp.where(has_t, taken(spread_t[0:8], at_t)[0:1], 1.0)
        b = jnp.where(has_u, taken(spread_t[0:8], at_u)[0:1], 0.0)
        d = jnp.where(has_u, taken(spread_u[0:8], at_u)[0:1], 1.0)
        own_t, own_u = rank == t, rank == u
        own = own_t | own_u
        head_t = jnp.where(own, jnp.where(own_t, -1.0, 0.0), row_t)
        head_u = jnp.where(own, jnp.where(own_u, -1.0, 0.0), row_u)
        inverse = 1.0 / a
        factor = b * inverse
        scaled_u = (head_u - factor * head_t) / (d - b * factor)
        scaled_t = head_t * inverse - factor * scaled_u
        column_t = jnp.where(exists, taken(spread_t, idx_ref[0:rows, :]), 0.0)
        column_u = jnp.where(exists, taken(spread_u, idx_ref[0:rows, :]), 0.0)
        on_t, on_u = row == t, row == u
        on = on_t | on_u
        column_t = jnp.where(on, jnp.where(on_t, -1.0, 0.0), column_t)
        column_u = jnp.where(on, jnp.where(on_u, -1.0, 0.0), column_u)
        x = jnp.where(on | own, 0.0, x_ref[0:rows, :])
        x_ref[0:rows, :] = x - column_t * scaled_t - column_u * scaled_u
        return carry

    lax.fori_loop(0, (count + 1) // 2, step, 0)


def in_hbm(*arrays):
    return [pltpu.with_memory_space_constraint(array, pltpu.HBM) for array in arrays]


def fetch(pairs, sems):
    copies = [pltpu.make_async_copy(src, dst, sems.at[k]) for k, (src, dst) in enumerate(pairs)]
    for copy in copies:
        copy.start()
    return copies


def weigh_kernel(
    pred_hbm, mv_hbm, var_hbm, jit_hbm, obs_hbm, params_hbm, out_ref, params_ref,
    pred_ref, mv_ref, var_ref, jit_ref, obs_ref, x_ref, idx_ref, full_ref, sems,
):
    members = pred_ref.shape[0]
    tile_x = lax.axis_index("gx")
    tile_y = lax.axis_index("gy")
    square = (OBS_TILE, OBS_TILE)
    pairs = [
        (pred_hbm.at[0, 0], pred_ref),
        (obs_hbm.at[tile_x], obs_ref),
        (var_hbm.at[0], var_ref),
        (mv_hbm.at[0], mv_ref),
        (jit_hbm.at[0, 0], jit_ref),
        (params_hbm, params_ref),
    ]
    copies = fetch(pairs, sems)
    for copy in copies[:3]:
        copy.wait()
    pred = pred_ref[...]
    var = var_ref[...]
    mean = jnp.sum(pred, axis=0, keepdims=True) / members
    deviation = (pred - mean).astype(BF16)
    out_ref[0] = deviation
    obs = obs_ref[pl.ds(tile_y, 1), :]
    groups = (iota((BLOCKS, OBS_TILE), 0) == obs).astype(BF16)
    same = dot(groups, groups, ((0,), (0,)))
    gram = dot(deviation, deviation, ((0,), (0,))) / (members - 1)
    row, col = iota(square, 0), iota(square, 1)
    system = jnp.where(same > 0.5, gram, 0.0) + jnp.where(row == col, var, 0.0)
    size = jnp.sum(same, axis=0, keepdims=True)
    count = jnp.max(size).astype(jnp.int32)
    size = size.astype(jnp.int32)
    rank = jnp.sum(jnp.where(row < col, same, 0.0), axis=0, keepdims=True).astype(jnp.int32)
    place = row == rank
    hot = place.astype(BF16)
    high, mid, low = split3(system)
    x_ref[...] = (
        dot(hot, low, ((1,), (0,))) + dot(hot, mid, ((1,), (0,))) + dot(hot, high, ((1,), (0,)))
    )
    numbered = jnp.where(place, col, 0).astype(F32).astype(BF16)
    idx_ref[...] = dot(numbered, same.astype(BF16), ((1,), (0,))).astype(jnp.int32)

    def solve(rows):
        sweep(rows, count, x_ref, idx_ref, rank, size)
        high, mid, low = split3(x_ref[0:rows, :])
        taken = hot[0:rows]
        full = dot(taken, low, ((0,), (0,))) + dot(taken, mid, ((0,), (0,))) + dot(taken, high, ((0,), (0,)))
        full_ref[...] = jnp.where(same > 0.5, -full, 0.0)

    @pl.when(count <= SMALL)
    def _():
        solve(SMALL)

    @pl.when(count > SMALL)
    def _():
        solve(OBS_TILE)

    for copy in copies[3:]:
        copy.wait()
    innovation = mv_ref[...] + jnp.sqrt(var) * jit_ref[...] - pred
    weighted = dot(innovation, full_ref[...], ((1,), (0,)), lax.Precision.HIGHEST)
    out_ref[1] = weighted.astype(BF16)


def weigh(predicted, measured_value, measurement_variance, observation_jitter, obs_block, params):
    members = predicted.shape[2]
    return pl.pallas_call(
        weigh_kernel,
        out_shape=(jax.ShapeDtypeStruct((2, members, OBS_TILE), BF16), jax.ShapeDtypeStruct(params.shape, BF16)),
        in_specs=[pl.BlockSpec(memory_space=pltpu.HBM)] * 6,
        out_specs=(pl.BlockSpec(memory_space=pltpu.VMEM), pl.BlockSpec(memory_space=pltpu.VMEM)),
        scratch_shapes=[
            pltpu.VMEM((members, OBS_TILE), F32),
            pltpu.VMEM((1, OBS_TILE), F32),
            pltpu.VMEM((1, OBS_TILE), F32),
            pltpu.VMEM((members, OBS_TILE), F32),
            pltpu.VMEM((obs_block.shape[1], OBS_TILE), jnp.int32),
            pltpu.VMEM((OBS_TILE, OBS_TILE), F32),
            pltpu.VMEM((OBS_TILE, OBS_TILE), jnp.int32),
            pltpu.VMEM((OBS_TILE, OBS_TILE), F32),
            pltpu.SemaphoreType.DMA((6,)),
        ],
        compiler_params=pltpu.CompilerParams(vmem_limit_bytes=16 * 2**20),
        name="weigh",
    )(*in_hbm(predicted, measured_value, measurement_variance, observation_jitter, obs_block, params))


def offset(which, place):
    even = 1 - 2 * (place & 1)
    return (0, even, -even)[which]


def prepare_kernel(
    params_ref, radius_hbm, pattern_hbm, obs_hbm, turned_ref, taper_ref, radius_ref, pattern_ref, obs_ref, sems
):
    members = params_ref.shape[1]
    tile_x = lax.axis_index("gx")
    tile_y = lax.axis_index("gy")
    count_x, count_y = obs_ref.shape[0], obs_ref.shape[1]
    copies = fetch([(radius_hbm, radius_ref), (pattern_hbm, pattern_ref), (obs_hbm, obs_ref)], sems)

    for b in range(BLOCKS):
        block = params_ref[b].astype(F32)
        mean = jnp.sum(block, axis=0, keepdims=True) / members
        turned_ref[b] = (block - mean).T.astype(BF16)
    for copy in copies:
        copy.wait()
    shape = (BLOCKS, OBS_TILE)
    block = iota(shape, 0)
    radius = jnp.zeros(shape, jnp.int32)
    for b in range(BLOCKS):
        radius = jnp.where(block == b, radius_ref[b // BLK_Y, b % BLK_Y], radius)
    reach = (radius + 1).astype(F32)
    reach = reach * reach
    pattern = jnp.concatenate([pattern_ref[i] for i in range(BLK_X)], axis=0).astype(F32)
    slots = [jnp.broadcast_to(pattern[:, p : p + 1], shape) for p in range(PATTERN)]

    for t in range(9):
        iy, ix = t // 3, t % 3
        dx, dy = offset(ix, tile_x), offset(iy, tile_y)
        at_x, at_y = tile_x + dx, tile_y + dy
        valid = (at_x >= 0) & (at_x < count_x) & (at_y >= 0) & (at_y < count_y)
        at_x = jnp.clip(at_x, 0, count_x - 1)
        at_y = jnp.clip(at_y, 0, count_y - 1)
        obs = obs_ref[at_x, pl.ds(at_y, 1), :]
        step_x = dx * BLK_X + (obs >> 2) - (block >> 2)
        step_y = dy * BLK_Y + (obs & 3) - (block & 3)
        inside = (jnp.abs(step_x) <= 2) & (jnp.abs(step_y) <= 2) & valid
        slot = (step_x + 2) * 5 + (step_y + 2)
        picked = jnp.zeros(shape, F32)
        for p in range(PATTERN):
            picked = jnp.where(slot == p, slots[p], picked)
        spread = (step_x * step_x + step_y * step_y).astype(F32)
        shaped = jnp.maximum(1.0 - spread / reach, 0.0)
        taper_ref[iy, ix] = jnp.where(inside, picked, 0.0) * shaped / (members - 1)


def prepare(by_block, taper_radius, taper_pattern, obs_block):
    members = by_block.shape[1]
    return pl.pallas_call(
        prepare_kernel,
        out_shape=(
            jax.ShapeDtypeStruct((BLOCKS, CELLS, members), BF16),
            jax.ShapeDtypeStruct((3, 3, BLOCKS, OBS_TILE), F32),
        ),
        in_specs=[pl.BlockSpec(memory_space=pltpu.VMEM)] + [pl.BlockSpec(memory_space=pltpu.HBM)] * 3,
        out_specs=(pl.BlockSpec(memory_space=pltpu.VMEM), pl.BlockSpec(memory_space=pltpu.VMEM)),
        scratch_shapes=[
            pltpu.SMEM(taper_radius.shape, jnp.int32),
            pltpu.VMEM(taper_pattern.shape, jnp.int32),
            pltpu.VMEM(obs_block.shape, jnp.int32),
            pltpu.SemaphoreType.DMA((3,)),
        ],
        compiler_params=pltpu.CompilerParams(vmem_limit_bytes=16 * 2**20),
        cost_estimate=pl.CostEstimate(flops=4_000_000, bytes_accessed=1_000_000, transcendentals=0),
        name="prepare",
    )(by_block, *in_hbm(taper_radius, taper_pattern, obs_block))


def moved(b, which, turned_ref, taper_ref, tiles_ref):
    cross = dot(turned_ref[b], tiles_ref[0], ((1,), (0,)))
    count = tiles_ref.shape[2] // OBS_TILE
    taper = jnp.concatenate([taper_ref[which, k, pl.ds(b, 1), :] for k in range(count)], axis=1)
    gain = (cross * taper).astype(BF16)
    return dot(tiles_ref[1], gain, ((1,), (1,)))


def first_of(side, tile_y):
    return 2 * ((tile_y & 1) ^ 1 ^ side)


def block_of(k, side, tile_y):
    return (k >> 1) * BLK_Y + first_of(side, tile_y) + (k & 1)


def target(chip, r, chips):
    return chip ^ r if chips & (chips - 1) == 0 else (chip + r) % chips


def source(chip, r, chips):
    return chip ^ r if chips & (chips - 1) == 0 else (chip + chips - r) % chips


def put(piece_refs, rows_ref, k, updated):
    chips, share = len(piece_refs), piece_refs[0].shape[2]
    mine = lax.axis_index("gy")
    rows_ref[k] = updated
    for r, ref in enumerate(piece_refs):
        for flip in (0, 1):
            owner = 2 * target(mine >> 1, r, chips) + ((mine & 1) ^ flip)
            ref[flip, k] = rows_ref[k, pl.ds(pl.multiple_of(owner * share, share), share), :]


def near_kernel(params_ref, turned_ref, taper_ref, own_ref, even_ref, part_ref, *refs):
    piece_refs, rows_ref = refs[:-1], refs[-1]
    tile_y = lax.axis_index("gy")
    for k in range(SIDE):
        b = block_of(k, 0, tile_y)
        delta = moved(b, 0, turned_ref, taper_ref, own_ref) + moved(b, 1, turned_ref, taper_ref, even_ref)
        put(piece_refs, rows_ref, k, (params_ref[b].astype(F32) + delta).astype(BF16))
    for k in range(SIDE):
        b = block_of(k, 1, tile_y)
        part_ref[k] = params_ref[b].astype(F32) + moved(b, 0, turned_ref, taper_ref, own_ref)


def far_kernel(turned_ref, taper_ref, odd_ref, part_ref, near_ref, *refs):
    both_ref, rows_ref = refs[1], refs[-1]
    piece_refs = (refs[0], both_ref.at[1], *refs[2:-1])
    both_ref[0] = near_ref[...]
    tile_y = lax.axis_index("gy")
    for k in range(SIDE):
        b = block_of(k, 1, tile_y)
        put(piece_refs, rows_ref, k, (part_ref[k] + moved(b, 2, turned_ref, taper_ref, odd_ref)).astype(BF16))


def pack_kernel(*refs):
    at = 0
    for ref in refs[:-1]:
        for piece in halves(ref):
            refs[-1][at] = piece[1]
            at += 1


def halves(ref):
    return [ref] if len(ref.shape) == 4 else [ref.at[side] for side in range(ref.shape[0])]


def settle(chips, sides, refs, rows_ref):
    even_ref, pieces = refs[0], [piece for ref in refs[1:] for piece in halves(ref)]
    share = even_ref.shape[2]
    mine = lax.axis_index("gy")
    chip, core = mine >> 1, mine & 1
    line = 2 * chips * BLK_Y
    for at, ((side, r), own) in enumerate(zip(sides, pieces)):
        for flip in (0, 1):
            other = core ^ flip
            tile = 2 * source(chip, r, chips) + other
            for k in range(SIDE):
                piece = even_ref[at, k] if flip else own[0, k]
                start = (k >> 1) * line + tile * BLK_Y + first_of(side, other) + (k & 1)
                rows_ref[pl.ds(start, share, stride=BLK_X * line), :] = piece.astype(F32)


def early_kernel(chips, *refs):
    settle(chips, [(0, 0), (1, 0)] + [(0, r) for r in range(2, chips)], refs[:-1], refs[-1])


def late_kernel(chips, *refs):
    late_refs, out_hbm, rows_ref, out_ref, sems = refs[1:-4], *refs[-4:]
    settle(chips, [(0, 1), (1, 1)] + [(1, r) for r in range(2, chips)], late_refs, rows_ref)
    pieces = sems.shape[0]
    step = rows_ref.shape[0] // pieces
    copies = []
    for p in range(pieces):
        place = slice(p * step, (p + 1) * step)
        out_ref[place] = rows_ref[place].astype(BF16)
        copies.append(pltpu.make_async_copy(out_ref.at[pl.ds(p * step, step)], out_hbm.at[pl.ds(p * step, step)], sems.at[p]))
        copies[-1].start()
    for copy in copies:
        copy.wait()


VMEM = pl.BlockSpec(memory_space=pltpu.VMEM)
LONG = pl.CostEstimate(flops=4_000_000_000, bytes_accessed=10_000_000, transcendentals=0)
LIMIT = pltpu.CompilerParams(vmem_limit_bytes=24 * 2**20)


def update_near(by_block, turned, taper, own, even, parts):
    members = by_block.shape[1]
    pieces = [jax.ShapeDtypeStruct((2, SIDE, members // parts, CELLS), BF16)] * (parts // 2)
    return pl.pallas_call(
        near_kernel,
        out_shape=(jax.ShapeDtypeStruct((SIDE, members, CELLS), F32), *pieces),
        in_specs=[VMEM] * 5,
        out_specs=(VMEM,) * (1 + len(pieces)),
        scratch_shapes=[pltpu.VMEM((SIDE, members, CELLS), BF16)],
        compiler_params=LIMIT,
        cost_estimate=LONG,
        name="near",
    )(by_block, turned, taper, own, even)


def update_far(turned, taper, odd, part, near):
    members = part.shape[1]
    parts = members // near[0].shape[2]
    piece = jax.ShapeDtypeStruct(near[0].shape, BF16)
    shapes = (piece, jax.ShapeDtypeStruct((2, *piece.shape), BF16)) + (piece,) * (parts // 2 - 2)
    return pl.pallas_call(
        far_kernel,
        out_shape=shapes,
        in_specs=[VMEM] * 5,
        out_specs=(VMEM,) * len(shapes),
        scratch_shapes=[pltpu.VMEM((SIDE, members, CELLS), BF16)],
        compiler_params=LIMIT,
        cost_estimate=LONG,
        name="far",
    )(turned, taper, odd, part, near[1])


def pack(pieces):
    count = sum(1 if piece.ndim == 4 else piece.shape[0] for piece in pieces)
    return pl.pallas_call(
        pack_kernel,
        out_shape=jax.ShapeDtypeStruct((count, *pieces[-1].shape[-3:]), BF16),
        in_specs=[VMEM] * len(pieces),
        out_specs=VMEM,
        compiler_params=LIMIT,
        name="pack",
    )(*pieces)


def gather(chips, early_even, early, late_even, late):
    share = early[0].shape[2]
    rows = share * BLOCKS * 2 * chips
    placed = pl.pallas_call(
        functools.partial(early_kernel, chips),
        out_shape=jax.ShapeDtypeStruct((rows, CELLS), F32),
        in_specs=[VMEM] * (1 + len(early)),
        out_specs=VMEM,
        compiler_params=LIMIT,
        cost_estimate=LONG,
        name="early",
    )(early_even, *early)
    out, _ = pl.pallas_call(
        functools.partial(late_kernel, chips),
        out_shape=(jax.ShapeDtypeStruct((rows, CELLS), BF16), jax.ShapeDtypeStruct((rows, CELLS), F32)),
        in_specs=[VMEM] * (2 + len(late)),
        out_specs=(pl.BlockSpec(memory_space=pl.ANY), VMEM),
        scratch_shapes=[
            pltpu.VMEM((rows, CELLS), BF16),
            pltpu.SemaphoreType.DMA((4,)),
        ],
        input_output_aliases={0: 1},
        compiler_params=LIMIT,
        name="late",
    )(placed, late_even, *late)
    return out.reshape(share, BLK_X, 2 * chips * BLK_Y, CELLS)


def swap(block, axis, first, close=False):
    count = lax.axis_size(axis)
    pairs = [(i, i + 1) for i in range(first, count - 1, 2)]
    if close:
        pairs.append((count - 1, 0))
    return lax.ppermute(block, axis, pairs + [(b, a) for a, b in pairs])


def hop(piece, r):
    count = lax.axis_size("gy")
    pairs = [(i, 2 * target(i // 2, r, count // 2) + i % 2) for i in range(count)]
    return lax.ppermute(piece, "gy", pairs)


def per_device(
    params,
    predicted,
    measured_value,
    measurement_variance,
    observation_jitter,
    obs_block,
    taper_radius,
    taper_pattern,
):
    members = params.shape[0]
    parts = lax.axis_size("gy")
    own, params = weigh(
        predicted, measured_value, measurement_variance, observation_jitter, obs_block, params
    )
    by_block = params.reshape(members, BLOCKS, CELLS).transpose(1, 0, 2)
    even = swap(own, "gx", 0)
    odd = swap(own, "gx", 1, close=True)
    turned, taper = prepare(by_block, taper_radius, taper_pattern, obs_block)
    column = jnp.concatenate([own, even, odd], axis=2)
    column, turned, taper = lax.optimization_barrier((column, turned, taper))
    even = swap(column, "gy", 0)
    odd = swap(column, "gy", 1)
    part, *near = update_near(by_block, turned, taper, column, even, parts)
    chips = parts // 2
    near_hops = {r: hop(near[r], r) for r in range(2, chips)}
    own_far, both, *far = update_far(turned, taper, odd, part, near)
    far = {r: far[r - 2] for r in range(2, chips)}
    for r in range(2, chips):
        far[r], near_hops[r] = lax.optimization_barrier((far[r], near_hops[r]))
    far_hops = {r: hop(far[r], r) for r in range(2, chips)}
    early = [near[0], own_far, *(near_hops[r] for r in range(2, chips))]
    late = [hop(both, 1), *(far_hops[r] for r in range(2, chips))]
    late_even = swap(pack(late), "gy", 0)
    early_even = swap(pack(early), "gy", 0)
    return gather(chips, early_even, early, late_even, late)


def solution(mesh):
    placed = (
        P(None, "gx", "gy", None),
        P("gx", "gy", None, None),
        P("gx", "gy", None),
        P("gx", "gy", None),
        P("gx", "gy", None, None),
        P(),
        P("gx", "gy"),
        P("gx", "gy", None),
    )
    return jax.shard_map(
        per_device, mesh=mesh, in_specs=placed, out_specs=P("gy", "gx", None, None), check_vma=False
    )
```

```python
import functools

import jax
import jax.numpy as jnp
from jax import lax
from jax.experimental import pallas as pl
from jax.experimental.pallas import tpu as pltpu
from jax.sharding import PartitionSpec as P

CELLS = 128
BLK_X = 2
BLK_Y = 4
BLOCKS = BLK_X * BLK_Y
SIDE = BLOCKS // 2
OBS_TILE = 128
PATTERN = 25
SMALL = 32

F32 = jnp.float32
BF16 = jnp.bfloat16


def iota(shape, dim):
    return lax.broadcasted_iota(jnp.int32, shape, dim)


def split3(x):
    high = x.astype(BF16)
    rest = x - high.astype(F32)
    mid = rest.astype(BF16)
    low = (rest - mid.astype(F32)).astype(BF16)
    return high, mid, low


def dot(a, b, dims, precision=None):
    return lax.dot_general(a, b, ((dims[0], dims[1]), ((), ())), precision=precision, preferred_element_type=F32)


def sweep(rows, count, x_ref, idx_ref, rank, size):
    row = iota((rows, OBS_TILE), 0)
    exists = row < size

    def taken(spread, indices):
        return jnp.take_along_axis(spread, indices, axis=1, mode="promise_in_bounds")

    def step(k, carry):
        t = 2 * k
        u = t + 1
        row_t, row_u = x_ref[pl.ds(t, 1), :], x_ref[pl.ds(u, 1), :]
        spread_t = jnp.broadcast_to(row_t, (rows, OBS_TILE))
        spread_u = jnp.broadcast_to(row_u, (rows, OBS_TILE))
        at_t = jnp.broadcast_to(idx_ref[pl.ds(t, 1), :], (8, OBS_TILE))
        at_u = jnp.broadcast_to(idx_ref[pl.ds(u, 1), :], (8, OBS_TILE))
        has_t, has_u = t < size, u < size
        a = jnp.where(has_t, taken(spread_t[0:8], at_t)[0:1], 1.0)
        b = jnp.where(has_u, taken(spread_t[0:8], at_u)[0:1], 0.0)
        d = jnp.where(has_u, taken(spread_u[0:8], at_u)[0:1], 1.0)
        own_t, own_u = rank == t, rank == u
        own = own_t | own_u
        head_t = jnp.where(own, jnp.where(own_t, -1.0, 0.0), row_t)
        head_u = jnp.where(own, jnp.where(own_u, -1.0, 0.0), row_u)
        inverse = 1.0 / a
        factor = b * inverse
        scaled_u = (head_u - factor * head_t) / (d - b * factor)
        scaled_t = head_t * inverse - factor * scaled_u
        column_t = jnp.where(exists, taken(spread_t, idx_ref[0:rows, :]), 0.0)
        column_u = jnp.where(exists, taken(spread_u, idx_ref[0:rows, :]), 0.0)
        on_t, on_u = row == t, row == u
        on = on_t | on_u
        column_t = jnp.where(on, jnp.where(on_t, -1.0, 0.0), column_t)
        column_u = jnp.where(on, jnp.where(on_u, -1.0, 0.0), column_u)
        x = jnp.where(on | own, 0.0, x_ref[0:rows, :])
        x_ref[0:rows, :] = x - column_t * scaled_t - column_u * scaled_u
        return carry

    lax.fori_loop(0, (count + 1) // 2, step, 0)


def in_hbm(*arrays):
    return [pltpu.with_memory_space_constraint(array, pltpu.HBM) for array in arrays]


def fetch(pairs, sems):
    copies = [pltpu.make_async_copy(src, dst, sems.at[k]) for k, (src, dst) in enumerate(pairs)]
    for copy in copies:
        copy.start()
    return copies


def weigh_kernel(
    pred_hbm, mv_hbm, var_hbm, jit_hbm, obs_hbm, params_hbm, out_ref, params_ref,
    pred_ref, mv_ref, var_ref, jit_ref, obs_ref, x_ref, idx_ref, full_ref, sems,
):
    members = pred_ref.shape[0]
    tile_x = lax.axis_index("gx")
    tile_y = lax.axis_index("gy")
    square = (OBS_TILE, OBS_TILE)
    pairs = [
        (pred_hbm.at[0, 0], pred_ref),
        (obs_hbm.at[tile_x], obs_ref),
        (var_hbm.at[0], var_ref),
        (mv_hbm.at[0], mv_ref),
        (jit_hbm.at[0, 0], jit_ref),
        (params_hbm, params_ref),
    ]
    copies = fetch(pairs, sems)
    for copy in copies[:3]:
        copy.wait()
    pred = pred_ref[...]
    var = var_ref[...]
    mean = jnp.sum(pred, axis=0, keepdims=True) / members
    deviation = (pred - mean).astype(BF16)
    out_ref[0] = deviation
    obs = obs_ref[pl.ds(tile_y, 1), :]
    groups = (iota((BLOCKS, OBS_TILE), 0) == obs).astype(BF16)
    same = dot(groups, groups, ((0,), (0,)))
    gram = dot(deviation, deviation, ((0,), (0,))) / (members - 1)
    row, col = iota(square, 0), iota(square, 1)
    system = jnp.where(same > 0.5, gram, 0.0) + jnp.where(row == col, var, 0.0)
    size = jnp.sum(same, axis=0, keepdims=True)
    count = jnp.max(size).astype(jnp.int32)
    size = size.astype(jnp.int32)
    rank = jnp.sum(jnp.where(row < col, same, 0.0), axis=0, keepdims=True).astype(jnp.int32)
    place = row == rank
    hot = place.astype(BF16)
    high, mid, low = split3(system)
    x_ref[...] = (
        dot(hot, low, ((1,), (0,))) + dot(hot, mid, ((1,), (0,))) + dot(hot, high, ((1,), (0,)))
    )
    numbered = jnp.where(place, col, 0).astype(F32).astype(BF16)
    idx_ref[...] = dot(numbered, same.astype(BF16), ((1,), (0,))).astype(jnp.int32)

    def solve(rows):
        sweep(rows, count, x_ref, idx_ref, rank, size)
        high, mid, low = split3(x_ref[0:rows, :])
        taken = hot[0:rows]
        full = dot(taken, low, ((0,), (0,))) + dot(taken, mid, ((0,), (0,))) + dot(taken, high, ((0,), (0,)))
        full_ref[...] = jnp.where(same > 0.5, -full, 0.0)

    @pl.when(count <= SMALL)
    def _():
        solve(SMALL)

    @pl.when(count > SMALL)
    def _():
        solve(OBS_TILE)

    for copy in copies[3:]:
        copy.wait()
    innovation = mv_ref[...] + jnp.sqrt(var) * jit_ref[...] - pred
    weighted = dot(innovation, full_ref[...], ((1,), (0,)), lax.Precision.HIGHEST)
    out_ref[1] = weighted.astype(BF16)


def weigh(predicted, measured_value, measurement_variance, observation_jitter, obs_block, params):
    members = predicted.shape[2]
    return pl.pallas_call(
        weigh_kernel,
        out_shape=(jax.ShapeDtypeStruct((2, members, OBS_TILE), BF16), jax.ShapeDtypeStruct(params.shape, BF16)),
        in_specs=[pl.BlockSpec(memory_space=pltpu.HBM)] * 6,
        out_specs=(pl.BlockSpec(memory_space=pltpu.VMEM), pl.BlockSpec(memory_space=pltpu.VMEM)),
        scratch_shapes=[
            pltpu.VMEM((members, OBS_TILE), F32),
            pltpu.VMEM((1, OBS_TILE), F32),
            pltpu.VMEM((1, OBS_TILE), F32),
            pltpu.VMEM((members, OBS_TILE), F32),
            pltpu.VMEM((obs_block.shape[1], OBS_TILE), jnp.int32),
            pltpu.VMEM((OBS_TILE, OBS_TILE), F32),
            pltpu.VMEM((OBS_TILE, OBS_TILE), jnp.int32),
            pltpu.VMEM((OBS_TILE, OBS_TILE), F32),
            pltpu.SemaphoreType.DMA((6,)),
        ],
        compiler_params=pltpu.CompilerParams(vmem_limit_bytes=16 * 2**20),
        name="weigh",
    )(*in_hbm(predicted, measured_value, measurement_variance, observation_jitter, obs_block, params))


def offset(which, place):
    even = 1 - 2 * (place & 1)
    return (0, even, -even)[which]


def prepare_kernel(
    params_ref, radius_hbm, pattern_hbm, obs_hbm, turned_ref, taper_ref, radius_ref, pattern_ref, obs_ref, sems
):
    members = params_ref.shape[1]
    tile_x = lax.axis_index("gx")
    tile_y = lax.axis_index("gy")
    count_x, count_y = obs_ref.shape[0], obs_ref.shape[1]
    copies = fetch([(radius_hbm, radius_ref), (pattern_hbm, pattern_ref), (obs_hbm, obs_ref)], sems)

    for b in range(BLOCKS):
        block = params_ref[b].astype(F32)
        mean = jnp.sum(block, axis=0, keepdims=True) / members
        turned_ref[b] = (block - mean).T.astype(BF16)
    for copy in copies:
        copy.wait()
    shape = (BLOCKS, OBS_TILE)
    block = iota(shape, 0)
    radius = jnp.zeros(shape, jnp.int32)
    for b in range(BLOCKS):
        radius = jnp.where(block == b, radius_ref[b // BLK_Y, b % BLK_Y], radius)
    reach = (radius + 1).astype(F32)
    reach = reach * reach
    pattern = jnp.concatenate([pattern_ref[i] for i in range(BLK_X)], axis=0).astype(F32)
    slots = [jnp.broadcast_to(pattern[:, p : p + 1], shape) for p in range(PATTERN)]

    for t in range(9):
        iy, ix = t // 3, t % 3
        dx, dy = offset(ix, tile_x), offset(iy, tile_y)
        at_x, at_y = tile_x + dx, tile_y + dy
        valid = (at_x >= 0) & (at_x < count_x) & (at_y >= 0) & (at_y < count_y)
        at_x = jnp.clip(at_x, 0, count_x - 1)
        at_y = jnp.clip(at_y, 0, count_y - 1)
        obs = obs_ref[at_x, pl.ds(at_y, 1), :]
        step_x = dx * BLK_X + (obs >> 2) - (block >> 2)
        step_y = dy * BLK_Y + (obs & 3) - (block & 3)
        inside = (jnp.abs(step_x) <= 2) & (jnp.abs(step_y) <= 2) & valid
        slot = (step_x + 2) * 5 + (step_y + 2)
        picked = jnp.zeros(shape, F32)
        for p in range(PATTERN):
            picked = jnp.where(slot == p, slots[p], picked)
        spread = (step_x * step_x + step_y * step_y).astype(F32)
        shaped = jnp.maximum(1.0 - spread / reach, 0.0)
        taper_ref[iy, ix] = jnp.where(inside, picked, 0.0) * shaped / (members - 1)


def prepare(by_block, taper_radius, taper_pattern, obs_block):
    members = by_block.shape[1]
    return pl.pallas_call(
        prepare_kernel,
        out_shape=(
            jax.ShapeDtypeStruct((BLOCKS, CELLS, members), BF16),
            jax.ShapeDtypeStruct((3, 3, BLOCKS, OBS_TILE), F32),
        ),
        in_specs=[pl.BlockSpec(memory_space=pltpu.VMEM)] + [pl.BlockSpec(memory_space=pltpu.HBM)] * 3,
        out_specs=(pl.BlockSpec(memory_space=pltpu.VMEM), pl.BlockSpec(memory_space=pltpu.VMEM)),
        scratch_shapes=[
            pltpu.SMEM(taper_radius.shape, jnp.int32),
            pltpu.VMEM(taper_pattern.shape, jnp.int32),
            pltpu.VMEM(obs_block.shape, jnp.int32),
            pltpu.SemaphoreType.DMA((3,)),
        ],
        compiler_params=pltpu.CompilerParams(vmem_limit_bytes=16 * 2**20),
        cost_estimate=pl.CostEstimate(flops=4_000_000, bytes_accessed=1_000_000, transcendentals=0),
        name="prepare",
    )(by_block, *in_hbm(taper_radius, taper_pattern, obs_block))


def moved(b, which, turned_ref, taper_ref, tiles_ref):
    cross = dot(turned_ref[b], tiles_ref[0], ((1,), (0,)))
    count = tiles_ref.shape[2] // OBS_TILE
    taper = jnp.concatenate([taper_ref[which, k, pl.ds(b, 1), :] for k in range(count)], axis=1)
    gain = (cross * taper).astype(BF16)
    return dot(tiles_ref[1], gain, ((1,), (1,)))


def first_of(side, tile_y):
    return 2 * ((tile_y & 1) ^ 1 ^ side)


def block_of(k, side, tile_y):
    return (k >> 1) * BLK_Y + first_of(side, tile_y) + (k & 1)


def target(chip, r, chips):
    return chip ^ r if chips & (chips - 1) == 0 else (chip + r) % chips


def source(chip, r, chips):
    return chip ^ r if chips & (chips - 1) == 0 else (chip + chips - r) % chips


def put(piece_refs, rows_ref, k, updated):
    chips, share = len(piece_refs), piece_refs[0].shape[2]
    mine = lax.axis_index("gy")
    rows_ref[k] = updated
    for r, ref in enumerate(piece_refs):
        for flip in (0, 1):
            owner = 2 * target(mine >> 1, r, chips) + ((mine & 1) ^ flip)
            ref[flip, k] = rows_ref[k, pl.ds(pl.multiple_of(owner * share, share), share), :]


def near_kernel(params_ref, turned_ref, taper_ref, own_ref, even_ref, part_ref, *refs):
    piece_refs, rows_ref = refs[:-1], refs[-1]
    tile_y = lax.axis_index("gy")
    for k in range(SIDE):
        b = block_of(k, 0, tile_y)
        delta = moved(b, 0, turned_ref, taper_ref, own_ref) + moved(b, 1, turned_ref, taper_ref, even_ref)
        put(piece_refs, rows_ref, k, (params_ref[b].astype(F32) + delta).astype(BF16))
    for k in range(SIDE):
        b = block_of(k, 1, tile_y)
        part_ref[k] = params_ref[b].astype(F32) + moved(b, 0, turned_ref, taper_ref, own_ref)


def far_kernel(turned_ref, taper_ref, odd_ref, part_ref, near_ref, *refs):
    both_ref, rows_ref = refs[-2], refs[-1]
    piece_refs = (*refs[:-2], both_ref.at[1])
    both_ref[0] = near_ref[...]
    tile_y = lax.axis_index("gy")
    for k in range(SIDE):
        b = block_of(k, 1, tile_y)
        put(piece_refs, rows_ref, k, (part_ref[k] + moved(b, 2, turned_ref, taper_ref, odd_ref)).astype(BF16))


def pack_kernel(*refs):
    at = 0
    for ref in refs[:-1]:
        for piece in halves(ref):
            refs[-1][at] = piece[1]
            at += 1


def halves(ref):
    return [ref] if len(ref.shape) == 4 else [ref.at[side] for side in range(ref.shape[0])]


def settle(chips, sides, refs, rows_ref):
    even_ref, pieces = refs[0], [piece for ref in refs[1:] for piece in halves(ref)]
    share = even_ref.shape[2]
    mine = lax.axis_index("gy")
    chip, core = mine >> 1, mine & 1
    line = 2 * chips * BLK_Y
    for at, ((side, r), own) in enumerate(zip(sides, pieces)):
        for flip in (0, 1):
            other = core ^ flip
            tile = 2 * source(chip, r, chips) + other
            for k in range(SIDE):
                piece = even_ref[at, k] if flip else own[0, k]
                start = (k >> 1) * line + tile * BLK_Y + first_of(side, other) + (k & 1)
                rows_ref[pl.ds(start, share, stride=BLK_X * line), :] = piece.astype(F32)


def early_kernel(chips, *refs):
    settle(chips, [(0, 0), (1, 0)] + [(0, r) for r in range(1, chips - 1)], refs[:-1], refs[-1])


def late_kernel(chips, *refs):
    late_refs, out_hbm, rows_ref, out_ref, sems = refs[1:-4], *refs[-4:]
    last = chips - 1
    settle(chips, [(0, last), (1, last)] + [(1, r) for r in range(1, last)], late_refs, rows_ref)
    pieces = sems.shape[0]
    step = rows_ref.shape[0] // pieces
    copies = []
    for p in range(pieces):
        place = slice(p * step, (p + 1) * step)
        out_ref[place] = rows_ref[place].astype(BF16)
        copies.append(pltpu.make_async_copy(out_ref.at[pl.ds(p * step, step)], out_hbm.at[pl.ds(p * step, step)], sems.at[p]))
        copies[-1].start()
    for copy in copies:
        copy.wait()


VMEM = pl.BlockSpec(memory_space=pltpu.VMEM)
LONG = pl.CostEstimate(flops=4_000_000_000, bytes_accessed=10_000_000, transcendentals=0)
LIMIT = pltpu.CompilerParams(vmem_limit_bytes=24 * 2**20)


def update_near(by_block, turned, taper, own, even, parts):
    members = by_block.shape[1]
    pieces = [jax.ShapeDtypeStruct((2, SIDE, members // parts, CELLS), BF16)] * (parts // 2)
    return pl.pallas_call(
        near_kernel,
        out_shape=(jax.ShapeDtypeStruct((SIDE, members, CELLS), F32), *pieces),
        in_specs=[VMEM] * 5,
        out_specs=(VMEM,) * (1 + len(pieces)),
        scratch_shapes=[pltpu.VMEM((SIDE, members, CELLS), BF16)],
        compiler_params=LIMIT,
        cost_estimate=LONG,
        name="near",
    )(by_block, turned, taper, own, even)


def update_far(turned, taper, odd, part, near):
    members = part.shape[1]
    parts = members // near[0].shape[2]
    piece = jax.ShapeDtypeStruct(near[0].shape, BF16)
    shapes = (piece,) * (parts // 2 - 1) + (jax.ShapeDtypeStruct((2, *piece.shape), BF16),)
    return pl.pallas_call(
        far_kernel,
        out_shape=shapes,
        in_specs=[VMEM] * 5,
        out_specs=(VMEM,) * len(shapes),
        scratch_shapes=[pltpu.VMEM((SIDE, members, CELLS), BF16)],
        compiler_params=LIMIT,
        cost_estimate=LONG,
        name="far",
    )(turned, taper, odd, part, near[-1])


def pack(pieces):
    count = sum(1 if piece.ndim == 4 else piece.shape[0] for piece in pieces)
    return pl.pallas_call(
        pack_kernel,
        out_shape=jax.ShapeDtypeStruct((count, *pieces[-1].shape[-3:]), BF16),
        in_specs=[VMEM] * len(pieces),
        out_specs=VMEM,
        compiler_params=LIMIT,
        name="pack",
    )(*pieces)


def gather(chips, early_even, early, late_even, late):
    share = early[0].shape[2]
    rows = share * BLOCKS * 2 * chips
    placed = pl.pallas_call(
        functools.partial(early_kernel, chips),
        out_shape=jax.ShapeDtypeStruct((rows, CELLS), F32),
        in_specs=[VMEM] * (1 + len(early)),
        out_specs=VMEM,
        compiler_params=LIMIT,
        name="early",
    )(early_even, *early)
    out, _ = pl.pallas_call(
        functools.partial(late_kernel, chips),
        out_shape=(jax.ShapeDtypeStruct((rows, CELLS), BF16), jax.ShapeDtypeStruct((rows, CELLS), F32)),
        in_specs=[VMEM] * (2 + len(late)),
        out_specs=(pl.BlockSpec(memory_space=pl.ANY), VMEM),
        scratch_shapes=[
            pltpu.VMEM((rows, CELLS), BF16),
            pltpu.SemaphoreType.DMA((4,)),
        ],
        input_output_aliases={0: 1},
        compiler_params=LIMIT,
        name="late",
    )(placed, late_even, *late)
    return out.reshape(share, BLK_X, 2 * chips * BLK_Y, CELLS)


def swap(block, axis, first, close=False):
    count = lax.axis_size(axis)
    pairs = [(i, i + 1) for i in range(first, count - 1, 2)]
    if close:
        pairs.append((count - 1, 0))
    return lax.ppermute(block, axis, pairs + [(b, a) for a, b in pairs])


def hop(piece, r):
    count = lax.axis_size("gy")
    pairs = [(i, 2 * target(i // 2, r, count // 2) + i % 2) for i in range(count)]
    return lax.ppermute(piece, "gy", pairs)


def per_device(
    params,
    predicted,
    measured_value,
    measurement_variance,
    observation_jitter,
    obs_block,
    taper_radius,
    taper_pattern,
):
    members = params.shape[0]
    parts = lax.axis_size("gy")
    own, params = weigh(
        predicted, measured_value, measurement_variance, observation_jitter, obs_block, params
    )
    by_block = params.reshape(members, BLOCKS, CELLS).transpose(1, 0, 2)
    even = swap(own, "gx", 0)
    odd = swap(own, "gx", 1, close=True)
    turned, taper = prepare(by_block, taper_radius, taper_pattern, obs_block)
    column = jnp.concatenate([own, even, odd], axis=2)
    column, turned, taper = lax.optimization_barrier((column, turned, taper))
    even = swap(column, "gy", 0)
    odd = swap(column, "gy", 1)
    part, *near = update_near(by_block, turned, taper, column, even, parts)
    last = parts // 2 - 1
    near_hops = {r: hop(near[r], r) for r in range(1, last)}
    *far, both = update_far(turned, taper, odd, part, near)
    for r in range(1, last):
        far[r], near_hops[r] = lax.optimization_barrier((far[r], near_hops[r]))
    far_hops = {r: hop(far[r], r) for r in range(1, last)}
    early = [near[0], far[0], *(near_hops[r] for r in range(1, last))]
    late = [hop(both, last), *(far_hops[r] for r in range(1, last))]
    late_even = swap(pack(late), "gy", 0)
    early_even = swap(pack(early), "gy", 0)
    return gather(parts // 2, early_even, early, late_even, late)


def solution(mesh):
    placed = (
        P(None, "gx", "gy", None),
        P("gx", "gy", None, None),
        P("gx", "gy", None),
        P("gx", "gy", None),
        P("gx", "gy", None, None),
        P(),
        P("gx", "gy"),
        P("gx", "gy", None),
    )
    return jax.shard_map(
        per_device, mesh=mesh, in_specs=placed, out_specs=P("gy", "gx", None, None), check_vma=False
    )
```

```python
import functools

import jax
import jax.numpy as jnp
from jax import lax
from jax.experimental import pallas as pl
from jax.experimental.pallas import tpu as pltpu
from jax.sharding import PartitionSpec as P

CELLS = 128
BLK_X = 2
BLK_Y = 4
BLOCKS = BLK_X * BLK_Y
SIDE = BLOCKS // 2
OBS_TILE = 128
PATTERN = 25
SMALL = 32

F32 = jnp.float32
BF16 = jnp.bfloat16


def iota(shape, dim):
    return lax.broadcasted_iota(jnp.int32, shape, dim)


def split3(x):
    high = x.astype(BF16)
    rest = x - high.astype(F32)
    mid = rest.astype(BF16)
    low = (rest - mid.astype(F32)).astype(BF16)
    return high, mid, low


def dot(a, b, dims, precision=None):
    return lax.dot_general(a, b, ((dims[0], dims[1]), ((), ())), precision=precision, preferred_element_type=F32)


def sweep(rows, count, x_ref, idx_ref, rank, size):
    row = iota((rows, OBS_TILE), 0)
    exists = row < size

    def taken(spread, indices):
        return jnp.take_along_axis(spread, indices, axis=1, mode="promise_in_bounds")

    def step(k, carry):
        t = 2 * k
        u = t + 1
        row_t, row_u = x_ref[pl.ds(t, 1), :], x_ref[pl.ds(u, 1), :]
        spread_t = jnp.broadcast_to(row_t, (rows, OBS_TILE))
        spread_u = jnp.broadcast_to(row_u, (rows, OBS_TILE))
        at_t = jnp.broadcast_to(idx_ref[pl.ds(t, 1), :], (8, OBS_TILE))
        at_u = jnp.broadcast_to(idx_ref[pl.ds(u, 1), :], (8, OBS_TILE))
        has_t, has_u = t < size, u < size
        a = jnp.where(has_t, taken(spread_t[0:8], at_t)[0:1], 1.0)
        b = jnp.where(has_u, taken(spread_t[0:8], at_u)[0:1], 0.0)
        d = jnp.where(has_u, taken(spread_u[0:8], at_u)[0:1], 1.0)
        own_t, own_u = rank == t, rank == u
        own = own_t | own_u
        head_t = jnp.where(own, jnp.where(own_t, -1.0, 0.0), row_t)
        head_u = jnp.where(own, jnp.where(own_u, -1.0, 0.0), row_u)
        inverse = 1.0 / a
        factor = b * inverse
        scaled_u = (head_u - factor * head_t) / (d - b * factor)
        scaled_t = head_t * inverse - factor * scaled_u
        column_t = jnp.where(exists, taken(spread_t, idx_ref[0:rows, :]), 0.0)
        column_u = jnp.where(exists, taken(spread_u, idx_ref[0:rows, :]), 0.0)
        on_t, on_u = row == t, row == u
        on = on_t | on_u
        column_t = jnp.where(on, jnp.where(on_t, -1.0, 0.0), column_t)
        column_u = jnp.where(on, jnp.where(on_u, -1.0, 0.0), column_u)
        x = jnp.where(on | own, 0.0, x_ref[0:rows, :])
        x_ref[0:rows, :] = x - column_t * scaled_t - column_u * scaled_u
        return carry

    lax.fori_loop(0, (count + 1) // 2, step, 0)


def in_hbm(*arrays):
    return [pltpu.with_memory_space_constraint(array, pltpu.HBM) for array in arrays]


def fetch(pairs, sems):
    copies = [pltpu.make_async_copy(src, dst, sems.at[k]) for k, (src, dst) in enumerate(pairs)]
    for copy in copies:
        copy.start()
    return copies


def weigh_kernel(
    pred_hbm, mv_hbm, var_hbm, jit_hbm, obs_hbm, params_hbm, out_ref, params_ref,
    pred_ref, mv_ref, var_ref, jit_ref, obs_ref, x_ref, idx_ref, full_ref, sems,
):
    members = pred_ref.shape[0]
    tile_x = lax.axis_index("gx")
    tile_y = lax.axis_index("gy")
    square = (OBS_TILE, OBS_TILE)
    pairs = [
        (pred_hbm.at[0, 0], pred_ref),
        (obs_hbm.at[tile_x], obs_ref),
        (var_hbm.at[0], var_ref),
        (mv_hbm.at[0], mv_ref),
        (jit_hbm.at[0, 0], jit_ref),
        (params_hbm, params_ref),
    ]
    copies = fetch(pairs, sems)
    for copy in copies[:3]:
        copy.wait()
    pred = pred_ref[...]
    var = var_ref[...]
    mean = jnp.sum(pred, axis=0, keepdims=True) / members
    deviation = (pred - mean).astype(BF16)
    out_ref[0] = deviation
    obs = obs_ref[pl.ds(tile_y, 1), :]
    groups = (iota((BLOCKS, OBS_TILE), 0) == obs).astype(BF16)
    same = dot(groups, groups, ((0,), (0,)))
    gram = dot(deviation, deviation, ((0,), (0,))) / (members - 1)
    row, col = iota(square, 0), iota(square, 1)
    system = jnp.where(same > 0.5, gram, 0.0) + jnp.where(row == col, var, 0.0)
    size = jnp.sum(same, axis=0, keepdims=True)
    count = jnp.max(size).astype(jnp.int32)
    size = size.astype(jnp.int32)
    rank = jnp.sum(jnp.where(row < col, same, 0.0), axis=0, keepdims=True).astype(jnp.int32)
    place = row == rank
    hot = place.astype(BF16)
    high, mid, low = split3(system)
    x_ref[...] = (
        dot(hot, low, ((1,), (0,))) + dot(hot, mid, ((1,), (0,))) + dot(hot, high, ((1,), (0,)))
    )
    numbered = jnp.where(place, col, 0).astype(F32).astype(BF16)
    idx_ref[...] = dot(numbered, same.astype(BF16), ((1,), (0,))).astype(jnp.int32)

    def solve(rows):
        sweep(rows, count, x_ref, idx_ref, rank, size)
        high, mid, low = split3(x_ref[0:rows, :])
        taken = hot[0:rows]
        full = dot(taken, low, ((0,), (0,))) + dot(taken, mid, ((0,), (0,))) + dot(taken, high, ((0,), (0,)))
        full_ref[...] = jnp.where(same > 0.5, -full, 0.0)

    @pl.when(count <= SMALL)
    def _():
        solve(SMALL)

    @pl.when(count > SMALL)
    def _():
        solve(OBS_TILE)

    for copy in copies[3:]:
        copy.wait()
    innovation = mv_ref[...] + jnp.sqrt(var) * jit_ref[...] - pred
    weighted = dot(innovation, full_ref[...], ((1,), (0,)), lax.Precision.HIGHEST)
    out_ref[1] = weighted.astype(BF16)


def weigh(predicted, measured_value, measurement_variance, observation_jitter, obs_block, params):
    members = predicted.shape[2]
    return pl.pallas_call(
        weigh_kernel,
        out_shape=(jax.ShapeDtypeStruct((2, members, OBS_TILE), BF16), jax.ShapeDtypeStruct(params.shape, BF16)),
        in_specs=[pl.BlockSpec(memory_space=pltpu.HBM)] * 6,
        out_specs=(pl.BlockSpec(memory_space=pltpu.VMEM), pl.BlockSpec(memory_space=pltpu.VMEM)),
        scratch_shapes=[
            pltpu.VMEM((members, OBS_TILE), F32),
            pltpu.VMEM((1, OBS_TILE), F32),
            pltpu.VMEM((1, OBS_TILE), F32),
            pltpu.VMEM((members, OBS_TILE), F32),
            pltpu.VMEM((obs_block.shape[1], OBS_TILE), jnp.int32),
            pltpu.VMEM((OBS_TILE, OBS_TILE), F32),
            pltpu.VMEM((OBS_TILE, OBS_TILE), jnp.int32),
            pltpu.VMEM((OBS_TILE, OBS_TILE), F32),
            pltpu.SemaphoreType.DMA((6,)),
        ],
        compiler_params=pltpu.CompilerParams(vmem_limit_bytes=16 * 2**20),
        name="weigh",
    )(*in_hbm(predicted, measured_value, measurement_variance, observation_jitter, obs_block, params))


def offset(which, place):
    even = 1 - 2 * (place & 1)
    return (0, even, -even)[which]


def prepare_kernel(
    params_ref, radius_hbm, pattern_hbm, obs_hbm, turned_ref, taper_ref, radius_ref, pattern_ref, obs_ref, sems
):
    members = params_ref.shape[1]
    tile_x = lax.axis_index("gx")
    tile_y = lax.axis_index("gy")
    count_x, count_y = obs_ref.shape[0], obs_ref.shape[1]
    copies = fetch([(radius_hbm, radius_ref), (pattern_hbm, pattern_ref), (obs_hbm, obs_ref)], sems)

    for b in range(BLOCKS):
        block = params_ref[b].astype(F32)
        mean = jnp.sum(block, axis=0, keepdims=True) / members
        turned_ref[b] = (block - mean).T.astype(BF16)
    for copy in copies:
        copy.wait()
    shape = (BLOCKS, OBS_TILE)
    block = iota(shape, 0)
    radius = jnp.zeros(shape, jnp.int32)
    for b in range(BLOCKS):
        radius = jnp.where(block == b, radius_ref[b // BLK_Y, b % BLK_Y], radius)
    reach = (radius + 1).astype(F32)
    reach = reach * reach
    pattern = jnp.concatenate([pattern_ref[i] for i in range(BLK_X)], axis=0).astype(F32)
    slots = [jnp.broadcast_to(pattern[:, p : p + 1], shape) for p in range(PATTERN)]

    for t in range(9):
        iy, ix = t // 3, t % 3
        dx, dy = offset(ix, tile_x), offset(iy, tile_y)
        at_x, at_y = tile_x + dx, tile_y + dy
        valid = (at_x >= 0) & (at_x < count_x) & (at_y >= 0) & (at_y < count_y)
        at_x = jnp.clip(at_x, 0, count_x - 1)
        at_y = jnp.clip(at_y, 0, count_y - 1)
        obs = obs_ref[at_x, pl.ds(at_y, 1), :]
        step_x = dx * BLK_X + (obs >> 2) - (block >> 2)
        step_y = dy * BLK_Y + (obs & 3) - (block & 3)
        inside = (jnp.abs(step_x) <= 2) & (jnp.abs(step_y) <= 2) & valid
        slot = (step_x + 2) * 5 + (step_y + 2)
        picked = jnp.zeros(shape, F32)
        for p in range(PATTERN):
            picked = jnp.where(slot == p, slots[p], picked)
        spread = (step_x * step_x + step_y * step_y).astype(F32)
        shaped = jnp.maximum(1.0 - spread / reach, 0.0)
        taper_ref[iy, ix] = jnp.where(inside, picked, 0.0) * shaped / (members - 1)


def prepare(by_block, taper_radius, taper_pattern, obs_block):
    members = by_block.shape[1]
    return pl.pallas_call(
        prepare_kernel,
        out_shape=(
            jax.ShapeDtypeStruct((BLOCKS, CELLS, members), BF16),
            jax.ShapeDtypeStruct((3, 3, BLOCKS, OBS_TILE), F32),
        ),
        in_specs=[pl.BlockSpec(memory_space=pltpu.VMEM)] + [pl.BlockSpec(memory_space=pltpu.HBM)] * 3,
        out_specs=(pl.BlockSpec(memory_space=pltpu.VMEM), pl.BlockSpec(memory_space=pltpu.VMEM)),
        scratch_shapes=[
            pltpu.SMEM(taper_radius.shape, jnp.int32),
            pltpu.VMEM(taper_pattern.shape, jnp.int32),
            pltpu.VMEM(obs_block.shape, jnp.int32),
            pltpu.SemaphoreType.DMA((3,)),
        ],
        compiler_params=pltpu.CompilerParams(vmem_limit_bytes=16 * 2**20),
        cost_estimate=pl.CostEstimate(flops=4_000_000, bytes_accessed=1_000_000, transcendentals=0),
        name="prepare",
    )(by_block, *in_hbm(taper_radius, taper_pattern, obs_block))


def moved(b, which, turned_ref, taper_ref, tiles_ref):
    cross = dot(turned_ref[b], tiles_ref[0], ((1,), (0,)))
    count = tiles_ref.shape[2] // OBS_TILE
    taper = jnp.concatenate([taper_ref[which, k, pl.ds(b, 1), :] for k in range(count)], axis=1)
    gain = (cross * taper).astype(BF16)
    return dot(tiles_ref[1], gain, ((1,), (1,)))


def first_of(side, tile_y):
    return 2 * ((tile_y & 1) ^ 1 ^ side)


def block_of(k, side, tile_y):
    return (k >> 1) * BLK_Y + first_of(side, tile_y) + (k & 1)


def target(chip, r, chips):
    return chip ^ r if chips & (chips - 1) == 0 else (chip + r) % chips


def source(chip, r, chips):
    return chip ^ r if chips & (chips - 1) == 0 else (chip + chips - r) % chips


def put(piece_refs, rows_ref, k, updated):
    chips, share = len(piece_refs), piece_refs[0].shape[2]
    mine = lax.axis_index("gy")
    rows_ref[k] = updated
    for r, ref in enumerate(piece_refs):
        for flip in (0, 1):
            owner = 2 * target(mine >> 1, r, chips) + ((mine & 1) ^ flip)
            ref[flip, k] = rows_ref[k, pl.ds(pl.multiple_of(owner * share, share), share), :]


def begin_kernel(params_ref, turned_ref, taper_ref, own_ref, part_ref):
    tile_y = lax.axis_index("gy")
    for k in range(SIDE):
        b = block_of(k, 1, tile_y)
        part_ref[k] = params_ref[b].astype(F32) + moved(b, 0, turned_ref, taper_ref, own_ref)


def near_kernel(params_ref, turned_ref, taper_ref, own_ref, even_ref, *refs):
    piece_refs, rows_ref = refs[:-1], refs[-1]
    tile_y = lax.axis_index("gy")
    for k in range(SIDE):
        b = block_of(k, 0, tile_y)
        delta = moved(b, 0, turned_ref, taper_ref, own_ref) + moved(b, 1, turned_ref, taper_ref, even_ref)
        put(piece_refs, rows_ref, k, (params_ref[b].astype(F32) + delta).astype(BF16))


def far_kernel(turned_ref, taper_ref, odd_ref, part_ref, near_ref, *refs):
    both_ref, rows_ref = refs[-2], refs[-1]
    piece_refs = (*refs[:-2], both_ref.at[1])
    both_ref[0] = near_ref[...]
    tile_y = lax.axis_index("gy")
    for k in range(SIDE):
        b = block_of(k, 1, tile_y)
        put(piece_refs, rows_ref, k, (part_ref[k] + moved(b, 2, turned_ref, taper_ref, odd_ref)).astype(BF16))


def pack_kernel(*refs):
    at = 0
    for ref in refs[:-1]:
        for piece in halves(ref):
            refs[-1][at] = piece[1]
            at += 1


def halves(ref):
    return [ref] if len(ref.shape) == 4 else [ref.at[side] for side in range(ref.shape[0])]


def settle(chips, sides, refs, rows_ref):
    even_ref, pieces = refs[0], [piece for ref in refs[1:] for piece in halves(ref)]
    share = even_ref.shape[2]
    mine = lax.axis_index("gy")
    chip, core = mine >> 1, mine & 1
    line = 2 * chips * BLK_Y
    for at, ((side, r), own) in enumerate(zip(sides, pieces)):
        for flip in (0, 1):
            other = core ^ flip
            tile = 2 * source(chip, r, chips) + other
            for k in range(SIDE):
                piece = even_ref[at, k] if flip else own[0, k]
                start = (k >> 1) * line + tile * BLK_Y + first_of(side, other) + (k & 1)
                rows_ref[pl.ds(start, share, stride=BLK_X * line), :] = piece.astype(F32)


def early_kernel(chips, *refs):
    settle(chips, [(0, 0), (1, 0)] + [(0, r) for r in range(1, chips - 1)], refs[:-1], refs[-1])


def late_kernel(chips, *refs):
    late_refs, out_hbm, rows_ref, out_ref, sems = refs[1:-4], *refs[-4:]
    last = chips - 1
    settle(chips, [(0, last), (1, last)] + [(1, r) for r in range(1, last)], late_refs, rows_ref)
    pieces = sems.shape[0]
    step = rows_ref.shape[0] // pieces
    copies = []
    for p in range(pieces):
        place = slice(p * step, (p + 1) * step)
        out_ref[place] = rows_ref[place].astype(BF16)
        copies.append(pltpu.make_async_copy(out_ref.at[pl.ds(p * step, step)], out_hbm.at[pl.ds(p * step, step)], sems.at[p]))
        copies[-1].start()
    for copy in copies:
        copy.wait()


VMEM = pl.BlockSpec(memory_space=pltpu.VMEM)
LONG = pl.CostEstimate(flops=4_000_000_000, bytes_accessed=10_000_000, transcendentals=0)
LIMIT = pltpu.CompilerParams(vmem_limit_bytes=24 * 2**20)


def update_begin(by_block, turned, taper, own):
    return pl.pallas_call(
        begin_kernel,
        out_shape=jax.ShapeDtypeStruct((SIDE, by_block.shape[1], CELLS), F32),
        in_specs=[VMEM] * 4,
        out_specs=VMEM,
        compiler_params=LIMIT,
        cost_estimate=LONG,
        name="begin",
    )(by_block, turned, taper, own)


def update_near(by_block, turned, taper, own, even, parts):
    members = by_block.shape[1]
    pieces = [jax.ShapeDtypeStruct((2, SIDE, members // parts, CELLS), BF16)] * (parts // 2)
    return pl.pallas_call(
        near_kernel,
        out_shape=tuple(pieces),
        in_specs=[VMEM] * 5,
        out_specs=(VMEM,) * len(pieces),
        scratch_shapes=[pltpu.VMEM((SIDE, members, CELLS), BF16)],
        compiler_params=LIMIT,
        cost_estimate=LONG,
        name="near",
    )(by_block, turned, taper, own, even)


def update_far(turned, taper, odd, part, near):
    members = part.shape[1]
    parts = members // near[0].shape[2]
    piece = jax.ShapeDtypeStruct(near[0].shape, BF16)
    shapes = (piece,) * (parts // 2 - 1) + (jax.ShapeDtypeStruct((2, *piece.shape), BF16),)
    return pl.pallas_call(
        far_kernel,
        out_shape=shapes,
        in_specs=[VMEM] * 5,
        out_specs=(VMEM,) * len(shapes),
        scratch_shapes=[pltpu.VMEM((SIDE, members, CELLS), BF16)],
        compiler_params=LIMIT,
        cost_estimate=LONG,
        name="far",
    )(turned, taper, odd, part, near[-1])


def pack(pieces):
    count = sum(1 if piece.ndim == 4 else piece.shape[0] for piece in pieces)
    return pl.pallas_call(
        pack_kernel,
        out_shape=jax.ShapeDtypeStruct((count, *pieces[-1].shape[-3:]), BF16),
        in_specs=[VMEM] * len(pieces),
        out_specs=VMEM,
        compiler_params=LIMIT,
        name="pack",
    )(*pieces)


def gather(chips, early_even, early, late_even, late):
    share = early[0].shape[2]
    rows = share * BLOCKS * 2 * chips
    placed = pl.pallas_call(
        functools.partial(early_kernel, chips),
        out_shape=jax.ShapeDtypeStruct((rows, CELLS), F32),
        in_specs=[VMEM] * (1 + len(early)),
        out_specs=VMEM,
        compiler_params=LIMIT,
        name="early",
    )(early_even, *early)
    out, _ = pl.pallas_call(
        functools.partial(late_kernel, chips),
        out_shape=(jax.ShapeDtypeStruct((rows, CELLS), BF16), jax.ShapeDtypeStruct((rows, CELLS), F32)),
        in_specs=[VMEM] * (2 + len(late)),
        out_specs=(pl.BlockSpec(memory_space=pl.ANY), VMEM),
        scratch_shapes=[
            pltpu.VMEM((rows, CELLS), BF16),
            pltpu.SemaphoreType.DMA((4,)),
        ],
        input_output_aliases={0: 1},
        compiler_params=LIMIT,
        name="late",
    )(placed, late_even, *late)
    return out.reshape(share, BLK_X, 2 * chips * BLK_Y, CELLS)


def swap(block, axis, first, close=False):
    count = lax.axis_size(axis)
    pairs = [(i, i + 1) for i in range(first, count - 1, 2)]
    if close:
        pairs.append((count - 1, 0))
    return lax.ppermute(block, axis, pairs + [(b, a) for a, b in pairs])


def hop(piece, r):
    count = lax.axis_size("gy")
    pairs = [(i, 2 * target(i // 2, r, count // 2) + i % 2) for i in range(count)]
    return lax.ppermute(piece, "gy", pairs)


def per_device(
    params,
    predicted,
    measured_value,
    measurement_variance,
    observation_jitter,
    obs_block,
    taper_radius,
    taper_pattern,
):
    members = params.shape[0]
    parts = lax.axis_size("gy")
    own, params = weigh(
        predicted, measured_value, measurement_variance, observation_jitter, obs_block, params
    )
    by_block = params.reshape(members, BLOCKS, CELLS).transpose(1, 0, 2)
    even = swap(own, "gx", 0)
    odd = swap(own, "gx", 1, close=True)
    turned, taper = prepare(by_block, taper_radius, taper_pattern, obs_block)
    column = jnp.concatenate([own, even, odd], axis=2)
    column, turned, taper = lax.optimization_barrier((column, turned, taper))
    odd = swap(column, "gy", 1)
    even = swap(column, "gy", 0)
    part = update_begin(by_block, turned, taper, column)
    near = update_near(by_block, turned, taper, column, even, parts)
    last = parts // 2 - 1
    near_hops = {r: hop(near[r], r) for r in range(1, last)}
    *far, both = update_far(turned, taper, odd, part, near)
    for r in range(1, last):
        far[r], near_hops[r] = lax.optimization_barrier((far[r], near_hops[r]))
    far_hops = {r: hop(far[r], r) for r in range(1, last)}
    early = [near[0], far[0], *(near_hops[r] for r in range(1, last))]
    late = [hop(both, last), *(far_hops[r] for r in range(1, last))]
    late_even = swap(pack(late), "gy", 0)
    early_even = swap(pack(early), "gy", 0)
    return gather(parts // 2, early_even, early, late_even, late)


def solution(mesh):
    placed = (
        P(None, "gx", "gy", None),
        P("gx", "gy", None, None),
        P("gx", "gy", None),
        P("gx", "gy", None),
        P("gx", "gy", None, None),
        P(),
        P("gx", "gy"),
        P("gx", "gy", None),
    )
    return jax.shard_map(
        per_device, mesh=mesh, in_specs=placed, out_specs=P("gy", "gx", None, None), check_vma=False
    )
```

```python
import functools

import jax
import jax.numpy as jnp
from jax import lax
from jax.experimental import pallas as pl
from jax.experimental.pallas import tpu as pltpu
from jax.sharding import PartitionSpec as P

CELLS = 128
BLK_X = 2
BLK_Y = 4
BLOCKS = BLK_X * BLK_Y
SIDE = BLOCKS // 2
OBS_TILE = 128
PATTERN = 25
SMALL = 32

F32 = jnp.float32
BF16 = jnp.bfloat16


def iota(shape, dim):
    return lax.broadcasted_iota(jnp.int32, shape, dim)


def split3(x):
    high = x.astype(BF16)
    rest = x - high.astype(F32)
    mid = rest.astype(BF16)
    low = (rest - mid.astype(F32)).astype(BF16)
    return high, mid, low


def dot(a, b, dims, precision=None):
    return lax.dot_general(a, b, ((dims[0], dims[1]), ((), ())), precision=precision, preferred_element_type=F32)


def sweep(rows, count, x_ref, idx_ref, rank, size):
    row = iota((rows, OBS_TILE), 0)
    exists = row < size

    def taken(spread, indices):
        return jnp.take_along_axis(spread, indices, axis=1, mode="promise_in_bounds")

    def step(k, carry):
        t = 2 * k
        u = t + 1
        row_t, row_u = x_ref[pl.ds(t, 1), :], x_ref[pl.ds(u, 1), :]
        spread_t = jnp.broadcast_to(row_t, (rows, OBS_TILE))
        spread_u = jnp.broadcast_to(row_u, (rows, OBS_TILE))
        at_t = jnp.broadcast_to(idx_ref[pl.ds(t, 1), :], (8, OBS_TILE))
        at_u = jnp.broadcast_to(idx_ref[pl.ds(u, 1), :], (8, OBS_TILE))
        has_t, has_u = t < size, u < size
        a = jnp.where(has_t, taken(spread_t[0:8], at_t)[0:1], 1.0)
        b = jnp.where(has_u, taken(spread_t[0:8], at_u)[0:1], 0.0)
        d = jnp.where(has_u, taken(spread_u[0:8], at_u)[0:1], 1.0)
        own_t, own_u = rank == t, rank == u
        own = own_t | own_u
        head_t = jnp.where(own, jnp.where(own_t, -1.0, 0.0), row_t)
        head_u = jnp.where(own, jnp.where(own_u, -1.0, 0.0), row_u)
        inverse = 1.0 / a
        factor = b * inverse
        scaled_u = (head_u - factor * head_t) / (d - b * factor)
        scaled_t = head_t * inverse - factor * scaled_u
        column_t = jnp.where(exists, taken(spread_t, idx_ref[0:rows, :]), 0.0)
        column_u = jnp.where(exists, taken(spread_u, idx_ref[0:rows, :]), 0.0)
        on_t, on_u = row == t, row == u
        on = on_t | on_u
        column_t = jnp.where(on, jnp.where(on_t, -1.0, 0.0), column_t)
        column_u = jnp.where(on, jnp.where(on_u, -1.0, 0.0), column_u)
        x = jnp.where(on | own, 0.0, x_ref[0:rows, :])
        x_ref[0:rows, :] = x - column_t * scaled_t - column_u * scaled_u
        return carry

    lax.fori_loop(0, (count + 1) // 2, step, 0)


def in_hbm(*arrays):
    return [pltpu.with_memory_space_constraint(array, pltpu.HBM) for array in arrays]


def fetch(pairs, sems):
    copies = [pltpu.make_async_copy(src, dst, sems.at[k]) for k, (src, dst) in enumerate(pairs)]
    for copy in copies:
        copy.start()
    return copies


def weigh_kernel(
    pred_hbm, mv_hbm, var_hbm, jit_hbm, obs_hbm, params_hbm, out_ref, params_ref,
    pred_ref, mv_ref, var_ref, jit_ref, obs_ref, x_ref, idx_ref, full_ref, sems,
):
    members = pred_ref.shape[0]
    tile_x = lax.axis_index("gx")
    tile_y = lax.axis_index("gy")
    square = (OBS_TILE, OBS_TILE)
    pairs = [
        (pred_hbm.at[0, 0], pred_ref),
        (obs_hbm.at[tile_x], obs_ref),
        (var_hbm.at[0], var_ref),
        (mv_hbm.at[0], mv_ref),
        (jit_hbm.at[0, 0], jit_ref),
        (params_hbm, params_ref),
    ]
    copies = fetch(pairs, sems)
    for copy in copies[:3]:
        copy.wait()
    pred = pred_ref[...]
    var = var_ref[...]
    mean = jnp.sum(pred, axis=0, keepdims=True) / members
    deviation = (pred - mean).astype(BF16)
    out_ref[0] = deviation
    obs = obs_ref[pl.ds(tile_y, 1), :]
    groups = (iota((BLOCKS, OBS_TILE), 0) == obs).astype(BF16)
    same = dot(groups, groups, ((0,), (0,)))
    gram = dot(deviation, deviation, ((0,), (0,))) / (members - 1)
    row, col = iota(square, 0), iota(square, 1)
    system = jnp.where(same > 0.5, gram, 0.0) + jnp.where(row == col, var, 0.0)
    size = jnp.sum(same, axis=0, keepdims=True)
    count = jnp.max(size).astype(jnp.int32)
    size = size.astype(jnp.int32)
    rank = jnp.sum(jnp.where(row < col, same, 0.0), axis=0, keepdims=True).astype(jnp.int32)
    place = row == rank
    hot = place.astype(BF16)
    high, mid, low = split3(system)
    x_ref[...] = (
        dot(hot, low, ((1,), (0,))) + dot(hot, mid, ((1,), (0,))) + dot(hot, high, ((1,), (0,)))
    )
    numbered = jnp.where(place, col, 0).astype(F32).astype(BF16)
    idx_ref[...] = dot(numbered, same.astype(BF16), ((1,), (0,))).astype(jnp.int32)

    def solve(rows):
        sweep(rows, count, x_ref, idx_ref, rank, size)
        high, mid, low = split3(x_ref[0:rows, :])
        taken = hot[0:rows]
        full = dot(taken, low, ((0,), (0,))) + dot(taken, mid, ((0,), (0,))) + dot(taken, high, ((0,), (0,)))
        full_ref[...] = jnp.where(same > 0.5, -full, 0.0)

    @pl.when(count <= SMALL)
    def _():
        solve(SMALL)

    @pl.when(count > SMALL)
    def _():
        solve(OBS_TILE)

    for copy in copies[3:]:
        copy.wait()
    innovation = mv_ref[...] + jnp.sqrt(var) * jit_ref[...] - pred
    weighted = dot(innovation, full_ref[...], ((1,), (0,)), lax.Precision.HIGHEST)
    out_ref[1] = weighted.astype(BF16)


def weigh(predicted, measured_value, measurement_variance, observation_jitter, obs_block, params):
    members = predicted.shape[2]
    return pl.pallas_call(
        weigh_kernel,
        out_shape=(jax.ShapeDtypeStruct((2, members, OBS_TILE), BF16), jax.ShapeDtypeStruct(params.shape, BF16)),
        in_specs=[pl.BlockSpec(memory_space=pltpu.HBM)] * 6,
        out_specs=(pl.BlockSpec(memory_space=pltpu.VMEM), pl.BlockSpec(memory_space=pltpu.VMEM)),
        scratch_shapes=[
            pltpu.VMEM((members, OBS_TILE), F32),
            pltpu.VMEM((1, OBS_TILE), F32),
            pltpu.VMEM((1, OBS_TILE), F32),
            pltpu.VMEM((members, OBS_TILE), F32),
            pltpu.VMEM((obs_block.shape[1], OBS_TILE), jnp.int32),
            pltpu.VMEM((OBS_TILE, OBS_TILE), F32),
            pltpu.VMEM((OBS_TILE, OBS_TILE), jnp.int32),
            pltpu.VMEM((OBS_TILE, OBS_TILE), F32),
            pltpu.SemaphoreType.DMA((6,)),
        ],
        compiler_params=pltpu.CompilerParams(vmem_limit_bytes=16 * 2**20),
        name="weigh",
    )(*in_hbm(predicted, measured_value, measurement_variance, observation_jitter, obs_block, params))


def offset(which, place):
    even = 1 - 2 * (place & 1)
    return (0, even, -even)[which]


def prepare_kernel(
    params_ref, radius_hbm, pattern_hbm, obs_hbm, turned_ref, taper_ref, radius_ref, pattern_ref, obs_ref, sems
):
    members = params_ref.shape[1]
    tile_x = lax.axis_index("gx")
    tile_y = lax.axis_index("gy")
    count_x, count_y = obs_ref.shape[0], obs_ref.shape[1]
    copies = fetch([(radius_hbm, radius_ref), (pattern_hbm, pattern_ref), (obs_hbm, obs_ref)], sems)

    for b in range(BLOCKS):
        block = params_ref[b].astype(F32)
        mean = jnp.sum(block, axis=0, keepdims=True) / members
        turned_ref[b] = (block - mean).T.astype(BF16)
    for copy in copies:
        copy.wait()
    shape = (BLOCKS, OBS_TILE)
    block = iota(shape, 0)
    radius = jnp.zeros(shape, jnp.int32)
    for b in range(BLOCKS):
        radius = jnp.where(block == b, radius_ref[b // BLK_Y, b % BLK_Y], radius)
    reach = (radius + 1).astype(F32)
    reach = reach * reach
    pattern = jnp.concatenate([pattern_ref[i] for i in range(BLK_X)], axis=0).astype(F32)
    slots = [jnp.broadcast_to(pattern[:, p : p + 1], shape) for p in range(PATTERN)]

    for t in range(9):
        iy, ix = t // 3, t % 3
        dx, dy = offset(ix, tile_x), offset(iy, tile_y)
        at_x, at_y = tile_x + dx, tile_y + dy
        valid = (at_x >= 0) & (at_x < count_x) & (at_y >= 0) & (at_y < count_y)
        at_x = jnp.clip(at_x, 0, count_x - 1)
        at_y = jnp.clip(at_y, 0, count_y - 1)
        obs = obs_ref[at_x, pl.ds(at_y, 1), :]
        step_x = dx * BLK_X + (obs >> 2) - (block >> 2)
        step_y = dy * BLK_Y + (obs & 3) - (block & 3)
        inside = (jnp.abs(step_x) <= 2) & (jnp.abs(step_y) <= 2) & valid
        slot = (step_x + 2) * 5 + (step_y + 2)
        picked = jnp.zeros(shape, F32)
        for p in range(PATTERN):
            picked = jnp.where(slot == p, slots[p], picked)
        spread = (step_x * step_x + step_y * step_y).astype(F32)
        shaped = jnp.maximum(1.0 - spread / reach, 0.0)
        taper_ref[iy, ix] = jnp.where(inside, picked, 0.0) * shaped / (members - 1)


def prepare(by_block, taper_radius, taper_pattern, obs_block):
    members = by_block.shape[1]
    return pl.pallas_call(
        prepare_kernel,
        out_shape=(
            jax.ShapeDtypeStruct((BLOCKS, CELLS, members), BF16),
            jax.ShapeDtypeStruct((3, 3, BLOCKS, OBS_TILE), F32),
        ),
        in_specs=[pl.BlockSpec(memory_space=pltpu.VMEM)] + [pl.BlockSpec(memory_space=pltpu.HBM)] * 3,
        out_specs=(pl.BlockSpec(memory_space=pltpu.VMEM), pl.BlockSpec(memory_space=pltpu.VMEM)),
        scratch_shapes=[
            pltpu.SMEM(taper_radius.shape, jnp.int32),
            pltpu.VMEM(taper_pattern.shape, jnp.int32),
            pltpu.VMEM(obs_block.shape, jnp.int32),
            pltpu.SemaphoreType.DMA((3,)),
        ],
        compiler_params=pltpu.CompilerParams(vmem_limit_bytes=16 * 2**20),
        cost_estimate=pl.CostEstimate(flops=4_000_000, bytes_accessed=1_000_000, transcendentals=0),
        name="prepare",
    )(by_block, *in_hbm(taper_radius, taper_pattern, obs_block))


def moved(b, which, turned_ref, taper_ref, column_ref):
    members = turned_ref.shape[2]
    turned = turned_ref[pl.ds(b, 2)].reshape(2 * CELLS, members)
    cross = dot(turned, column_ref[0], ((1,), (0,)))
    gains = []
    for k in range(2):
        taper = jnp.concatenate([taper_ref[which, ix, pl.ds(b + k, 1), :] for ix in range(3)], axis=1)
        gains.append((cross[k * CELLS : (k + 1) * CELLS] * taper).astype(BF16))
    return dot(column_ref[1], jnp.concatenate(gains, axis=0), ((1,), (1,)))


def first_of(side, tile_y):
    return 2 * ((tile_y & 1) ^ 1 ^ side)


def block_of(k, side, tile_y):
    return (k >> 1) * BLK_Y + first_of(side, tile_y) + (k & 1)


def target(chip, r, chips):
    return chip ^ r if chips & (chips - 1) == 0 else (chip + r) % chips


def source(chip, r, chips):
    return chip ^ r if chips & (chips - 1) == 0 else (chip + chips - r) % chips


def put(piece_refs, rows_ref, k, updated):
    chips, share = len(piece_refs), piece_refs[0].shape[2]
    mine = lax.axis_index("gy")
    rows_ref[k] = updated
    for r, ref in enumerate(piece_refs):
        for flip in (0, 1):
            owner = 2 * target(mine >> 1, r, chips) + ((mine & 1) ^ flip)
            ref[flip, k] = rows_ref[k, pl.ds(pl.multiple_of(owner * share, share), share), :]


def near_kernel(params_ref, turned_ref, taper_ref, own_ref, even_ref, part_ref, *refs):
    piece_refs, rows_ref = refs[:-1], refs[-1]
    tile_y = lax.axis_index("gy")
    for k in range(0, SIDE, 2):
        b = block_of(k, 0, tile_y)
        delta = moved(b, 0, turned_ref, taper_ref, own_ref) + moved(b, 1, turned_ref, taper_ref, even_ref)
        for j in range(2):
            half = delta[:, j * CELLS : (j + 1) * CELLS]
            put(piece_refs, rows_ref, k + j, (params_ref[b + j].astype(F32) + half).astype(BF16))
    for k in range(0, SIDE, 2):
        b = block_of(k, 1, tile_y)
        delta = moved(b, 0, turned_ref, taper_ref, own_ref)
        for j in range(2):
            part_ref[k + j] = params_ref[b + j].astype(F32) + delta[:, j * CELLS : (j + 1) * CELLS]


def far_kernel(turned_ref, taper_ref, odd_ref, part_ref, near_ref, *refs):
    both_ref, rows_ref = refs[-2], refs[-1]
    piece_refs = (*refs[:-2], both_ref.at[1])
    both_ref[0] = near_ref[...]
    tile_y = lax.axis_index("gy")
    for k in range(0, SIDE, 2):
        delta = moved(block_of(k, 1, tile_y), 2, turned_ref, taper_ref, odd_ref)
        for j in range(2):
            half = delta[:, j * CELLS : (j + 1) * CELLS]
            put(piece_refs, rows_ref, k + j, (part_ref[k + j] + half).astype(BF16))


def pack_kernel(*refs):
    at = 0
    for ref in refs[:-1]:
        for piece in halves(ref):
            refs[-1][at] = piece[1]
            at += 1


def halves(ref):
    return [ref] if len(ref.shape) == 4 else [ref.at[side] for side in range(ref.shape[0])]


def settle(chips, sides, refs, rows_ref):
    even_ref, pieces = refs[0], [piece for ref in refs[1:] for piece in halves(ref)]
    share = even_ref.shape[2]
    mine = lax.axis_index("gy")
    chip, core = mine >> 1, mine & 1
    line = 2 * chips * BLK_Y
    for at, ((side, r), own) in enumerate(zip(sides, pieces)):
        for flip in (0, 1):
            other = core ^ flip
            tile = 2 * source(chip, r, chips) + other
            for k in range(SIDE):
                piece = even_ref[at, k] if flip else own[0, k]
                start = (k >> 1) * line + tile * BLK_Y + first_of(side, other) + (k & 1)
                rows_ref[pl.ds(start, share, stride=BLK_X * line), :] = piece.astype(F32)


def early_kernel(chips, *refs):
    settle(chips, [(0, 0), (1, 0)] + [(0, r) for r in range(1, chips - 1)], refs[:-1], refs[-1])


def late_kernel(chips, *refs):
    late_refs, out_hbm, rows_ref, out_ref, sems = refs[1:-4], *refs[-4:]
    last = chips - 1
    settle(chips, [(0, last), (1, last)] + [(1, r) for r in range(1, last)], late_refs, rows_ref)
    pieces = sems.shape[0]
    step = rows_ref.shape[0] // pieces
    copies = []
    for p in range(pieces):
        place = slice(p * step, (p + 1) * step)
        out_ref[place] = rows_ref[place].astype(BF16)
        copies.append(pltpu.make_async_copy(out_ref.at[pl.ds(p * step, step)], out_hbm.at[pl.ds(p * step, step)], sems.at[p]))
        copies[-1].start()
    for copy in copies:
        copy.wait()


VMEM = pl.BlockSpec(memory_space=pltpu.VMEM)
LONG = pl.CostEstimate(flops=4_000_000_000, bytes_accessed=10_000_000, transcendentals=0)
LIMIT = pltpu.CompilerParams(vmem_limit_bytes=24 * 2**20)


def update_near(by_block, turned, taper, own, even, parts):
    members = by_block.shape[1]
    pieces = [jax.ShapeDtypeStruct((2, SIDE, members // parts, CELLS), BF16)] * (parts // 2)
    return pl.pallas_call(
        near_kernel,
        out_shape=(jax.ShapeDtypeStruct((SIDE, members, CELLS), F32), *pieces),
        in_specs=[VMEM] * 5,
        out_specs=(VMEM,) * (1 + len(pieces)),
        scratch_shapes=[pltpu.VMEM((SIDE, members, CELLS), BF16)],
        compiler_params=LIMIT,
        cost_estimate=LONG,
        name="near",
    )(by_block, turned, taper, own, even)


def update_far(turned, taper, odd, part, near):
    members = part.shape[1]
    parts = members // near[0].shape[2]
    piece = jax.ShapeDtypeStruct(near[0].shape, BF16)
    shapes = (piece,) * (parts // 2 - 1) + (jax.ShapeDtypeStruct((2, *piece.shape), BF16),)
    return pl.pallas_call(
        far_kernel,
        out_shape=shapes,
        in_specs=[VMEM] * 5,
        out_specs=(VMEM,) * len(shapes),
        scratch_shapes=[pltpu.VMEM((SIDE, members, CELLS), BF16)],
        compiler_params=LIMIT,
        cost_estimate=LONG,
        name="far",
    )(turned, taper, odd, part, near[-1])


def pack(pieces):
    count = sum(1 if piece.ndim == 4 else piece.shape[0] for piece in pieces)
    return pl.pallas_call(
        pack_kernel,
        out_shape=jax.ShapeDtypeStruct((count, *pieces[-1].shape[-3:]), BF16),
        in_specs=[VMEM] * len(pieces),
        out_specs=VMEM,
        compiler_params=LIMIT,
        name="pack",
    )(*pieces)


def gather(chips, early_even, early, late_even, late):
    share = early[0].shape[2]
    rows = share * BLOCKS * 2 * chips
    placed = pl.pallas_call(
        functools.partial(early_kernel, chips),
        out_shape=jax.ShapeDtypeStruct((rows, CELLS), F32),
        in_specs=[VMEM] * (1 + len(early)),
        out_specs=VMEM,
        compiler_params=LIMIT,
        name="early",
    )(early_even, *early)
    out, _ = pl.pallas_call(
        functools.partial(late_kernel, chips),
        out_shape=(jax.ShapeDtypeStruct((rows, CELLS), BF16), jax.ShapeDtypeStruct((rows, CELLS), F32)),
        in_specs=[VMEM] * (2 + len(late)),
        out_specs=(pl.BlockSpec(memory_space=pl.ANY), VMEM),
        scratch_shapes=[
            pltpu.VMEM((rows, CELLS), BF16),
            pltpu.SemaphoreType.DMA((4,)),
        ],
        input_output_aliases={0: 1},
        compiler_params=LIMIT,
        name="late",
    )(placed, late_even, *late)
    return out.reshape(share, BLK_X, 2 * chips * BLK_Y, CELLS)


def swap(block, axis, first, close=False):
    count = lax.axis_size(axis)
    pairs = [(i, i + 1) for i in range(first, count - 1, 2)]
    if close:
        pairs.append((count - 1, 0))
    return lax.ppermute(block, axis, pairs + [(b, a) for a, b in pairs])


def hop(piece, r):
    count = lax.axis_size("gy")
    pairs = [(i, 2 * target(i // 2, r, count // 2) + i % 2) for i in range(count)]
    return lax.ppermute(piece, "gy", pairs)


def per_device(
    params,
    predicted,
    measured_value,
    measurement_variance,
    observation_jitter,
    obs_block,
    taper_radius,
    taper_pattern,
):
    members = params.shape[0]
    parts = lax.axis_size("gy")
    own, params = weigh(
        predicted, measured_value, measurement_variance, observation_jitter, obs_block, params
    )
    by_block = params.reshape(members, BLOCKS, CELLS).transpose(1, 0, 2)
    even = swap(own, "gx", 0)
    odd = swap(own, "gx", 1, close=True)
    turned, taper = prepare(by_block, taper_radius, taper_pattern, obs_block)
    column = jnp.concatenate([own, even, odd], axis=2)
    column, turned, taper = lax.optimization_barrier((column, turned, taper))
    even = swap(column, "gy", 0)
    odd = swap(column, "gy", 1)
    part, *near = update_near(by_block, turned, taper, column, even, parts)
    last = parts // 2 - 1
    near_hops = {r: hop(near[r], r) for r in range(1, last)}
    *far, both = update_far(turned, taper, odd, part, near)
    if last > 1:
        far[1], near_hops = lax.optimization_barrier((far[1], near_hops))
    far_hops = {r: hop(far[r], r) for r in range(1, last)}
    early = [near[0], far[0], *(near_hops[r] for r in range(1, last))]
    late = [hop(both, last), *(far_hops[r] for r in range(1, last))]
    late_even = swap(pack(late), "gy", 0)
    early_even = swap(pack(early), "gy", 0)
    return gather(parts // 2, early_even, early, late_even, late)


def solution(mesh):
    placed = (
        P(None, "gx", "gy", None),
        P("gx", "gy", None, None),
        P("gx", "gy", None),
        P("gx", "gy", None),
        P("gx", "gy", None, None),
        P(),
        P("gx", "gy"),
        P("gx", "gy", None),
    )
    return jax.shard_map(
        per_device, mesh=mesh, in_specs=placed, out_specs=P("gy", "gx", None, None), check_vma=False
    )
```

```python
import functools

import jax
import jax.numpy as jnp
from jax import lax
from jax.experimental import pallas as pl
from jax.experimental.pallas import tpu as pltpu
from jax.sharding import PartitionSpec as P

CELLS = 128
BLK_X = 2
BLK_Y = 4
BLOCKS = BLK_X * BLK_Y
SIDE = BLOCKS // 2
OBS_TILE = 128
PATTERN = 25
SMALL = 32

F32 = jnp.float32
BF16 = jnp.bfloat16


def iota(shape, dim):
    return lax.broadcasted_iota(jnp.int32, shape, dim)


def split3(x):
    high = x.astype(BF16)
    rest = x - high.astype(F32)
    mid = rest.astype(BF16)
    low = (rest - mid.astype(F32)).astype(BF16)
    return high, mid, low


def dot(a, b, dims):
    return lax.dot_general(a, b, (dims, ((), ())), preferred_element_type=F32)


def sweep(rows, count, x_ref, idx_ref, rank, size):
    row = iota((rows, OBS_TILE), 0)
    exists = row < size

    def taken(spread, indices):
        return jnp.take_along_axis(spread, indices, axis=1, mode="promise_in_bounds")

    def step(k, carry):
        t = 2 * k
        u = t + 1
        row_t, row_u = x_ref[pl.ds(t, 1), :], x_ref[pl.ds(u, 1), :]
        spread_t = jnp.broadcast_to(row_t, (rows, OBS_TILE))
        spread_u = jnp.broadcast_to(row_u, (rows, OBS_TILE))
        at_t = jnp.broadcast_to(idx_ref[pl.ds(t, 1), :], (8, OBS_TILE))
        at_u = jnp.broadcast_to(idx_ref[pl.ds(u, 1), :], (8, OBS_TILE))
        has_t, has_u = t < size, u < size
        a = jnp.where(has_t, taken(spread_t[0:8], at_t)[0:1], 1.0)
        b = jnp.where(has_u, taken(spread_t[0:8], at_u)[0:1], 0.0)
        d = jnp.where(has_u, taken(spread_u[0:8], at_u)[0:1], 1.0)
        own_t, own_u = rank == t, rank == u
        own = own_t | own_u
        head_t = jnp.where(own, jnp.where(own_t, -1.0, 0.0), row_t)
        head_u = jnp.where(own, jnp.where(own_u, -1.0, 0.0), row_u)
        inverse = 1.0 / a
        factor = b * inverse
        scaled_u = (head_u - factor * head_t) / (d - b * factor)
        scaled_t = head_t * inverse - factor * scaled_u
        column_t = jnp.where(exists, taken(spread_t, idx_ref[0:rows, :]), 0.0)
        column_u = jnp.where(exists, taken(spread_u, idx_ref[0:rows, :]), 0.0)
        on_t, on_u = row == t, row == u
        on = on_t | on_u
        column_t = jnp.where(on, jnp.where(on_t, -1.0, 0.0), column_t)
        column_u = jnp.where(on, jnp.where(on_u, -1.0, 0.0), column_u)
        x = jnp.where(on | own, 0.0, x_ref[0:rows, :])
        x_ref[0:rows, :] = x - column_t * scaled_t - column_u * scaled_u
        return carry

    lax.fori_loop(0, (count + 1) // 2, step, 0)


def in_hbm(*arrays):
    return [pltpu.with_memory_space_constraint(array, pltpu.HBM) for array in arrays]


def fetch(pairs, sems):
    copies = [pltpu.make_async_copy(src, dst, sems.at[k]) for k, (src, dst) in enumerate(pairs)]
    for copy in copies:
        copy.start()
    return copies


def weigh_kernel(
    pred_hbm, mv_hbm, var_hbm, jit_hbm, obs_hbm, params_hbm, out_ref, params_ref,
    pred_ref, mv_ref, var_ref, jit_ref, obs_ref, x_ref, idx_ref, full_ref, sems,
):
    members = pred_ref.shape[0]
    tile_x = lax.axis_index("gx")
    tile_y = lax.axis_index("gy")
    square = (OBS_TILE, OBS_TILE)
    pairs = [
        (pred_hbm.at[0, 0], pred_ref),
        (obs_hbm.at[tile_x], obs_ref),
        (var_hbm.at[0], var_ref),
        (mv_hbm.at[0], mv_ref),
        (jit_hbm.at[0, 0], jit_ref),
        (params_hbm, params_ref),
    ]
    copies = fetch(pairs, sems)
    for copy in copies[:3]:
        copy.wait()
    pred = pred_ref[...]
    var = var_ref[...]
    mean = jnp.sum(pred, axis=0, keepdims=True) / members
    deviation = (pred - mean).astype(BF16)
    out_ref[0] = deviation
    obs = obs_ref[pl.ds(tile_y, 1), :]
    groups = (iota((BLOCKS, OBS_TILE), 0) == obs).astype(BF16)
    same = dot(groups, groups, ((0,), (0,)))
    gram = dot(deviation, deviation, ((0,), (0,))) / (members - 1)
    row, col = iota(square, 0), iota(square, 1)
    system = jnp.where(same > 0.5, gram, 0.0) + jnp.where(row == col, var, 0.0)
    size = jnp.sum(same, axis=0, keepdims=True)
    count = jnp.max(size).astype(jnp.int32)
    size = size.astype(jnp.int32)
    rank = jnp.sum(jnp.where(row < col, same, 0.0), axis=0, keepdims=True).astype(jnp.int32)
    place = row == rank
    hot = place.astype(BF16)
    x_ref[...] = dot(jnp.concatenate([hot] * 3, axis=1), jnp.concatenate(split3(system), axis=0), ((1,), (0,)))
    numbered = jnp.where(place, col, 0).astype(F32).astype(BF16)
    idx_ref[...] = dot(numbered, same.astype(BF16), ((1,), (0,))).astype(jnp.int32)

    def solve(rows):
        sweep(rows, count, x_ref, idx_ref, rank, size)
        taken = jnp.concatenate([hot[0:rows]] * 3, axis=0)
        full = dot(taken, jnp.concatenate(split3(x_ref[0:rows, :]), axis=0), ((0,), (0,)))
        full_ref[...] = jnp.where(same > 0.5, -full, 0.0)

    @pl.when(count <= SMALL)
    def _():
        solve(SMALL)

    @pl.when(count > SMALL)
    def _():
        solve(OBS_TILE)

    for copy in copies[3:]:
        copy.wait()
    innovation = mv_ref[...] + jnp.sqrt(var) * jit_ref[...] - pred
    high, mid, low = split3(innovation)
    full_high, full_mid, full_low = split3(full_ref[...])
    left = jnp.concatenate([low, mid, high, mid, high, high], axis=1)
    right = jnp.concatenate([full_high, full_mid, full_low, full_high, full_mid, full_high], axis=0)
    weighted = dot(left, right, ((1,), (0,)))
    out_ref[1] = weighted.astype(BF16)


def weigh(predicted, measured_value, measurement_variance, observation_jitter, obs_block, params):
    members = predicted.shape[2]
    return pl.pallas_call(
        weigh_kernel,
        out_shape=(jax.ShapeDtypeStruct((2, members, OBS_TILE), BF16), jax.ShapeDtypeStruct(params.shape, BF16)),
        in_specs=[pl.BlockSpec(memory_space=pltpu.HBM)] * 6,
        out_specs=(pl.BlockSpec(memory_space=pltpu.VMEM), pl.BlockSpec(memory_space=pltpu.VMEM)),
        scratch_shapes=[
            pltpu.VMEM((members, OBS_TILE), F32),
            pltpu.VMEM((1, OBS_TILE), F32),
            pltpu.VMEM((1, OBS_TILE), F32),
            pltpu.VMEM((members, OBS_TILE), F32),
            pltpu.VMEM((obs_block.shape[1], OBS_TILE), jnp.int32),
            pltpu.VMEM((OBS_TILE, OBS_TILE), F32),
            pltpu.VMEM((OBS_TILE, OBS_TILE), jnp.int32),
            pltpu.VMEM((OBS_TILE, OBS_TILE), F32),
            pltpu.SemaphoreType.DMA((6,)),
        ],
        compiler_params=pltpu.CompilerParams(vmem_limit_bytes=16 * 2**20),
        name="weigh",
    )(*in_hbm(predicted, measured_value, measurement_variance, observation_jitter, obs_block, params))


def offset(which, place):
    even = 1 - 2 * (place & 1)
    return (0, even, -even)[which]


def prepare_kernel(
    params_ref, radius_hbm, pattern_hbm, obs_hbm, turned_ref, taper_ref, radius_ref, pattern_ref, obs_ref, sems
):
    members = params_ref.shape[1]
    tile_x = lax.axis_index("gx")
    tile_y = lax.axis_index("gy")
    count_x, count_y = obs_ref.shape[0], obs_ref.shape[1]
    copies = fetch([(radius_hbm, radius_ref), (pattern_hbm, pattern_ref), (obs_hbm, obs_ref)], sems)

    for b in range(BLOCKS):
        block = params_ref[b].astype(F32)
        mean = jnp.sum(block, axis=0, keepdims=True) / members
        turned_ref[b] = (block - mean).T.astype(BF16)
    for copy in copies:
        copy.wait()
    shape = (BLOCKS, OBS_TILE)
    block = iota(shape, 0)
    radius = jnp.zeros(shape, jnp.int32)
    for b in range(BLOCKS):
        radius = jnp.where(block == b, radius_ref[b // BLK_Y, b % BLK_Y], radius)
    reach = (radius + 1).astype(F32)
    reach = reach * reach
    pattern = jnp.concatenate([pattern_ref[i] for i in range(BLK_X)], axis=0).astype(F32)
    slots = [jnp.broadcast_to(pattern[:, p : p + 1], shape) for p in range(PATTERN)]

    for t in range(9):
        iy, ix = t // 3, t % 3
        dx, dy = offset(ix, tile_x), offset(iy, tile_y)
        at_x, at_y = tile_x + dx, tile_y + dy
        valid = (at_x >= 0) & (at_x < count_x) & (at_y >= 0) & (at_y < count_y)
        at_x = jnp.clip(at_x, 0, count_x - 1)
        at_y = jnp.clip(at_y, 0, count_y - 1)
        obs = obs_ref[at_x, pl.ds(at_y, 1), :]
        step_x = dx * BLK_X + (obs >> 2) - (block >> 2)
        step_y = dy * BLK_Y + (obs & 3) - (block & 3)
        inside = (jnp.abs(step_x) <= 2) & (jnp.abs(step_y) <= 2) & valid
        slot = (step_x + 2) * 5 + (step_y + 2)
        picked = jnp.zeros(shape, F32)
        for p in range(PATTERN):
            picked = jnp.where(slot == p, slots[p], picked)
        spread = (step_x * step_x + step_y * step_y).astype(F32)
        shaped = jnp.maximum(1.0 - spread / reach, 0.0)
        taper_ref[iy, ix] = jnp.where(inside, picked, 0.0) * shaped / (members - 1)


def prepare(by_block, taper_radius, taper_pattern, obs_block):
    members = by_block.shape[1]
    return pl.pallas_call(
        prepare_kernel,
        out_shape=(
            jax.ShapeDtypeStruct((BLOCKS, CELLS, members), BF16),
            jax.ShapeDtypeStruct((3, 3, BLOCKS, OBS_TILE), F32),
        ),
        in_specs=[pl.BlockSpec(memory_space=pltpu.VMEM)] + [pl.BlockSpec(memory_space=pltpu.HBM)] * 3,
        out_specs=(pl.BlockSpec(memory_space=pltpu.VMEM), pl.BlockSpec(memory_space=pltpu.VMEM)),
        scratch_shapes=[
            pltpu.SMEM(taper_radius.shape, jnp.int32),
            pltpu.VMEM(taper_pattern.shape, jnp.int32),
            pltpu.VMEM(obs_block.shape, jnp.int32),
            pltpu.SemaphoreType.DMA((3,)),
        ],
        compiler_params=pltpu.CompilerParams(vmem_limit_bytes=16 * 2**20),
        cost_estimate=pl.CostEstimate(flops=4_000_000, bytes_accessed=1_000_000, transcendentals=0),
        name="prepare",
    )(by_block, *in_hbm(taper_radius, taper_pattern, obs_block))


def moved(b, which, turned_ref, taper_ref, column_ref):
    members = turned_ref.shape[2]
    turned = turned_ref[pl.ds(b, 2)].reshape(2 * CELLS, members)
    cross = dot(turned, column_ref[0], ((1,), (0,)))
    gains = []
    for k in range(2):
        taper = jnp.concatenate([taper_ref[which, ix, pl.ds(b + k, 1), :] for ix in range(3)], axis=1)
        gains.append((cross[k * CELLS : (k + 1) * CELLS] * taper).astype(BF16))
    return dot(column_ref[1], jnp.concatenate(gains, axis=0), ((1,), (1,)))


def first_of(side, tile_y):
    return 2 * ((tile_y & 1) ^ 1 ^ side)


def block_of(k, side, tile_y):
    return (k >> 1) * BLK_Y + first_of(side, tile_y) + (k & 1)


def target(chip, r, chips):
    return chip ^ r if chips & (chips - 1) == 0 else (chip + r) % chips


def source(chip, r, chips):
    return chip ^ r if chips & (chips - 1) == 0 else (chip + chips - r) % chips


def put(piece_refs, rows_ref, k, updated):
    chips, share = len(piece_refs), piece_refs[0].shape[2]
    mine = lax.axis_index("gy")
    rows_ref[k] = updated
    for r, ref in enumerate(piece_refs):
        for flip in (0, 1):
            owner = 2 * target(mine >> 1, r, chips) + ((mine & 1) ^ flip)
            ref[flip, k] = rows_ref[k, pl.ds(pl.multiple_of(owner * share, share), share), :]


def near_kernel(params_ref, turned_ref, taper_ref, own_ref, even_ref, part_ref, *refs):
    piece_refs, rows_ref = refs[:-1], refs[-1]
    tile_y = lax.axis_index("gy")
    for k in range(0, SIDE, 2):
        b = block_of(k, 0, tile_y)
        delta = moved(b, 0, turned_ref, taper_ref, own_ref) + moved(b, 1, turned_ref, taper_ref, even_ref)
        for j in range(2):
            half = delta[:, j * CELLS : (j + 1) * CELLS]
            put(piece_refs, rows_ref, k + j, (params_ref[b + j].astype(F32) + half).astype(BF16))
    for k in range(0, SIDE, 2):
        b = block_of(k, 1, tile_y)
        delta = moved(b, 0, turned_ref, taper_ref, own_ref)
        for j in range(2):
            part_ref[k + j] = params_ref[b + j].astype(F32) + delta[:, j * CELLS : (j + 1) * CELLS]


def far_kernel(turned_ref, taper_ref, odd_ref, part_ref, near_ref, *refs):
    both_ref, rows_ref = refs[-2], refs[-1]
    piece_refs = (*refs[:-2], both_ref.at[1])
    both_ref[0] = near_ref[...]
    tile_y = lax.axis_index("gy")
    for k in range(0, SIDE, 2):
        delta = moved(block_of(k, 1, tile_y), 2, turned_ref, taper_ref, odd_ref)
        for j in range(2):
            half = delta[:, j * CELLS : (j + 1) * CELLS]
            put(piece_refs, rows_ref, k + j, (part_ref[k + j] + half).astype(BF16))


def pack_kernel(*refs):
    at = 0
    for ref in refs[:-1]:
        for piece in halves(ref):
            refs[-1][at] = piece[1]
            at += 1


def halves(ref):
    return [ref] if len(ref.shape) == 4 else [ref.at[side] for side in range(ref.shape[0])]


def settle(chips, sides, refs, rows_ref):
    even_ref, pieces = refs[0], [piece for ref in refs[1:] for piece in halves(ref)]
    share = even_ref.shape[2]
    mine = lax.axis_index("gy")
    chip, core = mine >> 1, mine & 1
    line = 2 * chips * BLK_Y
    for at, ((side, r), own) in enumerate(zip(sides, pieces)):
        for flip in (0, 1):
            other = core ^ flip
            tile = 2 * source(chip, r, chips) + other
            for k in range(SIDE):
                piece = even_ref[at, k] if flip else own[0, k]
                start = (k >> 1) * line + tile * BLK_Y + first_of(side, other) + (k & 1)
                rows_ref[pl.ds(start, share, stride=BLK_X * line), :] = piece.astype(F32)


def early_kernel(chips, *refs):
    settle(chips, [(0, 0), (1, 0)] + [(0, r) for r in range(1, chips - 1)], refs[:-1], refs[-1])


def late_kernel(chips, *refs):
    late_refs, out_hbm, rows_ref, out_ref, sems = refs[1:-4], *refs[-4:]
    last = chips - 1
    settle(chips, [(0, last), (1, last)] + [(1, r) for r in range(1, last)], late_refs, rows_ref)
    pieces = sems.shape[0]
    step = rows_ref.shape[0] // pieces
    copies = []
    for p in range(pieces):
        place = slice(p * step, (p + 1) * step)
        out_ref[place] = rows_ref[place].astype(BF16)
        copies.append(pltpu.make_async_copy(out_ref.at[pl.ds(p * step, step)], out_hbm.at[pl.ds(p * step, step)], sems.at[p]))
        copies[-1].start()
    for copy in copies:
        copy.wait()


VMEM = pl.BlockSpec(memory_space=pltpu.VMEM)
LONG = pl.CostEstimate(flops=4_000_000_000, bytes_accessed=10_000_000, transcendentals=0)
LIMIT = pltpu.CompilerParams(vmem_limit_bytes=24 * 2**20)


def update_near(by_block, turned, taper, own, even, parts):
    members = by_block.shape[1]
    pieces = [jax.ShapeDtypeStruct((2, SIDE, members // parts, CELLS), BF16)] * (parts // 2)
    return pl.pallas_call(
        near_kernel,
        out_shape=(jax.ShapeDtypeStruct((SIDE, members, CELLS), F32), *pieces),
        in_specs=[VMEM] * 5,
        out_specs=(VMEM,) * (1 + len(pieces)),
        scratch_shapes=[pltpu.VMEM((SIDE, members, CELLS), BF16)],
        compiler_params=LIMIT,
        cost_estimate=LONG,
        name="near",
    )(by_block, turned, taper, own, even)


def update_far(turned, taper, odd, part, near):
    members = part.shape[1]
    parts = members // near[0].shape[2]
    piece = jax.ShapeDtypeStruct(near[0].shape, BF16)
    shapes = (piece,) * (parts // 2 - 1) + (jax.ShapeDtypeStruct((2, *piece.shape), BF16),)
    return pl.pallas_call(
        far_kernel,
        out_shape=shapes,
        in_specs=[VMEM] * 5,
        out_specs=(VMEM,) * len(shapes),
        scratch_shapes=[pltpu.VMEM((SIDE, members, CELLS), BF16)],
        compiler_params=LIMIT,
        cost_estimate=LONG,
        name="far",
    )(turned, taper, odd, part, near[-1])


def pack(pieces):
    count = sum(1 if piece.ndim == 4 else piece.shape[0] for piece in pieces)
    return pl.pallas_call(
        pack_kernel,
        out_shape=jax.ShapeDtypeStruct((count, *pieces[-1].shape[-3:]), BF16),
        in_specs=[VMEM] * len(pieces),
        out_specs=VMEM,
        compiler_params=LIMIT,
        name="pack",
    )(*pieces)


def gather(chips, early_even, early, late_even, late):
    share = early[0].shape[2]
    rows = share * BLOCKS * 2 * chips
    placed = pl.pallas_call(
        functools.partial(early_kernel, chips),
        out_shape=jax.ShapeDtypeStruct((rows, CELLS), F32),
        in_specs=[VMEM] * (1 + len(early)),
        out_specs=VMEM,
        compiler_params=LIMIT,
        name="early",
    )(early_even, *early)
    out, _ = pl.pallas_call(
        functools.partial(late_kernel, chips),
        out_shape=(jax.ShapeDtypeStruct((rows, CELLS), BF16), jax.ShapeDtypeStruct((rows, CELLS), F32)),
        in_specs=[VMEM] * (2 + len(late)),
        out_specs=(pl.BlockSpec(memory_space=pl.ANY), VMEM),
        scratch_shapes=[
            pltpu.VMEM((rows, CELLS), BF16),
            pltpu.SemaphoreType.DMA((4,)),
        ],
        input_output_aliases={0: 1},
        compiler_params=LIMIT,
        name="late",
    )(placed, late_even, *late)
    return out.reshape(share, BLK_X, 2 * chips * BLK_Y, CELLS)


def swap(block, axis, first, close=False):
    count = lax.axis_size(axis)
    pairs = [(i, i + 1) for i in range(first, count - 1, 2)]
    if close:
        pairs.append((count - 1, 0))
    return lax.ppermute(block, axis, pairs + [(b, a) for a, b in pairs])


def hop(piece, r):
    count = lax.axis_size("gy")
    pairs = [(i, 2 * target(i // 2, r, count // 2) + i % 2) for i in range(count)]
    return lax.ppermute(piece, "gy", pairs)


def per_device(
    params,
    predicted,
    measured_value,
    measurement_variance,
    observation_jitter,
    obs_block,
    taper_radius,
    taper_pattern,
):
    members = params.shape[0]
    parts = lax.axis_size("gy")
    own, params = weigh(
        predicted, measured_value, measurement_variance, observation_jitter, obs_block, params
    )
    by_block = params.reshape(members, BLOCKS, CELLS).transpose(1, 0, 2)
    even = swap(own, "gx", 0)
    odd = swap(own, "gx", 1, close=True)
    turned, taper = prepare(by_block, taper_radius, taper_pattern, obs_block)
    column = jnp.concatenate([own, even, odd], axis=2)
    column, turned, taper = lax.optimization_barrier((column, turned, taper))
    even = swap(column, "gy", 0)
    odd = swap(column, "gy", 1)
    part, *near = update_near(by_block, turned, taper, column, even, parts)
    last = parts // 2 - 1
    near_hops = {r: hop(near[r], r) for r in range(1, last)}
    *far, both = update_far(turned, taper, odd, part, near)
    if last > 1:
        far[1], near_hops = lax.optimization_barrier((far[1], near_hops))
    far_hops = {r: hop(far[r], r) for r in range(1, last)}
    early = [near[0], far[0], *(near_hops[r] for r in range(1, last))]
    late = [hop(both, last), *(far_hops[r] for r in range(1, last))]
    late_even = swap(pack(late), "gy", 0)
    early_even = swap(pack(early), "gy", 0)
    return gather(parts // 2, early_even, early, late_even, late)


def solution(mesh):
    placed = (
        P(None, "gx", "gy", None),
        P("gx", "gy", None, None),
        P("gx", "gy", None),
        P("gx", "gy", None),
        P("gx", "gy", None, None),
        P(),
        P("gx", "gy"),
        P("gx", "gy", None),
    )
    return jax.shard_map(
        per_device, mesh=mesh, in_specs=placed, out_specs=P("gy", "gx", None, None), check_vma=False
    )
```

```python
import functools

import jax
import jax.numpy as jnp
from jax import lax
from jax.experimental import pallas as pl
from jax.experimental.pallas import tpu as pltpu
from jax.sharding import PartitionSpec as P

CELLS = 128
BLK_X = 2
BLK_Y = 4
BLOCKS = BLK_X * BLK_Y
SIDE = BLOCKS // 2
OBS_TILE = 128
PATTERN = 25
SMALL = 32

F32 = jnp.float32
BF16 = jnp.bfloat16


def iota(shape, dim):
    return lax.broadcasted_iota(jnp.int32, shape, dim)


def split3(x):
    high = x.astype(BF16)
    rest = x - high.astype(F32)
    mid = rest.astype(BF16)
    low = (rest - mid.astype(F32)).astype(BF16)
    return high, mid, low


def dot(a, b, dims):
    return lax.dot_general(a, b, (dims, ((), ())), preferred_element_type=F32)


def sweep(rows, count, x_ref, idx_ref, rank, size):
    row = iota((rows, OBS_TILE), 0)
    exists = row < size

    def taken(spread, indices):
        return jnp.take_along_axis(spread, indices, axis=1, mode="promise_in_bounds")

    def step(k, carry):
        t = 2 * k
        u = t + 1
        row_t, row_u = x_ref[pl.ds(t, 1), :], x_ref[pl.ds(u, 1), :]
        spread_t = jnp.broadcast_to(row_t, (rows, OBS_TILE))
        spread_u = jnp.broadcast_to(row_u, (rows, OBS_TILE))
        at_t = jnp.broadcast_to(idx_ref[pl.ds(t, 1), :], (8, OBS_TILE))
        at_u = jnp.broadcast_to(idx_ref[pl.ds(u, 1), :], (8, OBS_TILE))
        has_t, has_u = t < size, u < size
        a = jnp.where(has_t, taken(spread_t[0:8], at_t)[0:1], 1.0)
        b = jnp.where(has_u, taken(spread_t[0:8], at_u)[0:1], 0.0)
        d = jnp.where(has_u, taken(spread_u[0:8], at_u)[0:1], 1.0)
        own_t, own_u = rank == t, rank == u
        own = own_t | own_u
        head_t = jnp.where(own, jnp.where(own_t, -1.0, 0.0), row_t)
        head_u = jnp.where(own, jnp.where(own_u, -1.0, 0.0), row_u)
        inverse = 1.0 / a
        factor = b * inverse
        scaled_u = (head_u - factor * head_t) / (d - b * factor)
        scaled_t = head_t * inverse - factor * scaled_u
        column_t = jnp.where(exists, taken(spread_t, idx_ref[0:rows, :]), 0.0)
        column_u = jnp.where(exists, taken(spread_u, idx_ref[0:rows, :]), 0.0)
        on_t, on_u = row == t, row == u
        on = on_t | on_u
        column_t = jnp.where(on, jnp.where(on_t, -1.0, 0.0), column_t)
        column_u = jnp.where(on, jnp.where(on_u, -1.0, 0.0), column_u)
        x = jnp.where(on | own, 0.0, x_ref[0:rows, :])
        x_ref[0:rows, :] = x - column_t * scaled_t - column_u * scaled_u
        return carry

    lax.fori_loop(0, (count + 1) // 2, step, 0)


def in_hbm(*arrays):
    return [pltpu.with_memory_space_constraint(array, pltpu.HBM) for array in arrays]


def fetch(pairs, sems):
    copies = [pltpu.make_async_copy(src, dst, sems.at[k]) for k, (src, dst) in enumerate(pairs)]
    for copy in copies:
        copy.start()
    return copies


def weigh_kernel(
    pred_hbm, mv_hbm, var_hbm, jit_hbm, obs_hbm, params_hbm, out_ref, params_ref,
    pred_ref, mv_ref, var_ref, jit_ref, obs_ref, x_ref, idx_ref, full_ref, sems,
):
    members = pred_ref.shape[0]
    tile_x = lax.axis_index("gx")
    tile_y = lax.axis_index("gy")
    square = (OBS_TILE, OBS_TILE)
    pairs = [
        (pred_hbm.at[0, 0], pred_ref),
        (obs_hbm.at[tile_x], obs_ref),
        (var_hbm.at[0], var_ref),
        (mv_hbm.at[0], mv_ref),
        (jit_hbm.at[0, 0], jit_ref),
        (params_hbm, params_ref),
    ]
    copies = fetch(pairs, sems)
    for copy in copies[:3]:
        copy.wait()
    pred = pred_ref[...]
    var = var_ref[...]
    mean = jnp.sum(pred, axis=0, keepdims=True) / members
    deviation = (pred - mean).astype(BF16)
    out_ref[0] = deviation
    obs = obs_ref[pl.ds(tile_y, 1), :]
    groups = (iota((BLOCKS, OBS_TILE), 0) == obs).astype(BF16)
    same = dot(groups, groups, ((0,), (0,)))
    gram = dot(deviation, deviation, ((0,), (0,))) / (members - 1)
    row, col = iota(square, 0), iota(square, 1)
    system = jnp.where(same > 0.5, gram, 0.0) + jnp.where(row == col, var, 0.0)
    size = jnp.sum(same, axis=0, keepdims=True)
    count = jnp.max(size).astype(jnp.int32)
    size = size.astype(jnp.int32)
    rank = jnp.sum(jnp.where(row < col, same, 0.0), axis=0, keepdims=True).astype(jnp.int32)
    place = row == rank
    hot = place.astype(BF16)
    x_ref[...] = dot(jnp.concatenate([hot] * 3, axis=1), jnp.concatenate(split3(system), axis=0), ((1,), (0,)))
    numbered = jnp.where(place, col, 0).astype(F32).astype(BF16)
    idx_ref[...] = dot(numbered, same.astype(BF16), ((1,), (0,))).astype(jnp.int32)

    def solve(rows):
        sweep(rows, count, x_ref, idx_ref, rank, size)
        taken = jnp.concatenate([hot[0:rows]] * 3, axis=0)
        full = dot(taken, jnp.concatenate(split3(x_ref[0:rows, :]), axis=0), ((0,), (0,)))
        full_ref[...] = jnp.where(same > 0.5, -full, 0.0)

    @pl.when(count <= SMALL)
    def _():
        solve(SMALL)

    @pl.when(count > SMALL)
    def _():
        solve(OBS_TILE)

    for copy in copies[3:]:
        copy.wait()
    innovation = mv_ref[...] + jnp.sqrt(var) * jit_ref[...] - pred
    high, mid, low = split3(innovation)
    full_high, full_mid, full_low = split3(full_ref[...])
    left = jnp.concatenate([low, mid, high, mid, high, high], axis=1)
    right = jnp.concatenate([full_high, full_mid, full_low, full_high, full_mid, full_high], axis=0)
    weighted = dot(left, right, ((1,), (0,)))
    out_ref[1] = weighted.astype(BF16)


def weigh(predicted, measured_value, measurement_variance, observation_jitter, obs_block, params):
    members = predicted.shape[2]
    return pl.pallas_call(
        weigh_kernel,
        out_shape=(jax.ShapeDtypeStruct((2, members, OBS_TILE), BF16), jax.ShapeDtypeStruct(params.shape, BF16)),
        in_specs=[pl.BlockSpec(memory_space=pltpu.HBM)] * 6,
        out_specs=(pl.BlockSpec(memory_space=pltpu.VMEM), pl.BlockSpec(memory_space=pltpu.VMEM)),
        scratch_shapes=[
            pltpu.VMEM((members, OBS_TILE), F32),
            pltpu.VMEM((1, OBS_TILE), F32),
            pltpu.VMEM((1, OBS_TILE), F32),
            pltpu.VMEM((members, OBS_TILE), F32),
            pltpu.VMEM((obs_block.shape[1], OBS_TILE), jnp.int32),
            pltpu.VMEM((OBS_TILE, OBS_TILE), F32),
            pltpu.VMEM((OBS_TILE, OBS_TILE), jnp.int32),
            pltpu.VMEM((OBS_TILE, OBS_TILE), F32),
            pltpu.SemaphoreType.DMA((6,)),
        ],
        compiler_params=pltpu.CompilerParams(vmem_limit_bytes=16 * 2**20),
        name="weigh",
    )(*in_hbm(predicted, measured_value, measurement_variance, observation_jitter, obs_block, params))


def offset(which, place):
    even = 1 - 2 * (place & 1)
    return (0, even, -even)[which]


def prepare_kernel(
    params_ref, radius_hbm, pattern_hbm, obs_hbm, turned_ref, taper_ref, radius_ref, pattern_ref, obs_ref, sems
):
    members = params_ref.shape[1]
    tile_x = lax.axis_index("gx")
    tile_y = lax.axis_index("gy")
    count_x, count_y = obs_ref.shape[0], obs_ref.shape[1]
    copies = fetch([(radius_hbm, radius_ref), (pattern_hbm, pattern_ref), (obs_hbm, obs_ref)], sems)

    for b in range(BLOCKS):
        block = params_ref[b].astype(F32)
        mean = jnp.sum(block, axis=0, keepdims=True) / members
        turned_ref[b] = (block - mean).T.astype(BF16)
    for copy in copies:
        copy.wait()
    shape = (BLOCKS, OBS_TILE)
    block = iota(shape, 0)
    radius = jnp.zeros(shape, jnp.int32)
    for b in range(BLOCKS):
        radius = jnp.where(block == b, radius_ref[b // BLK_Y, b % BLK_Y], radius)
    reach = (radius + 1).astype(F32)
    reach = reach * reach
    pattern = jnp.concatenate([pattern_ref[i] for i in range(BLK_X)], axis=0).astype(F32)
    slots = [jnp.broadcast_to(pattern[:, p : p + 1], shape) for p in range(PATTERN)]

    for t in range(9):
        iy, ix = t // 3, t % 3
        dx, dy = offset(ix, tile_x), offset(iy, tile_y)
        at_x, at_y = tile_x + dx, tile_y + dy
        valid = (at_x >= 0) & (at_x < count_x) & (at_y >= 0) & (at_y < count_y)
        at_x = jnp.clip(at_x, 0, count_x - 1)
        at_y = jnp.clip(at_y, 0, count_y - 1)
        obs = obs_ref[at_x, pl.ds(at_y, 1), :]
        step_x = dx * BLK_X + (obs >> 2) - (block >> 2)
        step_y = dy * BLK_Y + (obs & 3) - (block & 3)
        inside = (jnp.abs(step_x) <= 2) & (jnp.abs(step_y) <= 2) & valid
        slot = (step_x + 2) * 5 + (step_y + 2)
        picked = jnp.zeros(shape, F32)
        for p in range(PATTERN):
            picked = jnp.where(slot == p, slots[p], picked)
        spread = (step_x * step_x + step_y * step_y).astype(F32)
        shaped = jnp.maximum(1.0 - spread / reach, 0.0)
        taper_ref[iy, ix] = jnp.where(inside, picked, 0.0) * shaped / (members - 1)


def prepare(by_block, taper_radius, taper_pattern, obs_block):
    members = by_block.shape[1]
    return pl.pallas_call(
        prepare_kernel,
        out_shape=(
            jax.ShapeDtypeStruct((BLOCKS, CELLS, members), BF16),
            jax.ShapeDtypeStruct((3, 3, BLOCKS, OBS_TILE), F32),
        ),
        in_specs=[pl.BlockSpec(memory_space=pltpu.VMEM)] + [pl.BlockSpec(memory_space=pltpu.HBM)] * 3,
        out_specs=(pl.BlockSpec(memory_space=pltpu.VMEM), pl.BlockSpec(memory_space=pltpu.VMEM)),
        scratch_shapes=[
            pltpu.SMEM(taper_radius.shape, jnp.int32),
            pltpu.VMEM(taper_pattern.shape, jnp.int32),
            pltpu.VMEM(obs_block.shape, jnp.int32),
            pltpu.SemaphoreType.DMA((3,)),
        ],
        compiler_params=pltpu.CompilerParams(vmem_limit_bytes=16 * 2**20),
        cost_estimate=pl.CostEstimate(flops=4_000_000, bytes_accessed=1_000_000, transcendentals=0),
        name="prepare",
    )(by_block, *in_hbm(taper_radius, taper_pattern, obs_block))


def moved(b, which, turned_ref, taper_ref, column_ref):
    members = turned_ref.shape[2]
    turned = turned_ref[pl.ds(b, 2)].reshape(2 * CELLS, members)
    cross = dot(turned, column_ref[0], ((1,), (0,)))
    gains = []
    for k in range(2):
        taper = jnp.concatenate([taper_ref[which, ix, pl.ds(b + k, 1), :] for ix in range(3)], axis=1)
        gains.append((cross[k * CELLS : (k + 1) * CELLS] * taper).astype(BF16))
    return dot(column_ref[1], jnp.concatenate(gains, axis=0), ((1,), (1,)))


def first_of(side, tile_y):
    return 2 * ((tile_y & 1) ^ 1 ^ side)


def block_of(k, side, tile_y):
    return (k >> 1) * BLK_Y + first_of(side, tile_y) + (k & 1)


def target(chip, r, chips):
    return chip ^ r if chips & (chips - 1) == 0 else (chip + r) % chips


def source(chip, r, chips):
    return chip ^ r if chips & (chips - 1) == 0 else (chip + chips - r) % chips


def put(piece_refs, rows_ref, k, updated):
    chips, share = len(piece_refs), piece_refs[0].shape[2]
    mine = lax.axis_index("gy")
    rows_ref[k] = updated
    for r, ref in enumerate(piece_refs):
        for flip in (0, 1):
            owner = 2 * target(mine >> 1, r, chips) + ((mine & 1) ^ flip)
            ref[flip, k] = rows_ref[k, pl.ds(pl.multiple_of(owner * share, share), share), :]


def near_kernel(params_ref, turned_ref, taper_ref, own_ref, even_ref, part_ref, *refs):
    piece_refs, rows_ref = refs[:-1], refs[-1]
    tile_y = lax.axis_index("gy")
    for k in range(0, SIDE, 2):
        b = block_of(k, 0, tile_y)
        delta = moved(b, 0, turned_ref, taper_ref, own_ref) + moved(b, 1, turned_ref, taper_ref, even_ref)
        for j in range(2):
            half = delta[:, j * CELLS : (j + 1) * CELLS]
            put(piece_refs, rows_ref, k + j, (params_ref[b + j].astype(F32) + half).astype(BF16))
    for k in range(0, SIDE, 2):
        b = block_of(k, 1, tile_y)
        delta = moved(b, 0, turned_ref, taper_ref, own_ref)
        for j in range(2):
            part_ref[k + j] = params_ref[b + j].astype(F32) + delta[:, j * CELLS : (j + 1) * CELLS]


def far_kernel(turned_ref, taper_ref, odd_ref, part_ref, near_ref, *refs):
    both_ref, rows_ref = refs[-2], refs[-1]
    piece_refs = (*refs[:-2], both_ref.at[1])
    both_ref[0] = near_ref[...]
    tile_y = lax.axis_index("gy")
    for k in range(0, SIDE, 2):
        delta = moved(block_of(k, 1, tile_y), 2, turned_ref, taper_ref, odd_ref)
        for j in range(2):
            half = delta[:, j * CELLS : (j + 1) * CELLS]
            put(piece_refs, rows_ref, k + j, (part_ref[k + j] + half).astype(BF16))


def pack_kernel(*refs):
    at = 0
    for ref in refs[:-1]:
        for piece in halves(ref):
            refs[-1][at] = piece[1]
            at += 1


def halves(ref):
    return [ref] if len(ref.shape) == 4 else [ref.at[side] for side in range(ref.shape[0])]


def settle(chips, sides, refs, rows_ref):
    even_ref, pieces = refs[0], [piece for ref in refs[1:] for piece in halves(ref)]
    share = even_ref.shape[2]
    mine = lax.axis_index("gy")
    chip, core = mine >> 1, mine & 1
    line = 2 * chips * BLK_Y
    for at, ((side, r), own) in enumerate(zip(sides, pieces)):
        for flip in (0, 1):
            other = core ^ flip
            tile = 2 * source(chip, r, chips) + other
            for k in range(SIDE):
                piece = even_ref[at, k] if flip else own[0, k]
                start = (k >> 1) * line + tile * BLK_Y + first_of(side, other) + (k & 1)
                rows_ref[pl.ds(start, share, stride=BLK_X * line), :] = piece.astype(F32)


def early_kernel(chips, *refs):
    settle(chips, [(0, 0), (1, 0)] + [(0, r) for r in range(1, chips - 1)], refs[:-1], refs[-1])


def late_kernel(chips, *refs):
    late_refs, out_hbm, rows_ref, out_ref, sems = refs[1:-4], *refs[-4:]
    last = chips - 1
    settle(chips, [(0, last), (1, last)] + [(1, r) for r in range(1, last)], late_refs, rows_ref)
    pieces = sems.shape[0]
    step = rows_ref.shape[0] // pieces
    copies = []
    for p in range(pieces):
        place = slice(p * step, (p + 1) * step)
        out_ref[place] = rows_ref[place].astype(BF16)
        copies.append(pltpu.make_async_copy(out_ref.at[pl.ds(p * step, step)], out_hbm.at[pl.ds(p * step, step)], sems.at[p]))
        copies[-1].start()
    for copy in copies:
        copy.wait()


VMEM = pl.BlockSpec(memory_space=pltpu.VMEM)
LONG = pl.CostEstimate(flops=4_000_000_000, bytes_accessed=10_000_000, transcendentals=0)
LIMIT = pltpu.CompilerParams(vmem_limit_bytes=24 * 2**20)


def update_near(by_block, turned, taper, own, even, parts):
    members = by_block.shape[1]
    pieces = [jax.ShapeDtypeStruct((2, SIDE, members // parts, CELLS), BF16)] * (parts // 2)
    return pl.pallas_call(
        near_kernel,
        out_shape=(jax.ShapeDtypeStruct((SIDE, members, CELLS), F32), *pieces),
        in_specs=[VMEM] * 5,
        out_specs=(VMEM,) * (1 + len(pieces)),
        scratch_shapes=[pltpu.VMEM((SIDE, members, CELLS), BF16)],
        compiler_params=LIMIT,
        cost_estimate=LONG,
        name="near",
    )(by_block, turned, taper, own, even)


def update_far(turned, taper, odd, part, near):
    members = part.shape[1]
    parts = members // near[0].shape[2]
    piece = jax.ShapeDtypeStruct(near[0].shape, BF16)
    shapes = (piece,) * (parts // 2 - 1) + (jax.ShapeDtypeStruct((2, *piece.shape), BF16),)
    return pl.pallas_call(
        far_kernel,
        out_shape=shapes,
        in_specs=[VMEM] * 5,
        out_specs=(VMEM,) * len(shapes),
        scratch_shapes=[pltpu.VMEM((SIDE, members, CELLS), BF16)],
        compiler_params=LIMIT,
        cost_estimate=LONG,
        name="far",
    )(turned, taper, odd, part, near[-1])


def pack(pieces):
    count = sum(1 if piece.ndim == 4 else piece.shape[0] for piece in pieces)
    return pl.pallas_call(
        pack_kernel,
        out_shape=jax.ShapeDtypeStruct((count, *pieces[-1].shape[-3:]), BF16),
        in_specs=[VMEM] * len(pieces),
        out_specs=VMEM,
        compiler_params=LIMIT,
        name="pack",
    )(*pieces)


def gather(chips, early_even, early, late_even, late):
    share = early[0].shape[2]
    rows = share * BLOCKS * 2 * chips
    placed = pl.pallas_call(
        functools.partial(early_kernel, chips),
        out_shape=jax.ShapeDtypeStruct((rows, CELLS), F32),
        in_specs=[VMEM] * (1 + len(early)),
        out_specs=VMEM,
        compiler_params=LIMIT,
        name="early",
    )(early_even, *early)
    out, _ = pl.pallas_call(
        functools.partial(late_kernel, chips),
        out_shape=(jax.ShapeDtypeStruct((rows, CELLS), BF16), jax.ShapeDtypeStruct((rows, CELLS), F32)),
        in_specs=[VMEM] * (2 + len(late)),
        out_specs=(pl.BlockSpec(memory_space=pl.ANY), VMEM),
        scratch_shapes=[
            pltpu.VMEM((rows, CELLS), BF16),
            pltpu.SemaphoreType.DMA((4,)),
        ],
        input_output_aliases={0: 1},
        compiler_params=LIMIT,
        name="late",
    )(placed, late_even, *late)
    return out.reshape(share, BLK_X, 2 * chips * BLK_Y, CELLS)


def swap(block, axis, first, close=False):
    count = lax.axis_size(axis)
    pairs = [(i, i + 1) for i in range(first, count - 1, 2)]
    if close:
        pairs.append((count - 1, 0))
    return lax.ppermute(block, axis, pairs + [(b, a) for a, b in pairs])


def hop(piece, r):
    count = lax.axis_size("gy")
    pairs = [(i, 2 * target(i // 2, r, count // 2) + i % 2) for i in range(count)]
    return lax.ppermute(piece, "gy", pairs)


def per_device(
    params,
    predicted,
    measured_value,
    measurement_variance,
    observation_jitter,
    obs_block,
    taper_radius,
    taper_pattern,
):
    members = params.shape[0]
    parts = lax.axis_size("gy")
    own, params = weigh(
        predicted, measured_value, measurement_variance, observation_jitter, obs_block, params
    )
    by_block = params.reshape(members, BLOCKS, CELLS).transpose(1, 0, 2)
    even = swap(own, "gx", 0)
    odd = swap(own, "gx", 1, close=True)
    turned, taper = prepare(by_block, taper_radius, taper_pattern, obs_block)
    column = jnp.concatenate([own, even, odd], axis=2)
    column, turned, taper = lax.optimization_barrier((column, turned, taper))
    even = swap(column, "gy", 0)
    odd = swap(column, "gy", 1)
    part, *near = update_near(by_block, turned, taper, column, even, parts)
    last = parts // 2 - 1
    near_hops = {r: hop(near[r], r) for r in range(1, last)}
    *far, both = update_far(turned, taper, odd, part, near)
    if last > 1:
        far[last - 1], near_hops = lax.optimization_barrier((far[last - 1], near_hops))
    far_hops = {r: hop(far[r], r) for r in range(1, last)}
    early = [near[0], far[0], *(near_hops[r] for r in range(1, last))]
    late = [hop(both, last), *(far_hops[r] for r in range(1, last))]
    late_even = swap(pack(late), "gy", 0)
    early_even = swap(pack(early), "gy", 0)
    return gather(parts // 2, early_even, early, late_even, late)


def solution(mesh):
    placed = (
        P(None, "gx", "gy", None),
        P("gx", "gy", None, None),
        P("gx", "gy", None),
        P("gx", "gy", None),
        P("gx", "gy", None, None),
        P(),
        P("gx", "gy"),
        P("gx", "gy", None),
    )
    return jax.shard_map(
        per_device, mesh=mesh, in_specs=placed, out_specs=P("gy", "gx", None, None), check_vma=False
    )
```

```python
import functools

import jax
import jax.numpy as jnp
from jax import lax
from jax.experimental import pallas as pl
from jax.experimental.pallas import tpu as pltpu
from jax.sharding import PartitionSpec as P

CELLS = 128
BLK_X = 2
BLK_Y = 4
BLOCKS = BLK_X * BLK_Y
SIDE = BLOCKS // 2
OBS_TILE = 128
PATTERN = 25
SMALL = 32

F32 = jnp.float32
BF16 = jnp.bfloat16


def iota(shape, dim):
    return lax.broadcasted_iota(jnp.int32, shape, dim)


def split3(x):
    high = x.astype(BF16)
    rest = x - high.astype(F32)
    mid = rest.astype(BF16)
    low = (rest - mid.astype(F32)).astype(BF16)
    return high, mid, low


def dot(a, b, dims):
    return lax.dot_general(a, b, (dims, ((), ())), preferred_element_type=F32)


def sweep(rows, count, x_ref, idx_ref, rank, size):
    row = iota((rows, OBS_TILE), 0)
    exists = row < size

    def taken(spread, indices):
        return jnp.take_along_axis(spread, indices, axis=1, mode="promise_in_bounds")

    def step(k, carry):
        t = 2 * k
        u = t + 1
        row_t, row_u = x_ref[pl.ds(t, 1), :], x_ref[pl.ds(u, 1), :]
        spread_t = jnp.broadcast_to(row_t, (rows, OBS_TILE))
        spread_u = jnp.broadcast_to(row_u, (rows, OBS_TILE))
        at_t = jnp.broadcast_to(idx_ref[pl.ds(t, 1), :], (8, OBS_TILE))
        at_u = jnp.broadcast_to(idx_ref[pl.ds(u, 1), :], (8, OBS_TILE))
        has_t, has_u = t < size, u < size
        a = jnp.where(has_t, taken(spread_t[0:8], at_t)[0:1], 1.0)
        b = jnp.where(has_u, taken(spread_t[0:8], at_u)[0:1], 0.0)
        d = jnp.where(has_u, taken(spread_u[0:8], at_u)[0:1], 1.0)
        own_t, own_u = rank == t, rank == u
        own = own_t | own_u
        head_t = jnp.where(own, jnp.where(own_t, -1.0, 0.0), row_t)
        head_u = jnp.where(own, jnp.where(own_u, -1.0, 0.0), row_u)
        inverse = 1.0 / a
        factor = b * inverse
        scaled_u = (head_u - factor * head_t) / (d - b * factor)
        scaled_t = head_t * inverse - factor * scaled_u
        column_t = jnp.where(exists, taken(spread_t, idx_ref[0:rows, :]), 0.0)
        column_u = jnp.where(exists, taken(spread_u, idx_ref[0:rows, :]), 0.0)
        on_t, on_u = row == t, row == u
        on = on_t | on_u
        column_t = jnp.where(on, jnp.where(on_t, -1.0, 0.0), column_t)
        column_u = jnp.where(on, jnp.where(on_u, -1.0, 0.0), column_u)
        x = jnp.where(on | own, 0.0, x_ref[0:rows, :])
        x_ref[0:rows, :] = x - column_t * scaled_t - column_u * scaled_u
        return carry

    lax.fori_loop(0, (count + 1) // 2, step, 0)


def in_hbm(*arrays):
    return [pltpu.with_memory_space_constraint(array, pltpu.HBM) for array in arrays]


def fetch(pairs, sems):
    copies = [pltpu.make_async_copy(src, dst, sems.at[k]) for k, (src, dst) in enumerate(pairs)]
    for copy in copies:
        copy.start()
    return copies


def weigh_kernel(
    pred_hbm, mv_hbm, var_hbm, jit_hbm, obs_hbm, params_hbm, out_ref, params_ref,
    pred_ref, mv_ref, var_ref, jit_ref, obs_ref, x_ref, idx_ref, full_ref, sems,
):
    members = pred_ref.shape[0]
    tile_x = lax.axis_index("gx")
    tile_y = lax.axis_index("gy")
    square = (OBS_TILE, OBS_TILE)
    pairs = [
        (pred_hbm.at[0, 0], pred_ref),
        (obs_hbm.at[tile_x], obs_ref),
        (var_hbm.at[0], var_ref),
        (mv_hbm.at[0], mv_ref),
        (jit_hbm.at[0, 0], jit_ref),
        (params_hbm, params_ref),
    ]
    copies = fetch(pairs, sems)
    for copy in copies[:3]:
        copy.wait()
    pred = pred_ref[...]
    var = var_ref[...]
    mean = jnp.sum(pred, axis=0, keepdims=True) / members
    deviation = (pred - mean).astype(BF16)
    out_ref[0] = deviation
    obs = obs_ref[pl.ds(tile_y, 1), :]
    groups = (iota((BLOCKS, OBS_TILE), 0) == obs).astype(BF16)
    same = dot(groups, groups, ((0,), (0,)))
    gram = dot(deviation, deviation, ((0,), (0,))) / (members - 1)
    row, col = iota(square, 0), iota(square, 1)
    system = jnp.where(same > 0.5, gram, 0.0) + jnp.where(row == col, var, 0.0)
    size = jnp.sum(same, axis=0, keepdims=True)
    count = jnp.max(size).astype(jnp.int32)
    size = size.astype(jnp.int32)
    rank = jnp.sum(jnp.where(row < col, same, 0.0), axis=0, keepdims=True).astype(jnp.int32)
    place = row == rank
    hot = place.astype(BF16)
    x_ref[...] = dot(jnp.concatenate([hot] * 3, axis=1), jnp.concatenate(split3(system), axis=0), ((1,), (0,)))
    numbered = jnp.where(place, col, 0).astype(F32).astype(BF16)
    idx_ref[...] = dot(numbered, same.astype(BF16), ((1,), (0,))).astype(jnp.int32)

    def solve(rows):
        sweep(rows, count, x_ref, idx_ref, rank, size)
        taken = jnp.concatenate([hot[0:rows]] * 3, axis=0)
        full = dot(taken, jnp.concatenate(split3(x_ref[0:rows, :]), axis=0), ((0,), (0,)))
        full_ref[...] = jnp.where(same > 0.5, -full, 0.0)

    @pl.when(count <= SMALL)
    def _():
        solve(SMALL)

    @pl.when(count > SMALL)
    def _():
        solve(OBS_TILE)

    for copy in copies[3:]:
        copy.wait()
    innovation = mv_ref[...] + jnp.sqrt(var) * jit_ref[...] - pred
    high, mid, low = split3(innovation)
    full_high, full_mid, full_low = split3(full_ref[...])
    left = jnp.concatenate([low, mid, high, mid, high, high], axis=1)
    right = jnp.concatenate([full_high, full_mid, full_low, full_high, full_mid, full_high], axis=0)
    weighted = dot(left, right, ((1,), (0,)))
    out_ref[1] = weighted.astype(BF16)


def weigh(predicted, measured_value, measurement_variance, observation_jitter, obs_block, params):
    members = predicted.shape[2]
    return pl.pallas_call(
        weigh_kernel,
        out_shape=(jax.ShapeDtypeStruct((2, members, OBS_TILE), BF16), jax.ShapeDtypeStruct(params.shape, BF16)),
        in_specs=[pl.BlockSpec(memory_space=pltpu.HBM)] * 6,
        out_specs=(pl.BlockSpec(memory_space=pltpu.VMEM), pl.BlockSpec(memory_space=pltpu.VMEM)),
        scratch_shapes=[
            pltpu.VMEM((members, OBS_TILE), F32),
            pltpu.VMEM((1, OBS_TILE), F32),
            pltpu.VMEM((1, OBS_TILE), F32),
            pltpu.VMEM((members, OBS_TILE), F32),
            pltpu.VMEM((obs_block.shape[1], OBS_TILE), jnp.int32),
            pltpu.VMEM((OBS_TILE, OBS_TILE), F32),
            pltpu.VMEM((OBS_TILE, OBS_TILE), jnp.int32),
            pltpu.VMEM((OBS_TILE, OBS_TILE), F32),
            pltpu.SemaphoreType.DMA((6,)),
        ],
        compiler_params=pltpu.CompilerParams(vmem_limit_bytes=16 * 2**20),
        name="weigh",
    )(*in_hbm(predicted, measured_value, measurement_variance, observation_jitter, obs_block, params))


def offset(which, place):
    even = 1 - 2 * (place & 1)
    return (0, even, -even)[which]


def prepare_kernel(
    params_ref, radius_hbm, pattern_hbm, obs_hbm, turned_ref, taper_ref, radius_ref, pattern_ref, obs_ref, sems
):
    members = params_ref.shape[1]
    tile_x = lax.axis_index("gx")
    tile_y = lax.axis_index("gy")
    count_x, count_y = obs_ref.shape[0], obs_ref.shape[1]
    copies = fetch([(radius_hbm, radius_ref), (pattern_hbm, pattern_ref), (obs_hbm, obs_ref)], sems)

    for b in range(BLOCKS):
        block = params_ref[b].astype(F32)
        mean = jnp.sum(block, axis=0, keepdims=True) / members
        turned_ref[b] = (block - mean).T.astype(BF16)
    for copy in copies:
        copy.wait()
    shape = (BLOCKS, OBS_TILE)
    block = iota(shape, 0)
    radius = jnp.zeros(shape, jnp.int32)
    for b in range(BLOCKS):
        radius = jnp.where(block == b, radius_ref[b // BLK_Y, b % BLK_Y], radius)
    reach = (radius + 1).astype(F32)
    reach = reach * reach
    pattern = jnp.concatenate([pattern_ref[i] for i in range(BLK_X)], axis=0).astype(F32)
    slots = [jnp.broadcast_to(pattern[:, p : p + 1], shape) for p in range(PATTERN)]

    for t in range(9):
        iy, ix = t // 3, t % 3
        dx, dy = offset(ix, tile_x), offset(iy, tile_y)
        at_x, at_y = tile_x + dx, tile_y + dy
        valid = (at_x >= 0) & (at_x < count_x) & (at_y >= 0) & (at_y < count_y)
        at_x = jnp.clip(at_x, 0, count_x - 1)
        at_y = jnp.clip(at_y, 0, count_y - 1)
        obs = obs_ref[at_x, pl.ds(at_y, 1), :]
        step_x = dx * BLK_X + (obs >> 2) - (block >> 2)
        step_y = dy * BLK_Y + (obs & 3) - (block & 3)
        inside = (jnp.abs(step_x) <= 2) & (jnp.abs(step_y) <= 2) & valid
        slot = (step_x + 2) * 5 + (step_y + 2)
        picked = jnp.zeros(shape, F32)
        for p in range(PATTERN):
            picked = jnp.where(slot == p, slots[p], picked)
        spread = (step_x * step_x + step_y * step_y).astype(F32)
        shaped = jnp.maximum(1.0 - spread / reach, 0.0)
        taper_ref[iy, ix] = jnp.where(inside, picked, 0.0) * shaped / (members - 1)


def prepare(by_block, taper_radius, taper_pattern, obs_block):
    members = by_block.shape[1]
    return pl.pallas_call(
        prepare_kernel,
        out_shape=(
            jax.ShapeDtypeStruct((BLOCKS, CELLS, members), BF16),
            jax.ShapeDtypeStruct((3, 3, BLOCKS, OBS_TILE), F32),
        ),
        in_specs=[pl.BlockSpec(memory_space=pltpu.VMEM)] + [pl.BlockSpec(memory_space=pltpu.HBM)] * 3,
        out_specs=(pl.BlockSpec(memory_space=pltpu.VMEM), pl.BlockSpec(memory_space=pltpu.VMEM)),
        scratch_shapes=[
            pltpu.SMEM(taper_radius.shape, jnp.int32),
            pltpu.VMEM(taper_pattern.shape, jnp.int32),
            pltpu.VMEM(obs_block.shape, jnp.int32),
            pltpu.SemaphoreType.DMA((3,)),
        ],
        compiler_params=pltpu.CompilerParams(vmem_limit_bytes=16 * 2**20),
        cost_estimate=pl.CostEstimate(flops=4_000_000, bytes_accessed=1_000_000, transcendentals=0),
        name="prepare",
    )(by_block, *in_hbm(taper_radius, taper_pattern, obs_block))


def moved(b, which, turned_ref, taper_ref, column_ref):
    members = turned_ref.shape[2]
    turned = turned_ref[pl.ds(b, 2)].reshape(2 * CELLS, members)
    cross = dot(turned, column_ref[0], ((1,), (0,)))
    gains = []
    for k in range(2):
        taper = jnp.concatenate([taper_ref[which, ix, pl.ds(b + k, 1), :] for ix in range(3)], axis=1)
        gains.append((cross[k * CELLS : (k + 1) * CELLS] * taper).astype(BF16))
    return dot(column_ref[1], jnp.concatenate(gains, axis=0), ((1,), (1,)))


def first_of(side, tile_y):
    return 2 * ((tile_y & 1) ^ 1 ^ side)


def block_of(k, side, tile_y):
    return (k >> 1) * BLK_Y + first_of(side, tile_y) + (k & 1)


def target(chip, r, chips):
    return chip ^ r if chips & (chips - 1) == 0 else (chip + r) % chips


def source(chip, r, chips):
    return chip ^ r if chips & (chips - 1) == 0 else (chip + chips - r) % chips


def put(piece_refs, rows_ref, k, updated):
    chips, share = len(piece_refs), piece_refs[0].shape[2]
    mine = lax.axis_index("gy")
    rows_ref[k] = updated
    for r, ref in enumerate(piece_refs):
        for flip in (0, 1):
            owner = 2 * target(mine >> 1, r, chips) + ((mine & 1) ^ flip)
            ref[flip, k] = rows_ref[k, pl.ds(pl.multiple_of(owner * share, share), share), :]


def near_kernel(params_ref, turned_ref, taper_ref, own_ref, even_ref, part_ref, *refs):
    piece_refs, rows_ref = refs[:-1], refs[-1]
    tile_y = lax.axis_index("gy")
    for k in range(0, SIDE, 2):
        b = block_of(k, 0, tile_y)
        delta = moved(b, 0, turned_ref, taper_ref, own_ref) + moved(b, 1, turned_ref, taper_ref, even_ref)
        for j in range(2):
            half = delta[:, j * CELLS : (j + 1) * CELLS]
            put(piece_refs, rows_ref, k + j, (params_ref[b + j].astype(F32) + half).astype(BF16))
    for k in range(0, SIDE, 2):
        b = block_of(k, 1, tile_y)
        delta = moved(b, 0, turned_ref, taper_ref, own_ref)
        for j in range(2):
            part_ref[k + j] = params_ref[b + j].astype(F32) + delta[:, j * CELLS : (j + 1) * CELLS]


def far_kernel(turned_ref, taper_ref, odd_ref, part_ref, near_ref, *refs):
    both_ref, rows_ref = refs[-2], refs[-1]
    piece_refs = (*refs[:-2], both_ref.at[1])
    both_ref[0] = near_ref[...]
    tile_y = lax.axis_index("gy")
    for k in range(0, SIDE, 2):
        delta = moved(block_of(k, 1, tile_y), 2, turned_ref, taper_ref, odd_ref)
        for j in range(2):
            half = delta[:, j * CELLS : (j + 1) * CELLS]
            put(piece_refs, rows_ref, k + j, (part_ref[k + j] + half).astype(BF16))


def pack_kernel(*refs):
    at = 0
    for ref in refs[:-1]:
        for piece in halves(ref):
            refs[-1][at] = piece[1]
            at += 1


def halves(ref):
    return [ref] if len(ref.shape) == 4 else [ref.at[side] for side in range(ref.shape[0])]


def settle(chips, sides, refs, rows_ref):
    even_ref, pieces = refs[0], [piece for ref in refs[1:] for piece in halves(ref)]
    share = even_ref.shape[2]
    mine = lax.axis_index("gy")
    chip, core = mine >> 1, mine & 1
    line = 2 * chips * BLK_Y
    for at, ((side, r), own) in enumerate(zip(sides, pieces)):
        for flip in (0, 1):
            other = core ^ flip
            tile = 2 * source(chip, r, chips) + other
            for k in range(SIDE):
                piece = even_ref[at, k] if flip else own[0, k]
                start = (k >> 1) * line + tile * BLK_Y + first_of(side, other) + (k & 1)
                rows_ref[pl.ds(start, share, stride=BLK_X * line), :] = piece.astype(F32)


def early_kernel(chips, *refs):
    settle(chips, [(0, 0), (1, 0)] + [(0, r) for r in range(1, chips - 1)], refs[:-1], refs[-1])


def late_kernel(chips, *refs):
    late_refs, out_hbm, rows_ref, out_ref, sems = refs[1:-4], *refs[-4:]
    last = chips - 1
    settle(chips, [(0, last), (1, last)] + [(1, r) for r in range(1, last)], late_refs, rows_ref)
    pieces = sems.shape[0]
    step = rows_ref.shape[0] // pieces
    copies = []
    for p in range(pieces):
        place = slice(p * step, (p + 1) * step)
        out_ref[place] = rows_ref[place].astype(BF16)
        copies.append(pltpu.make_async_copy(out_ref.at[pl.ds(p * step, step)], out_hbm.at[pl.ds(p * step, step)], sems.at[p]))
        copies[-1].start()
    for copy in copies:
        copy.wait()


VMEM = pl.BlockSpec(memory_space=pltpu.VMEM)
LONG = pl.CostEstimate(flops=4_000_000_000, bytes_accessed=10_000_000, transcendentals=0)
LIMIT = pltpu.CompilerParams(vmem_limit_bytes=24 * 2**20)


def update_near(by_block, turned, taper, own, even, parts):
    members = by_block.shape[1]
    pieces = [jax.ShapeDtypeStruct((2, SIDE, members // parts, CELLS), BF16)] * (parts // 2)
    return pl.pallas_call(
        near_kernel,
        out_shape=(jax.ShapeDtypeStruct((SIDE, members, CELLS), F32), *pieces),
        in_specs=[VMEM] * 5,
        out_specs=(VMEM,) * (1 + len(pieces)),
        scratch_shapes=[pltpu.VMEM((SIDE, members, CELLS), BF16)],
        compiler_params=LIMIT,
        cost_estimate=LONG,
        name="near",
    )(by_block, turned, taper, own, even)


def update_far(turned, taper, odd, part, near):
    members = part.shape[1]
    parts = members // near[0].shape[2]
    piece = jax.ShapeDtypeStruct(near[0].shape, BF16)
    shapes = (piece,) * (parts // 2 - 1) + (jax.ShapeDtypeStruct((2, *piece.shape), BF16),)
    return pl.pallas_call(
        far_kernel,
        out_shape=shapes,
        in_specs=[VMEM] * 5,
        out_specs=(VMEM,) * len(shapes),
        scratch_shapes=[pltpu.VMEM((SIDE, members, CELLS), BF16)],
        compiler_params=LIMIT,
        cost_estimate=LONG,
        name="far",
    )(turned, taper, odd, part, near[-1])


def pack(pieces):
    count = sum(1 if piece.ndim == 4 else piece.shape[0] for piece in pieces)
    return pl.pallas_call(
        pack_kernel,
        out_shape=jax.ShapeDtypeStruct((count, *pieces[-1].shape[-3:]), BF16),
        in_specs=[VMEM] * len(pieces),
        out_specs=VMEM,
        compiler_params=LIMIT,
        name="pack",
    )(*pieces)


def gather(chips, early_even, early, late_even, late):
    share = early[0].shape[2]
    rows = share * BLOCKS * 2 * chips
    placed = pl.pallas_call(
        functools.partial(early_kernel, chips),
        out_shape=jax.ShapeDtypeStruct((rows, CELLS), F32),
        in_specs=[VMEM] * (1 + len(early)),
        out_specs=VMEM,
        compiler_params=LIMIT,
        name="early",
    )(early_even, *early)
    out, _ = pl.pallas_call(
        functools.partial(late_kernel, chips),
        out_shape=(jax.ShapeDtypeStruct((rows, CELLS), BF16), jax.ShapeDtypeStruct((rows, CELLS), F32)),
        in_specs=[VMEM] * (2 + len(late)),
        out_specs=(pl.BlockSpec(memory_space=pl.ANY), VMEM),
        scratch_shapes=[
            pltpu.VMEM((rows, CELLS), BF16),
            pltpu.SemaphoreType.DMA((4,)),
        ],
        input_output_aliases={0: 1},
        compiler_params=LIMIT,
        name="late",
    )(placed, late_even, *late)
    return out.reshape(share, BLK_X, 2 * chips * BLK_Y, CELLS)


def swap(block, axis, first, close=False):
    count = lax.axis_size(axis)
    pairs = [(i, i + 1) for i in range(first, count - 1, 2)]
    if close:
        pairs.append((count - 1, 0))
    return lax.ppermute(block, axis, pairs + [(b, a) for a, b in pairs])


def swap_across():
    rows, count = lax.axis_size("gx"), lax.axis_size("gy")
    pairs = []
    for x in range(rows):
        for y in range(count):
            at, to = (x, y + 1 if y % 2 else y - 1), x * count + y
            if not 0 <= at[1] < count:
                at = (x ^ 1, y)
            pairs.append((to, at[0] * count + at[1]))
    return pairs


def hop(piece, r):
    count = lax.axis_size("gy")
    pairs = [(i, 2 * target(i // 2, r, count // 2) + i % 2) for i in range(count)]
    return lax.ppermute(piece, "gy", pairs)


def per_device(
    params,
    predicted,
    measured_value,
    measurement_variance,
    observation_jitter,
    obs_block,
    taper_radius,
    taper_pattern,
):
    members = params.shape[0]
    parts = lax.axis_size("gy")
    own, params = weigh(
        predicted, measured_value, measurement_variance, observation_jitter, obs_block, params
    )
    by_block = params.reshape(members, BLOCKS, CELLS).transpose(1, 0, 2)
    even = swap(own, "gx", 0)
    odd = swap(own, "gx", 1, close=True)
    turned, taper = prepare(by_block, taper_radius, taper_pattern, obs_block)
    column = jnp.concatenate([own, even, odd], axis=2)
    column, turned, taper = lax.optimization_barrier((column, turned, taper))
    even = swap(column, "gy", 0)
    odd = lax.ppermute(column, ("gx", "gy"), swap_across())
    part, *near = update_near(by_block, turned, taper, column, even, parts)
    last = parts // 2 - 1
    near_hops = {r: hop(near[r], r) for r in range(1, last)}
    *far, both = update_far(turned, taper, odd, part, near)
    if last > 1:
        far[1], near_hops = lax.optimization_barrier((far[1], near_hops))
    far_hops = {r: hop(far[r], r) for r in range(1, last)}
    early = [near[0], far[0], *(near_hops[r] for r in range(1, last))]
    late = [hop(both, last), *(far_hops[r] for r in range(1, last))]
    late_even = swap(pack(late), "gy", 0)
    early_even = swap(pack(early), "gy", 0)
    return gather(parts // 2, early_even, early, late_even, late)


def solution(mesh):
    placed = (
        P(None, "gx", "gy", None),
        P("gx", "gy", None, None),
        P("gx", "gy", None),
        P("gx", "gy", None),
        P("gx", "gy", None, None),
        P(),
        P("gx", "gy"),
        P("gx", "gy", None),
    )
    return jax.shard_map(
        per_device, mesh=mesh, in_specs=placed, out_specs=P("gy", "gx", None, None), check_vma=False
    )
```

```python
import functools

import jax
import jax.numpy as jnp
from jax import lax
from jax.experimental import pallas as pl
from jax.experimental.pallas import tpu as pltpu
from jax.sharding import PartitionSpec as P

CELLS = 128
BLK_X = 2
BLK_Y = 4
BLOCKS = BLK_X * BLK_Y
SIDE = BLOCKS // 2
OBS_TILE = 128
PATTERN = 25
SMALL = 32

F32 = jnp.float32
BF16 = jnp.bfloat16


def iota(shape, dim):
    return lax.broadcasted_iota(jnp.int32, shape, dim)


def split3(x):
    high = x.astype(BF16)
    rest = x - high.astype(F32)
    mid = rest.astype(BF16)
    low = (rest - mid.astype(F32)).astype(BF16)
    return high, mid, low


def dot(a, b, dims):
    return lax.dot_general(a, b, (dims, ((), ())), preferred_element_type=F32)


def sweep(rows, count, x_ref, idx_ref, rank, size):
    row = iota((rows, OBS_TILE), 0)
    exists = row < size

    def taken(spread, indices):
        return jnp.take_along_axis(spread, indices, axis=1, mode="promise_in_bounds")

    def step(k, carry):
        t = 2 * k
        u = t + 1
        row_t, row_u = x_ref[pl.ds(t, 1), :], x_ref[pl.ds(u, 1), :]
        spread_t = jnp.broadcast_to(row_t, (rows, OBS_TILE))
        spread_u = jnp.broadcast_to(row_u, (rows, OBS_TILE))
        at_t = jnp.broadcast_to(idx_ref[pl.ds(t, 1), :], (8, OBS_TILE))
        at_u = jnp.broadcast_to(idx_ref[pl.ds(u, 1), :], (8, OBS_TILE))
        has_t, has_u = t < size, u < size
        a = jnp.where(has_t, taken(spread_t[0:8], at_t)[0:1], 1.0)
        b = jnp.where(has_u, taken(spread_t[0:8], at_u)[0:1], 0.0)
        d = jnp.where(has_u, taken(spread_u[0:8], at_u)[0:1], 1.0)
        own_t, own_u = rank == t, rank == u
        own = own_t | own_u
        head_t = jnp.where(own, jnp.where(own_t, -1.0, 0.0), row_t)
        head_u = jnp.where(own, jnp.where(own_u, -1.0, 0.0), row_u)
        inverse = 1.0 / a
        factor = b * inverse
        scaled_u = (head_u - factor * head_t) / (d - b * factor)
        scaled_t = head_t * inverse - factor * scaled_u
        column_t = jnp.where(exists, taken(spread_t, idx_ref[0:rows, :]), 0.0)
        column_u = jnp.where(exists, taken(spread_u, idx_ref[0:rows, :]), 0.0)
        on_t, on_u = row == t, row == u
        on = on_t | on_u
        column_t = jnp.where(on, jnp.where(on_t, -1.0, 0.0), column_t)
        column_u = jnp.where(on, jnp.where(on_u, -1.0, 0.0), column_u)
        x = jnp.where(on | own, 0.0, x_ref[0:rows, :])
        x_ref[0:rows, :] = x - column_t * scaled_t - column_u * scaled_u
        return carry

    lax.fori_loop(0, (count + 1) // 2, step, 0)


def in_hbm(*arrays):
    return [pltpu.with_memory_space_constraint(array, pltpu.HBM) for array in arrays]


def fetch(pairs, sems):
    copies = [pltpu.make_async_copy(src, dst, sems.at[k]) for k, (src, dst) in enumerate(pairs)]
    for copy in copies:
        copy.start()
    return copies


def weigh_kernel(
    pred_hbm, mv_hbm, var_hbm, jit_hbm, obs_hbm, params_hbm, out_ref, params_ref,
    pred_ref, mv_ref, var_ref, jit_ref, obs_ref, x_ref, idx_ref, full_ref, sems,
):
    members = pred_ref.shape[0]
    tile_x = lax.axis_index("gx")
    tile_y = lax.axis_index("gy")
    square = (OBS_TILE, OBS_TILE)
    pairs = [
        (pred_hbm.at[0, 0], pred_ref),
        (obs_hbm.at[tile_x], obs_ref),
        (var_hbm.at[0], var_ref),
        (mv_hbm.at[0], mv_ref),
        (jit_hbm.at[0, 0], jit_ref),
        (params_hbm, params_ref),
    ]
    copies = fetch(pairs, sems)
    for copy in copies[:3]:
        copy.wait()
    pred = pred_ref[...]
    var = var_ref[...]
    mean = jnp.sum(pred, axis=0, keepdims=True) / members
    deviation = (pred - mean).astype(BF16)
    out_ref[0] = deviation
    obs = obs_ref[pl.ds(tile_y, 1), :]
    groups = (iota((BLOCKS, OBS_TILE), 0) == obs).astype(BF16)
    same = dot(groups, groups, ((0,), (0,)))
    gram = dot(deviation, deviation, ((0,), (0,))) / (members - 1)
    row, col = iota(square, 0), iota(square, 1)
    system = jnp.where(same > 0.5, gram, 0.0) + jnp.where(row == col, var, 0.0)
    size = jnp.sum(same, axis=0, keepdims=True)
    count = jnp.max(size).astype(jnp.int32)
    size = size.astype(jnp.int32)
    rank = jnp.sum(jnp.where(row < col, same, 0.0), axis=0, keepdims=True).astype(jnp.int32)
    place = row == rank
    hot = place.astype(BF16)
    x_ref[...] = dot(jnp.concatenate([hot] * 3, axis=1), jnp.concatenate(split3(system), axis=0), ((1,), (0,)))
    numbered = jnp.where(place, col, 0).astype(F32).astype(BF16)
    idx_ref[...] = dot(numbered, same.astype(BF16), ((1,), (0,))).astype(jnp.int32)

    def solve(rows):
        sweep(rows, count, x_ref, idx_ref, rank, size)
        taken = jnp.concatenate([hot[0:rows]] * 3, axis=0)
        full = dot(taken, jnp.concatenate(split3(x_ref[0:rows, :]), axis=0), ((0,), (0,)))
        full_ref[...] = jnp.where(same > 0.5, -full, 0.0)

    @pl.when(count <= SMALL)
    def _():
        solve(SMALL)

    @pl.when(count > SMALL)
    def _():
        solve(OBS_TILE)

    for copy in copies[3:]:
        copy.wait()
    innovation = mv_ref[...] + jnp.sqrt(var) * jit_ref[...] - pred
    high, mid, low = split3(innovation)
    full_high, full_mid, full_low = split3(full_ref[...])
    left = jnp.concatenate([low, mid, high, mid, high, high], axis=1)
    right = jnp.concatenate([full_high, full_mid, full_low, full_high, full_mid, full_high], axis=0)
    weighted = dot(left, right, ((1,), (0,)))
    out_ref[1] = weighted.astype(BF16)


def weigh(predicted, measured_value, measurement_variance, observation_jitter, obs_block, params):
    members = predicted.shape[2]
    return pl.pallas_call(
        weigh_kernel,
        out_shape=(jax.ShapeDtypeStruct((2, members, OBS_TILE), BF16), jax.ShapeDtypeStruct(params.shape, BF16)),
        in_specs=[pl.BlockSpec(memory_space=pltpu.HBM)] * 6,
        out_specs=(pl.BlockSpec(memory_space=pltpu.VMEM), pl.BlockSpec(memory_space=pltpu.VMEM)),
        scratch_shapes=[
            pltpu.VMEM((members, OBS_TILE), F32),
            pltpu.VMEM((1, OBS_TILE), F32),
            pltpu.VMEM((1, OBS_TILE), F32),
            pltpu.VMEM((members, OBS_TILE), F32),
            pltpu.VMEM((obs_block.shape[1], OBS_TILE), jnp.int32),
            pltpu.VMEM((OBS_TILE, OBS_TILE), F32),
            pltpu.VMEM((OBS_TILE, OBS_TILE), jnp.int32),
            pltpu.VMEM((OBS_TILE, OBS_TILE), F32),
            pltpu.SemaphoreType.DMA((6,)),
        ],
        compiler_params=pltpu.CompilerParams(vmem_limit_bytes=16 * 2**20),
        name="weigh",
    )(*in_hbm(predicted, measured_value, measurement_variance, observation_jitter, obs_block, params))


def offset(which, place):
    even = 1 - 2 * (place & 1)
    return (0, even, -even)[which]


def prepare_kernel(
    params_ref, radius_hbm, pattern_hbm, obs_hbm, turned_ref, taper_ref, radius_ref, pattern_ref, obs_ref, sems
):
    members = params_ref.shape[1]
    tile_x = lax.axis_index("gx")
    tile_y = lax.axis_index("gy")
    count_x, count_y = obs_ref.shape[0], obs_ref.shape[1]
    copies = fetch([(radius_hbm, radius_ref), (pattern_hbm, pattern_ref), (obs_hbm, obs_ref)], sems)

    for b in range(BLOCKS):
        block = params_ref[b].astype(F32)
        mean = jnp.sum(block, axis=0, keepdims=True) / members
        turned_ref[b] = (block - mean).T.astype(BF16)
    for copy in copies:
        copy.wait()
    shape = (BLOCKS, OBS_TILE)
    block = iota(shape, 0)
    radius = jnp.zeros(shape, jnp.int32)
    for b in range(BLOCKS):
        radius = jnp.where(block == b, radius_ref[b // BLK_Y, b % BLK_Y], radius)
    reach = (radius + 1).astype(F32)
    reach = reach * reach
    pattern = jnp.concatenate([pattern_ref[i] for i in range(BLK_X)], axis=0).astype(F32)
    slots = [jnp.broadcast_to(pattern[:, p : p + 1], shape) for p in range(PATTERN)]

    for t in range(9):
        iy, ix = t // 3, t % 3
        dx, dy = offset(ix, tile_x), offset(iy, tile_y)
        at_x, at_y = tile_x + dx, tile_y + dy
        valid = (at_x >= 0) & (at_x < count_x) & (at_y >= 0) & (at_y < count_y)
        at_x = jnp.clip(at_x, 0, count_x - 1)
        at_y = jnp.clip(at_y, 0, count_y - 1)
        obs = obs_ref[at_x, pl.ds(at_y, 1), :]
        step_x = dx * BLK_X + (obs >> 2) - (block >> 2)
        step_y = dy * BLK_Y + (obs & 3) - (block & 3)
        inside = (jnp.abs(step_x) <= 2) & (jnp.abs(step_y) <= 2) & valid
        slot = (step_x + 2) * 5 + (step_y + 2)
        picked = jnp.zeros(shape, F32)
        for p in range(PATTERN):
            picked = jnp.where(slot == p, slots[p], picked)
        spread = (step_x * step_x + step_y * step_y).astype(F32)
        shaped = jnp.maximum(1.0 - spread / reach, 0.0)
        taper_ref[iy, ix] = jnp.where(inside, picked, 0.0) * shaped / (members - 1)


def prepare(by_block, taper_radius, taper_pattern, obs_block):
    members = by_block.shape[1]
    return pl.pallas_call(
        prepare_kernel,
        out_shape=(
            jax.ShapeDtypeStruct((BLOCKS, CELLS, members), BF16),
            jax.ShapeDtypeStruct((3, 3, BLOCKS, OBS_TILE), F32),
        ),
        in_specs=[pl.BlockSpec(memory_space=pltpu.VMEM)] + [pl.BlockSpec(memory_space=pltpu.HBM)] * 3,
        out_specs=(pl.BlockSpec(memory_space=pltpu.VMEM), pl.BlockSpec(memory_space=pltpu.VMEM)),
        scratch_shapes=[
            pltpu.SMEM(taper_radius.shape, jnp.int32),
            pltpu.VMEM(taper_pattern.shape, jnp.int32),
            pltpu.VMEM(obs_block.shape, jnp.int32),
            pltpu.SemaphoreType.DMA((3,)),
        ],
        compiler_params=pltpu.CompilerParams(vmem_limit_bytes=16 * 2**20),
        cost_estimate=pl.CostEstimate(flops=4_000_000, bytes_accessed=1_000_000, transcendentals=0),
        name="prepare",
    )(by_block, *in_hbm(taper_radius, taper_pattern, obs_block))


def moved(b, which, turned_ref, taper_ref, tiles_refs):
    members = turned_ref.shape[2]
    turned = turned_ref[pl.ds(b, 2)].reshape(2 * CELLS, members)
    total, first = 0.0, 0
    for tiles_ref in tiles_refs:
        count = tiles_ref.shape[2] // OBS_TILE
        cross = dot(turned, tiles_ref[0], ((1,), (0,)))
        gains = []
        for k in range(2):
            tapers = [taper_ref[which, ix, pl.ds(b + k, 1), :] for ix in range(first, first + count)]
            gains.append((cross[k * CELLS : (k + 1) * CELLS] * jnp.concatenate(tapers, axis=1)).astype(BF16))
        total = total + dot(tiles_ref[1], jnp.concatenate(gains, axis=0), ((1,), (1,)))
        first += count
    return total


def first_of(side, tile_y):
    return 2 * ((tile_y & 1) ^ 1 ^ side)


def block_of(k, side, tile_y):
    return (k >> 1) * BLK_Y + first_of(side, tile_y) + (k & 1)


def target(chip, r, chips):
    return chip ^ r if chips & (chips - 1) == 0 else (chip + r) % chips


def source(chip, r, chips):
    return chip ^ r if chips & (chips - 1) == 0 else (chip + chips - r) % chips


def put(piece_refs, rows_ref, k, updated):
    chips, share = len(piece_refs), piece_refs[0].shape[2]
    mine = lax.axis_index("gy")
    rows_ref[k] = updated
    for r, ref in enumerate(piece_refs):
        for flip in (0, 1):
            owner = 2 * target(mine >> 1, r, chips) + ((mine & 1) ^ flip)
            ref[flip, k] = rows_ref[k, pl.ds(pl.multiple_of(owner * share, share), share), :]


def near_kernel(params_ref, turned_ref, taper_ref, own_ref, even_ref, part_ref, *refs):
    piece_refs, rows_ref = refs[:-1], refs[-1]
    tile_y = lax.axis_index("gy")
    for k in range(0, SIDE, 2):
        b = block_of(k, 0, tile_y)
        delta = moved(b, 0, turned_ref, taper_ref, [own_ref]) + moved(b, 1, turned_ref, taper_ref, [even_ref])
        for j in range(2):
            half = delta[:, j * CELLS : (j + 1) * CELLS]
            put(piece_refs, rows_ref, k + j, (params_ref[b + j].astype(F32) + half).astype(BF16))
    for k in range(0, SIDE, 2):
        b = block_of(k, 1, tile_y)
        delta = moved(b, 0, turned_ref, taper_ref, [own_ref])
        for j in range(2):
            part_ref[k + j] = params_ref[b + j].astype(F32) + delta[:, j * CELLS : (j + 1) * CELLS]


def far_kernel(turned_ref, taper_ref, odd_ref, beside_ref, part_ref, first_ref, last_ref, *refs):
    rows_ref, refs = refs[-1], refs[:-1]
    piece_refs = [halves(ref)[-1] for ref in refs]
    refs[1][0] = first_ref[...]
    refs[-1][0] = last_ref[...]
    tile_y = lax.axis_index("gy")
    for k in range(0, SIDE, 2):
        delta = moved(block_of(k, 1, tile_y), 2, turned_ref, taper_ref, [odd_ref, beside_ref])
        for j in range(2):
            half = delta[:, j * CELLS : (j + 1) * CELLS]
            put(piece_refs, rows_ref, k + j, (part_ref[k + j] + half).astype(BF16))


def pack_kernel(*refs):
    at = 0
    for ref in refs[:-1]:
        for piece in halves(ref):
            refs[-1][at] = piece[1]
            at += 1


def halves(ref):
    return [ref] if len(ref.shape) == 4 else [ref.at[side] for side in range(ref.shape[0])]


def settle(chips, sides, refs, rows_ref):
    even_ref, pieces = refs[0], [piece for ref in refs[1:] for piece in halves(ref)]
    share = even_ref.shape[2]
    mine = lax.axis_index("gy")
    chip, core = mine >> 1, mine & 1
    line = 2 * chips * BLK_Y
    for at, ((side, r), own) in enumerate(zip(sides, pieces)):
        for flip in (0, 1):
            other = core ^ flip
            tile = 2 * source(chip, r, chips) + other
            for k in range(SIDE):
                piece = even_ref[at, k] if flip else own[0, k]
                start = (k >> 1) * line + tile * BLK_Y + first_of(side, other) + (k & 1)
                rows_ref[pl.ds(start, share, stride=BLK_X * line), :] = piece.astype(F32)


def early_kernel(chips, *refs):
    settle(chips, [(0, 0), (1, 0)] + [(0, r) for r in range(2, chips - 1)], refs[:-1], refs[-1])


def late_kernel(chips, *refs):
    late_refs, out_hbm, rows_ref, out_ref, sems = refs[1:-4], *refs[-4:]
    sides = [(side, r) for r in range(1, chips) for side in ((0, 1) if r in (1, chips - 1) else (1,))]
    settle(chips, sides, late_refs, rows_ref)
    pieces = sems.shape[0]
    step = rows_ref.shape[0] // pieces
    copies = []
    for p in range(pieces):
        place = slice(p * step, (p + 1) * step)
        out_ref[place] = rows_ref[place].astype(BF16)
        copies.append(pltpu.make_async_copy(out_ref.at[pl.ds(p * step, step)], out_hbm.at[pl.ds(p * step, step)], sems.at[p]))
        copies[-1].start()
    for copy in copies:
        copy.wait()


VMEM = pl.BlockSpec(memory_space=pltpu.VMEM)
LONG = pl.CostEstimate(flops=4_000_000_000, bytes_accessed=10_000_000, transcendentals=0)
LIMIT = pltpu.CompilerParams(vmem_limit_bytes=24 * 2**20)


def update_near(by_block, turned, taper, own, even, parts):
    members = by_block.shape[1]
    pieces = [jax.ShapeDtypeStruct((2, SIDE, members // parts, CELLS), BF16)] * (parts // 2)
    return pl.pallas_call(
        near_kernel,
        out_shape=(jax.ShapeDtypeStruct((SIDE, members, CELLS), F32), *pieces),
        in_specs=[VMEM] * 5,
        out_specs=(VMEM,) * (1 + len(pieces)),
        scratch_shapes=[pltpu.VMEM((SIDE, members, CELLS), BF16)],
        compiler_params=LIMIT,
        cost_estimate=LONG,
        name="near",
    )(by_block, turned, taper, own, even)


def update_far(turned, taper, odd, beside, part, near):
    members = part.shape[1]
    chips = len(near)
    piece = jax.ShapeDtypeStruct(near[0].shape, BF16)
    both = jax.ShapeDtypeStruct((2, *piece.shape), BF16)
    shapes = [both if r in (1, chips - 1) else piece for r in range(chips)]
    return pl.pallas_call(
        far_kernel,
        out_shape=tuple(shapes),
        in_specs=[VMEM] * 7,
        out_specs=(VMEM,) * chips,
        scratch_shapes=[pltpu.VMEM((SIDE, members, CELLS), BF16)],
        compiler_params=LIMIT,
        cost_estimate=LONG,
        name="far",
    )(turned, taper, odd, beside, part, near[1], near[-1])


def pack(pieces):
    count = sum(1 if piece.ndim == 4 else piece.shape[0] for piece in pieces)
    return pl.pallas_call(
        pack_kernel,
        out_shape=jax.ShapeDtypeStruct((count, *pieces[-1].shape[-3:]), BF16),
        in_specs=[VMEM] * len(pieces),
        out_specs=VMEM,
        compiler_params=LIMIT,
        name="pack",
    )(*pieces)


def gather(chips, early_even, early, late_even, late):
    share = early[0].shape[2]
    rows = share * BLOCKS * 2 * chips
    placed = pl.pallas_call(
        functools.partial(early_kernel, chips),
        out_shape=jax.ShapeDtypeStruct((rows, CELLS), F32),
        in_specs=[VMEM] * (1 + len(early)),
        out_specs=VMEM,
        compiler_params=LIMIT,
        name="early",
    )(early_even, *early)
    out, _ = pl.pallas_call(
        functools.partial(late_kernel, chips),
        out_shape=(jax.ShapeDtypeStruct((rows, CELLS), BF16), jax.ShapeDtypeStruct((rows, CELLS), F32)),
        in_specs=[VMEM] * (2 + len(late)),
        out_specs=(pl.BlockSpec(memory_space=pl.ANY), VMEM),
        scratch_shapes=[
            pltpu.VMEM((rows, CELLS), BF16),
            pltpu.SemaphoreType.DMA((4,)),
        ],
        input_output_aliases={0: 1},
        compiler_params=LIMIT,
        name="late",
    )(placed, late_even, *late)
    return out.reshape(share, BLK_X, 2 * chips * BLK_Y, CELLS)


def swap(block, axis):
    return lax.ppermute(block, axis, [(i, i ^ 1) for i in range(lax.axis_size(axis))])


def swap_odd(block, axis):
    rows, count = lax.axis_size("gx"), lax.axis_size("gy")
    pairs = []
    for x in range(rows):
        for y in range(count):
            if axis == "gy":
                to = (x, y + 1 if y % 2 else y - 1)
                to = to if 0 <= to[1] < count else (x ^ 1, y)
            else:
                to = (x + 1 if x % 2 else x - 1, y)
                to = to if 0 <= to[0] < rows else (x, y ^ 1)
            pairs.append((x * count + y, to[0] * count + to[1]))
    return lax.ppermute(block, ("gx", "gy"), pairs)


def hop(piece, r):
    count = lax.axis_size("gy")
    pairs = [(i, 2 * target(i // 2, r, count // 2) + i % 2) for i in range(count)]
    return lax.ppermute(piece, "gy", pairs)


def per_device(
    params,
    predicted,
    measured_value,
    measurement_variance,
    observation_jitter,
    obs_block,
    taper_radius,
    taper_pattern,
):
    members = params.shape[0]
    parts = lax.axis_size("gy")
    own, params = weigh(
        predicted, measured_value, measurement_variance, observation_jitter, obs_block, params
    )
    by_block = params.reshape(members, BLOCKS, CELLS).transpose(1, 0, 2)
    sent, by_block = lax.optimization_barrier((own, by_block))
    across = swap_odd(sent, "gy")
    even = swap(own, "gx")
    odd = swap_odd(own, "gx")
    turned, taper = prepare(by_block, taper_radius, taper_pattern, obs_block)
    beside, column = jnp.concatenate([even, odd], axis=2), jnp.concatenate([own, even, odd], axis=2)
    beside, column, across, turned, taper = lax.optimization_barrier((beside, column, across, turned, taper))
    even = swap(column, "gy")
    beside = swap_odd(beside, "gy")
    part, *near = update_near(by_block, turned, taper, column, even, parts)
    chips = parts // 2
    near_hops = [hop(near[r], r) for r in range(2, chips - 1)]
    far = list(update_far(turned, taper, across, beside, part, near))
    if near_hops:
        far[1], near_hops = lax.optimization_barrier((far[1], near_hops))
    early = [near[0], far[0], *near_hops]
    late = [hop(far[r], r) for r in range(1, chips)]
    early_even = swap(pack(early), "gy")
    late, early_even = lax.optimization_barrier((late, early_even))
    late_even = swap(pack(late), "gy")
    return gather(chips, early_even, early, late_even, late)


def solution(mesh):
    placed = (
        P(None, "gx", "gy", None),
        P("gx", "gy", None, None),
        P("gx", "gy", None),
        P("gx", "gy", None),
        P("gx", "gy", None, None),
        P(),
        P("gx", "gy"),
        P("gx", "gy", None),
    )
    return jax.shard_map(
        per_device, mesh=mesh, in_specs=placed, out_specs=P("gy", "gx", None, None), check_vma=False
    )
```

```python
import functools

import jax
import jax.numpy as jnp
from jax import lax
from jax.experimental import pallas as pl
from jax.experimental.pallas import tpu as pltpu
from jax.sharding import PartitionSpec as P

CELLS = 128
BLK_X = 2
BLK_Y = 4
BLOCKS = BLK_X * BLK_Y
SIDE = BLOCKS // 2
OBS_TILE = 128
PATTERN = 25
SMALL = 32

F32 = jnp.float32
BF16 = jnp.bfloat16


def iota(shape, dim):
    return lax.broadcasted_iota(jnp.int32, shape, dim)


def split3(x):
    high = x.astype(BF16)
    rest = x - high.astype(F32)
    mid = rest.astype(BF16)
    low = (rest - mid.astype(F32)).astype(BF16)
    return high, mid, low


def dot(a, b, dims):
    return lax.dot_general(a, b, (dims, ((), ())), preferred_element_type=F32)


def sweep(rows, count, x_ref, idx_ref, rank, size):
    row = iota((rows, OBS_TILE), 0)
    exists = row < size

    def taken(spread, indices):
        return jnp.take_along_axis(spread, indices, axis=1, mode="promise_in_bounds")

    def step(k, carry):
        t = 2 * k
        u = t + 1
        row_t, row_u = x_ref[pl.ds(t, 1), :], x_ref[pl.ds(u, 1), :]
        spread_t = jnp.broadcast_to(row_t, (rows, OBS_TILE))
        spread_u = jnp.broadcast_to(row_u, (rows, OBS_TILE))
        at_t = jnp.broadcast_to(idx_ref[pl.ds(t, 1), :], (8, OBS_TILE))
        at_u = jnp.broadcast_to(idx_ref[pl.ds(u, 1), :], (8, OBS_TILE))
        has_t, has_u = t < size, u < size
        a = jnp.where(has_t, taken(spread_t[0:8], at_t)[0:1], 1.0)
        b = jnp.where(has_u, taken(spread_t[0:8], at_u)[0:1], 0.0)
        d = jnp.where(has_u, taken(spread_u[0:8], at_u)[0:1], 1.0)
        own_t, own_u = rank == t, rank == u
        own = own_t | own_u
        head_t = jnp.where(own, jnp.where(own_t, -1.0, 0.0), row_t)
        head_u = jnp.where(own, jnp.where(own_u, -1.0, 0.0), row_u)
        inverse = 1.0 / a
        factor = b * inverse
        scaled_u = (head_u - factor * head_t) / (d - b * factor)
        scaled_t = head_t * inverse - factor * scaled_u
        column_t = jnp.where(exists, taken(spread_t, idx_ref[0:rows, :]), 0.0)
        column_u = jnp.where(exists, taken(spread_u, idx_ref[0:rows, :]), 0.0)
        on_t, on_u = row == t, row == u
        on = on_t | on_u
        column_t = jnp.where(on, jnp.where(on_t, -1.0, 0.0), column_t)
        column_u = jnp.where(on, jnp.where(on_u, -1.0, 0.0), column_u)
        x = jnp.where(on | own, 0.0, x_ref[0:rows, :])
        x_ref[0:rows, :] = x - column_t * scaled_t - column_u * scaled_u
        return carry

    lax.fori_loop(0, (count + 1) // 2, step, 0)


def in_hbm(*arrays):
    return [pltpu.with_memory_space_constraint(array, pltpu.HBM) for array in arrays]


def fetch(pairs, sems):
    copies = [pltpu.make_async_copy(src, dst, sems.at[k]) for k, (src, dst) in enumerate(pairs)]
    for copy in copies:
        copy.start()
    return copies


def weigh_kernel(
    pred_hbm, mv_hbm, var_hbm, jit_hbm, obs_hbm, params_hbm, out_ref, params_ref,
    pred_ref, mv_ref, var_ref, jit_ref, obs_ref, x_ref, idx_ref, full_ref, sems,
):
    members = pred_ref.shape[0]
    tile_x = lax.axis_index("gx")
    tile_y = lax.axis_index("gy")
    square = (OBS_TILE, OBS_TILE)
    pairs = [
        (pred_hbm.at[0, 0], pred_ref),
        (obs_hbm.at[tile_x], obs_ref),
        (var_hbm.at[0], var_ref),
        (mv_hbm.at[0], mv_ref),
        (jit_hbm.at[0, 0], jit_ref),
        (params_hbm, params_ref),
    ]
    copies = fetch(pairs, sems)
    for copy in copies[:3]:
        copy.wait()
    pred = pred_ref[...]
    var = var_ref[...]
    mean = jnp.sum(pred, axis=0, keepdims=True) / members
    deviation = (pred - mean).astype(BF16)
    out_ref[0] = deviation
    obs = obs_ref[pl.ds(tile_y, 1), :]
    groups = (iota((BLOCKS, OBS_TILE), 0) == obs).astype(BF16)
    same = dot(groups, groups, ((0,), (0,)))
    gram = dot(deviation, deviation, ((0,), (0,))) / (members - 1)
    row, col = iota(square, 0), iota(square, 1)
    system = jnp.where(same > 0.5, gram, 0.0) + jnp.where(row == col, var, 0.0)
    size = jnp.sum(same, axis=0, keepdims=True)
    count = jnp.max(size).astype(jnp.int32)
    size = size.astype(jnp.int32)
    rank = jnp.sum(jnp.where(row < col, same, 0.0), axis=0, keepdims=True).astype(jnp.int32)
    place = row == rank
    hot = place.astype(BF16)
    x_ref[...] = dot(jnp.concatenate([hot] * 3, axis=1), jnp.concatenate(split3(system), axis=0), ((1,), (0,)))
    numbered = jnp.where(place, col, 0).astype(F32).astype(BF16)
    idx_ref[...] = dot(numbered, same.astype(BF16), ((1,), (0,))).astype(jnp.int32)

    def solve(rows):
        sweep(rows, count, x_ref, idx_ref, rank, size)
        taken = jnp.concatenate([hot[0:rows]] * 3, axis=0)
        full = dot(taken, jnp.concatenate(split3(x_ref[0:rows, :]), axis=0), ((0,), (0,)))
        full_ref[...] = jnp.where(same > 0.5, -full, 0.0)

    @pl.when(count <= SMALL)
    def _():
        solve(SMALL)

    @pl.when(count > SMALL)
    def _():
        solve(OBS_TILE)

    for copy in copies[3:]:
        copy.wait()
    innovation = mv_ref[...] + jnp.sqrt(var) * jit_ref[...] - pred
    high, mid, low = split3(innovation)
    full_high, full_mid, full_low = split3(full_ref[...])
    left = jnp.concatenate([low, mid, high, mid, high, high], axis=1)
    right = jnp.concatenate([full_high, full_mid, full_low, full_high, full_mid, full_high], axis=0)
    weighted = dot(left, right, ((1,), (0,)))
    out_ref[1] = weighted.astype(BF16)


def weigh(predicted, measured_value, measurement_variance, observation_jitter, obs_block, params):
    members = predicted.shape[2]
    return pl.pallas_call(
        weigh_kernel,
        out_shape=(jax.ShapeDtypeStruct((2, members, OBS_TILE), BF16), jax.ShapeDtypeStruct(params.shape, BF16)),
        in_specs=[pl.BlockSpec(memory_space=pltpu.HBM)] * 6,
        out_specs=(pl.BlockSpec(memory_space=pltpu.VMEM), pl.BlockSpec(memory_space=pltpu.VMEM)),
        scratch_shapes=[
            pltpu.VMEM((members, OBS_TILE), F32),
            pltpu.VMEM((1, OBS_TILE), F32),
            pltpu.VMEM((1, OBS_TILE), F32),
            pltpu.VMEM((members, OBS_TILE), F32),
            pltpu.VMEM((obs_block.shape[1], OBS_TILE), jnp.int32),
            pltpu.VMEM((OBS_TILE, OBS_TILE), F32),
            pltpu.VMEM((OBS_TILE, OBS_TILE), jnp.int32),
            pltpu.VMEM((OBS_TILE, OBS_TILE), F32),
            pltpu.SemaphoreType.DMA((6,)),
        ],
        compiler_params=pltpu.CompilerParams(vmem_limit_bytes=16 * 2**20),
        name="weigh",
    )(*in_hbm(predicted, measured_value, measurement_variance, observation_jitter, obs_block, params))


def offset(which, place):
    even = 1 - 2 * (place & 1)
    return (0, even, -even)[which]


def prepare_kernel(
    params_ref, radius_hbm, pattern_hbm, obs_hbm, turned_ref, taper_ref, radius_ref, pattern_ref, obs_ref, sems
):
    members = params_ref.shape[1]
    tile_x = lax.axis_index("gx")
    tile_y = lax.axis_index("gy")
    count_x, count_y = obs_ref.shape[0], obs_ref.shape[1]
    copies = fetch([(radius_hbm, radius_ref), (pattern_hbm, pattern_ref), (obs_hbm, obs_ref)], sems)

    for b in range(BLOCKS):
        block = params_ref[b].astype(F32)
        mean = jnp.sum(block, axis=0, keepdims=True) / members
        turned_ref[b] = (block - mean).T.astype(BF16)
    for copy in copies:
        copy.wait()
    shape = (BLOCKS, OBS_TILE)
    block = iota(shape, 0)
    radius = jnp.zeros(shape, jnp.int32)
    for b in range(BLOCKS):
        radius = jnp.where(block == b, radius_ref[b // BLK_Y, b % BLK_Y], radius)
    reach = (radius + 1).astype(F32)
    reach = reach * reach
    pattern = jnp.concatenate([pattern_ref[i] for i in range(BLK_X)], axis=0).astype(F32)
    slots = [jnp.broadcast_to(pattern[:, p : p + 1], shape) for p in range(PATTERN)]

    for t in range(9):
        iy, ix = t // 3, t % 3
        dx, dy = offset(ix, tile_x), offset(iy, tile_y)
        at_x, at_y = tile_x + dx, tile_y + dy
        valid = (at_x >= 0) & (at_x < count_x) & (at_y >= 0) & (at_y < count_y)
        at_x = jnp.clip(at_x, 0, count_x - 1)
        at_y = jnp.clip(at_y, 0, count_y - 1)
        obs = obs_ref[at_x, pl.ds(at_y, 1), :]
        step_x = dx * BLK_X + (obs >> 2) - (block >> 2)
        step_y = dy * BLK_Y + (obs & 3) - (block & 3)
        inside = (jnp.abs(step_x) <= 2) & (jnp.abs(step_y) <= 2) & valid
        slot = (step_x + 2) * 5 + (step_y + 2)
        picked = jnp.zeros(shape, F32)
        for p in range(PATTERN):
            picked = jnp.where(slot == p, slots[p], picked)
        spread = (step_x * step_x + step_y * step_y).astype(F32)
        shaped = jnp.maximum(1.0 - spread / reach, 0.0)
        taper_ref[iy, ix] = jnp.where(inside, picked, 0.0) * shaped / (members - 1)


def prepare(by_block, taper_radius, taper_pattern, obs_block):
    members = by_block.shape[1]
    return pl.pallas_call(
        prepare_kernel,
        out_shape=(
            jax.ShapeDtypeStruct((BLOCKS, CELLS, members), BF16),
            jax.ShapeDtypeStruct((3, 3, BLOCKS, OBS_TILE), F32),
        ),
        in_specs=[pl.BlockSpec(memory_space=pltpu.VMEM)] + [pl.BlockSpec(memory_space=pltpu.HBM)] * 3,
        out_specs=(pl.BlockSpec(memory_space=pltpu.VMEM), pl.BlockSpec(memory_space=pltpu.VMEM)),
        scratch_shapes=[
            pltpu.SMEM(taper_radius.shape, jnp.int32),
            pltpu.VMEM(taper_pattern.shape, jnp.int32),
            pltpu.VMEM(obs_block.shape, jnp.int32),
            pltpu.SemaphoreType.DMA((3,)),
        ],
        compiler_params=pltpu.CompilerParams(vmem_limit_bytes=16 * 2**20),
        cost_estimate=pl.CostEstimate(flops=4_000_000, bytes_accessed=1_000_000, transcendentals=0),
        name="prepare",
    )(by_block, *in_hbm(taper_radius, taper_pattern, obs_block))


def moved(b, which, turned_ref, taper_ref, tiles_refs):
    members = turned_ref.shape[2]
    turned = turned_ref[pl.ds(b, 2)].reshape(2 * CELLS, members)
    total, first = 0.0, 0
    for tiles_ref in tiles_refs:
        count = tiles_ref.shape[2] // OBS_TILE
        cross = dot(turned, tiles_ref[0], ((1,), (0,)))
        gains = []
        for k in range(2):
            tapers = [taper_ref[which, ix, pl.ds(b + k, 1), :] for ix in range(first, first + count)]
            gains.append((cross[k * CELLS : (k + 1) * CELLS] * jnp.concatenate(tapers, axis=1)).astype(BF16))
        total = total + dot(tiles_ref[1], jnp.concatenate(gains, axis=0), ((1,), (1,)))
        first += count
    return total


def first_of(side, tile_y):
    return 2 * ((tile_y & 1) ^ 1 ^ side)


def block_of(k, side, tile_y):
    return (k >> 1) * BLK_Y + first_of(side, tile_y) + (k & 1)


def target(chip, r, chips):
    return chip ^ r if chips & (chips - 1) == 0 else (chip + r) % chips


def source(chip, r, chips):
    return chip ^ r if chips & (chips - 1) == 0 else (chip + chips - r) % chips


def put(piece_refs, rows_ref, k, updated):
    chips, share = len(piece_refs), piece_refs[0].shape[2]
    mine = lax.axis_index("gy")
    rows_ref[k] = updated
    for r, ref in enumerate(piece_refs):
        for flip in (0, 1):
            owner = 2 * target(mine >> 1, r, chips) + ((mine & 1) ^ flip)
            ref[flip, k] = rows_ref[k, pl.ds(pl.multiple_of(owner * share, share), share), :]


def near_kernel(params_ref, turned_ref, taper_ref, own_ref, even_ref, part_ref, *refs):
    piece_refs, rows_ref = refs[:-1], refs[-1]
    tile_y = lax.axis_index("gy")
    for k in range(0, SIDE, 2):
        b = block_of(k, 0, tile_y)
        delta = moved(b, 0, turned_ref, taper_ref, [own_ref]) + moved(b, 1, turned_ref, taper_ref, [even_ref])
        for j in range(2):
            half = delta[:, j * CELLS : (j + 1) * CELLS]
            put(piece_refs, rows_ref, k + j, (params_ref[b + j].astype(F32) + half).astype(BF16))
    for k in range(0, SIDE, 2):
        b = block_of(k, 1, tile_y)
        delta = moved(b, 0, turned_ref, taper_ref, [own_ref])
        for j in range(2):
            part_ref[k + j] = params_ref[b + j].astype(F32) + delta[:, j * CELLS : (j + 1) * CELLS]


def far_kernel(turned_ref, taper_ref, odd_ref, beside_ref, part_ref, near_ref, *refs):
    rows_ref, refs = refs[-1], refs[:-1]
    piece_refs = [halves(ref)[-1] for ref in refs]
    refs[-1][0] = near_ref[...]
    tile_y = lax.axis_index("gy")
    for k in range(0, SIDE, 2):
        delta = moved(block_of(k, 1, tile_y), 2, turned_ref, taper_ref, [odd_ref, beside_ref])
        for j in range(2):
            half = delta[:, j * CELLS : (j + 1) * CELLS]
            put(piece_refs, rows_ref, k + j, (part_ref[k + j] + half).astype(BF16))


def pack_kernel(*refs):
    at = 0
    for ref in refs[:-1]:
        for piece in halves(ref):
            refs[-1][at] = piece[1]
            at += 1


def halves(ref):
    return [ref] if len(ref.shape) == 4 else [ref.at[side] for side in range(ref.shape[0])]


def settle(chips, sides, refs, rows_ref):
    even_ref, pieces = refs[0], [piece for ref in refs[1:] for piece in halves(ref)]
    share = even_ref.shape[2]
    mine = lax.axis_index("gy")
    chip, core = mine >> 1, mine & 1
    line = 2 * chips * BLK_Y
    for at, ((side, r), own) in enumerate(zip(sides, pieces)):
        for flip in (0, 1):
            other = core ^ flip
            tile = 2 * source(chip, r, chips) + other
            for k in range(SIDE):
                piece = even_ref[at, k] if flip else own[0, k]
                start = (k >> 1) * line + tile * BLK_Y + first_of(side, other) + (k & 1)
                rows_ref[pl.ds(start, share, stride=BLK_X * line), :] = piece.astype(F32)


def early_kernel(chips, *refs):
    settle(chips, [(0, 0), (1, 0)] + [(0, r) for r in range(1, chips - 1)], refs[:-1], refs[-1])


def late_kernel(chips, *refs):
    late_refs, out_hbm, rows_ref, out_ref, sems = refs[1:-4], *refs[-4:]
    sides = [(side, r) for r in range(1, chips) for side in ((0, 1) if r == chips - 1 else (1,))]
    settle(chips, sides, late_refs, rows_ref)
    pieces = sems.shape[0]
    step = rows_ref.shape[0] // pieces
    copies = []
    for p in range(pieces):
        place = slice(p * step, (p + 1) * step)
        out_ref[place] = rows_ref[place].astype(BF16)
        copies.append(pltpu.make_async_copy(out_ref.at[pl.ds(p * step, step)], out_hbm.at[pl.ds(p * step, step)], sems.at[p]))
        copies[-1].start()
    for copy in copies:
        copy.wait()


VMEM = pl.BlockSpec(memory_space=pltpu.VMEM)
LONG = pl.CostEstimate(flops=4_000_000_000, bytes_accessed=10_000_000, transcendentals=0)
LIMIT = pltpu.CompilerParams(vmem_limit_bytes=24 * 2**20)


def update_near(by_block, turned, taper, own, even, parts):
    members = by_block.shape[1]
    pieces = [jax.ShapeDtypeStruct((2, SIDE, members // parts, CELLS), BF16)] * (parts // 2)
    return pl.pallas_call(
        near_kernel,
        out_shape=(jax.ShapeDtypeStruct((SIDE, members, CELLS), F32), *pieces),
        in_specs=[VMEM] * 5,
        out_specs=(VMEM,) * (1 + len(pieces)),
        scratch_shapes=[pltpu.VMEM((SIDE, members, CELLS), BF16)],
        compiler_params=LIMIT,
        cost_estimate=LONG,
        name="near",
    )(by_block, turned, taper, own, even)


def update_far(turned, taper, odd, beside, part, near):
    members = part.shape[1]
    chips = len(near)
    piece = jax.ShapeDtypeStruct(near[0].shape, BF16)
    both = jax.ShapeDtypeStruct((2, *piece.shape), BF16)
    shapes = [piece] * (chips - 1) + [both]
    return pl.pallas_call(
        far_kernel,
        out_shape=tuple(shapes),
        in_specs=[VMEM] * 6,
        out_specs=(VMEM,) * chips,
        scratch_shapes=[pltpu.VMEM((SIDE, members, CELLS), BF16)],
        compiler_params=LIMIT,
        cost_estimate=LONG,
        name="far",
    )(turned, taper, odd, beside, part, near[-1])


def pack(pieces):
    count = sum(1 if piece.ndim == 4 else piece.shape[0] for piece in pieces)
    return pl.pallas_call(
        pack_kernel,
        out_shape=jax.ShapeDtypeStruct((count, *pieces[-1].shape[-3:]), BF16),
        in_specs=[VMEM] * len(pieces),
        out_specs=VMEM,
        compiler_params=LIMIT,
        name="pack",
    )(*pieces)


def gather(chips, early_even, early, late_even, late):
    share = early[0].shape[2]
    rows = share * BLOCKS * 2 * chips
    placed = pl.pallas_call(
        functools.partial(early_kernel, chips),
        out_shape=jax.ShapeDtypeStruct((rows, CELLS), F32),
        in_specs=[VMEM] * (1 + len(early)),
        out_specs=VMEM,
        compiler_params=LIMIT,
        name="early",
    )(early_even, *early)
    out, _ = pl.pallas_call(
        functools.partial(late_kernel, chips),
        out_shape=(jax.ShapeDtypeStruct((rows, CELLS), BF16), jax.ShapeDtypeStruct((rows, CELLS), F32)),
        in_specs=[VMEM] * (2 + len(late)),
        out_specs=(pl.BlockSpec(memory_space=pl.ANY), VMEM),
        scratch_shapes=[
            pltpu.VMEM((rows, CELLS), BF16),
            pltpu.SemaphoreType.DMA((4,)),
        ],
        input_output_aliases={0: 1},
        compiler_params=LIMIT,
        name="late",
    )(placed, late_even, *late)
    return out.reshape(share, BLK_X, 2 * chips * BLK_Y, CELLS)


def swap(block, axis):
    return lax.ppermute(block, axis, [(i, i ^ 1) for i in range(lax.axis_size(axis))])


def swap_odd(block, axis):
    rows, count = lax.axis_size("gx"), lax.axis_size("gy")
    pairs = []
    for x in range(rows):
        for y in range(count):
            if axis == "gy":
                to = (x, y + 1 if y % 2 else y - 1)
                to = to if 0 <= to[1] < count else (x ^ 1, y)
            else:
                to = (x + 1 if x % 2 else x - 1, y)
                to = to if 0 <= to[0] < rows else (x, y ^ 1)
            pairs.append((x * count + y, to[0] * count + to[1]))
    return lax.ppermute(block, ("gx", "gy"), pairs)


def hop(piece, r):
    count = lax.axis_size("gy")
    pairs = [(i, 2 * target(i // 2, r, count // 2) + i % 2) for i in range(count)]
    return lax.ppermute(piece, "gy", pairs)


def per_device(
    params,
    predicted,
    measured_value,
    measurement_variance,
    observation_jitter,
    obs_block,
    taper_radius,
    taper_pattern,
):
    members = params.shape[0]
    parts = lax.axis_size("gy")
    own, params = weigh(
        predicted, measured_value, measurement_variance, observation_jitter, obs_block, params
    )
    by_block = params.reshape(members, BLOCKS, CELLS).transpose(1, 0, 2)
    sent, by_block = lax.optimization_barrier((own, by_block))
    across = swap_odd(sent, "gy")
    even = swap(own, "gx")
    odd = swap_odd(own, "gx")
    turned, taper = prepare(by_block, taper_radius, taper_pattern, obs_block)
    beside, column = jnp.concatenate([even, odd], axis=2), jnp.concatenate([own, even, odd], axis=2)
    beside, column, across, turned, taper = lax.optimization_barrier((beside, column, across, turned, taper))
    even = swap(column, "gy")
    beside = swap_odd(beside, "gy")
    part, *near = update_near(by_block, turned, taper, column, even, parts)
    chips = parts // 2
    near_hops = [hop(near[r], r) for r in range(1, chips - 1)]
    far = list(update_far(turned, taper, across, beside, part, near))
    if near_hops:
        far[1], near_hops = lax.optimization_barrier((far[1], near_hops))
    early = [near[0], far[0], *near_hops]
    late = [hop(far[r], r) for r in range(1, chips)]
    late_even = swap(pack(late), "gy")
    early_even = swap(pack(early), "gy")
    return gather(chips, early_even, early, late_even, late)


def solution(mesh):
    placed = (
        P(None, "gx", "gy", None),
        P("gx", "gy", None, None),
        P("gx", "gy", None),
        P("gx", "gy", None),
        P("gx", "gy", None, None),
        P(),
        P("gx", "gy"),
        P("gx", "gy", None),
    )
    return jax.shard_map(
        per_device, mesh=mesh, in_specs=placed, out_specs=P("gy", "gx", None, None), check_vma=False
    )
```

```python
import functools

import jax
import jax.numpy as jnp
from jax import lax
from jax.experimental import pallas as pl
from jax.experimental.pallas import tpu as pltpu
from jax.sharding import PartitionSpec as P

CELLS = 128
BLK_X = 2
BLK_Y = 4
BLOCKS = BLK_X * BLK_Y
SIDE = BLOCKS // 2
OBS_TILE = 128
PATTERN = 25
SMALL = 32

F32 = jnp.float32
BF16 = jnp.bfloat16


def iota(shape, dim):
    return lax.broadcasted_iota(jnp.int32, shape, dim)


def split3(x):
    high = x.astype(BF16)
    rest = x - high.astype(F32)
    mid = rest.astype(BF16)
    low = (rest - mid.astype(F32)).astype(BF16)
    return high, mid, low


def dot(a, b, dims):
    return lax.dot_general(a, b, (dims, ((), ())), preferred_element_type=F32)


def sweep(rows, count, x_ref, idx_ref, rank, size):
    row = iota((rows, OBS_TILE), 0)
    exists = row < size

    def taken(spread, indices):
        return jnp.take_along_axis(spread, indices, axis=1, mode="promise_in_bounds")

    def step(k, carry):
        t = 2 * k
        u = t + 1
        row_t, row_u = x_ref[pl.ds(t, 1), :], x_ref[pl.ds(u, 1), :]
        spread_t = jnp.broadcast_to(row_t, (rows, OBS_TILE))
        spread_u = jnp.broadcast_to(row_u, (rows, OBS_TILE))
        at_t = jnp.broadcast_to(idx_ref[pl.ds(t, 1), :], (8, OBS_TILE))
        at_u = jnp.broadcast_to(idx_ref[pl.ds(u, 1), :], (8, OBS_TILE))
        has_t, has_u = t < size, u < size
        a = jnp.where(has_t, taken(spread_t[0:8], at_t)[0:1], 1.0)
        b = jnp.where(has_u, taken(spread_t[0:8], at_u)[0:1], 0.0)
        d = jnp.where(has_u, taken(spread_u[0:8], at_u)[0:1], 1.0)
        own_t, own_u = rank == t, rank == u
        own = own_t | own_u
        head_t = jnp.where(own, jnp.where(own_t, -1.0, 0.0), row_t)
        head_u = jnp.where(own, jnp.where(own_u, -1.0, 0.0), row_u)
        inverse = 1.0 / a
        factor = b * inverse
        scaled_u = (head_u - factor * head_t) / (d - b * factor)
        scaled_t = head_t * inverse - factor * scaled_u
        column_t = jnp.where(exists, taken(spread_t, idx_ref[0:rows, :]), 0.0)
        column_u = jnp.where(exists, taken(spread_u, idx_ref[0:rows, :]), 0.0)
        on_t, on_u = row == t, row == u
        on = on_t | on_u
        column_t = jnp.where(on, jnp.where(on_t, -1.0, 0.0), column_t)
        column_u = jnp.where(on, jnp.where(on_u, -1.0, 0.0), column_u)
        x = jnp.where(on | own, 0.0, x_ref[0:rows, :])
        x_ref[0:rows, :] = x - column_t * scaled_t - column_u * scaled_u
        return carry

    lax.fori_loop(0, (count + 1) // 2, step, 0)


def in_hbm(*arrays):
    return [pltpu.with_memory_space_constraint(array, pltpu.HBM) for array in arrays]


def fetch(pairs, sems):
    copies = [pltpu.make_async_copy(src, dst, sems.at[k]) for k, (src, dst) in enumerate(pairs)]
    for copy in copies:
        copy.start()
    return copies


def weigh_kernel(
    pred_hbm, mv_hbm, var_hbm, jit_hbm, obs_hbm, params_hbm, out_ref, params_ref,
    pred_ref, mv_ref, var_ref, jit_ref, obs_ref, x_ref, idx_ref, full_ref, sems,
):
    members = pred_ref.shape[0]
    tile_x = lax.axis_index("gx")
    tile_y = lax.axis_index("gy")
    square = (OBS_TILE, OBS_TILE)
    pairs = [
        (pred_hbm.at[0, 0], pred_ref),
        (obs_hbm.at[tile_x], obs_ref),
        (var_hbm.at[0], var_ref),
        (mv_hbm.at[0], mv_ref),
        (jit_hbm.at[0, 0], jit_ref),
        (params_hbm, params_ref),
    ]
    copies = fetch(pairs, sems)
    for copy in copies[:3]:
        copy.wait()
    pred = pred_ref[...]
    var = var_ref[...]
    mean = jnp.sum(pred, axis=0, keepdims=True) / members
    deviation = (pred - mean).astype(BF16)
    out_ref[0] = deviation
    obs = obs_ref[pl.ds(tile_y, 1), :]
    groups = (iota((BLOCKS, OBS_TILE), 0) == obs).astype(BF16)
    same = dot(groups, groups, ((0,), (0,)))
    gram = dot(deviation, deviation, ((0,), (0,))) / (members - 1)
    row, col = iota(square, 0), iota(square, 1)
    system = jnp.where(same > 0.5, gram, 0.0) + jnp.where(row == col, var, 0.0)
    size = jnp.sum(same, axis=0, keepdims=True)
    count = jnp.max(size).astype(jnp.int32)
    size = size.astype(jnp.int32)
    rank = jnp.sum(jnp.where(row < col, same, 0.0), axis=0, keepdims=True).astype(jnp.int32)
    place = row == rank
    hot = place.astype(BF16)
    x_ref[...] = dot(jnp.concatenate([hot] * 3, axis=1), jnp.concatenate(split3(system), axis=0), ((1,), (0,)))
    numbered = jnp.where(place, col, 0).astype(F32).astype(BF16)
    idx_ref[...] = dot(numbered, same.astype(BF16), ((1,), (0,))).astype(jnp.int32)

    def solve(rows):
        sweep(rows, count, x_ref, idx_ref, rank, size)
        taken = jnp.concatenate([hot[0:rows]] * 3, axis=0)
        full = dot(taken, jnp.concatenate(split3(x_ref[0:rows, :]), axis=0), ((0,), (0,)))
        full_ref[...] = jnp.where(same > 0.5, -full, 0.0)

    @pl.when(count <= SMALL)
    def _():
        solve(SMALL)

    @pl.when(count > SMALL)
    def _():
        solve(OBS_TILE)

    for copy in copies[3:]:
        copy.wait()
    innovation = mv_ref[...] + jnp.sqrt(var) * jit_ref[...] - pred
    high, mid, low = split3(innovation)
    full_high, full_mid, full_low = split3(full_ref[...])
    left = jnp.concatenate([low, mid, high, mid, high, high], axis=1)
    right = jnp.concatenate([full_high, full_mid, full_low, full_high, full_mid, full_high], axis=0)
    weighted = dot(left, right, ((1,), (0,)))
    out_ref[1] = weighted.astype(BF16)


def weigh(predicted, measured_value, measurement_variance, observation_jitter, obs_block, params):
    members = predicted.shape[2]
    return pl.pallas_call(
        weigh_kernel,
        out_shape=(jax.ShapeDtypeStruct((2, members, OBS_TILE), BF16), jax.ShapeDtypeStruct(params.shape, BF16)),
        in_specs=[pl.BlockSpec(memory_space=pltpu.HBM)] * 6,
        out_specs=(pl.BlockSpec(memory_space=pltpu.VMEM), pl.BlockSpec(memory_space=pltpu.VMEM)),
        scratch_shapes=[
            pltpu.VMEM((members, OBS_TILE), F32),
            pltpu.VMEM((1, OBS_TILE), F32),
            pltpu.VMEM((1, OBS_TILE), F32),
            pltpu.VMEM((members, OBS_TILE), F32),
            pltpu.VMEM((obs_block.shape[1], OBS_TILE), jnp.int32),
            pltpu.VMEM((OBS_TILE, OBS_TILE), F32),
            pltpu.VMEM((OBS_TILE, OBS_TILE), jnp.int32),
            pltpu.VMEM((OBS_TILE, OBS_TILE), F32),
            pltpu.SemaphoreType.DMA((6,)),
        ],
        compiler_params=pltpu.CompilerParams(vmem_limit_bytes=16 * 2**20),
        name="weigh",
    )(*in_hbm(predicted, measured_value, measurement_variance, observation_jitter, obs_block, params))


def offset(which, place):
    even = 1 - 2 * (place & 1)
    return (0, even, -even)[which]


def prepare_kernel(
    params_ref, radius_hbm, pattern_hbm, obs_hbm, turned_ref, taper_ref, radius_ref, pattern_ref, obs_ref, sems
):
    members = params_ref.shape[1]
    tile_x = lax.axis_index("gx")
    tile_y = lax.axis_index("gy")
    count_x, count_y = obs_ref.shape[0], obs_ref.shape[1]
    copies = fetch([(radius_hbm, radius_ref), (pattern_hbm, pattern_ref), (obs_hbm, obs_ref)], sems)

    for b in range(BLOCKS):
        block = params_ref[b].astype(F32)
        mean = jnp.sum(block, axis=0, keepdims=True) / members
        turned_ref[b] = (block - mean).T.astype(BF16)
    for copy in copies:
        copy.wait()
    shape = (BLOCKS, OBS_TILE)
    block = iota(shape, 0)
    radius = jnp.zeros(shape, jnp.int32)
    for b in range(BLOCKS):
        radius = jnp.where(block == b, radius_ref[b // BLK_Y, b % BLK_Y], radius)
    reach = (radius + 1).astype(F32)
    reach = reach * reach
    pattern = jnp.concatenate([pattern_ref[i] for i in range(BLK_X)], axis=0).astype(F32)
    slots = [jnp.broadcast_to(pattern[:, p : p + 1], shape) for p in range(PATTERN)]

    for t in range(9):
        iy, ix = t // 3, t % 3
        dx, dy = offset(ix, tile_x), offset(iy, tile_y)
        at_x, at_y = tile_x + dx, tile_y + dy
        valid = (at_x >= 0) & (at_x < count_x) & (at_y >= 0) & (at_y < count_y)
        at_x = jnp.clip(at_x, 0, count_x - 1)
        at_y = jnp.clip(at_y, 0, count_y - 1)
        obs = obs_ref[at_x, pl.ds(at_y, 1), :]
        step_x = dx * BLK_X + (obs >> 2) - (block >> 2)
        step_y = dy * BLK_Y + (obs & 3) - (block & 3)
        inside = (jnp.abs(step_x) <= 2) & (jnp.abs(step_y) <= 2) & valid
        slot = (step_x + 2) * 5 + (step_y + 2)
        picked = jnp.zeros(shape, F32)
        for p in range(PATTERN):
            picked = jnp.where(slot == p, slots[p], picked)
        spread = (step_x * step_x + step_y * step_y).astype(F32)
        shaped = jnp.maximum(1.0 - spread / reach, 0.0)
        taper_ref[iy, ix] = jnp.where(inside, picked, 0.0) * shaped / (members - 1)


def prepare(by_block, taper_radius, taper_pattern, obs_block):
    members = by_block.shape[1]
    return pl.pallas_call(
        prepare_kernel,
        out_shape=(
            jax.ShapeDtypeStruct((BLOCKS, CELLS, members), BF16),
            jax.ShapeDtypeStruct((3, 3, BLOCKS, OBS_TILE), F32),
        ),
        in_specs=[pl.BlockSpec(memory_space=pltpu.VMEM)] + [pl.BlockSpec(memory_space=pltpu.HBM)] * 3,
        out_specs=(pl.BlockSpec(memory_space=pltpu.VMEM), pl.BlockSpec(memory_space=pltpu.VMEM)),
        scratch_shapes=[
            pltpu.SMEM(taper_radius.shape, jnp.int32),
            pltpu.VMEM(taper_pattern.shape, jnp.int32),
            pltpu.VMEM(obs_block.shape, jnp.int32),
            pltpu.SemaphoreType.DMA((3,)),
        ],
        compiler_params=pltpu.CompilerParams(vmem_limit_bytes=16 * 2**20),
        cost_estimate=pl.CostEstimate(flops=4_000_000, bytes_accessed=1_000_000, transcendentals=0),
        name="prepare",
    )(by_block, *in_hbm(taper_radius, taper_pattern, obs_block))


def moved(b, which, turned_ref, taper_ref, tiles_refs):
    members = turned_ref.shape[2]
    turned = turned_ref[pl.ds(b, 2)].reshape(2 * CELLS, members)
    total, first = 0.0, 0
    for tiles_ref in tiles_refs:
        count = tiles_ref.shape[2] // OBS_TILE
        cross = dot(turned, tiles_ref[0], ((1,), (0,)))
        gains = []
        for k in range(2):
            tapers = [taper_ref[which, ix, pl.ds(b + k, 1), :] for ix in range(first, first + count)]
            gains.append((cross[k * CELLS : (k + 1) * CELLS] * jnp.concatenate(tapers, axis=1)).astype(BF16))
        total = total + dot(tiles_ref[1], jnp.concatenate(gains, axis=0), ((1,), (1,)))
        first += count
    return total


def first_of(side, tile_y):
    return 2 * ((tile_y & 1) ^ 1 ^ side)


def block_of(k, side, tile_y):
    return (k >> 1) * BLK_Y + first_of(side, tile_y) + (k & 1)


def target(chip, r, chips):
    return chip ^ r if chips & (chips - 1) == 0 else (chip + r) % chips


def source(chip, r, chips):
    return chip ^ r if chips & (chips - 1) == 0 else (chip + chips - r) % chips


def early_rounds(chips):
    return max(1, chips // 2)


def put(piece_refs, rows_ref, k, updated):
    chips, share = len(piece_refs), piece_refs[0].shape[2]
    mine = lax.axis_index("gy")
    rows_ref[k] = updated
    for r, ref in enumerate(piece_refs):
        for flip in (0, 1):
            owner = 2 * target(mine >> 1, r, chips) + ((mine & 1) ^ flip)
            ref[flip, k] = rows_ref[k, pl.ds(pl.multiple_of(owner * share, share), share), :]


def near_kernel(params_ref, turned_ref, taper_ref, own_ref, even_ref, part_ref, *refs):
    piece_refs, rows_ref = refs[:-1], refs[-1]
    tile_y = lax.axis_index("gy")
    for k in range(0, SIDE, 2):
        b = block_of(k, 0, tile_y)
        delta = moved(b, 0, turned_ref, taper_ref, [own_ref]) + moved(b, 1, turned_ref, taper_ref, [even_ref])
        for j in range(2):
            half = delta[:, j * CELLS : (j + 1) * CELLS]
            put(piece_refs, rows_ref, k + j, (params_ref[b + j].astype(F32) + half).astype(BF16))
    for k in range(0, SIDE, 2):
        b = block_of(k, 1, tile_y)
        delta = moved(b, 0, turned_ref, taper_ref, [own_ref])
        for j in range(2):
            part_ref[k + j] = params_ref[b + j].astype(F32) + delta[:, j * CELLS : (j + 1) * CELLS]


def far_kernel(late, turned_ref, taper_ref, odd_ref, beside_ref, part_ref, *refs):
    near_refs, refs, rows_ref = refs[:late], refs[late:-1], refs[-1]
    piece_refs = [halves(ref)[-1] for ref in refs]
    for near_ref, both_ref in zip(near_refs, refs[-late:]):
        both_ref[0] = near_ref[...]
    tile_y = lax.axis_index("gy")
    for k in range(0, SIDE, 2):
        delta = moved(block_of(k, 1, tile_y), 2, turned_ref, taper_ref, [odd_ref, beside_ref])
        for j in range(2):
            half = delta[:, j * CELLS : (j + 1) * CELLS]
            put(piece_refs, rows_ref, k + j, (part_ref[k + j] + half).astype(BF16))


def pack_kernel(*refs):
    at = 0
    for ref in refs[:-1]:
        for piece in halves(ref):
            refs[-1][at] = piece[1]
            at += 1


def halves(ref):
    return [ref] if len(ref.shape) == 4 else [ref.at[side] for side in range(ref.shape[0])]


def settle(chips, sides, refs, rows_ref):
    even_ref, pieces = refs[0], [piece for ref in refs[1:] for piece in halves(ref)]
    share = even_ref.shape[2]
    mine = lax.axis_index("gy")
    chip, core = mine >> 1, mine & 1
    line = 2 * chips * BLK_Y
    for at, ((side, r), own) in enumerate(zip(sides, pieces)):
        for flip in (0, 1):
            other = core ^ flip
            tile = 2 * source(chip, r, chips) + other
            for k in range(SIDE):
                piece = even_ref[at, k] if flip else own[0, k]
                start = (k >> 1) * line + tile * BLK_Y + first_of(side, other) + (k & 1)
                rows_ref[pl.ds(start, share, stride=BLK_X * line), :] = piece.astype(F32)


def early_kernel(chips, *refs):
    settle(chips, [(0, 0), (1, 0)] + [(0, r) for r in range(1, early_rounds(chips))], refs[:-1], refs[-1])


def late_kernel(chips, *refs):
    late_refs, out_hbm, rows_ref, out_ref, sems = refs[1:-4], *refs[-4:]
    sides = [(side, r) for r in range(chips - 1, 0, -1) for side in ((0, 1) if r >= early_rounds(chips) else (1,))]
    settle(chips, sides, late_refs, rows_ref)
    pieces = sems.shape[0]
    step = rows_ref.shape[0] // pieces
    copies = []
    for p in range(pieces):
        place = slice(p * step, (p + 1) * step)
        out_ref[place] = rows_ref[place].astype(BF16)
        copies.append(pltpu.make_async_copy(out_ref.at[pl.ds(p * step, step)], out_hbm.at[pl.ds(p * step, step)], sems.at[p]))
        copies[-1].start()
    for copy in copies:
        copy.wait()


VMEM = pl.BlockSpec(memory_space=pltpu.VMEM)
LONG = pl.CostEstimate(flops=4_000_000_000, bytes_accessed=10_000_000, transcendentals=0)
LIMIT = pltpu.CompilerParams(vmem_limit_bytes=24 * 2**20)


def update_near(by_block, turned, taper, own, even, parts):
    members = by_block.shape[1]
    pieces = [jax.ShapeDtypeStruct((2, SIDE, members // parts, CELLS), BF16)] * (parts // 2)
    return pl.pallas_call(
        near_kernel,
        out_shape=(jax.ShapeDtypeStruct((SIDE, members, CELLS), F32), *pieces),
        in_specs=[VMEM] * 5,
        out_specs=(VMEM,) * (1 + len(pieces)),
        scratch_shapes=[pltpu.VMEM((SIDE, members, CELLS), BF16)],
        compiler_params=LIMIT,
        cost_estimate=LONG,
        name="near",
    )(by_block, turned, taper, own, even)


def update_far(turned, taper, odd, beside, part, near):
    members = part.shape[1]
    chips = len(near)
    piece = jax.ShapeDtypeStruct(near[0].shape, BF16)
    both = jax.ShapeDtypeStruct((2, *piece.shape), BF16)
    late = chips - early_rounds(chips)
    shapes = [piece] * early_rounds(chips) + [both] * late
    return pl.pallas_call(
        functools.partial(far_kernel, late),
        out_shape=tuple(shapes),
        in_specs=[VMEM] * (5 + late),
        out_specs=(VMEM,) * chips,
        scratch_shapes=[pltpu.VMEM((SIDE, members, CELLS), BF16)],
        compiler_params=LIMIT,
        cost_estimate=LONG,
        name="far",
    )(turned, taper, odd, beside, part, *near[-late:])


def pack(pieces):
    count = sum(1 if piece.ndim == 4 else piece.shape[0] for piece in pieces)
    return pl.pallas_call(
        pack_kernel,
        out_shape=jax.ShapeDtypeStruct((count, *pieces[-1].shape[-3:]), BF16),
        in_specs=[VMEM] * len(pieces),
        out_specs=VMEM,
        compiler_params=LIMIT,
        name="pack",
    )(*pieces)


def gather(chips, early_even, early, late_even, late):
    share = early[0].shape[2]
    rows = share * BLOCKS * 2 * chips
    placed = pl.pallas_call(
        functools.partial(early_kernel, chips),
        out_shape=jax.ShapeDtypeStruct((rows, CELLS), F32),
        in_specs=[VMEM] * (1 + len(early)),
        out_specs=VMEM,
        compiler_params=LIMIT,
        name="early",
    )(early_even, *early)
    out, _ = pl.pallas_call(
        functools.partial(late_kernel, chips),
        out_shape=(jax.ShapeDtypeStruct((rows, CELLS), BF16), jax.ShapeDtypeStruct((rows, CELLS), F32)),
        in_specs=[VMEM] * (2 + len(late)),
        out_specs=(pl.BlockSpec(memory_space=pl.ANY), VMEM),
        scratch_shapes=[
            pltpu.VMEM((rows, CELLS), BF16),
            pltpu.SemaphoreType.DMA((4,)),
        ],
        input_output_aliases={0: 1},
        compiler_params=LIMIT,
        name="late",
    )(placed, late_even, *late)
    return out.reshape(share, BLK_X, 2 * chips * BLK_Y, CELLS)


def swap(block, axis):
    return lax.ppermute(block, axis, [(i, i ^ 1) for i in range(lax.axis_size(axis))])


def swap_odd(block, axis):
    rows, count = lax.axis_size("gx"), lax.axis_size("gy")
    pairs = []
    for x in range(rows):
        for y in range(count):
            if axis == "gy":
                to = (x, y + 1 if y % 2 else y - 1)
                to = to if 0 <= to[1] < count else (x ^ 1, y)
            else:
                to = (x + 1 if x % 2 else x - 1, y)
                to = to if 0 <= to[0] < rows else (x, y ^ 1)
            pairs.append((x * count + y, to[0] * count + to[1]))
    return lax.ppermute(block, ("gx", "gy"), pairs)


def hop(piece, r):
    count = lax.axis_size("gy")
    pairs = [(i, 2 * target(i // 2, r, count // 2) + i % 2) for i in range(count)]
    return lax.ppermute(piece, "gy", pairs)


def per_device(
    params,
    predicted,
    measured_value,
    measurement_variance,
    observation_jitter,
    obs_block,
    taper_radius,
    taper_pattern,
):
    members = params.shape[0]
    parts = lax.axis_size("gy")
    own, params = weigh(
        predicted, measured_value, measurement_variance, observation_jitter, obs_block, params
    )
    by_block = params.reshape(members, BLOCKS, CELLS).transpose(1, 0, 2)
    sent, by_block = lax.optimization_barrier((own, by_block))
    across = swap_odd(sent, "gy")
    even = swap(own, "gx")
    odd = swap_odd(own, "gx")
    turned, taper = prepare(by_block, taper_radius, taper_pattern, obs_block)
    beside, column = jnp.concatenate([even, odd], axis=2), jnp.concatenate([own, even, odd], axis=2)
    beside, column, across, turned, taper = lax.optimization_barrier((beside, column, across, turned, taper))
    even = swap(column, "gy")
    beside = swap_odd(beside, "gy")
    part, *near = update_near(by_block, turned, taper, column, even, parts)
    chips = parts // 2
    near_hops = [hop(near[r], r) for r in range(1, early_rounds(chips))]
    far = list(update_far(turned, taper, across, beside, part, near))
    if near_hops:
        far[1], near_hops = lax.optimization_barrier((far[1], near_hops))
    early = [near[0], far[0], *near_hops]
    late = [hop(far[r], r) for r in range(chips - 1, 0, -1)]
    early_even = swap(pack(early), "gy")
    late, early_even = lax.optimization_barrier((late, early_even))
    late_even = swap(pack(late), "gy")
    return gather(chips, early_even, early, late_even, late)


def solution(mesh):
    placed = (
        P(None, "gx", "gy", None),
        P("gx", "gy", None, None),
        P("gx", "gy", None),
        P("gx", "gy", None),
        P("gx", "gy", None, None),
        P(),
        P("gx", "gy"),
        P("gx", "gy", None),
    )
    return jax.shard_map(
        per_device, mesh=mesh, in_specs=placed, out_specs=P("gy", "gx", None, None), check_vma=False
    )
```

```python
import functools

import jax
import jax.numpy as jnp
from jax import lax
from jax.experimental import pallas as pl
from jax.experimental.pallas import tpu as pltpu
from jax.sharding import PartitionSpec as P

CELLS = 128
BLK_X = 2
BLK_Y = 4
BLOCKS = BLK_X * BLK_Y
SIDE = BLOCKS // 2
OBS_TILE = 128
PATTERN = 25
SMALL = 32

F32 = jnp.float32
BF16 = jnp.bfloat16


def iota(shape, dim):
    return lax.broadcasted_iota(jnp.int32, shape, dim)


def split3(x):
    high = x.astype(BF16)
    rest = x - high.astype(F32)
    mid = rest.astype(BF16)
    low = (rest - mid.astype(F32)).astype(BF16)
    return high, mid, low


def dot(a, b, dims):
    return lax.dot_general(a, b, (dims, ((), ())), preferred_element_type=F32)


def sweep(rows, count, x_ref, idx_ref, rank, size):
    row = iota((rows, OBS_TILE), 0)
    exists = row < size

    def taken(spread, indices):
        return jnp.take_along_axis(spread, indices, axis=1, mode="promise_in_bounds")

    def step(k, carry):
        t = 2 * k
        u = t + 1
        row_t, row_u = x_ref[pl.ds(t, 1), :], x_ref[pl.ds(u, 1), :]
        spread_t = jnp.broadcast_to(row_t, (rows, OBS_TILE))
        spread_u = jnp.broadcast_to(row_u, (rows, OBS_TILE))
        at_t = jnp.broadcast_to(idx_ref[pl.ds(t, 1), :], (8, OBS_TILE))
        at_u = jnp.broadcast_to(idx_ref[pl.ds(u, 1), :], (8, OBS_TILE))
        has_t, has_u = t < size, u < size
        a = jnp.where(has_t, taken(spread_t[0:8], at_t)[0:1], 1.0)
        b = jnp.where(has_u, taken(spread_t[0:8], at_u)[0:1], 0.0)
        d = jnp.where(has_u, taken(spread_u[0:8], at_u)[0:1], 1.0)
        own_t, own_u = rank == t, rank == u
        own = own_t | own_u
        head_t = jnp.where(own, jnp.where(own_t, -1.0, 0.0), row_t)
        head_u = jnp.where(own, jnp.where(own_u, -1.0, 0.0), row_u)
        inverse = 1.0 / a
        factor = b * inverse
        scaled_u = (head_u - factor * head_t) / (d - b * factor)
        scaled_t = head_t * inverse - factor * scaled_u
        column_t = jnp.where(exists, taken(spread_t, idx_ref[0:rows, :]), 0.0)
        column_u = jnp.where(exists, taken(spread_u, idx_ref[0:rows, :]), 0.0)
        on_t, on_u = row == t, row == u
        on = on_t | on_u
        column_t = jnp.where(on, jnp.where(on_t, -1.0, 0.0), column_t)
        column_u = jnp.where(on, jnp.where(on_u, -1.0, 0.0), column_u)
        x = jnp.where(on | own, 0.0, x_ref[0:rows, :])
        x_ref[0:rows, :] = x - column_t * scaled_t - column_u * scaled_u
        return carry

    lax.fori_loop(0, (count + 1) // 2, step, 0)


def in_hbm(*arrays):
    return [pltpu.with_memory_space_constraint(array, pltpu.HBM) for array in arrays]


def fetch(pairs, sems):
    copies = [pltpu.make_async_copy(src, dst, sems.at[k]) for k, (src, dst) in enumerate(pairs)]
    for copy in copies:
        copy.start()
    return copies


def weigh_kernel(
    pred_hbm, mv_hbm, var_hbm, jit_hbm, obs_hbm, params_hbm, out_ref, params_ref,
    pred_ref, mv_ref, var_ref, jit_ref, obs_ref, x_ref, idx_ref, full_ref, sems,
):
    members = pred_ref.shape[0]
    tile_x = lax.axis_index("gx")
    tile_y = lax.axis_index("gy")
    square = (OBS_TILE, OBS_TILE)
    pairs = [
        (pred_hbm.at[0, 0], pred_ref),
        (obs_hbm.at[tile_x], obs_ref),
        (var_hbm.at[0], var_ref),
        (mv_hbm.at[0], mv_ref),
        (jit_hbm.at[0, 0], jit_ref),
        (params_hbm, params_ref),
    ]
    copies = fetch(pairs, sems)
    for copy in copies[:3]:
        copy.wait()
    pred = pred_ref[...]
    var = var_ref[...]
    mean = jnp.sum(pred, axis=0, keepdims=True) / members
    deviation = (pred - mean).astype(BF16)
    out_ref[0] = deviation
    obs = obs_ref[pl.ds(tile_y, 1), :]
    groups = (iota((BLOCKS, OBS_TILE), 0) == obs).astype(BF16)
    same = dot(groups, groups, ((0,), (0,)))
    gram = dot(deviation, deviation, ((0,), (0,))) / (members - 1)
    row, col = iota(square, 0), iota(square, 1)
    system = jnp.where(same > 0.5, gram, 0.0) + jnp.where(row == col, var, 0.0)
    size = jnp.sum(same, axis=0, keepdims=True)
    count = jnp.max(size).astype(jnp.int32)
    size = size.astype(jnp.int32)
    rank = jnp.sum(jnp.where(row < col, same, 0.0), axis=0, keepdims=True).astype(jnp.int32)
    place = row == rank
    hot = place.astype(BF16)
    x_ref[...] = dot(jnp.concatenate([hot] * 3, axis=1), jnp.concatenate(split3(system), axis=0), ((1,), (0,)))
    numbered = jnp.where(place, col, 0).astype(F32).astype(BF16)
    idx_ref[...] = dot(numbered, same.astype(BF16), ((1,), (0,))).astype(jnp.int32)

    def solve(rows):
        sweep(rows, count, x_ref, idx_ref, rank, size)
        taken = jnp.concatenate([hot[0:rows]] * 3, axis=0)
        full = dot(taken, jnp.concatenate(split3(x_ref[0:rows, :]), axis=0), ((0,), (0,)))
        full_ref[...] = jnp.where(same > 0.5, -full, 0.0)

    @pl.when(count <= SMALL)
    def _():
        solve(SMALL)

    @pl.when(count > SMALL)
    def _():
        solve(OBS_TILE)

    for copy in copies[3:]:
        copy.wait()
    innovation = mv_ref[...] + jnp.sqrt(var) * jit_ref[...] - pred
    high, mid, low = split3(innovation)
    full_high, full_mid, full_low = split3(full_ref[...])
    left = jnp.concatenate([low, mid, high, mid, high, high], axis=1)
    right = jnp.concatenate([full_high, full_mid, full_low, full_high, full_mid, full_high], axis=0)
    weighted = dot(left, right, ((1,), (0,)))
    out_ref[1] = weighted.astype(BF16)


def weigh(predicted, measured_value, measurement_variance, observation_jitter, obs_block, params):
    members = predicted.shape[2]
    return pl.pallas_call(
        weigh_kernel,
        out_shape=(jax.ShapeDtypeStruct((2, members, OBS_TILE), BF16), jax.ShapeDtypeStruct(params.shape, BF16)),
        in_specs=[pl.BlockSpec(memory_space=pltpu.HBM)] * 6,
        out_specs=(pl.BlockSpec(memory_space=pltpu.VMEM), pl.BlockSpec(memory_space=pltpu.VMEM)),
        scratch_shapes=[
            pltpu.VMEM((members, OBS_TILE), F32),
            pltpu.VMEM((1, OBS_TILE), F32),
            pltpu.VMEM((1, OBS_TILE), F32),
            pltpu.VMEM((members, OBS_TILE), F32),
            pltpu.VMEM((obs_block.shape[1], OBS_TILE), jnp.int32),
            pltpu.VMEM((OBS_TILE, OBS_TILE), F32),
            pltpu.VMEM((OBS_TILE, OBS_TILE), jnp.int32),
            pltpu.VMEM((OBS_TILE, OBS_TILE), F32),
            pltpu.SemaphoreType.DMA((6,)),
        ],
        compiler_params=pltpu.CompilerParams(vmem_limit_bytes=16 * 2**20),
        name="weigh",
    )(*in_hbm(predicted, measured_value, measurement_variance, observation_jitter, obs_block, params))


def offset(which, place):
    even = 1 - 2 * (place & 1)
    return (0, even, -even)[which]


def prepare_kernel(
    params_ref, radius_hbm, pattern_hbm, obs_hbm, turned_ref, taper_ref, radius_ref, pattern_ref, obs_ref, sems
):
    members = params_ref.shape[1]
    tile_x = lax.axis_index("gx")
    tile_y = lax.axis_index("gy")
    count_x, count_y = obs_ref.shape[0], obs_ref.shape[1]
    copies = fetch([(radius_hbm, radius_ref), (pattern_hbm, pattern_ref), (obs_hbm, obs_ref)], sems)

    for b in range(BLOCKS):
        block = params_ref[b].astype(F32)
        mean = jnp.sum(block, axis=0, keepdims=True) / members
        turned_ref[b] = (block - mean).T.astype(BF16)
    for copy in copies:
        copy.wait()
    shape = (BLOCKS, OBS_TILE)
    block = iota(shape, 0)
    radius = jnp.zeros(shape, jnp.int32)
    for b in range(BLOCKS):
        radius = jnp.where(block == b, radius_ref[b // BLK_Y, b % BLK_Y], radius)
    reach = (radius + 1).astype(F32)
    reach = reach * reach
    pattern = jnp.concatenate([pattern_ref[i] for i in range(BLK_X)], axis=0).astype(F32)
    slots = [jnp.broadcast_to(pattern[:, p : p + 1], shape) for p in range(PATTERN)]

    for t in range(9):
        iy, ix = t // 3, t % 3
        dx, dy = offset(ix, tile_x), offset(iy, tile_y)
        at_x, at_y = tile_x + dx, tile_y + dy
        valid = (at_x >= 0) & (at_x < count_x) & (at_y >= 0) & (at_y < count_y)
        at_x = jnp.clip(at_x, 0, count_x - 1)
        at_y = jnp.clip(at_y, 0, count_y - 1)
        obs = obs_ref[at_x, pl.ds(at_y, 1), :]
        step_x = dx * BLK_X + (obs >> 2) - (block >> 2)
        step_y = dy * BLK_Y + (obs & 3) - (block & 3)
        inside = (jnp.abs(step_x) <= 2) & (jnp.abs(step_y) <= 2) & valid
        slot = (step_x + 2) * 5 + (step_y + 2)
        picked = jnp.zeros(shape, F32)
        for p in range(PATTERN):
            picked = jnp.where(slot == p, slots[p], picked)
        spread = (step_x * step_x + step_y * step_y).astype(F32)
        shaped = jnp.maximum(1.0 - spread / reach, 0.0)
        taper_ref[iy, ix] = jnp.where(inside, picked, 0.0) * shaped / (members - 1)


def prepare(by_block, taper_radius, taper_pattern, obs_block):
    members = by_block.shape[1]
    return pl.pallas_call(
        prepare_kernel,
        out_shape=(
            jax.ShapeDtypeStruct((BLOCKS, CELLS, members), BF16),
            jax.ShapeDtypeStruct((3, 3, BLOCKS, OBS_TILE), F32),
        ),
        in_specs=[pl.BlockSpec(memory_space=pltpu.VMEM)] + [pl.BlockSpec(memory_space=pltpu.HBM)] * 3,
        out_specs=(pl.BlockSpec(memory_space=pltpu.VMEM), pl.BlockSpec(memory_space=pltpu.VMEM)),
        scratch_shapes=[
            pltpu.SMEM(taper_radius.shape, jnp.int32),
            pltpu.VMEM(taper_pattern.shape, jnp.int32),
            pltpu.VMEM(obs_block.shape, jnp.int32),
            pltpu.SemaphoreType.DMA((3,)),
        ],
        compiler_params=pltpu.CompilerParams(vmem_limit_bytes=16 * 2**20),
        cost_estimate=pl.CostEstimate(flops=4_000_000, bytes_accessed=1_000_000, transcendentals=0),
        name="prepare",
    )(by_block, *in_hbm(taper_radius, taper_pattern, obs_block))


def moved(b, which, turned_ref, taper_ref, tiles_refs):
    members = turned_ref.shape[2]
    turned = turned_ref[pl.ds(b, 2)].reshape(2 * CELLS, members)
    total, first = 0.0, 0
    for tiles_ref in tiles_refs:
        count = tiles_ref.shape[2] // OBS_TILE
        cross = dot(turned, tiles_ref[0], ((1,), (0,)))
        gains = []
        for k in range(2):
            tapers = [taper_ref[which, ix, pl.ds(b + k, 1), :] for ix in range(first, first + count)]
            gains.append((cross[k * CELLS : (k + 1) * CELLS] * jnp.concatenate(tapers, axis=1)).astype(BF16))
        total = total + dot(tiles_ref[1], jnp.concatenate(gains, axis=0), ((1,), (1,)))
        first += count
    return total


def first_of(side, tile_y):
    return 2 * ((tile_y & 1) ^ 1 ^ side)


def block_of(k, side, tile_y):
    return (k >> 1) * BLK_Y + first_of(side, tile_y) + (k & 1)


def target(chip, r, chips):
    return chip ^ r if chips & (chips - 1) == 0 else (chip + r) % chips


def source(chip, r, chips):
    return chip ^ r if chips & (chips - 1) == 0 else (chip + chips - r) % chips


def put(piece_refs, rows_ref, k, updated):
    chips, share = len(piece_refs), piece_refs[0].shape[2]
    mine = lax.axis_index("gy")
    rows_ref[k] = updated
    for r, ref in enumerate(piece_refs):
        for flip in (0, 1):
            owner = 2 * target(mine >> 1, r, chips) + ((mine & 1) ^ flip)
            ref[flip, k] = rows_ref[k, pl.ds(pl.multiple_of(owner * share, share), share), :]


def near_kernel(params_ref, turned_ref, taper_ref, own_ref, even_ref, part_ref, *refs):
    piece_refs, rows_ref = refs[:-1], refs[-1]
    tile_y = lax.axis_index("gy")
    for k in range(0, SIDE, 2):
        b = block_of(k, 0, tile_y)
        delta = moved(b, 0, turned_ref, taper_ref, [own_ref]) + moved(b, 1, turned_ref, taper_ref, [even_ref])
        for j in range(2):
            half = delta[:, j * CELLS : (j + 1) * CELLS]
            put(piece_refs, rows_ref, k + j, (params_ref[b + j].astype(F32) + half).astype(BF16))
    for k in range(0, SIDE, 2):
        b = block_of(k, 1, tile_y)
        delta = moved(b, 0, turned_ref, taper_ref, [own_ref])
        for j in range(2):
            part_ref[k + j] = params_ref[b + j].astype(F32) + delta[:, j * CELLS : (j + 1) * CELLS]


def far_kernel(turned_ref, taper_ref, odd_ref, beside_ref, part_ref, first_ref, last_ref, *refs):
    rows_ref, refs = refs[-1], refs[:-1]
    piece_refs = [halves(ref)[-1] for ref in refs]
    refs[1][0] = first_ref[...]
    refs[-1][0] = last_ref[...]
    tile_y = lax.axis_index("gy")
    for k in range(0, SIDE, 2):
        delta = moved(block_of(k, 1, tile_y), 2, turned_ref, taper_ref, [odd_ref, beside_ref])
        for j in range(2):
            half = delta[:, j * CELLS : (j + 1) * CELLS]
            put(piece_refs, rows_ref, k + j, (part_ref[k + j] + half).astype(BF16))


def pack_kernel(*refs):
    at = 0
    for ref in refs[:-1]:
        for piece in halves(ref):
            refs[-1][at] = piece[1]
            at += 1


def halves(ref):
    return [ref] if len(ref.shape) == 4 else [ref.at[side] for side in range(ref.shape[0])]


def settle(chips, sides, refs, rows_ref):
    even_ref, pieces = refs[0], [piece for ref in refs[1:] for piece in halves(ref)]
    share = even_ref.shape[2]
    mine = lax.axis_index("gy")
    chip, core = mine >> 1, mine & 1
    line = 2 * chips * BLK_Y
    for at, ((side, r), own) in enumerate(zip(sides, pieces)):
        for flip in (0, 1):
            other = core ^ flip
            tile = 2 * source(chip, r, chips) + other
            for k in range(SIDE):
                piece = even_ref[at, k] if flip else own[0, k]
                start = (k >> 1) * line + tile * BLK_Y + first_of(side, other) + (k & 1)
                rows_ref[pl.ds(start, share, stride=BLK_X * line), :] = piece.astype(F32)


def early_kernel(chips, *refs):
    settle(chips, [(0, 0), (1, 0)] + [(0, r) for r in range(2, chips - 1)], refs[:-1], refs[-1])


def late_kernel(chips, *refs):
    late_refs, out_hbm, rows_ref, out_ref, sems = refs[1:-4], *refs[-4:]
    sides = [(side, r) for r in range(chips - 1, 0, -1) for side in ((0, 1) if r in (1, chips - 1) else (1,))]
    settle(chips, sides, late_refs, rows_ref)
    pieces = sems.shape[0]
    step = rows_ref.shape[0] // pieces
    copies = []
    for p in range(pieces):
        place = slice(p * step, (p + 1) * step)
        out_ref[place] = rows_ref[place].astype(BF16)
        copies.append(pltpu.make_async_copy(out_ref.at[pl.ds(p * step, step)], out_hbm.at[pl.ds(p * step, step)], sems.at[p]))
        copies[-1].start()
    for copy in copies:
        copy.wait()


VMEM = pl.BlockSpec(memory_space=pltpu.VMEM)
LONG = pl.CostEstimate(flops=4_000_000_000, bytes_accessed=10_000_000, transcendentals=0)
LIMIT = pltpu.CompilerParams(vmem_limit_bytes=24 * 2**20)


def update_near(by_block, turned, taper, own, even, parts):
    members = by_block.shape[1]
    pieces = [jax.ShapeDtypeStruct((2, SIDE, members // parts, CELLS), BF16)] * (parts // 2)
    return pl.pallas_call(
        near_kernel,
        out_shape=(jax.ShapeDtypeStruct((SIDE, members, CELLS), F32), *pieces),
        in_specs=[VMEM] * 5,
        out_specs=(VMEM,) * (1 + len(pieces)),
        scratch_shapes=[pltpu.VMEM((SIDE, members, CELLS), BF16)],
        compiler_params=LIMIT,
        cost_estimate=LONG,
        name="near",
    )(by_block, turned, taper, own, even)


def update_far(turned, taper, odd, beside, part, near):
    members = part.shape[1]
    chips = len(near)
    piece = jax.ShapeDtypeStruct(near[0].shape, BF16)
    both = jax.ShapeDtypeStruct((2, *piece.shape), BF16)
    shapes = [both if r in (1, chips - 1) else piece for r in range(chips)]
    return pl.pallas_call(
        far_kernel,
        out_shape=tuple(shapes),
        in_specs=[VMEM] * 7,
        out_specs=(VMEM,) * chips,
        scratch_shapes=[pltpu.VMEM((SIDE, members, CELLS), BF16)],
        compiler_params=LIMIT,
        cost_estimate=LONG,
        name="far",
    )(turned, taper, odd, beside, part, near[1], near[-1])


def pack(pieces):
    count = sum(1 if piece.ndim == 4 else piece.shape[0] for piece in pieces)
    return pl.pallas_call(
        pack_kernel,
        out_shape=jax.ShapeDtypeStruct((count, *pieces[-1].shape[-3:]), BF16),
        in_specs=[VMEM] * len(pieces),
        out_specs=VMEM,
        compiler_params=LIMIT,
        name="pack",
    )(*pieces)


def gather(chips, early_even, early, late_even, late):
    share = early[0].shape[2]
    rows = share * BLOCKS * 2 * chips
    placed = pl.pallas_call(
        functools.partial(early_kernel, chips),
        out_shape=jax.ShapeDtypeStruct((rows, CELLS), F32),
        in_specs=[VMEM] * (1 + len(early)),
        out_specs=VMEM,
        compiler_params=LIMIT,
        name="early",
    )(early_even, *early)
    out, _ = pl.pallas_call(
        functools.partial(late_kernel, chips),
        out_shape=(jax.ShapeDtypeStruct((rows, CELLS), BF16), jax.ShapeDtypeStruct((rows, CELLS), F32)),
        in_specs=[VMEM] * (2 + len(late)),
        out_specs=(pl.BlockSpec(memory_space=pl.ANY), VMEM),
        scratch_shapes=[
            pltpu.VMEM((rows, CELLS), BF16),
            pltpu.SemaphoreType.DMA((4,)),
        ],
        input_output_aliases={0: 1},
        compiler_params=LIMIT,
        name="late",
    )(placed, late_even, *late)
    return out.reshape(share, BLK_X, 2 * chips * BLK_Y, CELLS)


def swap(block, axis):
    return lax.ppermute(block, axis, [(i, i ^ 1) for i in range(lax.axis_size(axis))])


def swap_odd(block, axis):
    rows, count = lax.axis_size("gx"), lax.axis_size("gy")
    pairs = []
    for x in range(rows):
        for y in range(count):
            if axis == "gy":
                to = (x, y + 1 if y % 2 else y - 1)
                to = to if 0 <= to[1] < count else (x ^ 1, y)
            else:
                to = (x + 1 if x % 2 else x - 1, y)
                to = to if 0 <= to[0] < rows else (x, y ^ 1)
            pairs.append((x * count + y, to[0] * count + to[1]))
    return lax.ppermute(block, ("gx", "gy"), pairs)


def hop(piece, r):
    count = lax.axis_size("gy")
    pairs = [(i, 2 * target(i // 2, r, count // 2) + i % 2) for i in range(count)]
    return lax.ppermute(piece, "gy", pairs)


def per_device(
    params,
    predicted,
    measured_value,
    measurement_variance,
    observation_jitter,
    obs_block,
    taper_radius,
    taper_pattern,
):
    members = params.shape[0]
    parts = lax.axis_size("gy")
    own, params = weigh(
        predicted, measured_value, measurement_variance, observation_jitter, obs_block, params
    )
    by_block = params.reshape(members, BLOCKS, CELLS).transpose(1, 0, 2)
    sent, by_block = lax.optimization_barrier((own, by_block))
    across = swap_odd(sent, "gy")
    even = swap(own, "gx")
    odd = swap_odd(own, "gx")
    turned, taper = prepare(by_block, taper_radius, taper_pattern, obs_block)
    beside, column = jnp.concatenate([even, odd], axis=2), jnp.concatenate([own, even, odd], axis=2)
    beside, column, across, turned, taper = lax.optimization_barrier((beside, column, across, turned, taper))
    even = swap(column, "gy")
    beside = swap_odd(beside, "gy")
    part, *near = update_near(by_block, turned, taper, column, even, parts)
    chips = parts // 2
    near_hops = [hop(near[r], r) for r in range(2, chips - 1)]
    far = list(update_far(turned, taper, across, beside, part, near))
    for r in range(2, chips - 1):
        far[r], near_hops[r - 2] = lax.optimization_barrier((far[r], near_hops[r - 2]))
    early = [near[0], far[0], *near_hops]
    late = [hop(far[r], r) for r in range(chips - 1, 0, -1)]
    early_even = swap(pack(early), "gy")
    late, early_even = lax.optimization_barrier((late, early_even))
    late_even = swap(pack(late), "gy")
    return gather(chips, early_even, early, late_even, late)


def solution(mesh):
    placed = (
        P(None, "gx", "gy", None),
        P("gx", "gy", None, None),
        P("gx", "gy", None),
        P("gx", "gy", None),
        P("gx", "gy", None, None),
        P(),
        P("gx", "gy"),
        P("gx", "gy", None),
    )
    return jax.shard_map(
        per_device, mesh=mesh, in_specs=placed, out_specs=P("gy", "gx", None, None), check_vma=False
    )
```

```python
import functools

import jax
import jax.numpy as jnp
from jax import lax
from jax.experimental import pallas as pl
from jax.experimental.pallas import tpu as pltpu
from jax.sharding import PartitionSpec as P

CELLS = 128
BLK_X = 2
BLK_Y = 4
BLOCKS = BLK_X * BLK_Y
SIDE = BLOCKS // 2
OBS_TILE = 128
PATTERN = 25
SMALL = 32

F32 = jnp.float32
BF16 = jnp.bfloat16


def iota(shape, dim):
    return lax.broadcasted_iota(jnp.int32, shape, dim)


def split3(x):
    high = x.astype(BF16)
    rest = x - high.astype(F32)
    mid = rest.astype(BF16)
    low = (rest - mid.astype(F32)).astype(BF16)
    return high, mid, low


def dot(a, b, dims):
    return lax.dot_general(a, b, (dims, ((), ())), preferred_element_type=F32)


def sweep(rows, count, x_ref, idx_ref, rank, size):
    row = iota((rows, OBS_TILE), 0)
    exists = row < size

    def taken(spread, indices):
        return jnp.take_along_axis(spread, indices, axis=1, mode="promise_in_bounds")

    def step(k, carry):
        t = 2 * k
        u = t + 1
        row_t, row_u = x_ref[pl.ds(t, 1), :], x_ref[pl.ds(u, 1), :]
        spread_t = jnp.broadcast_to(row_t, (rows, OBS_TILE))
        spread_u = jnp.broadcast_to(row_u, (rows, OBS_TILE))
        at_t = jnp.broadcast_to(idx_ref[pl.ds(t, 1), :], (8, OBS_TILE))
        at_u = jnp.broadcast_to(idx_ref[pl.ds(u, 1), :], (8, OBS_TILE))
        has_t, has_u = t < size, u < size
        a = jnp.where(has_t, taken(spread_t[0:8], at_t)[0:1], 1.0)
        b = jnp.where(has_u, taken(spread_t[0:8], at_u)[0:1], 0.0)
        d = jnp.where(has_u, taken(spread_u[0:8], at_u)[0:1], 1.0)
        own_t, own_u = rank == t, rank == u
        own = own_t | own_u
        head_t = jnp.where(own, jnp.where(own_t, -1.0, 0.0), row_t)
        head_u = jnp.where(own, jnp.where(own_u, -1.0, 0.0), row_u)
        inverse = 1.0 / a
        factor = b * inverse
        scaled_u = (head_u - factor * head_t) / (d - b * factor)
        scaled_t = head_t * inverse - factor * scaled_u
        column_t = jnp.where(exists, taken(spread_t, idx_ref[0:rows, :]), 0.0)
        column_u = jnp.where(exists, taken(spread_u, idx_ref[0:rows, :]), 0.0)
        on_t, on_u = row == t, row == u
        on = on_t | on_u
        column_t = jnp.where(on, jnp.where(on_t, -1.0, 0.0), column_t)
        column_u = jnp.where(on, jnp.where(on_u, -1.0, 0.0), column_u)
        x = jnp.where(on | own, 0.0, x_ref[0:rows, :])
        x_ref[0:rows, :] = x - column_t * scaled_t - column_u * scaled_u
        return carry

    lax.fori_loop(0, (count + 1) // 2, step, 0)


def in_hbm(*arrays):
    return [pltpu.with_memory_space_constraint(array, pltpu.HBM) for array in arrays]


def fetch(pairs, sems):
    copies = [pltpu.make_async_copy(src, dst, sems.at[k]) for k, (src, dst) in enumerate(pairs)]
    for copy in copies:
        copy.start()
    return copies


def weigh_kernel(
    pred_hbm, mv_hbm, var_hbm, jit_hbm, obs_hbm, params_hbm, out_ref, params_ref,
    pred_ref, mv_ref, var_ref, jit_ref, obs_ref, x_ref, idx_ref, full_ref, left_ref, sems,
):
    members = pred_ref.shape[0]
    tile_x = lax.axis_index("gx")
    tile_y = lax.axis_index("gy")
    square = (OBS_TILE, OBS_TILE)
    pairs = [
        (pred_hbm.at[0, 0], pred_ref),
        (obs_hbm.at[tile_x], obs_ref),
        (var_hbm.at[0], var_ref),
        (mv_hbm.at[0], mv_ref),
        (jit_hbm.at[0, 0], jit_ref),
        (params_hbm, params_ref),
    ]
    copies = fetch(pairs, sems)
    for copy in copies[:5]:
        copy.wait()
    pred = pred_ref[...]
    var = var_ref[...]
    mean = jnp.sum(pred, axis=0, keepdims=True) / members
    deviation = (pred - mean).astype(BF16)
    out_ref[0] = deviation
    obs = obs_ref[pl.ds(tile_y, 1), :]
    groups = (iota((BLOCKS, OBS_TILE), 0) == obs).astype(BF16)
    same = dot(groups, groups, ((0,), (0,)))
    gram = dot(deviation, deviation, ((0,), (0,))) / (members - 1)
    row, col = iota(square, 0), iota(square, 1)
    system = jnp.where(same > 0.5, gram, 0.0) + jnp.where(row == col, var, 0.0)
    size = jnp.sum(same, axis=0, keepdims=True)
    count = jnp.max(size).astype(jnp.int32)
    size = size.astype(jnp.int32)
    rank = jnp.sum(jnp.where(row < col, same, 0.0), axis=0, keepdims=True).astype(jnp.int32)
    place = row == rank
    hot = place.astype(BF16)
    x_ref[...] = dot(jnp.concatenate([hot] * 3, axis=1), jnp.concatenate(split3(system), axis=0), ((1,), (0,)))
    numbered = jnp.where(place, col, 0).astype(F32).astype(BF16)
    idx_ref[...] = dot(numbered, same.astype(BF16), ((1,), (0,))).astype(jnp.int32)

    innovation = mv_ref[...] + jnp.sqrt(var) * jit_ref[...] - pred
    high, mid, low = split3(innovation)
    left_ref[...] = jnp.concatenate([low, mid, high, mid, high, high], axis=1)

    def solve(rows):
        sweep(rows, count, x_ref, idx_ref, rank, size)
        taken = jnp.concatenate([hot[0:rows]] * 3, axis=0)
        full = dot(taken, jnp.concatenate(split3(x_ref[0:rows, :]), axis=0), ((0,), (0,)))
        full_ref[...] = jnp.where(same > 0.5, -full, 0.0)

    @pl.when(count <= SMALL)
    def _():
        solve(SMALL)

    @pl.when(count > SMALL)
    def _():
        solve(OBS_TILE)

    full_high, full_mid, full_low = split3(full_ref[...])
    right = jnp.concatenate([full_high, full_mid, full_low, full_high, full_mid, full_high], axis=0)
    weighted = dot(left_ref[...], right, ((1,), (0,)))
    out_ref[1] = weighted.astype(BF16)
    copies[5].wait()


def weigh(predicted, measured_value, measurement_variance, observation_jitter, obs_block, params):
    members = predicted.shape[2]
    return pl.pallas_call(
        weigh_kernel,
        out_shape=(jax.ShapeDtypeStruct((2, members, OBS_TILE), BF16), jax.ShapeDtypeStruct(params.shape, BF16)),
        in_specs=[pl.BlockSpec(memory_space=pltpu.HBM)] * 6,
        out_specs=(pl.BlockSpec(memory_space=pltpu.VMEM), pl.BlockSpec(memory_space=pltpu.VMEM)),
        scratch_shapes=[
            pltpu.VMEM((members, OBS_TILE), F32),
            pltpu.VMEM((1, OBS_TILE), F32),
            pltpu.VMEM((1, OBS_TILE), F32),
            pltpu.VMEM((members, OBS_TILE), F32),
            pltpu.VMEM((obs_block.shape[1], OBS_TILE), jnp.int32),
            pltpu.VMEM((OBS_TILE, OBS_TILE), F32),
            pltpu.VMEM((OBS_TILE, OBS_TILE), jnp.int32),
            pltpu.VMEM((OBS_TILE, OBS_TILE), F32),
            pltpu.VMEM((members, 6 * OBS_TILE), BF16),
            pltpu.SemaphoreType.DMA((6,)),
        ],
        compiler_params=pltpu.CompilerParams(vmem_limit_bytes=16 * 2**20),
        name="weigh",
    )(*in_hbm(predicted, measured_value, measurement_variance, observation_jitter, obs_block, params))


def offset(which, place):
    even = 1 - 2 * (place & 1)
    return (0, even, -even)[which]


def prepare_kernel(
    params_ref, radius_hbm, pattern_hbm, obs_hbm, turned_ref, taper_ref, radius_ref, pattern_ref, obs_ref, sems
):
    members = params_ref.shape[1]
    tile_x = lax.axis_index("gx")
    tile_y = lax.axis_index("gy")
    count_x, count_y = obs_ref.shape[0], obs_ref.shape[1]
    copies = fetch([(radius_hbm, radius_ref), (pattern_hbm, pattern_ref), (obs_hbm, obs_ref)], sems)

    for b in range(BLOCKS):
        block = params_ref[b].astype(F32)
        mean = jnp.sum(block, axis=0, keepdims=True) / members
        turned_ref[b] = (block - mean).T.astype(BF16)
    for copy in copies:
        copy.wait()
    shape = (BLOCKS, OBS_TILE)
    block = iota(shape, 0)
    radius = jnp.zeros(shape, jnp.int32)
    for b in range(BLOCKS):
        radius = jnp.where(block == b, radius_ref[b // BLK_Y, b % BLK_Y], radius)
    reach = (radius + 1).astype(F32)
    reach = reach * reach
    pattern = jnp.concatenate([pattern_ref[i] for i in range(BLK_X)], axis=0).astype(F32)
    slots = [jnp.broadcast_to(pattern[:, p : p + 1], shape) for p in range(PATTERN)]

    for t in range(9):
        iy, ix = t // 3, t % 3
        dx, dy = offset(ix, tile_x), offset(iy, tile_y)
        at_x, at_y = tile_x + dx, tile_y + dy
        valid = (at_x >= 0) & (at_x < count_x) & (at_y >= 0) & (at_y < count_y)
        at_x = jnp.clip(at_x, 0, count_x - 1)
        at_y = jnp.clip(at_y, 0, count_y - 1)
        obs = obs_ref[at_x, pl.ds(at_y, 1), :]
        step_x = dx * BLK_X + (obs >> 2) - (block >> 2)
        step_y = dy * BLK_Y + (obs & 3) - (block & 3)
        inside = (jnp.abs(step_x) <= 2) & (jnp.abs(step_y) <= 2) & valid
        slot = (step_x + 2) * 5 + (step_y + 2)
        picked = jnp.zeros(shape, F32)
        for p in range(PATTERN):
            picked = jnp.where(slot == p, slots[p], picked)
        spread = (step_x * step_x + step_y * step_y).astype(F32)
        shaped = jnp.maximum(1.0 - spread / reach, 0.0)
        taper_ref[iy, ix] = jnp.where(inside, picked, 0.0) * shaped / (members - 1)


def prepare(by_block, taper_radius, taper_pattern, obs_block):
    members = by_block.shape[1]
    return pl.pallas_call(
        prepare_kernel,
        out_shape=(
            jax.ShapeDtypeStruct((BLOCKS, CELLS, members), BF16),
            jax.ShapeDtypeStruct((3, 3, BLOCKS, OBS_TILE), F32),
        ),
        in_specs=[pl.BlockSpec(memory_space=pltpu.VMEM)] + [pl.BlockSpec(memory_space=pltpu.HBM)] * 3,
        out_specs=(pl.BlockSpec(memory_space=pltpu.VMEM), pl.BlockSpec(memory_space=pltpu.VMEM)),
        scratch_shapes=[
            pltpu.SMEM(taper_radius.shape, jnp.int32),
            pltpu.VMEM(taper_pattern.shape, jnp.int32),
            pltpu.VMEM(obs_block.shape, jnp.int32),
            pltpu.SemaphoreType.DMA((3,)),
        ],
        compiler_params=pltpu.CompilerParams(vmem_limit_bytes=16 * 2**20),
        cost_estimate=pl.CostEstimate(flops=4_000_000, bytes_accessed=1_000_000, transcendentals=0),
        name="prepare",
    )(by_block, *in_hbm(taper_radius, taper_pattern, obs_block))


def moved(b, which, turned_ref, taper_ref, tiles_refs):
    members = turned_ref.shape[2]
    turned = turned_ref[pl.ds(b, 2)].reshape(2 * CELLS, members)
    total, first = 0.0, 0
    for tiles_ref in tiles_refs:
        count = tiles_ref.shape[2] // OBS_TILE
        cross = dot(turned, tiles_ref[0], ((1,), (0,)))
        gains = []
        for k in range(2):
            tapers = [taper_ref[which, ix, pl.ds(b + k, 1), :] for ix in range(first, first + count)]
            gains.append((cross[k * CELLS : (k + 1) * CELLS] * jnp.concatenate(tapers, axis=1)).astype(BF16))
        total = total + dot(tiles_ref[1], jnp.concatenate(gains, axis=0), ((1,), (1,)))
        first += count
    return total


def first_of(side, tile_y):
    return 2 * ((tile_y & 1) ^ 1 ^ side)


def block_of(k, side, tile_y):
    return (k >> 1) * BLK_Y + first_of(side, tile_y) + (k & 1)


def target(chip, r, chips):
    return chip ^ r if chips & (chips - 1) == 0 else (chip + r) % chips


def source(chip, r, chips):
    return chip ^ r if chips & (chips - 1) == 0 else (chip + chips - r) % chips


def put(piece_refs, rows_ref, k, updated):
    chips, share = len(piece_refs), piece_refs[0].shape[2]
    mine = lax.axis_index("gy")
    rows_ref[k] = updated
    for r, ref in enumerate(piece_refs):
        for flip in (0, 1):
            owner = 2 * target(mine >> 1, r, chips) + ((mine & 1) ^ flip)
            ref[flip, k] = rows_ref[k, pl.ds(pl.multiple_of(owner * share, share), share), :]


def near_kernel(params_ref, turned_ref, taper_ref, own_ref, even_ref, part_ref, *refs):
    piece_refs, rows_ref = refs[:-1], refs[-1]
    tile_y = lax.axis_index("gy")
    for k in range(0, SIDE, 2):
        b = block_of(k, 0, tile_y)
        delta = moved(b, 0, turned_ref, taper_ref, [own_ref]) + moved(b, 1, turned_ref, taper_ref, [even_ref])
        for j in range(2):
            half = delta[:, j * CELLS : (j + 1) * CELLS]
            put(piece_refs, rows_ref, k + j, (params_ref[b + j].astype(F32) + half).astype(BF16))
    for k in range(0, SIDE, 2):
        b = block_of(k, 1, tile_y)
        delta = moved(b, 0, turned_ref, taper_ref, [own_ref])
        for j in range(2):
            part_ref[k + j] = params_ref[b + j].astype(F32) + delta[:, j * CELLS : (j + 1) * CELLS]


def far_kernel(turned_ref, taper_ref, odd_ref, beside_ref, part_ref, first_ref, last_ref, *refs):
    rows_ref, refs = refs[-1], refs[:-1]
    piece_refs = [halves(ref)[-1] for ref in refs]
    refs[1][0] = first_ref[...]
    refs[-1][0] = last_ref[...]
    tile_y = lax.axis_index("gy")
    for k in range(0, SIDE, 2):
        delta = moved(block_of(k, 1, tile_y), 2, turned_ref, taper_ref, [odd_ref, beside_ref])
        for j in range(2):
            half = delta[:, j * CELLS : (j + 1) * CELLS]
            put(piece_refs, rows_ref, k + j, (part_ref[k + j] + half).astype(BF16))


def pack_kernel(*refs):
    at = 0
    for ref in refs[:-1]:
        for piece in halves(ref):
            refs[-1][at] = piece[1]
            at += 1


def halves(ref):
    return [ref] if len(ref.shape) == 4 else [ref.at[side] for side in range(ref.shape[0])]


def settle(chips, sides, refs, rows_ref):
    even_ref, pieces = refs[0], [piece for ref in refs[1:] for piece in halves(ref)]
    share = even_ref.shape[2]
    mine = lax.axis_index("gy")
    chip, core = mine >> 1, mine & 1
    line = 2 * chips * BLK_Y
    for at, ((side, r), own) in enumerate(zip(sides, pieces)):
        for flip in (0, 1):
            other = core ^ flip
            tile = 2 * source(chip, r, chips) + other
            for k in range(SIDE):
                piece = even_ref[at, k] if flip else own[0, k]
                start = (k >> 1) * line + tile * BLK_Y + first_of(side, other) + (k & 1)
                rows_ref[pl.ds(start, share, stride=BLK_X * line), :] = piece.astype(F32)


def early_kernel(chips, *refs):
    settle(chips, [(0, 0), (1, 0)] + [(0, r) for r in range(2, chips - 1)], refs[:-1], refs[-1])


def late_kernel(chips, *refs):
    late_refs, out_hbm, rows_ref, out_ref, sems = refs[1:-4], *refs[-4:]
    sides = [(side, r) for r in range(chips - 1, 0, -1) for side in ((0, 1) if r in (1, chips - 1) else (1,))]
    settle(chips, sides, late_refs, rows_ref)
    pieces = sems.shape[0]
    step = rows_ref.shape[0] // pieces
    copies = []
    for p in range(pieces):
        place = slice(p * step, (p + 1) * step)
        out_ref[place] = rows_ref[place].astype(BF16)
        copies.append(pltpu.make_async_copy(out_ref.at[pl.ds(p * step, step)], out_hbm.at[pl.ds(p * step, step)], sems.at[p]))
        copies[-1].start()
    for copy in copies:
        copy.wait()


VMEM = pl.BlockSpec(memory_space=pltpu.VMEM)
LONG = pl.CostEstimate(flops=4_000_000_000, bytes_accessed=10_000_000, transcendentals=0)
LIMIT = pltpu.CompilerParams(vmem_limit_bytes=24 * 2**20)


def update_near(by_block, turned, taper, own, even, parts):
    members = by_block.shape[1]
    pieces = [jax.ShapeDtypeStruct((2, SIDE, members // parts, CELLS), BF16)] * (parts // 2)
    return pl.pallas_call(
        near_kernel,
        out_shape=(jax.ShapeDtypeStruct((SIDE, members, CELLS), F32), *pieces),
        in_specs=[VMEM] * 5,
        out_specs=(VMEM,) * (1 + len(pieces)),
        scratch_shapes=[pltpu.VMEM((SIDE, members, CELLS), BF16)],
        compiler_params=LIMIT,
        cost_estimate=LONG,
        name="near",
    )(by_block, turned, taper, own, even)


def update_far(turned, taper, odd, beside, part, near):
    members = part.shape[1]
    chips = len(near)
    piece = jax.ShapeDtypeStruct(near[0].shape, BF16)
    both = jax.ShapeDtypeStruct((2, *piece.shape), BF16)
    shapes = [both if r in (1, chips - 1) else piece for r in range(chips)]
    return pl.pallas_call(
        far_kernel,
        out_shape=tuple(shapes),
        in_specs=[VMEM] * 7,
        out_specs=(VMEM,) * chips,
        scratch_shapes=[pltpu.VMEM((SIDE, members, CELLS), BF16)],
        compiler_params=LIMIT,
        cost_estimate=LONG,
        name="far",
    )(turned, taper, odd, beside, part, near[1], near[-1])


def pack(pieces):
    count = sum(1 if piece.ndim == 4 else piece.shape[0] for piece in pieces)
    return pl.pallas_call(
        pack_kernel,
        out_shape=jax.ShapeDtypeStruct((count, *pieces[-1].shape[-3:]), BF16),
        in_specs=[VMEM] * len(pieces),
        out_specs=VMEM,
        compiler_params=LIMIT,
        name="pack",
    )(*pieces)


def gather(chips, early_even, early, late_even, late):
    share = early[0].shape[2]
    rows = share * BLOCKS * 2 * chips
    placed = pl.pallas_call(
        functools.partial(early_kernel, chips),
        out_shape=jax.ShapeDtypeStruct((rows, CELLS), F32),
        in_specs=[VMEM] * (1 + len(early)),
        out_specs=VMEM,
        compiler_params=LIMIT,
        name="early",
    )(early_even, *early)
    out, _ = pl.pallas_call(
        functools.partial(late_kernel, chips),
        out_shape=(jax.ShapeDtypeStruct((rows, CELLS), BF16), jax.ShapeDtypeStruct((rows, CELLS), F32)),
        in_specs=[VMEM] * (2 + len(late)),
        out_specs=(pl.BlockSpec(memory_space=pl.ANY), VMEM),
        scratch_shapes=[
            pltpu.VMEM((rows, CELLS), BF16),
            pltpu.SemaphoreType.DMA((4,)),
        ],
        input_output_aliases={0: 1},
        compiler_params=LIMIT,
        name="late",
    )(placed, late_even, *late)
    return out.reshape(share, BLK_X, 2 * chips * BLK_Y, CELLS)


def swap(block, axis):
    return lax.ppermute(block, axis, [(i, i ^ 1) for i in range(lax.axis_size(axis))])


def swap_odd(block, axis):
    rows, count = lax.axis_size("gx"), lax.axis_size("gy")
    pairs = []
    for x in range(rows):
        for y in range(count):
            if axis == "gy":
                to = (x, y + 1 if y % 2 else y - 1)
                to = to if 0 <= to[1] < count else (x ^ 1, y)
            else:
                to = (x + 1 if x % 2 else x - 1, y)
                to = to if 0 <= to[0] < rows else (x, y ^ 1)
            pairs.append((x * count + y, to[0] * count + to[1]))
    return lax.ppermute(block, ("gx", "gy"), pairs)


def hop(piece, r):
    count = lax.axis_size("gy")
    pairs = [(i, 2 * target(i // 2, r, count // 2) + i % 2) for i in range(count)]
    return lax.ppermute(piece, "gy", pairs)


def per_device(
    params,
    predicted,
    measured_value,
    measurement_variance,
    observation_jitter,
    obs_block,
    taper_radius,
    taper_pattern,
):
    members = params.shape[0]
    parts = lax.axis_size("gy")
    own, params = weigh(
        predicted, measured_value, measurement_variance, observation_jitter, obs_block, params
    )
    by_block = params.reshape(members, BLOCKS, CELLS).transpose(1, 0, 2)
    sent, by_block = lax.optimization_barrier((own, by_block))
    across = swap_odd(sent, "gy")
    even = swap(own, "gx")
    odd = swap_odd(own, "gx")
    turned, taper = prepare(by_block, taper_radius, taper_pattern, obs_block)
    beside, column = jnp.concatenate([even, odd], axis=2), jnp.concatenate([own, even, odd], axis=2)
    beside, column, across, turned, taper = lax.optimization_barrier((beside, column, across, turned, taper))
    even = swap(column, "gy")
    beside = swap_odd(beside, "gy")
    part, *near = update_near(by_block, turned, taper, column, even, parts)
    chips = parts // 2
    near_hops = [hop(near[r], r) for r in range(2, chips - 1)]
    far = list(update_far(turned, taper, across, beside, part, near))
    for r in range(2, chips - 1):
        far[r], near_hops[r - 2] = lax.optimization_barrier((far[r], near_hops[r - 2]))
    early = [near[0], far[0], *near_hops]
    late = [hop(far[r], r) for r in range(chips - 1, 0, -1)]
    early_even = swap(pack(early), "gy")
    late, early_even = lax.optimization_barrier((late, early_even))
    late_even = swap(pack(late), "gy")
    return gather(chips, early_even, early, late_even, late)


def solution(mesh):
    placed = (
        P(None, "gx", "gy", None),
        P("gx", "gy", None, None),
        P("gx", "gy", None),
        P("gx", "gy", None),
        P("gx", "gy", None, None),
        P(),
        P("gx", "gy"),
        P("gx", "gy", None),
    )
    return jax.shard_map(
        per_device, mesh=mesh, in_specs=placed, out_specs=P("gy", "gx", None, None), check_vma=False
    )
```

```python
import functools

import jax
import jax.numpy as jnp
from jax import lax
from jax.experimental import pallas as pl
from jax.experimental.pallas import tpu as pltpu
from jax.sharding import PartitionSpec as P

CELLS = 128
BLK_X = 2
BLK_Y = 4
BLOCKS = BLK_X * BLK_Y
SIDE = BLOCKS // 2
OBS_TILE = 128
PATTERN = 25
SMALL = 32

F32 = jnp.float32
BF16 = jnp.bfloat16


def iota(shape, dim):
    return lax.broadcasted_iota(jnp.int32, shape, dim)


def split3(x):
    high = x.astype(BF16)
    rest = x - high.astype(F32)
    mid = rest.astype(BF16)
    low = (rest - mid.astype(F32)).astype(BF16)
    return high, mid, low


def dot(a, b, dims):
    return lax.dot_general(a, b, (dims, ((), ())), preferred_element_type=F32)


def sweep(rows, count, x_ref, idx_ref, rank, size):
    row = iota((rows, OBS_TILE), 0)
    exists = row < size

    def taken(spread, indices):
        return jnp.take_along_axis(spread, indices, axis=1, mode="promise_in_bounds")

    def step(k, carry):
        t = 2 * k
        u = t + 1
        row_t, row_u = x_ref[pl.ds(t, 1), :], x_ref[pl.ds(u, 1), :]
        spread_t = jnp.broadcast_to(row_t, (rows, OBS_TILE))
        spread_u = jnp.broadcast_to(row_u, (rows, OBS_TILE))
        at_t = jnp.broadcast_to(idx_ref[pl.ds(t, 1), :], (8, OBS_TILE))
        at_u = jnp.broadcast_to(idx_ref[pl.ds(u, 1), :], (8, OBS_TILE))
        has_t, has_u = t < size, u < size
        a = jnp.where(has_t, taken(spread_t[0:8], at_t)[0:1], 1.0)
        b = jnp.where(has_u, taken(spread_t[0:8], at_u)[0:1], 0.0)
        d = jnp.where(has_u, taken(spread_u[0:8], at_u)[0:1], 1.0)
        own_t, own_u = rank == t, rank == u
        own = own_t | own_u
        head_t = jnp.where(own, jnp.where(own_t, -1.0, 0.0), row_t)
        head_u = jnp.where(own, jnp.where(own_u, -1.0, 0.0), row_u)
        inverse = 1.0 / a
        factor = b * inverse
        scaled_u = (head_u - factor * head_t) / (d - b * factor)
        scaled_t = head_t * inverse - factor * scaled_u
        column_t = jnp.where(exists, taken(spread_t, idx_ref[0:rows, :]), 0.0)
        column_u = jnp.where(exists, taken(spread_u, idx_ref[0:rows, :]), 0.0)
        on_t, on_u = row == t, row == u
        on = on_t | on_u
        column_t = jnp.where(on, jnp.where(on_t, -1.0, 0.0), column_t)
        column_u = jnp.where(on, jnp.where(on_u, -1.0, 0.0), column_u)
        x = jnp.where(on | own, 0.0, x_ref[0:rows, :])
        x_ref[0:rows, :] = x - column_t * scaled_t - column_u * scaled_u
        return carry

    lax.fori_loop(0, (count + 1) // 2, step, 0)


def in_hbm(*arrays):
    return [pltpu.with_memory_space_constraint(array, pltpu.HBM) for array in arrays]


def fetch(pairs, sems):
    copies = [pltpu.make_async_copy(src, dst, sems.at[k]) for k, (src, dst) in enumerate(pairs)]
    for copy in copies:
        copy.start()
    return copies


def weigh_kernel(
    pred_hbm, mv_hbm, var_hbm, jit_hbm, obs_hbm, params_hbm, out_ref, params_ref,
    pred_ref, mv_ref, var_ref, jit_ref, obs_ref, x_ref, idx_ref, full_ref, sems,
):
    members = pred_ref.shape[0]
    tile_x = lax.axis_index("gx")
    tile_y = lax.axis_index("gy")
    square = (OBS_TILE, OBS_TILE)
    pairs = [
        (pred_hbm.at[0, 0], pred_ref),
        (obs_hbm.at[tile_x], obs_ref),
        (var_hbm.at[0], var_ref),
        (mv_hbm.at[0], mv_ref),
        (jit_hbm.at[0, 0], jit_ref),
        (params_hbm, params_ref),
    ]
    copies = fetch(pairs, sems)
    for copy in copies[:3]:
        copy.wait()
    pred = pred_ref[...]
    var = var_ref[...]
    mean = jnp.sum(pred, axis=0, keepdims=True) / members
    deviation = (pred - mean).astype(BF16)
    out_ref[0] = deviation
    obs = obs_ref[pl.ds(tile_y, 1), :]
    groups = (iota((BLOCKS, OBS_TILE), 0) == obs).astype(BF16)
    same = dot(groups, groups, ((0,), (0,)))
    gram = dot(deviation, deviation, ((0,), (0,))) / (members - 1)
    row, col = iota(square, 0), iota(square, 1)
    system = jnp.where(same > 0.5, gram, 0.0) + jnp.where(row == col, var, 0.0)
    size = jnp.sum(same, axis=0, keepdims=True)
    count = jnp.max(size).astype(jnp.int32)
    size = size.astype(jnp.int32)
    rank = jnp.sum(jnp.where(row < col, same, 0.0), axis=0, keepdims=True).astype(jnp.int32)
    place = row == rank
    hot = place.astype(BF16)
    x_ref[...] = dot(jnp.concatenate([hot] * 3, axis=1), jnp.concatenate(split3(system), axis=0), ((1,), (0,)))
    numbered = jnp.where(place, col, 0).astype(F32).astype(BF16)
    idx_ref[...] = dot(numbered, same.astype(BF16), ((1,), (0,))).astype(jnp.int32)

    def solve(rows):
        sweep(rows, count, x_ref, idx_ref, rank, size)
        taken = jnp.concatenate([hot[0:rows]] * 3, axis=0)
        full = dot(taken, jnp.concatenate(split3(x_ref[0:rows, :]), axis=0), ((0,), (0,)))
        full_ref[...] = jnp.where(same > 0.5, -full, 0.0)

    @pl.when(count <= SMALL)
    def _():
        solve(SMALL)

    @pl.when(count > SMALL)
    def _():
        solve(OBS_TILE)

    for copy in copies[3:]:
        copy.wait()
    innovation = mv_ref[...] + jnp.sqrt(var) * jit_ref[...] - pred
    high, mid, low = split3(innovation)
    full_high, full_mid, full_low = split3(full_ref[...])
    left = jnp.concatenate([low, mid, high, mid, high, high], axis=1)
    right = jnp.concatenate([full_high, full_mid, full_low, full_high, full_mid, full_high], axis=0)
    weighted = dot(left, right, ((1,), (0,)))
    out_ref[1] = weighted.astype(BF16)


def weigh(predicted, measured_value, measurement_variance, observation_jitter, obs_block, params):
    members = predicted.shape[2]
    return pl.pallas_call(
        weigh_kernel,
        out_shape=(jax.ShapeDtypeStruct((2, members, OBS_TILE), BF16), jax.ShapeDtypeStruct(params.shape, BF16)),
        in_specs=[pl.BlockSpec(memory_space=pltpu.HBM)] * 6,
        out_specs=(pl.BlockSpec(memory_space=pltpu.VMEM), pl.BlockSpec(memory_space=pltpu.VMEM)),
        scratch_shapes=[
            pltpu.VMEM((members, OBS_TILE), F32),
            pltpu.VMEM((1, OBS_TILE), F32),
            pltpu.VMEM((1, OBS_TILE), F32),
            pltpu.VMEM((members, OBS_TILE), F32),
            pltpu.VMEM((obs_block.shape[1], OBS_TILE), jnp.int32),
            pltpu.VMEM((OBS_TILE, OBS_TILE), F32),
            pltpu.VMEM((OBS_TILE, OBS_TILE), jnp.int32),
            pltpu.VMEM((OBS_TILE, OBS_TILE), F32),
            pltpu.SemaphoreType.DMA((6,)),
        ],
        compiler_params=pltpu.CompilerParams(vmem_limit_bytes=16 * 2**20),
        name="weigh",
    )(*in_hbm(predicted, measured_value, measurement_variance, observation_jitter, obs_block, params))


def offset(which, place):
    even = 1 - 2 * (place & 1)
    return (0, even, -even)[which]


def prepare_kernel(
    params_ref, radius_hbm, pattern_hbm, obs_hbm, turned_ref, taper_ref, radius_ref, pattern_ref, obs_ref, sems
):
    members = params_ref.shape[1]
    tile_x = lax.axis_index("gx")
    tile_y = lax.axis_index("gy")
    count_x, count_y = obs_ref.shape[0], obs_ref.shape[1]
    copies = fetch([(radius_hbm, radius_ref), (pattern_hbm, pattern_ref), (obs_hbm, obs_ref)], sems)

    for b in range(BLOCKS):
        block = params_ref[b].astype(F32)
        mean = jnp.sum(block, axis=0, keepdims=True) / members
        turned_ref[b] = (block - mean).T.astype(BF16)
    for copy in copies:
        copy.wait()
    shape = (BLOCKS, OBS_TILE)
    block = iota(shape, 0)
    radius = jnp.zeros(shape, jnp.int32)
    for b in range(BLOCKS):
        radius = jnp.where(block == b, radius_ref[b // BLK_Y, b % BLK_Y], radius)
    reach = (radius + 1).astype(F32)
    reach = reach * reach
    pattern = jnp.concatenate([pattern_ref[i] for i in range(BLK_X)], axis=0).astype(F32)
    slots = [jnp.broadcast_to(pattern[:, p : p + 1], shape) for p in range(PATTERN)]

    for t in range(9):
        iy, ix = t // 3, t % 3
        dx, dy = offset((0, 2, 1)[ix], tile_x), offset(iy, tile_y)
        at_x, at_y = tile_x + dx, tile_y + dy
        valid = (at_x >= 0) & (at_x < count_x) & (at_y >= 0) & (at_y < count_y)
        at_x = jnp.clip(at_x, 0, count_x - 1)
        at_y = jnp.clip(at_y, 0, count_y - 1)
        obs = obs_ref[at_x, pl.ds(at_y, 1), :]
        step_x = dx * BLK_X + (obs >> 2) - (block >> 2)
        step_y = dy * BLK_Y + (obs & 3) - (block & 3)
        inside = (jnp.abs(step_x) <= 2) & (jnp.abs(step_y) <= 2) & valid
        slot = (step_x + 2) * 5 + (step_y + 2)
        picked = jnp.zeros(shape, F32)
        for p in range(PATTERN):
            picked = jnp.where(slot == p, slots[p], picked)
        spread = (step_x * step_x + step_y * step_y).astype(F32)
        shaped = jnp.maximum(1.0 - spread / reach, 0.0)
        taper_ref[iy, ix] = jnp.where(inside, picked, 0.0) * shaped / (members - 1)


def prepare(by_block, taper_radius, taper_pattern, obs_block):
    members = by_block.shape[1]
    return pl.pallas_call(
        prepare_kernel,
        out_shape=(
            jax.ShapeDtypeStruct((BLOCKS, CELLS, members), BF16),
            jax.ShapeDtypeStruct((3, 3, BLOCKS, OBS_TILE), F32),
        ),
        in_specs=[pl.BlockSpec(memory_space=pltpu.VMEM)] + [pl.BlockSpec(memory_space=pltpu.HBM)] * 3,
        out_specs=(pl.BlockSpec(memory_space=pltpu.VMEM), pl.BlockSpec(memory_space=pltpu.VMEM)),
        scratch_shapes=[
            pltpu.SMEM(taper_radius.shape, jnp.int32),
            pltpu.VMEM(taper_pattern.shape, jnp.int32),
            pltpu.VMEM(obs_block.shape, jnp.int32),
            pltpu.SemaphoreType.DMA((3,)),
        ],
        compiler_params=pltpu.CompilerParams(vmem_limit_bytes=16 * 2**20),
        cost_estimate=pl.CostEstimate(flops=4_000_000, bytes_accessed=1_000_000, transcendentals=0),
        name="prepare",
    )(by_block, *in_hbm(taper_radius, taper_pattern, obs_block))


def moved(b, which, turned_ref, taper_ref, tiles_refs):
    members = turned_ref.shape[2]
    turned = turned_ref[pl.ds(b, 2)].reshape(2 * CELLS, members)
    total, first = 0.0, 0
    for tiles_ref in tiles_refs:
        count = tiles_ref.shape[2] // OBS_TILE
        cross = dot(turned, tiles_ref[0], ((1,), (0,)))
        gains = []
        for k in range(2):
            tapers = [taper_ref[which, ix, pl.ds(b + k, 1), :] for ix in range(first, first + count)]
            gains.append((cross[k * CELLS : (k + 1) * CELLS] * jnp.concatenate(tapers, axis=1)).astype(BF16))
        total = total + dot(tiles_ref[1], jnp.concatenate(gains, axis=0), ((1,), (1,)))
        first += count
    return total


def first_of(side, tile_y):
    return 2 * ((tile_y & 1) ^ 1 ^ side)


def block_of(k, side, tile_y):
    return (k >> 1) * BLK_Y + first_of(side, tile_y) + (k & 1)


def target(chip, r, chips):
    return chip ^ r if chips & (chips - 1) == 0 else (chip + r) % chips


def source(chip, r, chips):
    return chip ^ r if chips & (chips - 1) == 0 else (chip + chips - r) % chips


def put(piece_refs, rows_ref, k, updated):
    chips, share = len(piece_refs), piece_refs[0].shape[2]
    mine = lax.axis_index("gy")
    rows_ref[k] = updated
    for r, ref in enumerate(piece_refs):
        for flip in (0, 1):
            owner = 2 * target(mine >> 1, r, chips) + ((mine & 1) ^ flip)
            ref[flip, k] = rows_ref[k, pl.ds(pl.multiple_of(owner * share, share), share), :]


def near_kernel(params_ref, turned_ref, taper_ref, own_ref, even_ref, part_ref, *refs):
    piece_refs, rows_ref = refs[:-1], refs[-1]
    tile_y = lax.axis_index("gy")
    for k in range(0, SIDE, 2):
        b = block_of(k, 0, tile_y)
        delta = moved(b, 0, turned_ref, taper_ref, [own_ref]) + moved(b, 1, turned_ref, taper_ref, [even_ref])
        for j in range(2):
            half = delta[:, j * CELLS : (j + 1) * CELLS]
            put(piece_refs, rows_ref, k + j, (params_ref[b + j].astype(F32) + half).astype(BF16))
    for k in range(0, SIDE, 2):
        b = block_of(k, 1, tile_y)
        delta = moved(b, 0, turned_ref, taper_ref, [own_ref])
        for j in range(2):
            part_ref[k + j] = params_ref[b + j].astype(F32) + delta[:, j * CELLS : (j + 1) * CELLS]


def far_kernel(turned_ref, taper_ref, odd_ref, beside_ref, part_ref, first_ref, last_ref, *refs):
    rows_ref, refs = refs[-1], refs[:-1]
    piece_refs = [halves(ref)[-1] for ref in refs]
    refs[1][0] = first_ref[...]
    refs[-1][0] = last_ref[...]
    tile_y = lax.axis_index("gy")
    for k in range(0, SIDE, 2):
        delta = moved(block_of(k, 1, tile_y), 2, turned_ref, taper_ref, [odd_ref, beside_ref])
        for j in range(2):
            half = delta[:, j * CELLS : (j + 1) * CELLS]
            put(piece_refs, rows_ref, k + j, (part_ref[k + j] + half).astype(BF16))


def pack_kernel(*refs):
    at = 0
    for ref in refs[:-1]:
        for piece in halves(ref):
            refs[-1][at] = piece[1]
            at += 1


def halves(ref):
    return [ref] if len(ref.shape) == 4 else [ref.at[side] for side in range(ref.shape[0])]


def settle(chips, sides, refs, rows_ref):
    even_ref, pieces = refs[0], [piece for ref in refs[1:] for piece in halves(ref)]
    share = even_ref.shape[2]
    mine = lax.axis_index("gy")
    chip, core = mine >> 1, mine & 1
    line = 2 * chips * BLK_Y
    for at, ((side, r), own) in enumerate(zip(sides, pieces)):
        for flip in (0, 1):
            other = core ^ flip
            tile = 2 * source(chip, r, chips) + other
            for k in range(SIDE):
                piece = even_ref[at, k] if flip else own[0, k]
                start = (k >> 1) * line + tile * BLK_Y + first_of(side, other) + (k & 1)
                rows_ref[pl.ds(start, share, stride=BLK_X * line), :] = piece.astype(F32)


def early_kernel(chips, *refs):
    settle(chips, [(0, 0), (1, 0)] + [(0, r) for r in range(2, chips - 1)], refs[:-1], refs[-1])


def late_kernel(chips, *refs):
    late_refs, out_hbm, rows_ref, out_ref, sems = refs[1:-4], *refs[-4:]
    sides = [(side, r) for r in range(chips - 1, 0, -1) for side in ((0, 1) if r in (1, chips - 1) else (1,))]
    settle(chips, sides, late_refs, rows_ref)
    pieces = sems.shape[0]
    step = rows_ref.shape[0] // pieces
    copies = []
    for p in range(pieces):
        place = slice(p * step, (p + 1) * step)
        out_ref[place] = rows_ref[place].astype(BF16)
        copies.append(pltpu.make_async_copy(out_ref.at[pl.ds(p * step, step)], out_hbm.at[pl.ds(p * step, step)], sems.at[p]))
        copies[-1].start()
    for copy in copies:
        copy.wait()


VMEM = pl.BlockSpec(memory_space=pltpu.VMEM)
LONG = pl.CostEstimate(flops=4_000_000_000, bytes_accessed=10_000_000, transcendentals=0)
LIMIT = pltpu.CompilerParams(vmem_limit_bytes=24 * 2**20)


def update_near(by_block, turned, taper, own, even, parts):
    members = by_block.shape[1]
    pieces = [jax.ShapeDtypeStruct((2, SIDE, members // parts, CELLS), BF16)] * (parts // 2)
    return pl.pallas_call(
        near_kernel,
        out_shape=(jax.ShapeDtypeStruct((SIDE, members, CELLS), F32), *pieces),
        in_specs=[VMEM] * 5,
        out_specs=(VMEM,) * (1 + len(pieces)),
        scratch_shapes=[pltpu.VMEM((SIDE, members, CELLS), BF16)],
        compiler_params=LIMIT,
        cost_estimate=LONG,
        name="near",
    )(by_block, turned, taper, own, even)


def update_far(turned, taper, odd, beside, part, near):
    members = part.shape[1]
    chips = len(near)
    piece = jax.ShapeDtypeStruct(near[0].shape, BF16)
    both = jax.ShapeDtypeStruct((2, *piece.shape), BF16)
    shapes = [both if r in (1, chips - 1) else piece for r in range(chips)]
    return pl.pallas_call(
        far_kernel,
        out_shape=tuple(shapes),
        in_specs=[VMEM] * 7,
        out_specs=(VMEM,) * chips,
        scratch_shapes=[pltpu.VMEM((SIDE, members, CELLS), BF16)],
        compiler_params=LIMIT,
        cost_estimate=LONG,
        name="far",
    )(turned, taper, odd, beside, part, near[1], near[-1])


def pack(pieces):
    count = sum(1 if piece.ndim == 4 else piece.shape[0] for piece in pieces)
    return pl.pallas_call(
        pack_kernel,
        out_shape=jax.ShapeDtypeStruct((count, *pieces[-1].shape[-3:]), BF16),
        in_specs=[VMEM] * len(pieces),
        out_specs=VMEM,
        compiler_params=LIMIT,
        name="pack",
    )(*pieces)


def gather(chips, early_even, early, late_even, late):
    share = early[0].shape[2]
    rows = share * BLOCKS * 2 * chips
    placed = pl.pallas_call(
        functools.partial(early_kernel, chips),
        out_shape=jax.ShapeDtypeStruct((rows, CELLS), F32),
        in_specs=[VMEM] * (1 + len(early)),
        out_specs=VMEM,
        compiler_params=LIMIT,
        name="early",
    )(early_even, *early)
    out, _ = pl.pallas_call(
        functools.partial(late_kernel, chips),
        out_shape=(jax.ShapeDtypeStruct((rows, CELLS), BF16), jax.ShapeDtypeStruct((rows, CELLS), F32)),
        in_specs=[VMEM] * (2 + len(late)),
        out_specs=(pl.BlockSpec(memory_space=pl.ANY), VMEM),
        scratch_shapes=[
            pltpu.VMEM((rows, CELLS), BF16),
            pltpu.SemaphoreType.DMA((4,)),
        ],
        input_output_aliases={0: 1},
        compiler_params=LIMIT,
        name="late",
    )(placed, late_even, *late)
    return out.reshape(share, BLK_X, 2 * chips * BLK_Y, CELLS)


def swap(block, axis):
    return lax.ppermute(block, axis, [(i, i ^ 1) for i in range(lax.axis_size(axis))])


def swap_odd(block, axis):
    rows, count = lax.axis_size("gx"), lax.axis_size("gy")
    pairs = []
    for x in range(rows):
        for y in range(count):
            if axis == "gy":
                to = (x, y + 1 if y % 2 else y - 1)
                to = to if 0 <= to[1] < count else (x ^ 1, y)
            else:
                to = (x + 1 if x % 2 else x - 1, y)
                to = to if 0 <= to[0] < rows else (x, y ^ 1)
            pairs.append((x * count + y, to[0] * count + to[1]))
    return lax.ppermute(block, ("gx", "gy"), pairs)


def hop(piece, r):
    count = lax.axis_size("gy")
    pairs = [(i, 2 * target(i // 2, r, count // 2) + i % 2) for i in range(count)]
    return lax.ppermute(piece, "gy", pairs)


def per_device(
    params,
    predicted,
    measured_value,
    measurement_variance,
    observation_jitter,
    obs_block,
    taper_radius,
    taper_pattern,
):
    members = params.shape[0]
    parts = lax.axis_size("gy")
    own, params = weigh(
        predicted, measured_value, measurement_variance, observation_jitter, obs_block, params
    )
    by_block = params.reshape(members, BLOCKS, CELLS).transpose(1, 0, 2)
    sent, by_block = lax.optimization_barrier((own, by_block))
    across = swap_odd(sent, "gy")
    odd = swap_odd(own, "gx")
    even = swap(own, "gx")
    turned, taper = prepare(by_block, taper_radius, taper_pattern, obs_block)
    beside, column = jnp.concatenate([odd, even], axis=2), jnp.concatenate([own, odd, even], axis=2)
    beside, column, across, turned, taper = lax.optimization_barrier((beside, column, across, turned, taper))
    even = swap(column, "gy")
    beside = swap_odd(beside, "gy")
    part, *near = update_near(by_block, turned, taper, column, even, parts)
    chips = parts // 2
    near_hops = [hop(near[r], r) for r in range(2, chips - 1)]
    far = list(update_far(turned, taper, across, beside, part, near))
    for r in range(2, chips - 1):
        far[r], near_hops[r - 2] = lax.optimization_barrier((far[r], near_hops[r - 2]))
    early = [near[0], far[0], *near_hops]
    late = [hop(far[r], r) for r in range(chips - 1, 0, -1)]
    early_even = swap(pack(early), "gy")
    late, early_even = lax.optimization_barrier((late, early_even))
    late_even = swap(pack(late), "gy")
    return gather(chips, early_even, early, late_even, late)


def solution(mesh):
    placed = (
        P(None, "gx", "gy", None),
        P("gx", "gy", None, None),
        P("gx", "gy", None),
        P("gx", "gy", None),
        P("gx", "gy", None, None),
        P(),
        P("gx", "gy"),
        P("gx", "gy", None),
    )
    return jax.shard_map(
        per_device, mesh=mesh, in_specs=placed, out_specs=P("gy", "gx", None, None), check_vma=False
    )
```

```python
import functools

import jax
import jax.numpy as jnp
from jax import lax
from jax.experimental import pallas as pl
from jax.experimental.pallas import tpu as pltpu
from jax.sharding import PartitionSpec as P

CELLS = 128
BLK_X = 2
BLK_Y = 4
BLOCKS = BLK_X * BLK_Y
SIDE = BLOCKS // 2
OBS_TILE = 128
PATTERN = 25
SMALL = 32

F32 = jnp.float32
BF16 = jnp.bfloat16


def iota(shape, dim):
    return lax.broadcasted_iota(jnp.int32, shape, dim)


def split3(x):
    high = x.astype(BF16)
    rest = x - high.astype(F32)
    mid = rest.astype(BF16)
    low = (rest - mid.astype(F32)).astype(BF16)
    return high, mid, low


def dot(a, b, dims):
    return lax.dot_general(a, b, (dims, ((), ())), preferred_element_type=F32)


def sweep(rows, count, x_ref, idx_ref, rank, size):
    row = iota((rows, OBS_TILE), 0)
    exists = row < size

    def taken(spread, indices):
        return jnp.take_along_axis(spread, indices, axis=1, mode="promise_in_bounds")

    def step(k, carry):
        t = 2 * k
        u = t + 1
        row_t, row_u = x_ref[pl.ds(t, 1), :], x_ref[pl.ds(u, 1), :]
        spread_t = jnp.broadcast_to(row_t, (rows, OBS_TILE))
        spread_u = jnp.broadcast_to(row_u, (rows, OBS_TILE))
        at_t = jnp.broadcast_to(idx_ref[pl.ds(t, 1), :], (8, OBS_TILE))
        at_u = jnp.broadcast_to(idx_ref[pl.ds(u, 1), :], (8, OBS_TILE))
        has_t, has_u = t < size, u < size
        a = jnp.where(has_t, taken(spread_t[0:8], at_t)[0:1], 1.0)
        b = jnp.where(has_u, taken(spread_t[0:8], at_u)[0:1], 0.0)
        d = jnp.where(has_u, taken(spread_u[0:8], at_u)[0:1], 1.0)
        own_t, own_u = rank == t, rank == u
        own = own_t | own_u
        head_t = jnp.where(own, jnp.where(own_t, -1.0, 0.0), row_t)
        head_u = jnp.where(own, jnp.where(own_u, -1.0, 0.0), row_u)
        inverse = 1.0 / a
        factor = b * inverse
        scaled_u = (head_u - factor * head_t) / (d - b * factor)
        scaled_t = head_t * inverse - factor * scaled_u
        column_t = jnp.where(exists, taken(spread_t, idx_ref[0:rows, :]), 0.0)
        column_u = jnp.where(exists, taken(spread_u, idx_ref[0:rows, :]), 0.0)
        on_t, on_u = row == t, row == u
        on = on_t | on_u
        column_t = jnp.where(on, jnp.where(on_t, -1.0, 0.0), column_t)
        column_u = jnp.where(on, jnp.where(on_u, -1.0, 0.0), column_u)
        x = jnp.where(on | own, 0.0, x_ref[0:rows, :])
        x_ref[0:rows, :] = x - column_t * scaled_t - column_u * scaled_u
        return carry

    lax.fori_loop(0, (count + 1) // 2, step, 0)


def in_hbm(*arrays):
    return [pltpu.with_memory_space_constraint(array, pltpu.HBM) for array in arrays]


def fetch(pairs, sems):
    copies = [pltpu.make_async_copy(src, dst, sems.at[k]) for k, (src, dst) in enumerate(pairs)]
    for copy in copies:
        copy.start()
    return copies


def weigh_kernel(
    pred_hbm, mv_hbm, var_hbm, jit_hbm, obs_hbm, params_hbm, out_ref, params_ref,
    pred_ref, mv_ref, var_ref, jit_ref, obs_ref, x_ref, idx_ref, full_ref, sems,
):
    members = pred_ref.shape[0]
    tile_x = lax.axis_index("gx")
    tile_y = lax.axis_index("gy")
    square = (OBS_TILE, OBS_TILE)
    pairs = [
        (pred_hbm.at[0, 0], pred_ref),
        (obs_hbm.at[tile_x], obs_ref),
        (var_hbm.at[0], var_ref),
        (mv_hbm.at[0], mv_ref),
        (jit_hbm.at[0, 0], jit_ref),
        (params_hbm, params_ref),
    ]
    copies = fetch(pairs, sems)
    for copy in copies[:3]:
        copy.wait()
    pred = pred_ref[...]
    var = var_ref[...]
    mean = jnp.sum(pred, axis=0, keepdims=True) / members
    deviation = (pred - mean).astype(BF16)
    out_ref[0] = deviation
    obs = obs_ref[pl.ds(tile_y, 1), :]
    groups = (iota((BLOCKS, OBS_TILE), 0) == obs).astype(BF16)
    same = dot(groups, groups, ((0,), (0,)))
    gram = dot(deviation, deviation, ((0,), (0,))) / (members - 1)
    row, col = iota(square, 0), iota(square, 1)
    system = jnp.where(same > 0.5, gram, 0.0) + jnp.where(row == col, var, 0.0)
    size = jnp.sum(same, axis=0, keepdims=True)
    count = jnp.max(size).astype(jnp.int32)
    size = size.astype(jnp.int32)
    rank = jnp.sum(jnp.where(row < col, same, 0.0), axis=0, keepdims=True).astype(jnp.int32)
    place = row == rank
    hot = place.astype(BF16)
    x_ref[...] = dot(jnp.concatenate([hot] * 3, axis=1), jnp.concatenate(split3(system), axis=0), ((1,), (0,)))
    numbered = jnp.where(place, col, 0).astype(F32).astype(BF16)
    idx_ref[...] = dot(numbered, same.astype(BF16), ((1,), (0,))).astype(jnp.int32)

    def solve(rows):
        sweep(rows, count, x_ref, idx_ref, rank, size)
        taken = jnp.concatenate([hot[0:rows]] * 3, axis=0)
        full = dot(taken, jnp.concatenate(split3(x_ref[0:rows, :]), axis=0), ((0,), (0,)))
        full_ref[...] = jnp.where(same > 0.5, -full, 0.0)

    @pl.when(count <= SMALL)
    def _():
        solve(SMALL)

    @pl.when(count > SMALL)
    def _():
        solve(OBS_TILE)

    for copy in copies[3:]:
        copy.wait()
    innovation = mv_ref[...] + jnp.sqrt(var) * jit_ref[...] - pred
    high, mid, low = split3(innovation)
    full_high, full_mid, full_low = split3(full_ref[...])
    left = jnp.concatenate([low, mid, high, mid, high, high], axis=1)
    right = jnp.concatenate([full_high, full_mid, full_low, full_high, full_mid, full_high], axis=0)
    weighted = dot(left, right, ((1,), (0,)))
    out_ref[1] = weighted.astype(BF16)


def weigh(predicted, measured_value, measurement_variance, observation_jitter, obs_block, params):
    members = predicted.shape[2]
    return pl.pallas_call(
        weigh_kernel,
        out_shape=(jax.ShapeDtypeStruct((2, members, OBS_TILE), BF16), jax.ShapeDtypeStruct(params.shape, BF16)),
        in_specs=[pl.BlockSpec(memory_space=pltpu.HBM)] * 6,
        out_specs=(pl.BlockSpec(memory_space=pltpu.VMEM), pl.BlockSpec(memory_space=pltpu.VMEM)),
        scratch_shapes=[
            pltpu.VMEM((members, OBS_TILE), F32),
            pltpu.VMEM((1, OBS_TILE), F32),
            pltpu.VMEM((1, OBS_TILE), F32),
            pltpu.VMEM((members, OBS_TILE), F32),
            pltpu.VMEM((obs_block.shape[1], OBS_TILE), jnp.int32),
            pltpu.VMEM((OBS_TILE, OBS_TILE), F32),
            pltpu.VMEM((OBS_TILE, OBS_TILE), jnp.int32),
            pltpu.VMEM((OBS_TILE, OBS_TILE), F32),
            pltpu.SemaphoreType.DMA((6,)),
        ],
        compiler_params=pltpu.CompilerParams(vmem_limit_bytes=16 * 2**20),
        name="weigh",
    )(*in_hbm(predicted, measured_value, measurement_variance, observation_jitter, obs_block, params))


def offset(which, place):
    even = 1 - 2 * (place & 1)
    return (0, even, -even)[which]


def prepare_kernel(
    params_ref, radius_hbm, pattern_hbm, obs_hbm, turned_ref, taper_ref, radius_ref, pattern_ref, obs_ref, sems
):
    members = params_ref.shape[1]
    tile_x = lax.axis_index("gx")
    tile_y = lax.axis_index("gy")
    count_x, count_y = obs_ref.shape[0], obs_ref.shape[1]
    copies = fetch([(radius_hbm, radius_ref), (pattern_hbm, pattern_ref), (obs_hbm, obs_ref)], sems)

    for b in range(BLOCKS):
        block = params_ref[b].astype(F32)
        mean = jnp.sum(block, axis=0, keepdims=True) / members
        turned_ref[b] = (block - mean).T.astype(BF16)
    for copy in copies:
        copy.wait()
    shape = (BLOCKS, OBS_TILE)
    block = iota(shape, 0)
    radius = jnp.zeros(shape, jnp.int32)
    for b in range(BLOCKS):
        radius = jnp.where(block == b, radius_ref[b // BLK_Y, b % BLK_Y], radius)
    reach = (radius + 1).astype(F32)
    reach = reach * reach
    pattern = jnp.concatenate([pattern_ref[i] for i in range(BLK_X)], axis=0).astype(F32)
    slots = [jnp.broadcast_to(pattern[:, p : p + 1], shape) for p in range(PATTERN)]

    for t in range(9):
        iy, ix = t // 3, t % 3
        dx, dy = offset(ix, tile_x), offset(iy, tile_y)
        at_x, at_y = tile_x + dx, tile_y + dy
        valid = (at_x >= 0) & (at_x < count_x) & (at_y >= 0) & (at_y < count_y)
        at_x = jnp.clip(at_x, 0, count_x - 1)
        at_y = jnp.clip(at_y, 0, count_y - 1)
        obs = obs_ref[at_x, pl.ds(at_y, 1), :]
        step_x = dx * BLK_X + (obs >> 2) - (block >> 2)
        step_y = dy * BLK_Y + (obs & 3) - (block & 3)
        inside = (jnp.abs(step_x) <= 2) & (jnp.abs(step_y) <= 2) & valid
        slot = (step_x + 2) * 5 + (step_y + 2)
        picked = jnp.zeros(shape, F32)
        for p in range(PATTERN):
            picked = jnp.where(slot == p, slots[p], picked)
        spread = (step_x * step_x + step_y * step_y).astype(F32)
        shaped = jnp.maximum(1.0 - spread / reach, 0.0)
        taper_ref[iy, ix] = jnp.where(inside, picked, 0.0) * shaped / (members - 1)


def prepare(by_block, taper_radius, taper_pattern, obs_block):
    members = by_block.shape[1]
    return pl.pallas_call(
        prepare_kernel,
        out_shape=(
            jax.ShapeDtypeStruct((BLOCKS, CELLS, members), BF16),
            jax.ShapeDtypeStruct((3, 3, BLOCKS, OBS_TILE), F32),
        ),
        in_specs=[pl.BlockSpec(memory_space=pltpu.VMEM)] + [pl.BlockSpec(memory_space=pltpu.HBM)] * 3,
        out_specs=(pl.BlockSpec(memory_space=pltpu.VMEM), pl.BlockSpec(memory_space=pltpu.VMEM)),
        scratch_shapes=[
            pltpu.SMEM(taper_radius.shape, jnp.int32),
            pltpu.VMEM(taper_pattern.shape, jnp.int32),
            pltpu.VMEM(obs_block.shape, jnp.int32),
            pltpu.SemaphoreType.DMA((3,)),
        ],
        compiler_params=pltpu.CompilerParams(vmem_limit_bytes=16 * 2**20),
        cost_estimate=pl.CostEstimate(flops=4_000_000, bytes_accessed=1_000_000, transcendentals=0),
        name="prepare",
    )(by_block, *in_hbm(taper_radius, taper_pattern, obs_block))


def moved(b, which, turned_ref, taper_ref, tiles_refs):
    members = turned_ref.shape[2]
    turned = turned_ref[pl.ds(b, 2)].reshape(2 * CELLS, members)
    total, first = 0.0, 0
    for tiles_ref in tiles_refs:
        count = tiles_ref.shape[2] // OBS_TILE
        cross = dot(turned, tiles_ref[0], ((1,), (0,)))
        gains = []
        for k in range(2):
            tapers = [taper_ref[which, ix, pl.ds(b + k, 1), :] for ix in range(first, first + count)]
            gains.append((cross[k * CELLS : (k + 1) * CELLS] * jnp.concatenate(tapers, axis=1)).astype(BF16))
        total = total + dot(tiles_ref[1], jnp.concatenate(gains, axis=0), ((1,), (1,)))
        first += count
    return total


def first_of(side, tile_y):
    return 2 * ((tile_y & 1) ^ 1 ^ side)


def block_of(k, side, tile_y):
    return (k >> 1) * BLK_Y + first_of(side, tile_y) + (k & 1)


def target(chip, r, chips):
    return chip ^ r if chips & (chips - 1) == 0 else (chip + r) % chips


def source(chip, r, chips):
    return chip ^ r if chips & (chips - 1) == 0 else (chip + chips - r) % chips


def put(piece_refs, rows_ref, k, updated):
    chips, share = len(piece_refs), piece_refs[0].shape[2]
    mine = lax.axis_index("gy")
    rows_ref[k] = updated
    for r, ref in enumerate(piece_refs):
        for flip in (0, 1):
            owner = 2 * target(mine >> 1, r, chips) + ((mine & 1) ^ flip)
            ref[flip, k] = rows_ref[k, pl.ds(pl.multiple_of(owner * share, share), share), :]


def near_kernel(params_ref, turned_ref, taper_ref, own_ref, even_ref, part_ref, *refs):
    piece_refs, rows_ref = refs[:-1], refs[-1]
    tile_y = lax.axis_index("gy")
    for k in range(0, SIDE, 2):
        b = block_of(k, 0, tile_y)
        delta = moved(b, 0, turned_ref, taper_ref, [own_ref]) + moved(b, 1, turned_ref, taper_ref, [even_ref])
        for j in range(2):
            half = delta[:, j * CELLS : (j + 1) * CELLS]
            put(piece_refs, rows_ref, k + j, (params_ref[b + j].astype(F32) + half).astype(BF16))
    for k in range(0, SIDE, 2):
        b = block_of(k, 1, tile_y)
        delta = moved(b, 0, turned_ref, taper_ref, [own_ref])
        for j in range(2):
            part_ref[k + j] = params_ref[b + j].astype(F32) + delta[:, j * CELLS : (j + 1) * CELLS]


def far_kernel(turned_ref, taper_ref, odd_ref, beside_ref, part_ref, first_ref, last_ref, *refs):
    rows_ref, refs = refs[-1], refs[:-1]
    piece_refs = [halves(ref)[-1] for ref in refs]
    refs[1][0] = first_ref[...]
    refs[-1][0] = last_ref[...]
    tile_y = lax.axis_index("gy")
    for k in range(0, SIDE, 2):
        delta = moved(block_of(k, 1, tile_y), 2, turned_ref, taper_ref, [odd_ref, beside_ref])
        for j in range(2):
            half = delta[:, j * CELLS : (j + 1) * CELLS]
            put(piece_refs, rows_ref, k + j, (part_ref[k + j] + half).astype(BF16))


def pack_kernel(*refs):
    at = 0
    for ref in refs[:-1]:
        for piece in halves(ref):
            refs[-1][at] = piece[1]
            at += 1


def halves(ref):
    return [ref] if len(ref.shape) == 4 else [ref.at[side] for side in range(ref.shape[0])]


def settle(chips, sides, refs, rows_ref):
    even_ref, pieces = refs[0], [piece for ref in refs[1:] for piece in halves(ref)]
    share = even_ref.shape[2]
    mine = lax.axis_index("gy")
    chip, core = mine >> 1, mine & 1
    line = 2 * chips * BLK_Y
    for at, ((side, r), own) in enumerate(zip(sides, pieces)):
        for flip in (0, 1):
            other = core ^ flip
            tile = 2 * source(chip, r, chips) + other
            for k in range(SIDE):
                piece = even_ref[at, k] if flip else own[0, k]
                start = (k >> 1) * line + tile * BLK_Y + first_of(side, other) + (k & 1)
                rows_ref[pl.ds(start, share, stride=BLK_X * line), :] = piece.astype(F32)


def early_kernel(chips, *refs):
    settle(chips, [(0, 0), (1, 0)] + [(0, r) for r in range(2, chips - 1)], refs[:-1], refs[-1])


def late_kernel(chips, *refs):
    late_refs, out_hbm, rows_ref, out_ref, sems = refs[1:-4], *refs[-4:]
    sides = [(side, r) for r in range(chips - 1, 0, -1) for side in ((0, 1) if r in (1, chips - 1) else (1,))]
    settle(chips, sides, late_refs, rows_ref)
    pieces = sems.shape[0]
    step = rows_ref.shape[0] // pieces
    copies = []
    for p in range(pieces):
        place = slice(p * step, (p + 1) * step)
        out_ref[place] = rows_ref[place].astype(BF16)
        copies.append(pltpu.make_async_copy(out_ref.at[pl.ds(p * step, step)], out_hbm.at[pl.ds(p * step, step)], sems.at[p]))
        copies[-1].start()
    for copy in copies:
        copy.wait()


VMEM = pl.BlockSpec(memory_space=pltpu.VMEM)
LONG = pl.CostEstimate(flops=4_000_000_000, bytes_accessed=10_000_000, transcendentals=0)
LIMIT = pltpu.CompilerParams(vmem_limit_bytes=24 * 2**20)


def update_near(by_block, turned, taper, own, even, parts):
    members = by_block.shape[1]
    pieces = [jax.ShapeDtypeStruct((2, SIDE, members // parts, CELLS), BF16)] * (parts // 2)
    return pl.pallas_call(
        near_kernel,
        out_shape=(jax.ShapeDtypeStruct((SIDE, members, CELLS), F32), *pieces),
        in_specs=[VMEM] * 5,
        out_specs=(VMEM,) * (1 + len(pieces)),
        scratch_shapes=[pltpu.VMEM((SIDE, members, CELLS), BF16)],
        compiler_params=LIMIT,
        cost_estimate=LONG,
        name="near",
    )(by_block, turned, taper, own, even)


def update_far(turned, taper, odd, beside, part, near):
    members = part.shape[1]
    chips = len(near)
    piece = jax.ShapeDtypeStruct(near[0].shape, BF16)
    both = jax.ShapeDtypeStruct((2, *piece.shape), BF16)
    shapes = [both if r in (1, chips - 1) else piece for r in range(chips)]
    return pl.pallas_call(
        far_kernel,
        out_shape=tuple(shapes),
        in_specs=[VMEM] * 7,
        out_specs=(VMEM,) * chips,
        scratch_shapes=[pltpu.VMEM((SIDE, members, CELLS), BF16)],
        compiler_params=LIMIT,
        cost_estimate=LONG,
        name="far",
    )(turned, taper, odd, beside, part, near[1], near[-1])


def pack(pieces):
    count = sum(1 if piece.ndim == 4 else piece.shape[0] for piece in pieces)
    return pl.pallas_call(
        pack_kernel,
        out_shape=jax.ShapeDtypeStruct((count, *pieces[-1].shape[-3:]), BF16),
        in_specs=[VMEM] * len(pieces),
        out_specs=VMEM,
        compiler_params=LIMIT,
        name="pack",
    )(*pieces)


def gather(chips, early_even, early, late_even, late):
    share = early[0].shape[2]
    rows = share * BLOCKS * 2 * chips
    placed = pl.pallas_call(
        functools.partial(early_kernel, chips),
        out_shape=jax.ShapeDtypeStruct((rows, CELLS), F32),
        in_specs=[VMEM] * (1 + len(early)),
        out_specs=VMEM,
        compiler_params=LIMIT,
        name="early",
    )(early_even, *early)
    out, _ = pl.pallas_call(
        functools.partial(late_kernel, chips),
        out_shape=(jax.ShapeDtypeStruct((rows, CELLS), BF16), jax.ShapeDtypeStruct((rows, CELLS), F32)),
        in_specs=[VMEM] * (2 + len(late)),
        out_specs=(pl.BlockSpec(memory_space=pl.ANY), VMEM),
        scratch_shapes=[
            pltpu.VMEM((rows, CELLS), BF16),
            pltpu.SemaphoreType.DMA((8,)),
        ],
        input_output_aliases={0: 1},
        compiler_params=LIMIT,
        name="late",
    )(placed, late_even, *late)
    return out.reshape(share, BLK_X, 2 * chips * BLK_Y, CELLS)


def swap(block, axis):
    return lax.ppermute(block, axis, [(i, i ^ 1) for i in range(lax.axis_size(axis))])


def swap_odd(block, axis):
    rows, count = lax.axis_size("gx"), lax.axis_size("gy")
    pairs = []
    for x in range(rows):
        for y in range(count):
            if axis == "gy":
                to = (x, y + 1 if y % 2 else y - 1)
                to = to if 0 <= to[1] < count else (x ^ 1, y)
            else:
                to = (x + 1 if x % 2 else x - 1, y)
                to = to if 0 <= to[0] < rows else (x, y ^ 1)
            pairs.append((x * count + y, to[0] * count + to[1]))
    return lax.ppermute(block, ("gx", "gy"), pairs)


def hop(piece, r):
    count = lax.axis_size("gy")
    pairs = [(i, 2 * target(i // 2, r, count // 2) + i % 2) for i in range(count)]
    return lax.ppermute(piece, "gy", pairs)


def per_device(
    params,
    predicted,
    measured_value,
    measurement_variance,
    observation_jitter,
    obs_block,
    taper_radius,
    taper_pattern,
):
    members = params.shape[0]
    parts = lax.axis_size("gy")
    own, params = weigh(
        predicted, measured_value, measurement_variance, observation_jitter, obs_block, params
    )
    by_block = params.reshape(members, BLOCKS, CELLS).transpose(1, 0, 2)
    sent, by_block = lax.optimization_barrier((own, by_block))
    across = swap_odd(sent, "gy")
    even = swap(own, "gx")
    odd = swap_odd(own, "gx")
    turned, taper = prepare(by_block, taper_radius, taper_pattern, obs_block)
    beside, column = jnp.concatenate([even, odd], axis=2), jnp.concatenate([own, even, odd], axis=2)
    beside, column, across, turned, taper = lax.optimization_barrier((beside, column, across, turned, taper))
    even = swap(column, "gy")
    beside = swap_odd(beside, "gy")
    part, *near = update_near(by_block, turned, taper, column, even, parts)
    chips = parts // 2
    near_hops = [hop(near[r], r) for r in range(2, chips - 1)]
    far = list(update_far(turned, taper, across, beside, part, near))
    for r in range(2, chips - 1):
        far[r], near_hops[r - 2] = lax.optimization_barrier((far[r], near_hops[r - 2]))
    early = [near[0], far[0], *near_hops]
    late = [hop(far[r], r) for r in range(chips - 1, 0, -1)]
    early_even = swap(pack(early), "gy")
    late, early_even = lax.optimization_barrier((late, early_even))
    late_even = swap(pack(late), "gy")
    return gather(chips, early_even, early, late_even, late)


def solution(mesh):
    placed = (
        P(None, "gx", "gy", None),
        P("gx", "gy", None, None),
        P("gx", "gy", None),
        P("gx", "gy", None),
        P("gx", "gy", None, None),
        P(),
        P("gx", "gy"),
        P("gx", "gy", None),
    )
    return jax.shard_map(
        per_device, mesh=mesh, in_specs=placed, out_specs=P("gy", "gx", None, None), check_vma=False
    )
```
